32 devices in a mesh: ctx: 16 (over z, x, core), grp: 2 (over y).
Axes of the slice: x: 2, y: 2, z: 4, core: 2. Of those that a mesh axis runs over, the one named last changes fastest.
Arguments:
- doc_lengths: int32 [8], replicated, may hold values from 1 to 2048, 4096 in all
- query_raw: bfloat16 [4096, 2048], P(('ctx', 'grp')), may hold values from -40 to 40
- key_raw: bfloat16 [4096, 1024], P(('ctx', 'grp')), may hold values from -40 to 40
- value_matrix: bfloat16 [4096, 1024], P(('ctx', 'grp')), may hold values from -5 to 5
- out_grad: bfloat16 [4096, 2048], P(('ctx', 'grp')), may hold values from -5 to 5
- query_gain: float32 [128], replicated, may hold values from 0.5 to 6
- key_gain: float32 [128], replicated, may hold values from 0.5 to 6
Outputs:
- grad_query: bfloat16 [4096, 2048], P(('ctx', 'grp'))
- grad_key: bfloat16 [4096, 1024], P(('ctx', 'grp'))
- grad_value: bfloat16 [4096, 1024], P(('ctx', 'grp'))
- grad_query_gain: float32 [128], replicated
- grad_key_gain: float32 [128], replicated
The draws below stay inside these ranges and needn't reach their ends.
Inputs may be any that keep to these rules, and one draw needn't show every extreme that they name: `doc_lengths`: lengths of the packed documents in order; they sum to 4096, and one of them is exactly 2048.
All inputs are finite; a program needn't handle non-finite values.
Results may differ from the reference program's by a relative error of at most 0.035.
The reference program's roundings to bfloat16 on the way (of `probs_low` and `score_grad`) count: a program that leaves them out, or rounds other values in their place, can miss the bound.
Values may be sent and summed in bfloat16 or wider, within the bound.
No kernel may reach another device: no remote copies, remote signals or barrier semaphores. Data moves between devices by JAX's collectives and lax.ppermute only.
A program may use at most 64 MiB of HBM per device.

```python
import math
import jax
import jax.numpy as jnp
import numpy as np
from jax import lax

QUERY_HEADS = 16
KEY_VALUE_HEADS = 8
HEAD_SIZE = 128
WINDOW = 256
TOK_DEV = 128
PACKED_TOKENS = 4096
DOCS = 8
MOST = 2048


def row_scales(key, row_count):
    return jnp.exp(jax.random.uniform(key, (row_count, 1), jnp.float32, 0.0, math.log(10.0)))


def draw_query_raw(key, part):
    scale_factors = row_scales(jax.random.fold_in(key, 1), PACKED_TOKENS)
    starting_rows = jnp.clip(jax.random.normal(jax.random.fold_in(key, 2), (PACKED_TOKENS, QUERY_HEADS, HEAD_SIZE), jnp.float32), -4.0, 4.0)
    return (starting_rows.reshape(PACKED_TOKENS, QUERY_HEADS * HEAD_SIZE) * scale_factors).astype(jnp.bfloat16)


def draw_key_raw(key, part):
    scale_factors = row_scales(jax.random.fold_in(key, 3), PACKED_TOKENS)
    starting_rows = jnp.clip(jax.random.normal(jax.random.fold_in(key, 4), (PACKED_TOKENS, KEY_VALUE_HEADS, HEAD_SIZE), jnp.float32), -4.0, 4.0)
    return (starting_rows.reshape(PACKED_TOKENS, KEY_VALUE_HEADS * HEAD_SIZE) * scale_factors).astype(jnp.bfloat16)


def draw_query_gain(key, part):
    return jnp.exp(jax.random.uniform(jax.random.fold_in(key, 21), (HEAD_SIZE,), jnp.float32, math.log(0.5), math.log(2.0)))


def draw_key_gain(key, part):
    return jnp.exp(jax.random.uniform(jax.random.fold_in(key, 22), (HEAD_SIZE,), jnp.float32, math.log(0.5), math.log(2.0)))


def shard_levels(key, dims, shards, smallest, high):
    loudness = 1.0
    for position, parts in shards:
        draws = jax.random.uniform(jax.random.fold_in(jax.random.fold_in(key, 6), position), (parts,), jnp.float32, smallest / len(shards), high / len(shards))
        loudness = loudness * jnp.repeat(jnp.exp(draws), dims[position] // parts).reshape((-1,) + (1,) * (len(dims) - 1 - position))
    return loudness


def profile(amount, total, most, slope):
    loads = [(1 << 20) // math.isqrt(rank ** slope) + 1 for rank in range(2, amount + 1)]
    surplus, holding = total - most - (amount - 1), [1] * (amount - 1)
    while surplus > 0:
        candidates = [i for i in range(amount - 1) if holding[i] < most]
        mass, remaining = sum([loads[i] for i in candidates]), surplus
        for i in candidates:
            more = min(most - holding[i], max(1, remaining * loads[i] // mass), surplus)
            holding[i] = holding[i] + more
            surplus = surplus - more
    return np.array([most] + holding)


def uneven_parts(rng, number_of, total, most, lean):
    if number_of == 2:
        one = jax.random.randint(rng, (), max(1, total - most), min(most, total - 1) + 1)
        return jnp.stack([one, total - one])
    sizes = jnp.asarray(profile(number_of, total, most, lean), jnp.int32)
    pairs = (number_of - 1) // 2
    giver, receiver = sizes[1:1 + 2 * pairs:2], sizes[2:2 + 2 * pairs:2]
    room = jnp.minimum(giver - 1, most - receiver)
    shifted = jax.random.randint(jax.random.fold_in(rng, 1), (pairs,), 0, 1 << 20) % (room + 1)
    sizes = sizes.at[1:1 + 2 * pairs:2].set(giver - shifted).at[2:2 + 2 * pairs:2].set(receiver + shifted)
    return sizes[jax.random.permutation(jax.random.fold_in(rng, 2), number_of)]


def noise(stream_key, dims, deviation, bound, shards=(), held_as=jnp.bfloat16):
    level = shard_levels(stream_key, dims, shards, -0.22, 0.18) if shards else 1.0
    values = jax.random.normal(stream_key, dims, jnp.float32) * deviation * level
    return jnp.minimum(jnp.maximum(values, -bound), bound).astype(held_as)


def setup_inputs(seed: int = 0) -> dict:
    splits = jax.random.split(jax.random.key(seed), 8)
    doc_lengths = uneven_parts(splits[0], DOCS, PACKED_TOKENS, MOST, 2).astype(jnp.int32)
    query_raw = draw_query_raw(jax.random.fold_in(splits[7], 71), 0)
    key_raw = draw_key_raw(jax.random.fold_in(splits[7], 71), 0)
    value_matrix = noise(splits[3], (PACKED_TOKENS, KEY_VALUE_HEADS * HEAD_SIZE), 1.0, 5.0, ((0, 32),))
    out_grad = noise(splits[4], (PACKED_TOKENS, QUERY_HEADS * HEAD_SIZE), 1.0, 5.0, ((0, 32),))
    query_gain = draw_query_gain(jax.random.fold_in(splits[7], 71), 0)
    key_gain = draw_key_gain(jax.random.fold_in(splits[7], 71), 0)
    return {"doc_lengths": doc_lengths, "query_raw": query_raw, "key_raw": key_raw, "value_matrix": value_matrix, "out_grad": out_grad, "query_gain": query_gain, "key_gain": key_gain}


eps_norm = 1e-06
score_scale = 168.0 ** (-0.5)
rope_base = 10000.0
masked_score = -1e+30

def doc_places(token_ids, doc_lengths):
    doc_ends = jnp.cumsum(doc_lengths).astype(jnp.int32)
    before = doc_ends[None, :] <= token_ids[:, None]
    doc_ids = lax.optimization_barrier(jnp.sum(before.astype(jnp.int32), axis=1)).astype(jnp.int32)
    starts = lax.optimization_barrier(jnp.max(jnp.where(before, doc_ends[None, :], 0), axis=1)).astype(jnp.int32)
    return (doc_ids, (token_ids - starts).astype(jnp.int32))

def rotary_tables(positions):
    half_width = HEAD_SIZE // 2
    frequency = rope_base ** (-2.0 * jnp.arange(half_width, dtype=jnp.float32) / HEAD_SIZE)
    angles = positions.astype(jnp.float32)[:, None] * frequency[None, :]
    return (jnp.cos(angles), jnp.sin(angles))

def norm_rotate(raw_rows, norm_gain, cosine, sine_table):
    row_count = raw_rows.shape[0]
    raw_values = raw_rows.astype(jnp.float32).reshape(row_count, -1, HEAD_SIZE)
    row_scale = lax.rsqrt(lax.optimization_barrier(jnp.mean(raw_values * raw_values, axis=-1, keepdims=True)) + eps_norm)
    normed = raw_values * row_scale * norm_gain
    front_half = normed[..., :HEAD_SIZE // 2]
    back_half = normed[..., HEAD_SIZE // 2:]
    cos_rows = cosine[:, None, :]
    sin_rows = sine_table[:, None, :]
    rotated = jnp.concatenate([front_half * cos_rows - back_half * sin_rows, back_half * cos_rows + front_half * sin_rows], -1)
    return rotated.reshape(row_count, -1).astype(jnp.bfloat16)

def unrotate_norm(grad_rot, raw_rows, norm_gain, cosine, sine_table):
    row_count = grad_rot.shape[0]
    grad_rows = grad_rot.reshape(row_count, -1, HEAD_SIZE)
    front_half = grad_rows[..., :HEAD_SIZE // 2]
    back_half = grad_rows[..., HEAD_SIZE // 2:]
    cos_rows = cosine[:, None, :]
    sin_rows = sine_table[:, None, :]
    grad_normed = jnp.concatenate([front_half * cos_rows + back_half * sin_rows, back_half * cos_rows - front_half * sin_rows], -1)
    raw_values = raw_rows.astype(jnp.float32).reshape(row_count, -1, HEAD_SIZE)
    row_scale = lax.rsqrt(lax.optimization_barrier(jnp.mean(raw_values * raw_values, axis=-1, keepdims=True)) + eps_norm)
    gain_grad = lax.optimization_barrier(jnp.sum(grad_normed * raw_values * row_scale, axis=(0, 1)))
    weighted = grad_normed * norm_gain
    raw_grad = row_scale * weighted - raw_values * row_scale ** 3 * lax.optimization_barrier(jnp.mean(weighted * raw_values, axis=-1, keepdims=True))
    return (raw_grad.reshape(row_count, -1).astype(jnp.bfloat16), gain_grad)

def visibility(own_tokens, own_docs, key_tokens, key_docs):
    same_doc = own_docs[:, None] == key_docs[None, :]
    causal = key_tokens[None, :] <= own_tokens[:, None]
    inside = own_tokens[:, None] - key_tokens[None, :] < WINDOW
    real_key = key_tokens[None, :] >= 0
    return same_doc & causal & inside & real_key

def head_grads(queries, grads_out, key_block, value_block, visible):
    queries = queries.astype(jnp.float32)
    grads_out = grads_out.astype(jnp.float32)
    key_block = key_block.astype(jnp.float32)
    value_block = value_block.astype(jnp.float32)
    scores = jnp.einsum('qhd,kd->hqk', queries, key_block) * score_scale
    scores = jnp.where(visible[None], scores, masked_score)
    row_top = lax.optimization_barrier(jnp.max(scores, axis=-1, keepdims=True))
    exps_rows = jnp.exp(scores - row_top)
    weights = exps_rows / lax.optimization_barrier(jnp.sum(exps_rows, axis=-1, keepdims=True))
    probs_low = weights.astype(jnp.bfloat16).astype(jnp.float32)
    prob_grad = jnp.einsum('qhd,kd->hqk', grads_out, value_block)
    row_delta = lax.optimization_barrier(jnp.sum(weights * prob_grad, axis=-1, keepdims=True))
    score_grad = (weights * (prob_grad - row_delta)).astype(jnp.bfloat16).astype(jnp.float32)
    query_grad = jnp.einsum('hqk,kd->qhd', score_grad, key_block) * score_scale
    key_grad = jnp.einsum('hqk,qhd->kd', score_grad, queries) * score_scale
    value_grad = jnp.einsum('hqk,qhd->kd', probs_low, grads_out)
    return (query_grad, key_grad, value_grad)

def round_far(term_rows, cut_rows):
    low_rows = lax.optimization_barrier(term_rows[:cut_rows].astype(jnp.bfloat16))
    return jnp.concatenate([low_rows.astype(jnp.float32), term_rows[cut_rows:]], 0)

def reference(doc_lengths, query_raw, key_raw, value_matrix, out_grad, query_gain, key_gain):
    halo_depth = WINDOW // TOK_DEV
    key_count = (halo_depth + 1) * TOK_DEV
    blocks = PACKED_TOKENS // TOK_DEV
    group_width = QUERY_HEADS // KEY_VALUE_HEADS
    padding_rows = halo_depth * TOK_DEV
    all_tokens = jnp.arange(PACKED_TOKENS, dtype=jnp.int32)
    all_docs, all_pos = doc_places(all_tokens, doc_lengths)
    cosine, sine_table = rotary_tables(all_pos)
    query_rot = norm_rotate(query_raw, query_gain, cosine, sine_table)
    rotated_keys = norm_rotate(key_raw, key_gain, cosine, sine_table)
    padded_keys = jnp.concatenate([jnp.zeros((padding_rows, KEY_VALUE_HEADS * HEAD_SIZE), jnp.bfloat16), rotated_keys], 0)
    padded_values = jnp.concatenate([jnp.zeros((padding_rows, KEY_VALUE_HEADS * HEAD_SIZE), jnp.bfloat16), value_matrix], 0)

    def block_step(carried, block_index):
        key_acc, value_acc, gain_acc = carried
        row_start = (block_index * TOK_DEV).astype(jnp.int32)
        queries = lax.dynamic_slice_in_dim(query_rot, row_start, TOK_DEV, 0)
        grads_out = lax.dynamic_slice_in_dim(out_grad, row_start, TOK_DEV, 0)
        raw_block = lax.dynamic_slice_in_dim(query_raw, row_start, TOK_DEV, 0)
        cos_block = lax.dynamic_slice_in_dim(cosine, row_start, TOK_DEV, 0)
        sin_block = lax.dynamic_slice_in_dim(sine_table, row_start, TOK_DEV, 0)
        key_block = lax.dynamic_slice_in_dim(padded_keys, row_start, key_count, 0)
        value_block = lax.dynamic_slice_in_dim(padded_values, row_start, key_count, 0)
        key_tokens = (row_start - padding_rows + jnp.arange(key_count, dtype=jnp.int32)).astype(jnp.int32)
        key_docs, unused_pos = doc_places(key_tokens, doc_lengths)
        own_tokens = key_tokens[padding_rows:]
        own_docs = key_docs[padding_rows:]
        visible = visibility(own_tokens, own_docs, key_tokens, key_docs)
        query_parts, key_parts, value_parts = ([], [], [])
        for key_value_head in range(KEY_VALUE_HEADS):
            key_cols = slice(key_value_head * HEAD_SIZE, (key_value_head + 1) * HEAD_SIZE)
            query_cols = slice(key_value_head * group_width * HEAD_SIZE, (key_value_head + 1) * group_width * HEAD_SIZE)
            query_grad, key_grad, value_grad = head_grads(queries[:, query_cols].reshape(TOK_DEV, group_width, HEAD_SIZE), grads_out[:, query_cols].reshape(TOK_DEV, group_width, HEAD_SIZE), key_block[:, key_cols], value_block[:, key_cols], visible)
            query_parts.append(query_grad.reshape(TOK_DEV, group_width * HEAD_SIZE))
            key_parts.append(key_grad)
            value_parts.append(value_grad)
        query_term = jnp.concatenate(query_parts, 1)
        key_term = round_far(jnp.concatenate(key_parts, 1), padding_rows)
        value_term = round_far(jnp.concatenate(value_parts, 1), padding_rows)
        key_acc = lax.dynamic_update_slice_in_dim(key_acc, lax.dynamic_slice_in_dim(key_acc, row_start, key_count, 0) + key_term, row_start, 0)
        value_acc = lax.dynamic_update_slice_in_dim(value_acc, lax.dynamic_slice_in_dim(value_acc, row_start, key_count, 0) + value_term, row_start, 0)
        raw_grad, gain_part = unrotate_norm(query_term, raw_block, query_gain, cos_block, sin_block)
        return ((key_acc, value_acc, gain_acc + gain_part), raw_grad)
    initial_state = (jnp.zeros((PACKED_TOKENS + padding_rows, KEY_VALUE_HEADS * HEAD_SIZE), jnp.float32), jnp.zeros((PACKED_TOKENS + padding_rows, KEY_VALUE_HEADS * HEAD_SIZE), jnp.float32), jnp.zeros((HEAD_SIZE,), jnp.float32))
    final_state, query_blocks = lax.scan(block_step, initial_state, jnp.arange(blocks, dtype=jnp.int32))
    key_acc, value_acc, grad_query_gain = final_state
    grad_query = query_blocks.reshape(PACKED_TOKENS, QUERY_HEADS * HEAD_SIZE)
    grad_key, grad_key_gain = unrotate_norm(key_acc[padding_rows:], key_raw, key_gain, cosine, sine_table)
    grad_value = value_acc[padding_rows:].astype(jnp.bfloat16)
    return (grad_query, grad_key, grad_value, grad_query_gain, grad_key_gain)
```

```python
import math

import jax
import jax.numpy as jnp
import numpy as np
from jax import lax
from jax.experimental import pallas as pl
from jax.experimental.pallas import tpu as pltpu
from jax.sharding import PartitionSpec as P

HEAD = 128
HALF = HEAD // 2
WINDOW = 256
EPS = 1e-06
SCALE = 168.0 ** (-0.5)
ROPE_BASE = 10000.0
MASKED = -1e30
AXES = ("ctx", "grp")
F32 = jnp.float32
BF16 = jnp.bfloat16
VMEM_LIMIT = 40 * 1024 * 1024


def frequencies():
    half = ROPE_BASE ** (-2.0 * np.arange(HALF, dtype=np.float64) / HEAD)
    return np.concatenate([half, half]).astype(np.float32)[None, :]


def shift(value, steps):
    count = lax.axis_size(AXES)
    first, last = max(0, -steps), min(count, count - steps)
    return lax.ppermute(value, AXES, [(s, s + steps) for s in range(first, last)])


def sum_everywhere(value):
    count = lax.axis_size(AXES)
    stride = 1
    while stride < count:
        left = count // stride
        radix = next(p for p in range(2, left + 1) if left % p == 0)
        total = value
        for turn in range(1, radix):
            pairs = []
            for source in range(count):
                digit = source // stride % radix
                pairs.append((source, source + ((digit + turn) % radix - digit) * stride))
            total = total + lax.ppermute(value, AXES, pairs)
        value = total
        stride *= radix
    return value


def own_index():
    return lax.axis_index("ctx") * lax.axis_size("grp") + lax.axis_index("grp")


def roll_half(x):
    return pltpu.roll(x, HALF, 1)


def doc_starts(tokens, lengths_ref):
    def step(doc, carry):
        end, starts = carry
        end = end + lengths_ref[doc]
        return end, jnp.where(tokens >= end, end, starts)

    count = lengths_ref.shape[0]
    return lax.fori_loop(
        0, count, step, (jnp.int32(0), jnp.zeros_like(tokens)), unroll=count if count <= 8 else 1
    )[1]


def cos_sin_lanes(angle, lane):
    turns = jnp.floor(angle * (2.0 / math.pi) + 0.5)
    r = angle - turns * 1.5703125
    r = r - turns * 4.837512969970703125e-4
    r = r - turns * 7.549789948768648e-8
    z = r * r
    sin_r = r + r * z * (-1.6666654611e-1 + z * (8.3321608736e-3 + z * -1.9515295891e-4))
    cos_r = 1.0 - 0.5 * z + z * z * (
        4.166664568298827e-2 + z * (-1.388731625493765e-3 + z * 2.443315711809948e-5)
    )
    quadrant = turns.astype(jnp.int32) - jnp.where(lane >= HALF, 1, 0)
    odd = (quadrant & 1) == 1
    value = jnp.where(odd, sin_r, cos_r)
    negative = ((quadrant + 1) & 2) == 2
    return jnp.where(negative, -value, value)


def row_scale(x):
    return lax.rsqrt(jnp.sum(x * x, axis=1, keepdims=True) * (1.0 / HEAD) + EPS)


def prepare_kernel(
    lengths_ref, query_ref, key_ref, query_gain_ref, key_gain_ref, freq_ref,
    query_rot_ref, key_rot_ref, cos_ref, sin_ref, bias_ref,
):
    rows = query_ref.shape[0]
    keys = cos_ref.shape[0]
    base = own_index() * rows - (keys - rows)
    shape = (keys, HEAD)
    lane = lax.broadcasted_iota(jnp.int32, shape, 1)
    tokens = base + lax.broadcasted_iota(jnp.int32, shape, 0)
    positions = tokens - doc_starts(tokens, lengths_ref)
    mixed = cos_sin_lanes(positions.astype(F32) * freq_ref[...], lane)
    turned = roll_half(mixed)
    cos = jnp.where(lane < HALF, mixed, turned)
    sin = jnp.where(lane < HALF, -turned, mixed)
    cos_ref[...] = cos
    sin_ref[...] = sin
    queries = base + (keys - rows) + lax.broadcasted_iota(jnp.int32, (1, rows), 1)
    lowest = jnp.maximum(doc_starts(queries, lengths_ref), queries - (WINDOW - 1))
    key_tokens = base + lax.broadcasted_iota(jnp.int32, (keys, rows), 0)
    visible = (key_tokens >= lowest) & (key_tokens <= queries)
    bias_ref[...] = jnp.where(visible, 0.0, MASKED)
    own_cos, own_sin = cos[keys - rows :], sin[keys - rows :]
    for raw_ref, gain_ref, out_ref in (
        (query_ref, query_gain_ref, query_rot_ref),
        (key_ref, key_gain_ref, key_rot_ref),
    ):
        gain = gain_ref[...]
        cos_gain = own_cos * gain
        sin_gain = own_sin * roll_half(jnp.broadcast_to(gain, (8, HEAD)))[:1]
        for head in range(raw_ref.shape[1] // HEAD):
            x = raw_ref[:, head * HEAD : (head + 1) * HEAD].astype(F32)
            rotated = (x * cos_gain + roll_half(x) * sin_gain) * row_scale(x)
            out_ref[head * rows : (head + 1) * rows, :] = rotated.astype(BF16)


def attend_kernel(
    query_ref, out_grad_ref, key_ref, value_ref, far_ref, near_ref,
    query_rot_ref, key_rot_ref, cos_ref, sin_ref, bias_ref, query_gain_ref, key_gain_ref,
    grad_query_ref, far_term_ref, near_term_ref, own_key_ref, own_value_ref, gain_ref,
):
    rows = query_ref.shape[0]
    heads = key_ref.shape[1] // HEAD
    group = query_ref.shape[1] // key_ref.shape[1]
    halo = WINDOW // rows
    far_cos, far_sin = cos_ref[: halo * rows], sin_ref[: halo * rows]
    key_gain = key_gain_ref[...]
    query_gain = query_gain_ref[...]
    cos_gain = far_cos * key_gain
    sin_gain = far_sin * roll_half(jnp.broadcast_to(key_gain, (8, HEAD)))[:1]
    own_cos, own_sin = cos_ref[halo * rows :], sin_ref[halo * rows :]
    bias = jnp.concatenate([bias_ref[...]] * group, 1)
    query_gain_acc = jnp.zeros((rows, HEAD), F32)
    key_acc = jnp.zeros(((halo + 1) * rows, HEAD), F32)
    key_acc_turned = jnp.zeros(((halo + 1) * rows, HEAD), F32)
    for head in range(heads):
        cols = slice(head * HEAD, (head + 1) * HEAD)
        raw_far = jnp.concatenate([far_ref[0, :, cols], near_ref[0, :, cols]], 0).astype(F32)
        raw_own = key_ref[:, cols].astype(F32)
        raw_all = jnp.concatenate([raw_far, raw_own], 0)
        scale_all = row_scale(raw_all)
        turned_all = roll_half(raw_all)
        far_rows = halo * rows
        far_rot = (raw_far * cos_gain + turned_all[:far_rows] * sin_gain) * scale_all[:far_rows]
        keys = jnp.concatenate(
            [far_rot.astype(BF16), key_rot_ref[head * rows : (head + 1) * rows, :]], 0
        )
        values = jnp.concatenate(
            [far_ref[1, :, cols], near_ref[1, :, cols], value_ref[:, cols]], 0
        )
        queries = query_rot_ref[head * group * rows : (head + 1) * group * rows, :]
        grads_out = jnp.concatenate(
            [
                out_grad_ref[:, (head * group + one) * HEAD : (head * group + one + 1) * HEAD]
                for one in range(group)
            ],
            0,
        )
        both_last = (((1,), (1,)), ((), ()))
        scores = lax.dot_general(keys, queries, both_last, preferred_element_type=F32)
        scores = scores * (SCALE * math.log2(math.e)) + bias
        exps = jnp.exp2(scores - jnp.max(scores, axis=0, keepdims=True))
        probs = exps * (1.0 / jnp.sum(exps, axis=0, keepdims=True))
        prob_grad = lax.dot_general(values, grads_out, both_last, preferred_element_type=F32)
        delta = jnp.sum(probs * prob_grad, axis=0, keepdims=True)
        score_grad = (probs * (prob_grad - delta)).astype(BF16)
        value_term = jnp.dot(probs.astype(BF16), grads_out, preferred_element_type=F32)
        key_term = jnp.dot(score_grad, queries, preferred_element_type=F32) * SCALE
        query_term = (
            lax.dot_general(
                score_grad, keys, (((0,), (0,)), ((), ())), preferred_element_type=F32
            )
            * SCALE
        )
        far_key = key_term[:far_rows].astype(BF16)
        far_value = value_term[:far_rows].astype(BF16)
        far_term_ref[0, :, cols] = far_key[:rows]
        far_term_ref[1, :, cols] = far_value[:rows]
        near_term_ref[0, :, cols] = far_key[rows:]
        near_term_ref[1, :, cols] = far_value[rows:]
        own_key_ref[:, cols] = key_term[far_rows:]
        own_value_ref[:, cols] = value_term[far_rows:]
        weighted = jnp.concatenate([far_key.astype(F32), key_term[far_rows:]], 0) * scale_all
        key_acc = key_acc + weighted * raw_all
        key_acc_turned = key_acc_turned + weighted * turned_all
        for one in range(group):
            query_cols = slice((head * group + one) * HEAD, (head * group + one + 1) * HEAD)
            grad, part = norm_backward(
                query_term[one * rows : (one + 1) * rows],
                query_ref[:, query_cols].astype(F32), query_gain, own_cos, own_sin,
            )
            grad_query_ref[:, query_cols] = grad.astype(BF16)
            query_gain_acc = query_gain_acc + part
    query_sum = jnp.sum(query_gain_acc, axis=0, keepdims=True)
    key_sum = jnp.sum(key_acc * cos_ref[...], axis=0, keepdims=True)
    turned_sum = jnp.sum(key_acc_turned * sin_ref[...], axis=0, keepdims=True)
    key_sum = key_sum + roll_half(jnp.broadcast_to(turned_sum, (8, HEAD)))[:1]
    gain_ref[...] = jnp.concatenate([query_sum, key_sum, jnp.zeros((6, HEAD), F32)], 0)


def norm_backward(grad_rot, x, gain, cos, sin):
    scale = row_scale(x)
    normed_grad = grad_rot * cos - roll_half(grad_rot) * sin
    x_scaled = x * scale
    part = normed_grad * x_scaled
    mean = jnp.sum(part * gain, axis=1, keepdims=True) * (1.0 / HEAD)
    return scale * (normed_grad * gain - x_scaled * mean), part


def finish_kernel(
    key_ref, own_key_ref, own_value_ref, near_ref, far_ref, cos_ref, sin_ref, key_gain_ref,
    grad_key_ref, grad_value_ref,
):
    rows = key_ref.shape[0]
    keys = cos_ref.shape[0]
    cos, sin = cos_ref[keys - rows :], sin_ref[keys - rows :]
    gain = key_gain_ref[...]
    for head in range(key_ref.shape[1] // HEAD):
        cols = slice(head * HEAD, (head + 1) * HEAD)
        key_sum = (
            own_key_ref[:, cols] + near_ref[0, :, cols].astype(F32) + far_ref[0, :, cols].astype(F32)
        )
        grad, _ = norm_backward(key_sum, key_ref[:, cols].astype(F32), gain, cos, sin)
        grad_key_ref[:, cols] = grad.astype(BF16)
        value_sum = (
            own_value_ref[:, cols]
            + near_ref[1, :, cols].astype(F32)
            + far_ref[1, :, cols].astype(F32)
        )
        grad_value_ref[:, cols] = value_sum.astype(BF16)


def pack_kernel(key_ref, value_ref, out_ref, sems):
    first = pltpu.make_async_copy(key_ref, out_ref.at[0], sems.at[0])
    second = pltpu.make_async_copy(value_ref, out_ref.at[1], sems.at[1])
    first.start()
    second.start()
    first.wait()
    second.wait()


def params():
    return pltpu.CompilerParams(vmem_limit_bytes=VMEM_LIMIT)


def vmem(count):
    return [pl.BlockSpec(memory_space=pltpu.VMEM)] * count


def shape(dims, dtype):
    return jax.ShapeDtypeStruct(dims, dtype)


def on_device(doc_lengths, query_raw, key_raw, value_matrix, out_grad, query_gain, key_gain):
    rows, query_width = query_raw.shape
    width = key_raw.shape[1]
    keys = WINDOW + rows
    query_gain = query_gain.reshape(1, HEAD)
    key_gain = key_gain.reshape(1, HEAD)
    packed = pl.pallas_call(
        pack_kernel,
        out_shape=shape((2, rows, width), BF16),
        in_specs=[pl.BlockSpec(memory_space=pl.ANY)] * 2,
        out_specs=pl.BlockSpec(memory_space=pl.ANY),
        scratch_shapes=[pltpu.SemaphoreType.DMA((2,))],
        name="pack_kv",
    )(key_raw, value_matrix)
    near = shift(packed, 1)
    far = shift(packed, 2)
    query_rot, key_rot, cos, sin, bias = pl.pallas_call(
        prepare_kernel,
        out_shape=[
            shape((query_width // HEAD * rows, HEAD), BF16),
            shape((width // HEAD * rows, HEAD), BF16),
            shape((keys, HEAD), F32),
            shape((keys, HEAD), F32),
            shape((keys, rows), F32),
        ],
        in_specs=[pl.BlockSpec(memory_space=pltpu.SMEM)] + vmem(5),
        out_specs=vmem(5),
        compiler_params=params(),
        cost_estimate=pl.CostEstimate(flops=4_000_000, bytes_accessed=3_000_000, transcendentals=0),
        name="prepare",
    )(doc_lengths, query_raw, key_raw, query_gain, key_gain, jnp.asarray(frequencies()))
    grad_query, far_term, near_term, own_key, own_value, gains = pl.pallas_call(
        attend_kernel,
        out_shape=[
            shape((rows, query_width), BF16),
            shape((2, rows, width), BF16),
            shape((2, rows, width), BF16),
            shape((rows, width), F32),
            shape((rows, width), F32),
            shape((8, HEAD), F32),
        ],
        in_specs=vmem(13),
        out_specs=vmem(6),
        compiler_params=params(),
        cost_estimate=pl.CostEstimate(
            flops=1_000_000_000, bytes_accessed=8_000_000, transcendentals=800_000
        ),
        name="attend",
    )(
        query_raw, out_grad, key_raw, value_matrix, far, near,
        query_rot, key_rot, cos, sin, bias, query_gain, key_gain,
    )
    near_back = shift(near_term, -1)
    far_back = shift(far_term, -2)
    gains = sum_everywhere(gains[:2])
    grad_key, grad_value = pl.pallas_call(
        finish_kernel,
        out_shape=[shape((rows, width), BF16), shape((rows, width), BF16)],
        in_specs=vmem(8),
        out_specs=vmem(2),
        compiler_params=params(),
        cost_estimate=pl.CostEstimate(flops=4_000_000, bytes_accessed=4_000_000, transcendentals=0),
        name="finish",
    )(key_raw, own_key, own_value, near_back, far_back, cos, sin, key_gain)
    return grad_query, grad_key, grad_value, gains[0], gains[1]


def solution(mesh):
    rows = P(AXES, None)
    return jax.shard_map(
        on_device,
        mesh=mesh,
        in_specs=(P(), rows, rows, rows, rows, P(), P()),
        out_specs=(rows, rows, rows, P(), P()),
        check_vma=False,
    )
```

```python
import math

import jax
import jax.numpy as jnp
import numpy as np
from jax import lax
from jax.experimental import pallas as pl
from jax.experimental.pallas import tpu as pltpu
from jax.sharding import PartitionSpec as P

HEAD = 128
HALF = HEAD // 2
WINDOW = 256
EPS = 1e-06
SCALE = 168.0 ** (-0.5)
ROPE_BASE = 10000.0
MASKED = -1e30
AXES = ("ctx", "grp")
F32 = jnp.float32
BF16 = jnp.bfloat16
VMEM_LIMIT = 40 * 1024 * 1024


def frequencies():
    half = ROPE_BASE ** (-2.0 * np.arange(HALF, dtype=np.float64) / HEAD)
    return np.concatenate([half, half]).astype(np.float32)[None, :]


def shift(value, steps):
    count = lax.axis_size(AXES)
    first, last = max(0, -steps), min(count, count - steps)
    return lax.ppermute(value, AXES, [(s, s + steps) for s in range(first, last)])


def sum_everywhere(value):
    count = lax.axis_size(AXES)
    stride = 1
    while stride < count:
        left = count // stride
        radix = next(p for p in range(2, left + 1) if left % p == 0)
        total = value
        for turn in range(1, radix):
            pairs = []
            for source in range(count):
                digit = source // stride % radix
                pairs.append((source, source + ((digit + turn) % radix - digit) * stride))
            total = total + lax.ppermute(value, AXES, pairs)
        value = total
        stride *= radix
    return value


def own_index():
    return lax.axis_index("ctx") * lax.axis_size("grp") + lax.axis_index("grp")


def roll_half(x):
    return pltpu.roll(x, HALF, 1)


def doc_starts(tokens, lengths_ref):
    def step(doc, carry):
        end, starts = carry
        end = end + lengths_ref[doc]
        return end, jnp.where(tokens >= end, end, starts)

    count = lengths_ref.shape[0]
    return lax.fori_loop(
        0, count, step, (jnp.int32(0), jnp.zeros_like(tokens)), unroll=count if count <= 8 else 1
    )[1]


def cos_sin_lanes(angle, lane):
    turns = jnp.floor(angle * (2.0 / math.pi) + 0.5)
    r = angle - turns * 1.5703125
    r = r - turns * 4.837512969970703125e-4
    r = r - turns * 7.549789948768648e-8
    z = r * r
    sin_r = r + r * z * (-1.6666654611e-1 + z * (8.3321608736e-3 + z * -1.9515295891e-4))
    cos_r = 1.0 - 0.5 * z + z * z * (
        4.166664568298827e-2 + z * (-1.388731625493765e-3 + z * 2.443315711809948e-5)
    )
    quadrant = turns.astype(jnp.int32) - jnp.where(lane >= HALF, 1, 0)
    odd = (quadrant & 1) == 1
    value = jnp.where(odd, sin_r, cos_r)
    negative = ((quadrant + 1) & 2) == 2
    return jnp.where(negative, -value, value)


def row_scale(x):
    return lax.rsqrt(jnp.sum(x * x, axis=1, keepdims=True) * (1.0 / HEAD) + EPS)


def prepare_kernel(
    lengths_ref, query_ref, key_ref, query_gain_ref, key_gain_ref, freq_ref,
    query_rot_ref, key_rot_ref, cos_ref, sin_ref, bias_ref,
):
    rows = query_ref.shape[0]
    keys = cos_ref.shape[0]
    base = own_index() * rows - (keys - rows)
    shape = (keys, HEAD)
    lane = lax.broadcasted_iota(jnp.int32, shape, 1)
    tokens = base + lax.broadcasted_iota(jnp.int32, shape, 0)
    positions = tokens - doc_starts(tokens, lengths_ref)
    mixed = cos_sin_lanes(positions.astype(F32) * freq_ref[...], lane)
    turned = roll_half(mixed)
    cos = jnp.where(lane < HALF, mixed, turned)
    sin = jnp.where(lane < HALF, -turned, mixed)
    cos_ref[...] = cos
    sin_ref[...] = sin
    queries = base + (keys - rows) + lax.broadcasted_iota(jnp.int32, (1, rows), 1)
    lowest = jnp.maximum(doc_starts(queries, lengths_ref), queries - (WINDOW - 1))
    key_tokens = base + lax.broadcasted_iota(jnp.int32, (keys, rows), 0)
    visible = (key_tokens >= lowest) & (key_tokens <= queries)
    bias_ref[...] = jnp.where(visible, 0.0, MASKED)
    own_cos, own_sin = cos[keys - rows :], sin[keys - rows :]
    for raw_ref, gain_ref, out_ref in (
        (query_ref, query_gain_ref, query_rot_ref),
        (key_ref, key_gain_ref, key_rot_ref),
    ):
        gain = gain_ref[...]
        cos_gain = own_cos * gain
        sin_gain = own_sin * roll_half(jnp.broadcast_to(gain, (8, HEAD)))[:1]
        for head in range(raw_ref.shape[1] // HEAD):
            x = raw_ref[:, head * HEAD : (head + 1) * HEAD].astype(F32)
            rotated = (x * cos_gain + roll_half(x) * sin_gain) * row_scale(x)
            out_ref[head * rows : (head + 1) * rows, :] = rotated.astype(BF16)


def attend_kernel(
    query_ref, out_grad_ref, key_ref, value_ref, far_ref, near_ref,
    query_rot_ref, key_rot_ref, cos_ref, sin_ref, bias_ref, query_gain_ref, key_gain_ref,
    grad_query_ref, far_term_ref, near_term_ref, own_key_ref, own_value_ref, gain_ref,
):
    rows = query_ref.shape[0]
    heads = key_ref.shape[1] // HEAD
    group = query_ref.shape[1] // key_ref.shape[1]
    halo = WINDOW // rows
    far_cos, far_sin = cos_ref[: halo * rows], sin_ref[: halo * rows]
    key_gain = key_gain_ref[...]
    query_gain = query_gain_ref[...]
    cos_gain = far_cos * key_gain
    sin_gain = far_sin * roll_half(jnp.broadcast_to(key_gain, (8, HEAD)))[:1]
    own_cos, own_sin = cos_ref[halo * rows :], sin_ref[halo * rows :]
    bias = jnp.concatenate([bias_ref[...]] * group, 1)
    query_gain_acc = jnp.zeros((rows, HEAD), F32)
    key_acc = jnp.zeros(((halo + 1) * rows, HEAD), F32)
    key_acc_turned = jnp.zeros(((halo + 1) * rows, HEAD), F32)
    for head in range(heads):
        cols = slice(head * HEAD, (head + 1) * HEAD)
        raw_far = jnp.concatenate([far_ref[0, :, cols], near_ref[0, :, cols]], 0).astype(F32)
        raw_own = key_ref[:, cols].astype(F32)
        raw_all = jnp.concatenate([raw_far, raw_own], 0)
        scale_all = row_scale(raw_all)
        turned_all = roll_half(raw_all)
        far_rows = halo * rows
        far_rot = (raw_far * cos_gain + turned_all[:far_rows] * sin_gain) * scale_all[:far_rows]
        keys = jnp.concatenate(
            [far_rot.astype(BF16), key_rot_ref[head * rows : (head + 1) * rows, :]], 0
        )
        values = jnp.concatenate(
            [far_ref[1, :, cols], near_ref[1, :, cols], value_ref[:, cols]], 0
        )
        queries = query_rot_ref[head * group * rows : (head + 1) * group * rows, :]
        grads_out = jnp.concatenate(
            [
                out_grad_ref[:, (head * group + one) * HEAD : (head * group + one + 1) * HEAD]
                for one in range(group)
            ],
            0,
        )
        both_last = (((1,), (1,)), ((), ()))
        scores = lax.dot_general(keys, queries, both_last, preferred_element_type=F32)
        scores = scores * (SCALE * math.log2(math.e)) + bias
        exps = jnp.exp2(scores - jnp.max(scores, axis=0, keepdims=True))
        probs = exps * (1.0 / jnp.sum(exps, axis=0, keepdims=True))
        prob_grad = lax.dot_general(values, grads_out, both_last, preferred_element_type=F32)
        delta = jnp.sum(probs * prob_grad, axis=0, keepdims=True)
        score_grad = (probs * (prob_grad - delta)).astype(BF16)
        value_term = jnp.dot(probs.astype(BF16), grads_out, preferred_element_type=F32)
        key_term = jnp.dot(score_grad, queries, preferred_element_type=F32) * SCALE
        query_term = (
            lax.dot_general(
                score_grad, keys, (((0,), (0,)), ((), ())), preferred_element_type=F32
            )
            * SCALE
        )
        far_key = key_term[:far_rows].astype(BF16)
        far_value = value_term[:far_rows].astype(BF16)
        far_term_ref[0, :, cols] = far_key[:rows]
        far_term_ref[1, :, cols] = far_value[:rows]
        near_term_ref[0, :, cols] = far_key[rows:]
        near_term_ref[1, :, cols] = far_value[rows:]
        own_key_ref[:, cols] = key_term[far_rows:]
        own_value_ref[:, cols] = value_term[far_rows:]
        weighted = jnp.concatenate([far_key.astype(F32), key_term[far_rows:]], 0) * scale_all
        key_acc = key_acc + weighted * raw_all
        key_acc_turned = key_acc_turned + weighted * turned_all
        for one in range(group):
            query_cols = slice((head * group + one) * HEAD, (head * group + one + 1) * HEAD)
            grad, part = norm_backward(
                query_term[one * rows : (one + 1) * rows],
                query_ref[:, query_cols].astype(F32), query_gain, own_cos, own_sin,
            )
            grad_query_ref[:, query_cols] = grad.astype(BF16)
            query_gain_acc = query_gain_acc + part
    query_sum = jnp.sum(query_gain_acc, axis=0, keepdims=True)
    key_sum = jnp.sum(key_acc * cos_ref[...], axis=0, keepdims=True)
    turned_sum = jnp.sum(key_acc_turned * sin_ref[...], axis=0, keepdims=True)
    key_sum = key_sum + roll_half(jnp.broadcast_to(turned_sum, (8, HEAD)))[:1]
    gain_ref[...] = jnp.concatenate([query_sum, key_sum, jnp.zeros((6, HEAD), F32)], 0)


def norm_backward(grad_rot, x, gain, cos, sin):
    scale = row_scale(x)
    normed_grad = grad_rot * cos - roll_half(grad_rot) * sin
    x_scaled = x * scale
    part = normed_grad * x_scaled
    mean = jnp.sum(part * gain, axis=1, keepdims=True) * (1.0 / HEAD)
    return scale * (normed_grad * gain - x_scaled * mean), part


def finish_kernel(
    key_ref, own_key_ref, own_value_ref, near_ref, far_ref, cos_ref, sin_ref, key_gain_ref,
    grad_key_ref, grad_value_ref,
):
    rows = key_ref.shape[0]
    keys = cos_ref.shape[0]
    cos, sin = cos_ref[keys - rows :], sin_ref[keys - rows :]
    gain = key_gain_ref[...]
    for head in range(key_ref.shape[1] // HEAD):
        cols = slice(head * HEAD, (head + 1) * HEAD)
        key_sum = (
            own_key_ref[:, cols] + near_ref[0, :, cols].astype(F32) + far_ref[0, :, cols].astype(F32)
        )
        grad, _ = norm_backward(key_sum, key_ref[:, cols].astype(F32), gain, cos, sin)
        grad_key_ref[:, cols] = grad.astype(BF16)
        value_sum = (
            own_value_ref[:, cols]
            + near_ref[1, :, cols].astype(F32)
            + far_ref[1, :, cols].astype(F32)
        )
        grad_value_ref[:, cols] = value_sum.astype(BF16)


def pack_kernel(key_ref, value_ref, out_ref):
    out_ref[0] = key_ref[...]
    out_ref[1] = value_ref[...]


def params():
    return pltpu.CompilerParams(vmem_limit_bytes=VMEM_LIMIT)


def vmem(count):
    return [pl.BlockSpec(memory_space=pltpu.VMEM)] * count


def shape(dims, dtype):
    return jax.ShapeDtypeStruct(dims, dtype)


def on_device(doc_lengths, query_raw, key_raw, value_matrix, out_grad, query_gain, key_gain):
    rows, query_width = query_raw.shape
    width = key_raw.shape[1]
    keys = WINDOW + rows
    query_gain = query_gain.reshape(1, HEAD)
    key_gain = key_gain.reshape(1, HEAD)
    packed = pl.pallas_call(
        pack_kernel,
        out_shape=shape((2, rows, width), BF16),
        in_specs=vmem(2),
        out_specs=vmem(1)[0],
        name="pack_kv",
    )(key_raw, value_matrix)
    near = shift(packed, 1)
    far = shift(packed, 2)
    query_rot, key_rot, cos, sin, bias = pl.pallas_call(
        prepare_kernel,
        out_shape=[
            shape((query_width // HEAD * rows, HEAD), BF16),
            shape((width // HEAD * rows, HEAD), BF16),
            shape((keys, HEAD), F32),
            shape((keys, HEAD), F32),
            shape((keys, rows), F32),
        ],
        in_specs=[pl.BlockSpec(memory_space=pltpu.SMEM)] + vmem(5),
        out_specs=vmem(5),
        compiler_params=params(),
        cost_estimate=pl.CostEstimate(flops=4_000_000, bytes_accessed=3_000_000, transcendentals=0),
        name="prepare",
    )(doc_lengths, query_raw, key_raw, query_gain, key_gain, jnp.asarray(frequencies()))
    grad_query, far_term, near_term, own_key, own_value, gains = pl.pallas_call(
        attend_kernel,
        out_shape=[
            shape((rows, query_width), BF16),
            shape((2, rows, width), BF16),
            shape((2, rows, width), BF16),
            shape((rows, width), F32),
            shape((rows, width), F32),
            shape((8, HEAD), F32),
        ],
        in_specs=vmem(13),
        out_specs=vmem(6),
        compiler_params=params(),
        cost_estimate=pl.CostEstimate(
            flops=1_000_000_000, bytes_accessed=8_000_000, transcendentals=800_000
        ),
        name="attend",
    )(
        query_raw, out_grad, key_raw, value_matrix, far, near,
        query_rot, key_rot, cos, sin, bias, query_gain, key_gain,
    )
    near_back = shift(near_term, -1)
    far_back = shift(far_term, -2)
    gains = jnp.sum(lax.all_gather(gains[:2], AXES), axis=0)
    grad_key, grad_value = pl.pallas_call(
        finish_kernel,
        out_shape=[shape((rows, width), BF16), shape((rows, width), BF16)],
        in_specs=vmem(8),
        out_specs=vmem(2),
        compiler_params=params(),
        cost_estimate=pl.CostEstimate(flops=4_000_000, bytes_accessed=4_000_000, transcendentals=0),
        name="finish",
    )(key_raw, own_key, own_value, near_back, far_back, cos, sin, key_gain)
    return grad_query, grad_key, grad_value, gains[0], gains[1]


def solution(mesh):
    rows = P(AXES, None)
    return jax.shard_map(
        on_device,
        mesh=mesh,
        in_specs=(P(), rows, rows, rows, rows, P(), P()),
        out_specs=(rows, rows, rows, P(), P()),
        check_vma=False,
    )
```

```python
import math

import jax
import jax.numpy as jnp
import numpy as np
from jax import lax
from jax.experimental import pallas as pl
from jax.experimental.pallas import tpu as pltpu
from jax.sharding import PartitionSpec as P

HEAD = 128
HALF = HEAD // 2
WINDOW = 256
EPS = 1e-06
SCALE = 168.0 ** (-0.5)
ROPE_BASE = 10000.0
MASKED = -1e30
AXES = ("ctx", "grp")
F32 = jnp.float32
BF16 = jnp.bfloat16
VMEM_LIMIT = 40 * 1024 * 1024


def frequencies():
    half = ROPE_BASE ** (-2.0 * np.arange(HALF, dtype=np.float64) / HEAD)
    return np.concatenate([half, half]).astype(np.float32)[None, :]


def shift(value, steps):
    count = lax.axis_size(AXES)
    return lax.ppermute(value, AXES, [(s, (s + steps) % count) for s in range(count)])


def sum_everywhere(value):
    count = lax.axis_size(AXES)
    stages, stride = [], 1
    while stride < count:
        left = count // stride
        radix = next(p for p in range(2, left + 1) if left % p == 0)
        stages.append((stride, radix))
        stride *= radix
    for stride, radix in stages[1:] + stages[:1]:
        total = value
        for turn in range(1, radix):
            pairs = []
            for source in range(count):
                digit = source // stride % radix
                pairs.append((source, source + ((digit + turn) % radix - digit) * stride))
            total = total + lax.ppermute(value, AXES, pairs)
        value = total
    return value


def own_index():
    return lax.axis_index("ctx") * lax.axis_size("grp") + lax.axis_index("grp")


def roll_half(x):
    return pltpu.roll(x, HALF, 1)


def doc_starts(tokens, lengths_ref):
    def step(doc, carry):
        end, starts = carry
        end = end + lengths_ref[doc]
        return end, jnp.where(tokens >= end, end, starts)

    count = lengths_ref.shape[0]
    return lax.fori_loop(
        0, count, step, (jnp.int32(0), jnp.zeros_like(tokens)), unroll=count if count <= 8 else 1
    )[1]


def cos_sin_lanes(angle, lane):
    turns = jnp.floor(angle * (2.0 / math.pi) + 0.5)
    r = angle - turns * 1.5703125
    r = r - turns * 4.837512969970703125e-4
    r = r - turns * 7.549789948768648e-8
    z = r * r
    sin_r = r + r * z * (-1.6666654611e-1 + z * (8.3321608736e-3 + z * -1.9515295891e-4))
    cos_r = 1.0 - 0.5 * z + z * z * (
        4.166664568298827e-2 + z * (-1.388731625493765e-3 + z * 2.443315711809948e-5)
    )
    quadrant = turns.astype(jnp.int32) - jnp.where(lane >= HALF, 1, 0)
    odd = (quadrant & 1) == 1
    value = jnp.where(odd, sin_r, cos_r)
    negative = ((quadrant + 1) & 2) == 2
    return jnp.where(negative, -value, value)


def row_scale(x):
    return lax.rsqrt(jnp.sum(x * x, axis=1, keepdims=True) * (1.0 / HEAD) + EPS)


def prepare_kernel(
    lengths_ref, query_ref, key_ref, query_gain_ref, key_gain_ref, freq_ref,
    query_rot_ref, key_rot_ref, cos_ref, sin_ref, bias_ref,
):
    rows = query_ref.shape[0]
    keys = cos_ref.shape[0]
    base = own_index() * rows - (keys - rows)
    shape = (keys, HEAD)
    lane = lax.broadcasted_iota(jnp.int32, shape, 1)
    tokens = base + lax.broadcasted_iota(jnp.int32, shape, 0)
    positions = tokens - doc_starts(tokens, lengths_ref)
    mixed = cos_sin_lanes(positions.astype(F32) * freq_ref[...], lane)
    turned = roll_half(mixed)
    cos = jnp.where(lane < HALF, mixed, turned)
    sin = jnp.where(lane < HALF, -turned, mixed)
    cos_ref[...] = cos
    sin_ref[...] = sin
    queries = base + (keys - rows) + lax.broadcasted_iota(jnp.int32, (1, rows), 1)
    lowest = jnp.maximum(doc_starts(queries, lengths_ref), queries - (WINDOW - 1))
    key_tokens = base + lax.broadcasted_iota(jnp.int32, (keys, rows), 0)
    visible = (key_tokens >= lowest) & (key_tokens <= queries)
    bias_ref[...] = jnp.where(visible, 0.0, MASKED)
    own_cos, own_sin = cos[keys - rows :], sin[keys - rows :]
    for raw_ref, gain_ref, out_ref in (
        (query_ref, query_gain_ref, query_rot_ref),
        (key_ref, key_gain_ref, key_rot_ref),
    ):
        gain = gain_ref[...]
        cos_gain = own_cos * gain
        sin_gain = own_sin * roll_half(jnp.broadcast_to(gain, (8, HEAD)))[:1]
        for head in range(raw_ref.shape[1] // HEAD):
            x = raw_ref[:, head * HEAD : (head + 1) * HEAD].astype(F32)
            rotated = (x * cos_gain + roll_half(x) * sin_gain) * row_scale(x)
            out_ref[head * rows : (head + 1) * rows, :] = rotated.astype(BF16)


def attend_kernel(
    query_ref, out_grad_ref, key_ref, value_ref, far_ref, near_ref,
    query_rot_ref, key_rot_ref, cos_ref, sin_ref, bias_ref, query_gain_ref, key_gain_ref,
    grad_query_ref, far_term_ref, near_term_ref, own_key_ref, own_value_ref, gain_ref,
):
    rows = query_ref.shape[0]
    heads = key_ref.shape[1] // HEAD
    group = query_ref.shape[1] // key_ref.shape[1]
    halo = WINDOW // rows
    far_cos, far_sin = cos_ref[: halo * rows], sin_ref[: halo * rows]
    key_gain = key_gain_ref[...]
    query_gain = query_gain_ref[...]
    cos_gain = far_cos * key_gain
    sin_gain = far_sin * roll_half(jnp.broadcast_to(key_gain, (8, HEAD)))[:1]
    own_cos, own_sin = cos_ref[halo * rows :], sin_ref[halo * rows :]
    bias = jnp.concatenate([bias_ref[...]] * group, 1)
    query_gain_acc = jnp.zeros((rows, HEAD), F32)
    key_acc = jnp.zeros(((halo + 1) * rows, HEAD), F32)
    key_acc_turned = jnp.zeros(((halo + 1) * rows, HEAD), F32)
    for head in range(heads):
        cols = slice(head * HEAD, (head + 1) * HEAD)
        raw_far = jnp.concatenate([far_ref[0, :, cols], near_ref[0, :, cols]], 0).astype(F32)
        raw_own = key_ref[:, cols].astype(F32)
        raw_all = jnp.concatenate([raw_far, raw_own], 0)
        scale_all = row_scale(raw_all)
        turned_all = roll_half(raw_all)
        far_rows = halo * rows
        far_rot = (raw_far * cos_gain + turned_all[:far_rows] * sin_gain) * scale_all[:far_rows]
        keys = jnp.concatenate(
            [far_rot.astype(BF16), key_rot_ref[head * rows : (head + 1) * rows, :]], 0
        )
        values = jnp.concatenate(
            [far_ref[1, :, cols], near_ref[1, :, cols], value_ref[:, cols]], 0
        )
        queries = query_rot_ref[head * group * rows : (head + 1) * group * rows, :]
        grads_out = jnp.concatenate(
            [
                out_grad_ref[:, (head * group + one) * HEAD : (head * group + one + 1) * HEAD]
                for one in range(group)
            ],
            0,
        )
        both_last = (((1,), (1,)), ((), ()))
        scores = lax.dot_general(keys, queries, both_last, preferred_element_type=F32)
        scores = scores * (SCALE * math.log2(math.e)) + bias
        exps = jnp.exp2(scores - jnp.max(scores, axis=0, keepdims=True))
        probs = exps * (1.0 / jnp.sum(exps, axis=0, keepdims=True))
        prob_grad = lax.dot_general(values, grads_out, both_last, preferred_element_type=F32)
        delta = jnp.sum(probs * prob_grad, axis=0, keepdims=True)
        score_grad = (probs * (prob_grad - delta)).astype(BF16)
        value_term = jnp.dot(probs.astype(BF16), grads_out, preferred_element_type=F32)
        key_term = jnp.dot(score_grad, queries, preferred_element_type=F32) * SCALE
        query_term = (
            lax.dot_general(
                score_grad, keys, (((0,), (0,)), ((), ())), preferred_element_type=F32
            )
            * SCALE
        )
        far_key = key_term[:far_rows].astype(BF16)
        far_value = value_term[:far_rows].astype(BF16)
        far_term_ref[0, :, cols] = far_key[:rows]
        far_term_ref[1, :, cols] = far_value[:rows]
        near_term_ref[0, :, cols] = far_key[rows:]
        near_term_ref[1, :, cols] = far_value[rows:]
        own_key_ref[:, cols] = key_term[far_rows:]
        own_value_ref[:, cols] = value_term[far_rows:]
        weighted = jnp.concatenate([far_key.astype(F32), key_term[far_rows:]], 0) * scale_all
        key_acc = key_acc + weighted * raw_all
        key_acc_turned = key_acc_turned + weighted * turned_all
        for one in range(group):
            query_cols = slice((head * group + one) * HEAD, (head * group + one + 1) * HEAD)
            grad, part = norm_backward(
                query_term[one * rows : (one + 1) * rows],
                query_ref[:, query_cols].astype(F32), query_gain, own_cos, own_sin,
            )
            grad_query_ref[:, query_cols] = grad.astype(BF16)
            query_gain_acc = query_gain_acc + part
    query_sum = jnp.sum(query_gain_acc, axis=0, keepdims=True)
    key_sum = jnp.sum(key_acc * cos_ref[...], axis=0, keepdims=True)
    turned_sum = jnp.sum(key_acc_turned * sin_ref[...], axis=0, keepdims=True)
    key_sum = key_sum + roll_half(jnp.broadcast_to(turned_sum, (8, HEAD)))[:1]
    gain_ref[...] = jnp.concatenate([query_sum, key_sum, jnp.zeros((6, HEAD), F32)], 0)


def norm_backward(grad_rot, x, gain, cos, sin):
    scale = row_scale(x)
    normed_grad = grad_rot * cos - roll_half(grad_rot) * sin
    x_scaled = x * scale
    part = normed_grad * x_scaled
    mean = jnp.sum(part * gain, axis=1, keepdims=True) * (1.0 / HEAD)
    return scale * (normed_grad * gain - x_scaled * mean), part


def finish_kernel(
    key_ref, own_key_ref, own_value_ref, near_ref, far_ref, cos_ref, sin_ref, key_gain_ref,
    grad_key_ref, grad_value_ref,
):
    rows = key_ref.shape[0]
    keys = cos_ref.shape[0]
    cos, sin = cos_ref[keys - rows :], sin_ref[keys - rows :]
    gain = key_gain_ref[...]
    for head in range(key_ref.shape[1] // HEAD):
        cols = slice(head * HEAD, (head + 1) * HEAD)
        key_sum = (
            own_key_ref[:, cols] + near_ref[0, :, cols].astype(F32) + far_ref[0, :, cols].astype(F32)
        )
        grad, _ = norm_backward(key_sum, key_ref[:, cols].astype(F32), gain, cos, sin)
        grad_key_ref[:, cols] = grad.astype(BF16)
        value_sum = (
            own_value_ref[:, cols]
            + near_ref[1, :, cols].astype(F32)
            + far_ref[1, :, cols].astype(F32)
        )
        grad_value_ref[:, cols] = value_sum.astype(BF16)


def pack_kernel(key_ref, value_ref, out_ref):
    out_ref[0] = key_ref[...]
    out_ref[1] = value_ref[...]


def params():
    return pltpu.CompilerParams(vmem_limit_bytes=VMEM_LIMIT)


def vmem(count):
    return [pl.BlockSpec(memory_space=pltpu.VMEM)] * count


def shape(dims, dtype):
    return jax.ShapeDtypeStruct(dims, dtype)


def on_device(doc_lengths, query_raw, key_raw, value_matrix, out_grad, query_gain, key_gain):
    rows, query_width = query_raw.shape
    width = key_raw.shape[1]
    keys = WINDOW + rows
    query_gain = query_gain.reshape(1, HEAD)
    key_gain = key_gain.reshape(1, HEAD)
    packed = pl.pallas_call(
        pack_kernel,
        out_shape=shape((2, rows, width), BF16),
        in_specs=vmem(2),
        out_specs=vmem(1)[0],
        name="pack_kv",
    )(key_raw, value_matrix)
    near = shift(packed, 1)
    far = shift(packed, 2)
    query_rot, key_rot, cos, sin, bias = pl.pallas_call(
        prepare_kernel,
        out_shape=[
            shape((query_width // HEAD * rows, HEAD), BF16),
            shape((width // HEAD * rows, HEAD), BF16),
            shape((keys, HEAD), F32),
            shape((keys, HEAD), F32),
            shape((keys, rows), F32),
        ],
        in_specs=[pl.BlockSpec(memory_space=pltpu.SMEM)] + vmem(5),
        out_specs=vmem(5),
        compiler_params=params(),
        cost_estimate=pl.CostEstimate(flops=4_000_000, bytes_accessed=3_000_000, transcendentals=0),
        name="prepare",
    )(doc_lengths, query_raw, key_raw, query_gain, key_gain, jnp.asarray(frequencies()))
    grad_query, far_term, near_term, own_key, own_value, gains = pl.pallas_call(
        attend_kernel,
        out_shape=[
            shape((rows, query_width), BF16),
            shape((2, rows, width), BF16),
            shape((2, rows, width), BF16),
            shape((rows, width), F32),
            shape((rows, width), F32),
            shape((8, HEAD), F32),
        ],
        in_specs=vmem(13),
        out_specs=vmem(6),
        compiler_params=params(),
        cost_estimate=pl.CostEstimate(
            flops=1_000_000_000, bytes_accessed=8_000_000, transcendentals=800_000
        ),
        name="attend",
    )(
        query_raw, out_grad, key_raw, value_matrix, far, near,
        query_rot, key_rot, cos, sin, bias, query_gain, key_gain,
    )
    near_back = shift(near_term, -1)
    far_back = shift(far_term, -2)
    gains = sum_everywhere(gains[:2])
    grad_key, grad_value = pl.pallas_call(
        finish_kernel,
        out_shape=[shape((rows, width), BF16), shape((rows, width), BF16)],
        in_specs=vmem(8),
        out_specs=vmem(2),
        compiler_params=params(),
        cost_estimate=pl.CostEstimate(flops=4_000_000, bytes_accessed=4_000_000, transcendentals=0),
        name="finish",
    )(key_raw, own_key, own_value, near_back, far_back, cos, sin, key_gain)
    return grad_query, grad_key, grad_value, gains[0], gains[1]


def solution(mesh):
    rows = P(AXES, None)
    return jax.shard_map(
        on_device,
        mesh=mesh,
        in_specs=(P(), rows, rows, rows, rows, P(), P()),
        out_specs=(rows, rows, rows, P(), P()),
        check_vma=False,
    )
```

```python
import math

import jax
import jax.numpy as jnp
import numpy as np
from jax import lax
from jax.experimental import pallas as pl
from jax.experimental.pallas import tpu as pltpu
from jax.sharding import PartitionSpec as P

HEAD = 128
HALF = HEAD // 2
WINDOW = 256
EPS = 1e-06
SCALE = 168.0 ** (-0.5)
ROPE_BASE = 10000.0
MASKED = -1e30
AXES = ("ctx", "grp")
F32 = jnp.float32
BF16 = jnp.bfloat16
VMEM_LIMIT = 40 * 1024 * 1024


def frequencies():
    half = ROPE_BASE ** (-2.0 * np.arange(HALF, dtype=np.float64) / HEAD)
    return np.concatenate([half, half]).astype(np.float32)[None, :]


def shift(value, steps):
    count = lax.axis_size(AXES)
    return lax.ppermute(value, AXES, [(s, (s + steps) % count) for s in range(count)])


def sum_everywhere(value):
    count = lax.axis_size(AXES)
    copies = jnp.broadcast_to(value[None], (count,) + value.shape)
    return jnp.sum(lax.all_to_all(copies, AXES, 0, 0), axis=0)


def own_index():
    return lax.axis_index("ctx") * lax.axis_size("grp") + lax.axis_index("grp")


def roll_half(x):
    return pltpu.roll(x, HALF, 1)


def doc_starts(tokens, lengths_ref):
    def step(doc, carry):
        end, starts = carry
        end = end + lengths_ref[doc]
        return end, jnp.where(tokens >= end, end, starts)

    count = lengths_ref.shape[0]
    return lax.fori_loop(
        0, count, step, (jnp.int32(0), jnp.zeros_like(tokens)), unroll=count if count <= 8 else 1
    )[1]


def cos_sin_lanes(angle, lane):
    turns = jnp.floor(angle * (2.0 / math.pi) + 0.5)
    r = angle - turns * 1.5703125
    r = r - turns * 4.837512969970703125e-4
    r = r - turns * 7.549789948768648e-8
    z = r * r
    sin_r = r + r * z * (-1.6666654611e-1 + z * (8.3321608736e-3 + z * -1.9515295891e-4))
    cos_r = 1.0 - 0.5 * z + z * z * (
        4.166664568298827e-2 + z * (-1.388731625493765e-3 + z * 2.443315711809948e-5)
    )
    quadrant = turns.astype(jnp.int32) - jnp.where(lane >= HALF, 1, 0)
    odd = (quadrant & 1) == 1
    value = jnp.where(odd, sin_r, cos_r)
    negative = ((quadrant + 1) & 2) == 2
    return jnp.where(negative, -value, value)


def row_scale(x):
    return lax.rsqrt(jnp.sum(x * x, axis=1, keepdims=True) * (1.0 / HEAD) + EPS)


def prepare_kernel(
    lengths_ref, query_ref, key_ref, query_gain_ref, key_gain_ref, freq_ref,
    query_rot_ref, key_rot_ref, cos_ref, sin_ref, bias_ref,
):
    rows = query_ref.shape[0]
    keys = cos_ref.shape[0]
    base = own_index() * rows - (keys - rows)
    shape = (keys, HEAD)
    lane = lax.broadcasted_iota(jnp.int32, shape, 1)
    tokens = base + lax.broadcasted_iota(jnp.int32, shape, 0)
    positions = tokens - doc_starts(tokens, lengths_ref)
    mixed = cos_sin_lanes(positions.astype(F32) * freq_ref[...], lane)
    turned = roll_half(mixed)
    cos = jnp.where(lane < HALF, mixed, turned)
    sin = jnp.where(lane < HALF, -turned, mixed)
    cos_ref[...] = cos
    sin_ref[...] = sin
    queries = base + (keys - rows) + lax.broadcasted_iota(jnp.int32, (1, rows), 1)
    lowest = jnp.maximum(doc_starts(queries, lengths_ref), queries - (WINDOW - 1))
    key_tokens = base + lax.broadcasted_iota(jnp.int32, (keys, rows), 0)
    visible = (key_tokens >= lowest) & (key_tokens <= queries)
    bias_ref[...] = jnp.where(visible, 0.0, MASKED)
    own_cos, own_sin = cos[keys - rows :], sin[keys - rows :]
    for raw_ref, gain_ref, out_ref in (
        (query_ref, query_gain_ref, query_rot_ref),
        (key_ref, key_gain_ref, key_rot_ref),
    ):
        gain = gain_ref[...]
        cos_gain = own_cos * gain
        sin_gain = own_sin * roll_half(jnp.broadcast_to(gain, (8, HEAD)))[:1]
        for head in range(raw_ref.shape[1] // HEAD):
            x = raw_ref[:, head * HEAD : (head + 1) * HEAD].astype(F32)
            rotated = (x * cos_gain + roll_half(x) * sin_gain) * row_scale(x)
            out_ref[head * rows : (head + 1) * rows, :] = rotated.astype(BF16)


def attend_kernel(
    query_ref, out_grad_ref, key_ref, value_ref, far_ref, near_ref,
    query_rot_ref, key_rot_ref, cos_ref, sin_ref, bias_ref, query_gain_ref, key_gain_ref,
    grad_query_ref, far_term_ref, near_term_ref, own_key_ref, own_value_ref, gain_ref,
):
    rows = query_ref.shape[0]
    heads = key_ref.shape[1] // HEAD
    group = query_ref.shape[1] // key_ref.shape[1]
    halo = WINDOW // rows
    far_cos, far_sin = cos_ref[: halo * rows], sin_ref[: halo * rows]
    key_gain = key_gain_ref[...]
    query_gain = query_gain_ref[...]
    cos_gain = far_cos * key_gain
    sin_gain = far_sin * roll_half(jnp.broadcast_to(key_gain, (8, HEAD)))[:1]
    own_cos, own_sin = cos_ref[halo * rows :], sin_ref[halo * rows :]
    bias = jnp.concatenate([bias_ref[...]] * group, 1)
    query_gain_acc = jnp.zeros((rows, HEAD), F32)
    key_acc = jnp.zeros(((halo + 1) * rows, HEAD), F32)
    key_acc_turned = jnp.zeros(((halo + 1) * rows, HEAD), F32)
    for head in range(heads):
        cols = slice(head * HEAD, (head + 1) * HEAD)
        raw_far = jnp.concatenate([far_ref[0, :, cols], near_ref[0, :, cols]], 0).astype(F32)
        raw_own = key_ref[:, cols].astype(F32)
        raw_all = jnp.concatenate([raw_far, raw_own], 0)
        scale_all = row_scale(raw_all)
        turned_all = roll_half(raw_all)
        far_rows = halo * rows
        far_rot = (raw_far * cos_gain + turned_all[:far_rows] * sin_gain) * scale_all[:far_rows]
        keys = jnp.concatenate(
            [far_rot.astype(BF16), key_rot_ref[head * rows : (head + 1) * rows, :]], 0
        )
        values = jnp.concatenate(
            [far_ref[1, :, cols], near_ref[1, :, cols], value_ref[:, cols]], 0
        )
        queries = query_rot_ref[head * group * rows : (head + 1) * group * rows, :]
        grads_out = jnp.concatenate(
            [
                out_grad_ref[:, (head * group + one) * HEAD : (head * group + one + 1) * HEAD]
                for one in range(group)
            ],
            0,
        )
        both_last = (((1,), (1,)), ((), ()))
        scores = lax.dot_general(keys, queries, both_last, preferred_element_type=F32)
        scores = scores * (SCALE * math.log2(math.e)) + bias
        exps = jnp.exp2(scores - jnp.max(scores, axis=0, keepdims=True))
        probs = exps * (1.0 / jnp.sum(exps, axis=0, keepdims=True))
        prob_grad = lax.dot_general(values, grads_out, both_last, preferred_element_type=F32)
        delta = jnp.sum(probs * prob_grad, axis=0, keepdims=True)
        score_grad = (probs * (prob_grad - delta)).astype(BF16)
        value_term = jnp.dot(probs.astype(BF16), grads_out, preferred_element_type=F32)
        key_term = jnp.dot(score_grad, queries, preferred_element_type=F32) * SCALE
        query_term = (
            lax.dot_general(
                score_grad, keys, (((0,), (0,)), ((), ())), preferred_element_type=F32
            )
            * SCALE
        )
        far_key = key_term[:far_rows].astype(BF16)
        far_value = value_term[:far_rows].astype(BF16)
        far_term_ref[0, :, cols] = far_key[:rows]
        far_term_ref[1, :, cols] = far_value[:rows]
        near_term_ref[0, :, cols] = far_key[rows:]
        near_term_ref[1, :, cols] = far_value[rows:]
        own_key_ref[:, cols] = key_term[far_rows:]
        own_value_ref[:, cols] = value_term[far_rows:]
        weighted = jnp.concatenate([far_key.astype(F32), key_term[far_rows:]], 0) * scale_all
        key_acc = key_acc + weighted * raw_all
        key_acc_turned = key_acc_turned + weighted * turned_all
        for one in range(group):
            query_cols = slice((head * group + one) * HEAD, (head * group + one + 1) * HEAD)
            grad, part = norm_backward(
                query_term[one * rows : (one + 1) * rows],
                query_ref[:, query_cols].astype(F32), query_gain, own_cos, own_sin,
            )
            grad_query_ref[:, query_cols] = grad.astype(BF16)
            query_gain_acc = query_gain_acc + part
    query_sum = jnp.sum(query_gain_acc, axis=0, keepdims=True)
    key_sum = jnp.sum(key_acc * cos_ref[...], axis=0, keepdims=True)
    turned_sum = jnp.sum(key_acc_turned * sin_ref[...], axis=0, keepdims=True)
    key_sum = key_sum + roll_half(jnp.broadcast_to(turned_sum, (8, HEAD)))[:1]
    gain_ref[...] = jnp.concatenate([query_sum, key_sum, jnp.zeros((6, HEAD), F32)], 0)


def norm_backward(grad_rot, x, gain, cos, sin):
    scale = row_scale(x)
    normed_grad = grad_rot * cos - roll_half(grad_rot) * sin
    x_scaled = x * scale
    part = normed_grad * x_scaled
    mean = jnp.sum(part * gain, axis=1, keepdims=True) * (1.0 / HEAD)
    return scale * (normed_grad * gain - x_scaled * mean), part


def finish_kernel(
    key_ref, own_key_ref, own_value_ref, near_ref, far_ref, cos_ref, sin_ref, key_gain_ref,
    grad_key_ref, grad_value_ref,
):
    rows = key_ref.shape[0]
    keys = cos_ref.shape[0]
    cos, sin = cos_ref[keys - rows :], sin_ref[keys - rows :]
    gain = key_gain_ref[...]
    for head in range(key_ref.shape[1] // HEAD):
        cols = slice(head * HEAD, (head + 1) * HEAD)
        key_sum = (
            own_key_ref[:, cols] + near_ref[0, :, cols].astype(F32) + far_ref[0, :, cols].astype(F32)
        )
        grad, _ = norm_backward(key_sum, key_ref[:, cols].astype(F32), gain, cos, sin)
        grad_key_ref[:, cols] = grad.astype(BF16)
        value_sum = (
            own_value_ref[:, cols]
            + near_ref[1, :, cols].astype(F32)
            + far_ref[1, :, cols].astype(F32)
        )
        grad_value_ref[:, cols] = value_sum.astype(BF16)


def pack_kernel(key_ref, value_ref, out_ref):
    out_ref[0] = key_ref[...]
    out_ref[1] = value_ref[...]


def params():
    return pltpu.CompilerParams(vmem_limit_bytes=VMEM_LIMIT)


def vmem(count):
    return [pl.BlockSpec(memory_space=pltpu.VMEM)] * count


def shape(dims, dtype):
    return jax.ShapeDtypeStruct(dims, dtype)


def on_device(doc_lengths, query_raw, key_raw, value_matrix, out_grad, query_gain, key_gain):
    rows, query_width = query_raw.shape
    width = key_raw.shape[1]
    keys = WINDOW + rows
    query_gain = query_gain.reshape(1, HEAD)
    key_gain = key_gain.reshape(1, HEAD)
    packed = pl.pallas_call(
        pack_kernel,
        out_shape=shape((2, rows, width), BF16),
        in_specs=vmem(2),
        out_specs=vmem(1)[0],
        name="pack_kv",
    )(key_raw, value_matrix)
    near = shift(packed, 1)
    far = shift(packed, 2)
    query_rot, key_rot, cos, sin, bias = pl.pallas_call(
        prepare_kernel,
        out_shape=[
            shape((query_width // HEAD * rows, HEAD), BF16),
            shape((width // HEAD * rows, HEAD), BF16),
            shape((keys, HEAD), F32),
            shape((keys, HEAD), F32),
            shape((keys, rows), F32),
        ],
        in_specs=[pl.BlockSpec(memory_space=pltpu.SMEM)] + vmem(5),
        out_specs=vmem(5),
        compiler_params=params(),
        cost_estimate=pl.CostEstimate(flops=4_000_000, bytes_accessed=3_000_000, transcendentals=0),
        name="prepare",
    )(doc_lengths, query_raw, key_raw, query_gain, key_gain, jnp.asarray(frequencies()))
    grad_query, far_term, near_term, own_key, own_value, gains = pl.pallas_call(
        attend_kernel,
        out_shape=[
            shape((rows, query_width), BF16),
            shape((2, rows, width), BF16),
            shape((2, rows, width), BF16),
            shape((rows, width), F32),
            shape((rows, width), F32),
            shape((8, HEAD), F32),
        ],
        in_specs=vmem(13),
        out_specs=vmem(6),
        compiler_params=params(),
        cost_estimate=pl.CostEstimate(
            flops=1_000_000_000, bytes_accessed=8_000_000, transcendentals=800_000
        ),
        name="attend",
    )(
        query_raw, out_grad, key_raw, value_matrix, far, near,
        query_rot, key_rot, cos, sin, bias, query_gain, key_gain,
    )
    near_back = shift(near_term, -1)
    far_back = shift(far_term, -2)
    gains = sum_everywhere(gains[:2])
    grad_key, grad_value = pl.pallas_call(
        finish_kernel,
        out_shape=[shape((rows, width), BF16), shape((rows, width), BF16)],
        in_specs=vmem(8),
        out_specs=vmem(2),
        compiler_params=params(),
        cost_estimate=pl.CostEstimate(flops=4_000_000, bytes_accessed=4_000_000, transcendentals=0),
        name="finish",
    )(key_raw, own_key, own_value, near_back, far_back, cos, sin, key_gain)
    return grad_query, grad_key, grad_value, gains[0], gains[1]


def solution(mesh):
    rows = P(AXES, None)
    return jax.shard_map(
        on_device,
        mesh=mesh,
        in_specs=(P(), rows, rows, rows, rows, P(), P()),
        out_specs=(rows, rows, rows, P(), P()),
        check_vma=False,
    )
```

```python
import math

import jax
import jax.numpy as jnp
import numpy as np
from jax import lax
from jax.experimental import pallas as pl
from jax.experimental.pallas import tpu as pltpu
from jax.sharding import PartitionSpec as P

HEAD = 128
HALF = HEAD // 2
WINDOW = 256
EPS = 1e-06
SCALE = 168.0 ** (-0.5)
ROPE_BASE = 10000.0
MASKED = -1e30
AXES = ("ctx", "grp")
F32 = jnp.float32
BF16 = jnp.bfloat16
VMEM_LIMIT = 40 * 1024 * 1024


def frequencies():
    half = ROPE_BASE ** (-2.0 * np.arange(HALF, dtype=np.float64) / HEAD)
    return np.concatenate([half, half]).astype(np.float32)[None, :]


def shift(value, steps):
    count = lax.axis_size(AXES)
    return lax.ppermute(value, AXES, [(s, (s + steps) % count) for s in range(count)])


def exchange(copies):
    return lax.all_to_all(copies, AXES, 0, 0)


def own_index():
    return lax.axis_index("ctx") * lax.axis_size("grp") + lax.axis_index("grp")


def roll_half(x):
    return pltpu.roll(x, HALF, 1)


def doc_starts(tokens, lengths_ref):
    def step(doc, carry):
        end, starts = carry
        end = end + lengths_ref[doc]
        return end, jnp.where(tokens >= end, end, starts)

    count = lengths_ref.shape[0]
    return lax.fori_loop(
        0, count, step, (jnp.int32(0), jnp.zeros_like(tokens)), unroll=count if count <= 8 else 1
    )[1]


def cos_sin_lanes(angle, lane):
    turns = jnp.floor(angle * (2.0 / math.pi) + 0.5)
    r = angle - turns * 1.5703125
    r = r - turns * 4.837512969970703125e-4
    r = r - turns * 7.549789948768648e-8
    z = r * r
    sin_r = r + r * z * (-1.6666654611e-1 + z * (8.3321608736e-3 + z * -1.9515295891e-4))
    cos_r = 1.0 - 0.5 * z + z * z * (
        4.166664568298827e-2 + z * (-1.388731625493765e-3 + z * 2.443315711809948e-5)
    )
    quadrant = turns.astype(jnp.int32) - jnp.where(lane >= HALF, 1, 0)
    odd = (quadrant & 1) == 1
    value = jnp.where(odd, sin_r, cos_r)
    negative = ((quadrant + 1) & 2) == 2
    return jnp.where(negative, -value, value)


def row_scale(x):
    return lax.rsqrt(jnp.sum(x * x, axis=1, keepdims=True) * (1.0 / HEAD) + EPS)


def turned_gain(gain):
    return roll_half(jnp.broadcast_to(gain, (8, HEAD)))[:1]


def prepare_kernel(
    lengths_ref, query_ref, key_ref, query_gain_ref, key_gain_ref, freq_ref,
    query_rot_ref, query_scaled_ref, query_scale_ref,
    key_rot_ref, key_scaled_ref, key_scale_ref, cos_ref, sin_ref, bias_ref,
):
    rows = query_ref.shape[0]
    keys = cos_ref.shape[0]
    base = own_index() * rows - (keys - rows)
    shape = (keys, HEAD)
    lane = lax.broadcasted_iota(jnp.int32, shape, 1)
    tokens = base + lax.broadcasted_iota(jnp.int32, shape, 0)
    positions = tokens - doc_starts(tokens, lengths_ref)
    mixed = cos_sin_lanes(positions.astype(F32) * freq_ref[...], lane)
    turned = roll_half(mixed)
    cos = jnp.where(lane < HALF, mixed, turned)
    sin = jnp.where(lane < HALF, -turned, mixed)
    cos_ref[...] = cos
    sin_ref[...] = sin
    queries = base + (keys - rows) + lax.broadcasted_iota(jnp.int32, (1, rows), 1)
    lowest = jnp.maximum(doc_starts(queries, lengths_ref), queries - (WINDOW - 1))
    key_tokens = base + lax.broadcasted_iota(jnp.int32, (keys, rows), 0)
    visible = (key_tokens >= lowest) & (key_tokens <= queries)
    bias_ref[...] = jnp.where(visible, 0.0, MASKED)
    own_cos, own_sin = cos[keys - rows :], sin[keys - rows :]
    for raw_ref, gain_ref, rot_ref, scaled_ref, scale_ref in (
        (query_ref, query_gain_ref, query_rot_ref, query_scaled_ref, query_scale_ref),
        (key_ref, key_gain_ref, key_rot_ref, key_scaled_ref, key_scale_ref),
    ):
        gain = gain_ref[...]
        cos_gain = own_cos * gain
        sin_gain = own_sin * turned_gain(gain)
        for head in range(raw_ref.shape[1] // HEAD):
            part = slice(head * rows, (head + 1) * rows)
            x = raw_ref[:, head * HEAD : (head + 1) * HEAD].astype(F32)
            scale = jnp.broadcast_to(row_scale(x), x.shape)
            scaled = x * scale
            scale_ref[part, :] = scale
            scaled_ref[part, :] = scaled
            rot_ref[part, :] = (scaled * cos_gain + roll_half(scaled) * sin_gain).astype(BF16)


def stacked(ref, head, group):
    return jnp.concatenate(
        [ref[:, (head * group + one) * HEAD : (head * group + one + 1) * HEAD] for one in range(group)],
        0,
    )


def attend_keys_kernel(
    far_ref, near_ref, out_grad_ref, query_rot_ref, key_rot_ref, cos_ref, sin_ref, bias_ref,
    key_gain_ref,
    probs_ref, halo_rot_ref, halo_scaled_ref, far_value_ref, near_value_ref, own_value_ref,
):
    rows = far_ref.shape[0]
    heads = far_ref.shape[1] // HEAD
    group = out_grad_ref.shape[1] // far_ref.shape[1]
    halo = WINDOW
    keys = halo + rows
    key_gain = key_gain_ref[...]
    cos_gain = cos_ref[:halo] * key_gain
    sin_gain = sin_ref[:halo] * turned_gain(key_gain)
    bias = jnp.concatenate([bias_ref[...]] * group, 1)

    def scores_of(head):
        cols = slice(head * HEAD, (head + 1) * HEAD)
        raw = jnp.concatenate([far_ref[:, cols], near_ref[:, cols]], 0).astype(F32)
        scaled = raw * row_scale(raw)
        halo_scaled_ref[head * halo : (head + 1) * halo, :] = scaled
        rotated = (scaled * cos_gain + roll_half(scaled) * sin_gain).astype(BF16)
        halo_rot_ref[head * halo : (head + 1) * halo, :] = rotated
        both = jnp.concatenate([rotated, key_rot_ref[head * rows : (head + 1) * rows, :]], 0)
        queries = query_rot_ref[head * group * rows : (head + 1) * group * rows, :]
        return lax.dot_general(
            both, queries, (((1,), (1,)), ((), ())), preferred_element_type=F32
        )

    later = scores_of(0)
    for head in range(heads):
        scores = later
        if head + 1 < heads:
            later = scores_of(head + 1)
        cols = slice(head * HEAD, (head + 1) * HEAD)
        scores = scores * (SCALE * math.log2(math.e)) + bias
        exps = jnp.exp2(scores - jnp.max(scores, axis=0, keepdims=True))
        probs = exps * (1.0 / jnp.sum(exps, axis=0, keepdims=True))
        probs_ref[head * keys : (head + 1) * keys, :] = probs
        value_term = jnp.dot(
            probs.astype(BF16), stacked(out_grad_ref, head, group), preferred_element_type=F32
        )
        far_value_ref[:, cols] = value_term[:rows].astype(BF16)
        near_value_ref[:, cols] = value_term[rows:halo].astype(BF16)
        own_value_ref[:, cols] = value_term[halo:]


def norm_backward(grad_rot, scaled, scale, gain, cos, sin):
    normed_grad = grad_rot * cos - roll_half(grad_rot) * sin
    part = normed_grad * scaled
    mean = jnp.sum(part * gain, axis=1, keepdims=True) * (1.0 / HEAD)
    return scale * (normed_grad * gain - scaled * mean), part


def attend_values_kernel(
    far_ref, near_ref, value_ref, out_grad_ref, probs_ref, query_rot_ref, key_rot_ref,
    halo_rot_ref, halo_scaled_ref, key_scaled_ref, query_scaled_ref, query_scale_ref,
    cos_ref, sin_ref, query_gain_ref,
    far_key_ref, near_key_ref, own_key_ref, grad_query_ref, gain_ref,
):
    rows = far_ref.shape[0]
    heads = far_ref.shape[1] // HEAD
    group = out_grad_ref.shape[1] // far_ref.shape[1]
    halo = WINDOW
    keys = halo + rows
    query_gain = query_gain_ref[...]
    own_cos, own_sin = cos_ref[halo:] * SCALE, sin_ref[halo:] * SCALE
    query_gain_acc = jnp.zeros((rows, HEAD), F32)
    key_acc = jnp.zeros((keys, HEAD), F32)
    key_acc_turned = jnp.zeros((keys, HEAD), F32)

    def prob_grad_of(head):
        cols = slice(head * HEAD, (head + 1) * HEAD)
        values = jnp.concatenate([far_ref[:, cols], near_ref[:, cols], value_ref[:, cols]], 0)
        return lax.dot_general(
            values, stacked(out_grad_ref, head, group), (((1,), (1,)), ((), ())),
            preferred_element_type=F32,
        )

    later = prob_grad_of(0)
    for head in range(heads):
        prob_grad = later
        if head + 1 < heads:
            later = prob_grad_of(head + 1)
        cols = slice(head * HEAD, (head + 1) * HEAD)
        halo_part = slice(head * halo, (head + 1) * halo)
        own_part = slice(head * rows, (head + 1) * rows)
        group_part = slice(head * group * rows, (head + 1) * group * rows)
        probs = probs_ref[head * keys : (head + 1) * keys, :]
        delta = jnp.sum(probs * prob_grad, axis=0, keepdims=True)
        score_grad = (probs * (prob_grad - delta)).astype(BF16)
        key_term = (
            jnp.dot(score_grad, query_rot_ref[group_part, :], preferred_element_type=F32) * SCALE
        )
        keys_rot = jnp.concatenate([halo_rot_ref[halo_part, :], key_rot_ref[own_part, :]], 0)
        query_term = lax.dot_general(
            score_grad, keys_rot, (((0,), (0,)), ((), ())), preferred_element_type=F32
        )
        halo_key = key_term[:halo].astype(BF16)
        far_key_ref[:, cols] = halo_key[:rows]
        near_key_ref[:, cols] = halo_key[rows:]
        own_key_ref[:, cols] = key_term[halo:]
        term = jnp.concatenate([halo_key.astype(F32), key_term[halo:]], 0)
        scaled = jnp.concatenate([halo_scaled_ref[halo_part, :], key_scaled_ref[own_part, :]], 0)
        key_acc = key_acc + term * scaled
        key_acc_turned = key_acc_turned + term * roll_half(scaled)
        for one in range(group):
            index = head * group + one
            part = slice(index * rows, (index + 1) * rows)
            grad, gain_part = norm_backward(
                query_term[one * rows : (one + 1) * rows],
                query_scaled_ref[part, :], query_scale_ref[part, :], query_gain, own_cos, own_sin,
            )
            grad_query_ref[:, index * HEAD : (index + 1) * HEAD] = grad.astype(BF16)
            query_gain_acc = query_gain_acc + gain_part
    query_sum = jnp.sum(query_gain_acc, axis=0, keepdims=True)
    key_sum = jnp.sum(key_acc * cos_ref[...], axis=0, keepdims=True)
    turned_sum = jnp.sum(key_acc_turned * sin_ref[...], axis=0, keepdims=True)
    both = jnp.concatenate([query_sum, key_sum + turned_gain(turned_sum)], 0)
    gain_ref[...] = jnp.broadcast_to(both[None], gain_ref.shape)


def finish_kernel(
    own_key_ref, own_value_ref, near_key_ref, far_key_ref, near_value_ref, far_value_ref,
    key_scaled_ref, key_scale_ref, cos_ref, sin_ref, key_gain_ref, gains_ref,
    grad_key_ref, grad_value_ref, query_gain_ref, grad_key_gain_ref,
):
    rows = own_key_ref.shape[0]
    cos, sin = cos_ref[WINDOW:], sin_ref[WINDOW:]
    gain = key_gain_ref[...]
    for head in range(own_key_ref.shape[1] // HEAD):
        cols = slice(head * HEAD, (head + 1) * HEAD)
        part = slice(head * rows, (head + 1) * rows)
        key_sum = (
            own_key_ref[:, cols] + near_key_ref[:, cols].astype(F32) + far_key_ref[:, cols].astype(F32)
        )
        grad, _ = norm_backward(
            key_sum, key_scaled_ref[part, :], key_scale_ref[part, :], gain, cos, sin
        )
        grad_key_ref[:, cols] = grad.astype(BF16)
        value_sum = (
            own_value_ref[:, cols]
            + near_value_ref[:, cols].astype(F32)
            + far_value_ref[:, cols].astype(F32)
        )
        grad_value_ref[:, cols] = value_sum.astype(BF16)
    total = jnp.sum(gains_ref[...], axis=0)
    query_gain_ref[...] = total[:1]
    grad_key_gain_ref[...] = total[1:]


def call(kernel, name, outs, operands, cost=None, smem=0):
    return pl.pallas_call(
        kernel,
        out_shape=outs,
        in_specs=[pl.BlockSpec(memory_space=pltpu.SMEM)] * smem
        + [pl.BlockSpec(memory_space=pltpu.VMEM)] * (len(operands) - smem),
        out_specs=[pl.BlockSpec(memory_space=pltpu.VMEM)] * len(outs),
        compiler_params=pltpu.CompilerParams(vmem_limit_bytes=VMEM_LIMIT),
        cost_estimate=cost,
        name=name,
    )(*operands)


def cost(flops, size, exps=0):
    return pl.CostEstimate(flops=flops, bytes_accessed=size, transcendentals=exps)


def shape(dims, dtype):
    return jax.ShapeDtypeStruct(dims, dtype)


def on_device(doc_lengths, query_raw, key_raw, value_matrix, out_grad, query_gain, key_gain):
    rows, query_width = query_raw.shape
    width = key_raw.shape[1]
    heads = width // HEAD
    query_heads = query_width // HEAD
    keys = WINDOW + rows
    devices = lax.axis_size(AXES)
    query_gain = query_gain.reshape(1, HEAD)
    key_gain = key_gain.reshape(1, HEAD)
    near_key, far_key = shift(key_raw, 1), shift(key_raw, 2)
    near_value, far_value = shift(value_matrix, 1), shift(value_matrix, 2)
    term = shape((rows, width), BF16)
    own = shape((rows, width), F32)
    (
        query_rot, query_scaled, query_scale, key_rot, key_scaled, key_scale, cos, sin, bias,
    ) = call(
        prepare_kernel,
        "prepare",
        [
            shape((query_heads * rows, HEAD), BF16),
            shape((query_heads * rows, HEAD), F32),
            shape((query_heads * rows, HEAD), F32),
            shape((heads * rows, HEAD), BF16),
            shape((heads * rows, HEAD), F32),
            shape((heads * rows, HEAD), F32),
            shape((keys, HEAD), F32),
            shape((keys, HEAD), F32),
            shape((keys, rows), F32),
        ],
        (doc_lengths, query_raw, key_raw, query_gain, key_gain, jnp.asarray(frequencies())),
        cost(4_000_000, 3_000_000),
        smem=1,
    )
    probs, halo_rot, halo_scaled, far_value_term, near_value_term, own_value = call(
        attend_keys_kernel,
        "attend_keys",
        [
            shape((heads * keys, query_heads // heads * rows), F32),
            shape((heads * WINDOW, HEAD), BF16),
            shape((heads * WINDOW, HEAD), F32),
            term,
            term,
            own,
        ],
        (far_key, near_key, out_grad, query_rot, key_rot, cos, sin, bias, key_gain),
        cost(400_000_000, 4_000_000, 800_000),
    )
    near_value_back, far_value_back = shift(near_value_term, -1), shift(far_value_term, -2)
    far_key_term, near_key_term, own_key, grad_query, gains = call(
        attend_values_kernel,
        "attend_values",
        [term, term, own, shape((rows, query_width), BF16), shape((devices, 2, HEAD), F32)],
        (
            far_value, near_value, value_matrix, out_grad, probs, query_rot, key_rot,
            halo_rot, halo_scaled, key_scaled, query_scaled, query_scale, cos, sin, query_gain,
        ),
        cost(600_000_000, 4_000_000),
    )
    near_key_back, far_key_back = shift(near_key_term, -1), shift(far_key_term, -2)
    gains = exchange(gains)
    grad_key, grad_value, grad_query_gain, grad_key_gain = call(
        finish_kernel,
        "finish",
        [term, term, shape((1, HEAD), F32), shape((1, HEAD), F32)],
        (
            own_key, own_value, near_key_back, far_key_back, near_value_back, far_value_back,
            key_scaled, key_scale, cos, sin, key_gain, gains,
        ),
        cost(4_000_000, 4_000_000),
    )
    return (
        grad_query, grad_key, grad_value, grad_query_gain.reshape(HEAD), grad_key_gain.reshape(HEAD)
    )


def solution(mesh):
    rows = P(AXES, None)
    return jax.shard_map(
        on_device,
        mesh=mesh,
        in_specs=(P(), rows, rows, rows, rows, P(), P()),
        out_specs=(rows, rows, rows, P(), P()),
        check_vma=False,
    )
```

```python
import math

import jax
import jax.numpy as jnp
import numpy as np
from jax import lax
from jax.experimental import pallas as pl
from jax.experimental.pallas import tpu as pltpu
from jax.sharding import PartitionSpec as P

HEAD = 128
HALF = HEAD // 2
WINDOW = 256
EPS = 1e-06
SCALE = 168.0 ** (-0.5)
ROPE_BASE = 10000.0
MASKED = -1e30
AXES = ("ctx", "grp")
F32 = jnp.float32
BF16 = jnp.bfloat16
VMEM_LIMIT = 40 * 1024 * 1024


def frequencies():
    lane = lax.broadcasted_iota(jnp.int32, (1, HEAD), 1) % HALF
    values = jnp.zeros((1, HEAD), F32)
    for m in range(HALF):
        values = jnp.where(lane == m, np.float32(ROPE_BASE ** (-2.0 * m / HEAD)), values)
    return values


def shift(value, steps):
    count = lax.axis_size(AXES)
    return lax.ppermute(value, AXES, [(s, (s + steps) % count) for s in range(count)])


def own_index():
    return lax.axis_index("ctx") * lax.axis_size("grp") + lax.axis_index("grp")


def roll_half(x):
    return pltpu.roll(x, HALF, 1)


def doc_starts(tokens, lengths_ref):
    def step(doc, carry):
        end, starts = carry
        end = end + lengths_ref[doc]
        return end, jnp.where(tokens >= end, end, starts)

    count = lengths_ref.shape[0]
    return lax.fori_loop(
        0, count, step, (jnp.int32(0), jnp.zeros_like(tokens)), unroll=count if count <= 8 else 1
    )[1]


def cos_sin_lanes(angle, lane):
    turns = jnp.floor(angle * (2.0 / math.pi) + 0.5)
    r = angle - turns * 1.5703125
    r = r - turns * 4.837512969970703125e-4
    r = r - turns * 7.549789948768648e-8
    z = r * r
    sin_r = r + r * z * (-1.6666654611e-1 + z * (8.3321608736e-3 + z * -1.9515295891e-4))
    cos_r = 1.0 - 0.5 * z + z * z * (
        4.166664568298827e-2 + z * (-1.388731625493765e-3 + z * 2.443315711809948e-5)
    )
    quadrant = turns.astype(jnp.int32) - jnp.where(lane >= HALF, 1, 0)
    odd = (quadrant & 1) == 1
    value = jnp.where(odd, sin_r, cos_r)
    negative = ((quadrant + 1) & 2) == 2
    return jnp.where(negative, -value, value)


def row_scale(x):
    return lax.rsqrt(jnp.sum(x * x, axis=1, keepdims=True) * (1.0 / HEAD) + EPS)


def turned_gain(gain):
    return roll_half(jnp.broadcast_to(gain, (8, HEAD)))[:1]


def prepare_kernel(
    lengths_hbm, query_hbm, key_hbm, value_hbm, out_grad_hbm, query_gain_hbm, key_gain_hbm,
    query_rot_ref, query_scaled_ref, query_scale_ref,
    key_rot_ref, key_scaled_ref, key_scale_ref, cos_ref, sin_ref, bias_ref,
    value_ref, out_grad_ref, gains_ref,
    lengths_ref, query_ref, key_ref, sems,
):
    moves = [
        pltpu.make_async_copy(source, target, sems.at[place])
        for place, (source, target) in enumerate(
            (
                (lengths_hbm, lengths_ref),
                (query_gain_hbm, gains_ref.at[0:1]),
                (key_gain_hbm, gains_ref.at[1:2]),
                (key_hbm, key_ref),
                (query_hbm, query_ref),
                (out_grad_hbm, out_grad_ref),
                (value_hbm, value_ref),
            )
        )
    ]
    for move in moves:
        move.start()
    rows = query_ref.shape[0]
    keys = cos_ref.shape[0]
    base = own_index() * rows - (keys - rows)
    shape = (keys, HEAD)
    lane = lax.broadcasted_iota(jnp.int32, shape, 1)
    tokens = base + lax.broadcasted_iota(jnp.int32, shape, 0)
    frequency = frequencies()
    moves[0].wait()
    positions = tokens - doc_starts(tokens, lengths_ref)
    mixed = cos_sin_lanes(positions.astype(F32) * frequency, lane)
    turned = roll_half(mixed)
    cos = jnp.where(lane < HALF, mixed, turned)
    sin = jnp.where(lane < HALF, -turned, mixed)
    cos_ref[...] = cos
    sin_ref[...] = sin
    queries = base + (keys - rows) + lax.broadcasted_iota(jnp.int32, (1, rows), 1)
    lowest = jnp.maximum(doc_starts(queries, lengths_ref), queries - (WINDOW - 1))
    key_tokens = base + lax.broadcasted_iota(jnp.int32, (keys, rows), 0)
    visible = (key_tokens >= lowest) & (key_tokens <= queries)
    bias_ref[...] = jnp.where(visible, 0.0, MASKED)
    own_cos, own_sin = cos[keys - rows :], sin[keys - rows :]
    moves[1].wait()
    moves[2].wait()
    for raw_ref, move, row, rot_ref, scaled_ref, scale_ref in (
        (key_ref, moves[3], 1, key_rot_ref, key_scaled_ref, key_scale_ref),
        (query_ref, moves[4], 0, query_rot_ref, query_scaled_ref, query_scale_ref),
    ):
        gain = gains_ref[row : row + 1]
        cos_gain = own_cos * gain
        sin_gain = own_sin * turned_gain(gain)
        move.wait()
        for head in range(raw_ref.shape[1] // HEAD):
            part = slice(head * rows, (head + 1) * rows)
            x = raw_ref[:, head * HEAD : (head + 1) * HEAD].astype(F32)
            scale = jnp.broadcast_to(row_scale(x), x.shape)
            scaled = x * scale
            scale_ref[part, :] = scale
            scaled_ref[part, :] = scaled
            rot_ref[part, :] = (scaled * cos_gain + roll_half(scaled) * sin_gain).astype(BF16)
    moves[5].wait()
    moves[6].wait()


def stacked(ref, head, group):
    return jnp.concatenate(
        [ref[:, (head * group + one) * HEAD : (head * group + one + 1) * HEAD] for one in range(group)],
        0,
    )


def attend_keys_kernel(
    far_ref, near_ref, out_grad_ref, query_rot_ref, key_rot_ref, cos_ref, sin_ref, bias_ref,
    gains_ref,
    probs_ref, halo_rot_ref, halo_scaled_ref, far_value_ref, near_value_ref, own_value_ref,
):
    rows = far_ref.shape[0]
    heads = far_ref.shape[1] // HEAD
    group = out_grad_ref.shape[1] // far_ref.shape[1]
    halo = WINDOW
    keys = halo + rows
    key_gain = gains_ref[1:2]
    cos_gain = cos_ref[:halo] * key_gain
    sin_gain = sin_ref[:halo] * turned_gain(key_gain)
    bias = jnp.concatenate([bias_ref[...]] * group, 1)

    def scores_of(head):
        cols = slice(head * HEAD, (head + 1) * HEAD)
        raw = jnp.concatenate([far_ref[:, cols], near_ref[:, cols]], 0).astype(F32)
        scaled = raw * row_scale(raw)
        halo_scaled_ref[head * halo : (head + 1) * halo, :] = scaled
        rotated = (scaled * cos_gain + roll_half(scaled) * sin_gain).astype(BF16)
        halo_rot_ref[head * halo : (head + 1) * halo, :] = rotated
        both = jnp.concatenate([rotated, key_rot_ref[head * rows : (head + 1) * rows, :]], 0)
        queries = query_rot_ref[head * group * rows : (head + 1) * group * rows, :]
        return lax.dot_general(
            both, queries, (((1,), (1,)), ((), ())), preferred_element_type=F32
        )

    later = scores_of(0)
    for head in range(heads):
        scores = later
        if head + 1 < heads:
            later = scores_of(head + 1)
        cols = slice(head * HEAD, (head + 1) * HEAD)
        scores = scores * (SCALE * math.log2(math.e)) + bias
        exps = jnp.exp2(scores - jnp.max(scores, axis=0, keepdims=True))
        probs = exps * (1.0 / jnp.sum(exps, axis=0, keepdims=True))
        probs_ref[head * keys : (head + 1) * keys, :] = probs
        value_term = jnp.dot(
            probs.astype(BF16), stacked(out_grad_ref, head, group), preferred_element_type=F32
        )
        far_value_ref[:, cols] = value_term[:rows].astype(BF16)
        near_value_ref[:, cols] = value_term[rows:halo].astype(BF16)
        own_value_ref[:, cols] = value_term[halo:]


def norm_backward(grad_rot, scaled, scale, gain, cos, sin):
    normed_grad = grad_rot * cos - roll_half(grad_rot) * sin
    part = normed_grad * scaled
    mean = jnp.sum(part * gain, axis=1, keepdims=True) * (1.0 / HEAD)
    return scale * (normed_grad * gain - scaled * mean), part


def attend_values_kernel(
    far_ref, near_ref, value_ref, out_grad_ref, probs_ref, query_rot_ref, key_rot_ref,
    halo_rot_ref, halo_scaled_ref, key_scaled_ref, query_scaled_ref, query_scale_ref,
    cos_ref, sin_ref, gains_ref,
    far_key_ref, near_key_ref, own_key_ref, grad_query_ref, gain_ref,
):
    rows = far_ref.shape[0]
    heads = far_ref.shape[1] // HEAD
    group = out_grad_ref.shape[1] // far_ref.shape[1]
    halo = WINDOW
    keys = halo + rows
    query_gain = gains_ref[0:1]
    own_cos, own_sin = cos_ref[halo:] * SCALE, sin_ref[halo:] * SCALE
    query_gain_acc = jnp.zeros((rows, HEAD), F32)
    key_acc = jnp.zeros((keys, HEAD), F32)
    key_acc_turned = jnp.zeros((keys, HEAD), F32)

    def prob_grad_of(head):
        cols = slice(head * HEAD, (head + 1) * HEAD)
        values = jnp.concatenate([far_ref[:, cols], near_ref[:, cols], value_ref[:, cols]], 0)
        return lax.dot_general(
            values, stacked(out_grad_ref, head, group), (((1,), (1,)), ((), ())),
            preferred_element_type=F32,
        )

    later = prob_grad_of(0)
    for head in range(heads):
        prob_grad = later
        if head + 1 < heads:
            later = prob_grad_of(head + 1)
        cols = slice(head * HEAD, (head + 1) * HEAD)
        halo_part = slice(head * halo, (head + 1) * halo)
        own_part = slice(head * rows, (head + 1) * rows)
        group_part = slice(head * group * rows, (head + 1) * group * rows)
        probs = probs_ref[head * keys : (head + 1) * keys, :]
        delta = jnp.sum(probs * prob_grad, axis=0, keepdims=True)
        score_grad = (probs * (prob_grad - delta)).astype(BF16)
        key_term = (
            jnp.dot(score_grad, query_rot_ref[group_part, :], preferred_element_type=F32) * SCALE
        )
        keys_rot = jnp.concatenate([halo_rot_ref[halo_part, :], key_rot_ref[own_part, :]], 0)
        query_term = lax.dot_general(
            score_grad, keys_rot, (((0,), (0,)), ((), ())), preferred_element_type=F32
        )
        halo_key = key_term[:halo].astype(BF16)
        far_key_ref[:, cols] = halo_key[:rows]
        near_key_ref[:, cols] = halo_key[rows:]
        own_key_ref[:, cols] = key_term[halo:]
        term = jnp.concatenate([halo_key.astype(F32), key_term[halo:]], 0)
        scaled = jnp.concatenate([halo_scaled_ref[halo_part, :], key_scaled_ref[own_part, :]], 0)
        key_acc = key_acc + term * scaled
        key_acc_turned = key_acc_turned + term * roll_half(scaled)
        for one in range(group):
            index = head * group + one
            part = slice(index * rows, (index + 1) * rows)
            grad, gain_part = norm_backward(
                query_term[one * rows : (one + 1) * rows],
                query_scaled_ref[part, :], query_scale_ref[part, :], query_gain, own_cos, own_sin,
            )
            grad_query_ref[:, index * HEAD : (index + 1) * HEAD] = grad.astype(BF16)
            query_gain_acc = query_gain_acc + gain_part
    query_sum = jnp.sum(query_gain_acc, axis=0, keepdims=True)
    key_sum = jnp.sum(key_acc * cos_ref[...], axis=0, keepdims=True)
    turned_sum = jnp.sum(key_acc_turned * sin_ref[...], axis=0, keepdims=True)
    gain_ref[...] = jnp.concatenate([query_sum, key_sum + turned_gain(turned_sum)], 0)


def finish_values_kernel(own_ref, near_ref, far_ref, gain_ref, grad_value_ref, copies_ref):
    total = own_ref[...] + near_ref[...].astype(F32) + far_ref[...].astype(F32)
    grad_value_ref[...] = total.astype(BF16)
    copies_ref[...] = jnp.broadcast_to(gain_ref[...][None], copies_ref.shape)


def finish_keys_kernel(
    own_ref, near_ref, far_ref, key_scaled_ref, key_scale_ref, cos_ref, sin_ref, gains_ref, parts_ref,
    grad_key_ref, query_gain_ref, key_gain_ref,
):
    rows = own_ref.shape[0]
    cos, sin = cos_ref[WINDOW:], sin_ref[WINDOW:]
    gain = gains_ref[1:2]
    for head in range(own_ref.shape[1] // HEAD):
        cols = slice(head * HEAD, (head + 1) * HEAD)
        part = slice(head * rows, (head + 1) * rows)
        total = own_ref[:, cols] + near_ref[:, cols].astype(F32) + far_ref[:, cols].astype(F32)
        grad, _ = norm_backward(total, key_scaled_ref[part, :], key_scale_ref[part, :], gain, cos, sin)
        grad_key_ref[:, cols] = grad.astype(BF16)
    sums = jnp.sum(parts_ref[...], axis=0)
    query_gain_ref[...] = sums[:1]
    key_gain_ref[...] = sums[1:]


def call(kernel, name, outs, operands, cost=None, space=pltpu.VMEM, scratch=()):
    return pl.pallas_call(
        kernel,
        out_shape=outs,
        in_specs=[pl.BlockSpec(memory_space=space)] * len(operands),
        out_specs=[pl.BlockSpec(memory_space=pltpu.VMEM)] * len(outs),
        scratch_shapes=scratch,
        compiler_params=pltpu.CompilerParams(vmem_limit_bytes=VMEM_LIMIT),
        cost_estimate=cost,
        name=name,
    )(*operands)


def cost(flops, size, exps=0):
    return pl.CostEstimate(flops=flops, bytes_accessed=size, transcendentals=exps)


def shape(dims, dtype):
    return jax.ShapeDtypeStruct(dims, dtype)


def on_device(doc_lengths, query_raw, key_raw, value_matrix, out_grad, query_gain, key_gain):
    rows, query_width = query_raw.shape
    width = key_raw.shape[1]
    heads = width // HEAD
    query_heads = query_width // HEAD
    keys = WINDOW + rows
    devices = lax.axis_size(AXES)
    query_gain = query_gain.reshape(1, HEAD)
    key_gain = key_gain.reshape(1, HEAD)
    near_key, far_key = shift(key_raw, 1), shift(key_raw, 2)
    near_value, far_value = shift(value_matrix, 1), shift(value_matrix, 2)
    term = shape((rows, width), BF16)
    own = shape((rows, width), F32)
    (
        query_rot, query_scaled, query_scale, key_rot, key_scaled, key_scale, cos, sin, bias,
        values, grads_out, gains,
    ) = call(
        prepare_kernel,
        "prepare",
        [
            shape((query_heads * rows, HEAD), BF16),
            shape((query_heads * rows, HEAD), F32),
            shape((query_heads * rows, HEAD), F32),
            shape((heads * rows, HEAD), BF16),
            shape((heads * rows, HEAD), F32),
            shape((heads * rows, HEAD), F32),
            shape((keys, HEAD), F32),
            shape((keys, HEAD), F32),
            shape((keys, rows), F32),
            term,
            shape((rows, query_width), BF16),
            shape((8, HEAD), F32),
        ],
        [
            pltpu.with_memory_space_constraint(x, pltpu.HBM)
            for x in (doc_lengths, query_raw, key_raw, value_matrix, out_grad, query_gain, key_gain)
        ],
        cost(4_000_000, 6_000_000),
        space=pltpu.HBM,
        scratch=[
            pltpu.SMEM(doc_lengths.shape, jnp.int32),
            pltpu.VMEM((rows, query_width), BF16),
            pltpu.VMEM((rows, width), BF16),
            pltpu.SemaphoreType.DMA((7,)),
        ],
    )
    probs, halo_rot, halo_scaled, far_value_term, near_value_term, own_value = call(
        attend_keys_kernel,
        "attend_keys",
        [
            shape((heads * keys, query_heads // heads * rows), F32),
            shape((heads * WINDOW, HEAD), BF16),
            shape((heads * WINDOW, HEAD), F32),
            term,
            term,
            own,
        ],
        (far_key, near_key, grads_out, query_rot, key_rot, cos, sin, bias, gains),
        cost(400_000_000, 4_000_000, 800_000),
    )
    near_value_back, far_value_back = shift(near_value_term, -1), shift(far_value_term, -2)
    far_key_term, near_key_term, own_key, grad_query, gain_part = call(
        attend_values_kernel,
        "attend_values",
        [term, term, own, shape((rows, query_width), BF16), shape((2, HEAD), F32)],
        (
            far_value, near_value, values, grads_out, probs, query_rot, key_rot,
            halo_rot, halo_scaled, key_scaled, query_scaled, query_scale, cos, sin, gains,
        ),
        cost(600_000_000, 4_000_000),
    )
    near_key_back, far_key_back = shift(near_key_term, -1), shift(far_key_term, -2)
    grad_value, copies = call(
        finish_values_kernel,
        "finish_values",
        [term, shape((devices, 2, HEAD), F32)],
        (own_value, near_value_back, far_value_back, gain_part),
        cost(1_000_000, 2_000_000),
    )
    parts = lax.all_to_all(copies, AXES, 0, 0)
    grad_key, grad_query_gain, grad_key_gain = call(
        finish_keys_kernel,
        "finish_keys",
        [term, shape((1, HEAD), F32), shape((1, HEAD), F32)],
        (own_key, near_key_back, far_key_back, key_scaled, key_scale, cos, sin, gains, parts),
        cost(4_000_000, 3_000_000),
    )
    return (
        grad_query, grad_key, grad_value, grad_query_gain.reshape(HEAD), grad_key_gain.reshape(HEAD)
    )


def solution(mesh):
    rows = P(AXES, None)
    return jax.shard_map(
        on_device,
        mesh=mesh,
        in_specs=(P(), rows, rows, rows, rows, P(), P()),
        out_specs=(rows, rows, rows, P(), P()),
        check_vma=False,
    )
```

```python
import math

import jax
import jax.numpy as jnp
import numpy as np
from jax import lax
from jax.experimental import pallas as pl
from jax.experimental.pallas import tpu as pltpu
from jax.sharding import PartitionSpec as P

HEAD = 128
HALF = HEAD // 2
WINDOW = 256
EPS = 1e-06
SCALE = 168.0 ** (-0.5)
ROPE_BASE = 10000.0
MASKED = -1e30
AXES = ("ctx", "grp")
F32 = jnp.float32
BF16 = jnp.bfloat16
VMEM_LIMIT = 40 * 1024 * 1024


def frequencies():
    lane = lax.broadcasted_iota(jnp.int32, (1, HEAD), 1) % HALF
    values = jnp.zeros((1, HEAD), F32)
    for m in range(HALF):
        values = jnp.where(lane == m, np.float32(ROPE_BASE ** (-2.0 * m / HEAD)), values)
    return values


def shift(value, steps):
    count = lax.axis_size(AXES)
    return lax.ppermute(value, AXES, [(s, (s + steps) % count) for s in range(count)])


def stage_sizes(count):
    sizes = []
    while count > 1:
        sizes.append(next(size for size in range(min(count, 8), 0, -1) if count % size == 0))
        count //= sizes[-1]
    return sizes


def exchange(copies, stride):
    count, size = lax.axis_size(AXES), copies.shape[0]
    groups = [
        [base + low + digit * stride for digit in range(size)]
        for base in range(0, count, stride * size)
        for low in range(stride)
    ]
    return lax.all_to_all(copies, AXES, 0, 0, axis_index_groups=groups)


def own_index():
    return lax.axis_index("ctx") * lax.axis_size("grp") + lax.axis_index("grp")


def roll_half(x):
    return pltpu.roll(x, HALF, 1)


def doc_starts(tokens, lengths_ref):
    def step(doc, carry):
        end, starts = carry
        end = end + lengths_ref[doc]
        return end, jnp.where(tokens >= end, end, starts)

    count = lengths_ref.shape[0]
    return lax.fori_loop(
        0, count, step, (jnp.int32(0), jnp.zeros_like(tokens)), unroll=count if count <= 8 else 1
    )[1]


def cos_sin_lanes(angle, lane):
    turns = jnp.floor(angle * (2.0 / math.pi) + 0.5)
    r = angle - turns * 1.5703125
    r = r - turns * 4.837512969970703125e-4
    r = r - turns * 7.549789948768648e-8
    z = r * r
    sin_r = r + r * z * (-1.6666654611e-1 + z * (8.3321608736e-3 + z * -1.9515295891e-4))
    cos_r = 1.0 - 0.5 * z + z * z * (
        4.166664568298827e-2 + z * (-1.388731625493765e-3 + z * 2.443315711809948e-5)
    )
    quadrant = turns.astype(jnp.int32) - jnp.where(lane >= HALF, 1, 0)
    odd = (quadrant & 1) == 1
    value = jnp.where(odd, sin_r, cos_r)
    negative = ((quadrant + 1) & 2) == 2
    return jnp.where(negative, -value, value)


def row_sums(x):
    high = x.astype(BF16)
    low = (x - high.astype(F32)).astype(BF16)
    ones = jnp.ones((2 * HEAD, HEAD), BF16)
    return jnp.dot(jnp.concatenate([high, low], 1), ones, preferred_element_type=F32)


def row_scale(x):
    return lax.rsqrt(row_sums(x * x) * (1.0 / HEAD) + EPS)


def turning():
    source = lax.broadcasted_iota(jnp.int32, (HEAD, HEAD), 0)
    target = lax.broadcasted_iota(jnp.int32, (HEAD, HEAD), 1)
    return jnp.where(target == (source + HALF) % HEAD, 1.0, 0.0).astype(BF16)


def turned_rows(raw, matrix):
    return jnp.dot(raw, matrix, preferred_element_type=F32)


def turned_gain(gain):
    return roll_half(jnp.broadcast_to(gain, (8, HEAD)))[:1]


def prepare_kernel(
    lengths_hbm, query_hbm, key_hbm, value_hbm, out_grad_hbm, query_gain_hbm, key_gain_hbm,
    query_rot_ref, query_scaled_ref, query_scale_ref,
    key_rot_ref, key_scaled_ref, key_turned_ref, key_scale_ref, cos_ref, sin_ref, bias_ref,
    value_ref, out_grad_ref, gains_ref,
    lengths_ref, query_ref, key_ref, sems,
):
    moves = [
        pltpu.make_async_copy(source, target, sems.at[place])
        for place, (source, target) in enumerate(
            (
                (lengths_hbm, lengths_ref),
                (query_gain_hbm, gains_ref.at[0:1]),
                (key_gain_hbm, gains_ref.at[1:2]),
                (key_hbm, key_ref),
                (query_hbm, query_ref),
                (out_grad_hbm, out_grad_ref),
                (value_hbm, value_ref),
            )
        )
    ]
    for move in moves:
        move.start()
    rows = query_ref.shape[0]
    keys = cos_ref.shape[0]
    base = own_index() * rows - (keys - rows)
    shape = (keys, HEAD)
    lane = lax.broadcasted_iota(jnp.int32, shape, 1)
    tokens = base + lax.broadcasted_iota(jnp.int32, shape, 0)
    frequency = frequencies()
    moves[0].wait()
    positions = tokens - doc_starts(tokens, lengths_ref)
    mixed = cos_sin_lanes(positions.astype(F32) * frequency, lane)
    turned = roll_half(mixed)
    cos = jnp.where(lane < HALF, mixed, turned)
    sin = jnp.where(lane < HALF, -turned, mixed)
    cos_ref[...] = cos
    sin_ref[...] = sin
    queries = base + (keys - rows) + lax.broadcasted_iota(jnp.int32, (1, rows), 1)
    lowest = jnp.maximum(doc_starts(queries, lengths_ref), queries - (WINDOW - 1))
    key_tokens = base + lax.broadcasted_iota(jnp.int32, (keys, rows), 0)
    visible = (key_tokens >= lowest) & (key_tokens <= queries)
    bias_ref[...] = jnp.where(visible, 0.0, MASKED)
    own_cos, own_sin = cos[keys - rows :], sin[keys - rows :]
    moves[1].wait()
    moves[2].wait()
    matrix = turning()
    for raw_ref, move, row, rot_ref, scaled_ref, scale_ref in (
        (key_ref, moves[3], 1, key_rot_ref, key_scaled_ref, key_scale_ref),
        (query_ref, moves[4], 0, query_rot_ref, query_scaled_ref, query_scale_ref),
    ):
        gain = gains_ref[row : row + 1]
        cos_gain = own_cos * gain
        sin_gain = own_sin * turned_gain(gain)
        move.wait()
        for head in range(raw_ref.shape[1] // HEAD):
            part = slice(head * rows, (head + 1) * rows)
            raw = raw_ref[:, head * HEAD : (head + 1) * HEAD]
            x = raw.astype(F32)
            scale = row_scale(x)
            scaled = x * scale
            turned = turned_rows(raw, matrix) * scale
            scale_ref[part, :] = scale
            scaled_ref[part, :] = scaled
            rot_ref[part, :HEAD] = (scaled * cos_gain + turned * sin_gain).astype(BF16)
            if raw_ref is key_ref:
                key_turned_ref[part, :] = turned
                rot_ref[part, HEAD:] = (
                    turned * roll_half(cos_gain) + scaled * roll_half(sin_gain)
                ).astype(BF16)
    moves[5].wait()
    moves[6].wait()


def stacked(ref, head, group):
    return jnp.concatenate(
        [ref[:, (head * group + one) * HEAD : (head * group + one + 1) * HEAD] for one in range(group)],
        0,
    )


def attend_keys_kernel(
    far_ref, near_ref, out_grad_ref, query_rot_ref, key_rot_ref, cos_ref, sin_ref, bias_ref,
    gains_ref,
    probs_ref, halo_rot_ref, halo_scaled_ref, halo_turned_ref, far_value_ref, near_value_ref, own_value_ref,
):
    rows = far_ref.shape[0]
    heads = far_ref.shape[1] // HEAD
    group = out_grad_ref.shape[1] // far_ref.shape[1]
    halo = WINDOW
    keys = halo + rows
    key_gain = gains_ref[1:2]
    cos_gain = cos_ref[:halo] * key_gain
    sin_gain = sin_ref[:halo] * turned_gain(key_gain)
    cos_turned, sin_turned = roll_half(cos_gain), roll_half(sin_gain)
    bias = jnp.concatenate([bias_ref[...]] * group, 1)
    matrix = turning()

    def scores_of(head):
        cols = slice(head * HEAD, (head + 1) * HEAD)
        raw = jnp.concatenate([far_ref[:, cols], near_ref[:, cols]], 0)
        x = raw.astype(F32)
        scale = row_scale(x)
        scaled = x * scale
        turned = turned_rows(raw, matrix) * scale
        part = slice(head * halo, (head + 1) * halo)
        halo_scaled_ref[part, :] = scaled
        halo_turned_ref[part, :] = turned
        rotated = (scaled * cos_gain + turned * sin_gain).astype(BF16)
        halo_rot_ref[part, :HEAD] = rotated
        halo_rot_ref[part, HEAD:] = (turned * cos_turned + scaled * sin_turned).astype(BF16)
        both = jnp.concatenate([rotated, key_rot_ref[head * rows : (head + 1) * rows, :HEAD]], 0)
        queries = query_rot_ref[head * group * rows : (head + 1) * group * rows, :]
        return lax.dot_general(
            both, queries, (((1,), (1,)), ((), ())), preferred_element_type=F32
        )

    later = scores_of(0)
    for head in range(heads):
        scores = later
        if head + 1 < heads:
            later = scores_of(head + 1)
        cols = slice(head * HEAD, (head + 1) * HEAD)
        scores = scores * (SCALE * math.log2(math.e)) + bias
        exps = jnp.exp2(scores - jnp.max(scores, axis=0, keepdims=True))
        probs = exps * (1.0 / jnp.sum(exps, axis=0, keepdims=True))
        probs_ref[head * keys : (head + 1) * keys, :] = probs
        value_term = jnp.dot(
            probs.astype(BF16), stacked(out_grad_ref, head, group), preferred_element_type=F32
        )
        far_value_ref[:, cols] = value_term[:rows].astype(BF16)
        near_value_ref[:, cols] = value_term[rows:halo].astype(BF16)
        own_value_ref[:, cols] = value_term[halo:]


def norm_backward(grad_rot, grad_turned, scaled, scale, gain, cos, sin):
    normed_grad = grad_rot * cos - grad_turned * sin
    part = normed_grad * scaled
    mean = row_sums(part * gain) * (1.0 / HEAD)
    return scale * (normed_grad * gain - scaled * mean), part


def attend_values_kernel(
    far_ref, near_ref, value_ref, out_grad_ref, probs_ref, query_rot_ref, key_rot_ref,
    halo_rot_ref, halo_scaled_ref, halo_turned_ref, key_scaled_ref, key_turned_ref,
    query_scaled_ref, query_scale_ref, cos_ref, sin_ref, gains_ref,
    far_key_ref, near_key_ref, own_key_ref, grad_query_ref, gain_ref,
):
    rows = far_ref.shape[0]
    heads = far_ref.shape[1] // HEAD
    group = out_grad_ref.shape[1] // far_ref.shape[1]
    halo = WINDOW
    keys = halo + rows
    query_gain = gains_ref[0:1]
    own_cos, own_sin = cos_ref[halo:] * SCALE, sin_ref[halo:] * SCALE
    query_gain_acc = jnp.zeros((rows, HEAD), F32)
    key_acc = jnp.zeros((keys, HEAD), F32)
    key_acc_turned = jnp.zeros((keys, HEAD), F32)

    def prob_grad_of(head):
        cols = slice(head * HEAD, (head + 1) * HEAD)
        values = jnp.concatenate([far_ref[:, cols], near_ref[:, cols], value_ref[:, cols]], 0)
        return lax.dot_general(
            values, stacked(out_grad_ref, head, group), (((1,), (1,)), ((), ())),
            preferred_element_type=F32,
        )

    later = prob_grad_of(0)
    for head in range(heads):
        prob_grad = later
        if head + 1 < heads:
            later = prob_grad_of(head + 1)
        cols = slice(head * HEAD, (head + 1) * HEAD)
        halo_part = slice(head * halo, (head + 1) * halo)
        own_part = slice(head * rows, (head + 1) * rows)
        group_part = slice(head * group * rows, (head + 1) * group * rows)
        probs = probs_ref[head * keys : (head + 1) * keys, :]
        delta = jnp.sum(probs * prob_grad, axis=0, keepdims=True)
        score_grad = (probs * (prob_grad - delta)).astype(BF16)
        key_term = (
            jnp.dot(score_grad, query_rot_ref[group_part, :], preferred_element_type=F32) * SCALE
        )
        keys_rot = jnp.concatenate([halo_rot_ref[halo_part, :], key_rot_ref[own_part, :]], 0)
        query_term = lax.dot_general(
            score_grad, keys_rot, (((0,), (0,)), ((), ())), preferred_element_type=F32
        )
        halo_key = key_term[:halo].astype(BF16)
        far_key_ref[:, cols] = halo_key[:rows]
        near_key_ref[:, cols] = halo_key[rows:]
        own_key_ref[:, cols] = key_term[halo:]
        term = jnp.concatenate([halo_key.astype(F32), key_term[halo:]], 0)
        scaled = jnp.concatenate([halo_scaled_ref[halo_part, :], key_scaled_ref[own_part, :]], 0)
        key_acc = key_acc + term * scaled
        turned = jnp.concatenate([halo_turned_ref[halo_part, :], key_turned_ref[own_part, :]], 0)
        key_acc_turned = key_acc_turned + term * turned
        for one in range(group):
            index = head * group + one
            part = slice(index * rows, (index + 1) * rows)
            term = query_term[one * rows : (one + 1) * rows]
            grad, gain_part = norm_backward(
                term[:, :HEAD], term[:, HEAD:],
                query_scaled_ref[part, :], query_scale_ref[part, :], query_gain, own_cos, own_sin,
            )
            grad_query_ref[:, index * HEAD : (index + 1) * HEAD] = grad.astype(BF16)
            query_gain_acc = query_gain_acc + gain_part
    query_sum = jnp.sum(query_gain_acc, axis=0, keepdims=True)
    key_sum = jnp.sum(key_acc * cos_ref[...], axis=0, keepdims=True)
    turned_sum = jnp.sum(key_acc_turned * sin_ref[...], axis=0, keepdims=True)
    both = jnp.concatenate([query_sum, key_sum + turned_gain(turned_sum)], 0)
    gain_ref[...] = jnp.broadcast_to(both[None], gain_ref.shape)


def finish_values_kernel(own_ref, near_ref, far_ref, parts_ref, grad_value_ref, copies_ref):
    total = own_ref[...] + near_ref[...].astype(F32) + far_ref[...].astype(F32)
    grad_value_ref[...] = total.astype(BF16)
    copies_ref[...] = jnp.broadcast_to(jnp.sum(parts_ref[...], axis=0)[None], copies_ref.shape)


def finish_keys_kernel(
    own_ref, near_ref, far_ref, key_scaled_ref, key_scale_ref, cos_ref, sin_ref, gains_ref, parts_ref,
    grad_key_ref, query_gain_ref, key_gain_ref,
):
    rows = own_ref.shape[0]
    cos, sin = cos_ref[WINDOW:], sin_ref[WINDOW:]
    gain = gains_ref[1:2]
    for head in range(own_ref.shape[1] // HEAD):
        cols = slice(head * HEAD, (head + 1) * HEAD)
        part = slice(head * rows, (head + 1) * rows)
        total = own_ref[:, cols] + near_ref[:, cols].astype(F32) + far_ref[:, cols].astype(F32)
        grad, _ = norm_backward(
            total, roll_half(total), key_scaled_ref[part, :], key_scale_ref[part, :], gain, cos, sin
        )
        grad_key_ref[:, cols] = grad.astype(BF16)
    sums = jnp.sum(parts_ref[...], axis=0)
    query_gain_ref[...] = sums[:1]
    key_gain_ref[...] = sums[1:]


def call(kernel, name, outs, operands, cost=None, space=pltpu.VMEM, scratch=()):
    return pl.pallas_call(
        kernel,
        out_shape=outs,
        in_specs=[pl.BlockSpec(memory_space=space)] * len(operands),
        out_specs=[pl.BlockSpec(memory_space=pltpu.VMEM)] * len(outs),
        scratch_shapes=scratch,
        compiler_params=pltpu.CompilerParams(vmem_limit_bytes=VMEM_LIMIT),
        cost_estimate=cost,
        name=name,
    )(*operands)


def cost(flops, size, exps=0):
    return pl.CostEstimate(flops=flops, bytes_accessed=size, transcendentals=exps)


def shape(dims, dtype):
    return jax.ShapeDtypeStruct(dims, dtype)


def on_device(doc_lengths, query_raw, key_raw, value_matrix, out_grad, query_gain, key_gain):
    rows, query_width = query_raw.shape
    width = key_raw.shape[1]
    heads = width // HEAD
    query_heads = query_width // HEAD
    keys = WINDOW + rows
    sizes = stage_sizes(lax.axis_size(AXES))
    query_gain = query_gain.reshape(1, HEAD)
    key_gain = key_gain.reshape(1, HEAD)
    near_key, far_key = shift(key_raw, 1), shift(key_raw, 2)
    near_value, far_value = shift(value_matrix, 1), shift(value_matrix, 2)
    term = shape((rows, width), BF16)
    own = shape((rows, width), F32)
    (
        query_rot, query_scaled, query_scale, key_rot, key_scaled, key_turned, key_scale, cos, sin, bias,
        values, grads_out, gains,
    ) = call(
        prepare_kernel,
        "prepare",
        [
            shape((query_heads * rows, HEAD), BF16),
            shape((query_heads * rows, HEAD), F32),
            shape((query_heads * rows, HEAD), F32),
            shape((heads * rows, 2 * HEAD), BF16),
            shape((heads * rows, HEAD), F32),
            shape((heads * rows, HEAD), F32),
            shape((heads * rows, HEAD), F32),
            shape((keys, HEAD), F32),
            shape((keys, HEAD), F32),
            shape((keys, rows), F32),
            term,
            shape((rows, query_width), BF16),
            shape((8, HEAD), F32),
        ],
        [
            pltpu.with_memory_space_constraint(x, pltpu.HBM)
            for x in (doc_lengths, query_raw, key_raw, value_matrix, out_grad, query_gain, key_gain)
        ],
        cost(4_000_000, 6_000_000),
        space=pltpu.HBM,
        scratch=[
            pltpu.SMEM(doc_lengths.shape, jnp.int32),
            pltpu.VMEM((rows, query_width), BF16),
            pltpu.VMEM((rows, width), BF16),
            pltpu.SemaphoreType.DMA((7,)),
        ],
    )
    probs, halo_rot, halo_scaled, halo_turned, far_value_term, near_value_term, own_value = call(
        attend_keys_kernel,
        "attend_keys",
        [
            shape((heads * keys, query_heads // heads * rows), F32),
            shape((heads * WINDOW, 2 * HEAD), BF16),
            shape((heads * WINDOW, HEAD), F32),
            shape((heads * WINDOW, HEAD), F32),
            term,
            term,
            own,
        ],
        (far_key, near_key, grads_out, query_rot, key_rot, cos, sin, bias, gains),
        cost(400_000_000, 4_000_000, 800_000),
    )
    near_value_back, far_value_back = shift(near_value_term, -1), shift(far_value_term, -2)
    far_key_term, near_key_term, own_key, grad_query, copies = call(
        attend_values_kernel,
        "attend_values",
        [term, term, own, shape((rows, query_width), BF16), shape((sizes[0], 2, HEAD), F32)],
        (
            far_value, near_value, values, grads_out, probs, query_rot, key_rot,
            halo_rot, halo_scaled, halo_turned, key_scaled, key_turned,
            query_scaled, query_scale, cos, sin, gains,
        ),
        cost(600_000_000, 4_000_000),
    )
    near_key_back, far_key_back = shift(near_key_term, -1), shift(far_key_term, -2)
    grad_value, copies = call(
        finish_values_kernel,
        "finish_values",
        [term, shape((sizes[1], 2, HEAD), F32)],
        (own_value, near_value_back, far_value_back, exchange(copies, 1)),
        cost(1_000_000, 2_000_000),
    )
    stride = sizes[0]
    parts = exchange(copies, stride)
    for before, size in zip(sizes[1:], sizes[2:]):
        stride *= before
        total = jnp.sum(parts, axis=0)[None]
        parts = exchange(jnp.broadcast_to(total, (size, 2, HEAD)), stride)
    grad_key, grad_query_gain, grad_key_gain = call(
        finish_keys_kernel,
        "finish_keys",
        [term, shape((1, HEAD), F32), shape((1, HEAD), F32)],
        (own_key, near_key_back, far_key_back, key_scaled, key_scale, cos, sin, gains, parts),
        cost(4_000_000, 3_000_000),
    )
    return (
        grad_query, grad_key, grad_value, grad_query_gain.reshape(HEAD), grad_key_gain.reshape(HEAD)
    )


def solution(mesh):
    rows = P(AXES, None)
    return jax.shard_map(
        on_device,
        mesh=mesh,
        in_specs=(P(), rows, rows, rows, rows, P(), P()),
        out_specs=(rows, rows, rows, P(), P()),
        check_vma=False,
    )
```

```python
import math

import jax
import jax.numpy as jnp
import numpy as np
from jax import lax
from jax.experimental import pallas as pl
from jax.experimental.pallas import tpu as pltpu
from jax.sharding import PartitionSpec as P

HEAD = 128
HALF = HEAD // 2
WINDOW = 256
EPS = 1e-06
SCALE = 168.0 ** (-0.5)
ROPE_BASE = 10000.0
MASKED = -1e30
AXES = ("ctx", "grp")
F32 = jnp.float32
BF16 = jnp.bfloat16
VMEM_LIMIT = 40 * 1024 * 1024


def frequencies():
    lane = lax.broadcasted_iota(jnp.int32, (1, HEAD), 1) % HALF
    values = jnp.zeros((1, HEAD), F32)
    for m in range(HALF):
        values = jnp.where(lane == m, np.float32(ROPE_BASE ** (-2.0 * m / HEAD)), values)
    return values


def shift(value, steps):
    count = lax.axis_size(AXES)
    return lax.ppermute(value, AXES, [(s, (s + steps) % count) for s in range(count)])


def own_index():
    return lax.axis_index("ctx") * lax.axis_size("grp") + lax.axis_index("grp")


def roll_half(x):
    return pltpu.roll(x, HALF, 1)


def doc_starts(tokens, lengths_ref):
    def step(doc, carry):
        end, starts = carry
        end = end + lengths_ref[doc]
        return end, jnp.where(tokens >= end, end, starts)

    count = lengths_ref.shape[0]
    return lax.fori_loop(
        0, count, step, (jnp.int32(0), jnp.zeros_like(tokens)), unroll=count if count <= 8 else 1
    )[1]


def cos_sin_lanes(angle, lane):
    turns = jnp.floor(angle * (2.0 / math.pi) + 0.5)
    r = angle - turns * 1.5703125
    r = r - turns * 4.837512969970703125e-4
    r = r - turns * 7.549789948768648e-8
    z = r * r
    sin_r = r + r * z * (-1.6666654611e-1 + z * (8.3321608736e-3 + z * -1.9515295891e-4))
    cos_r = 1.0 - 0.5 * z + z * z * (
        4.166664568298827e-2 + z * (-1.388731625493765e-3 + z * 2.443315711809948e-5)
    )
    quadrant = turns.astype(jnp.int32) - jnp.where(lane >= HALF, 1, 0)
    odd = (quadrant & 1) == 1
    value = jnp.where(odd, sin_r, cos_r)
    negative = ((quadrant + 1) & 2) == 2
    return jnp.where(negative, -value, value)


def row_sums(x):
    high = x.astype(BF16)
    low = (x - high.astype(F32)).astype(BF16)
    ones = jnp.ones((2 * HEAD, HEAD), BF16)
    return jnp.dot(jnp.concatenate([high, low], 1), ones, preferred_element_type=F32)


def row_scale(x):
    return lax.rsqrt(row_sums(x * x) * (1.0 / HEAD) + EPS)


def turning():
    source = lax.broadcasted_iota(jnp.int32, (HEAD, HEAD), 0)
    target = lax.broadcasted_iota(jnp.int32, (HEAD, HEAD), 1)
    return jnp.where(target == (source + HALF) % HEAD, 1.0, 0.0).astype(BF16)


def turned_rows(raw, matrix):
    return jnp.dot(raw, matrix, preferred_element_type=F32)


def turned_gain(gain):
    return roll_half(jnp.broadcast_to(gain, (8, HEAD)))[:1]


def prepare_kernel(
    lengths_hbm, query_hbm, key_hbm, value_hbm, out_grad_hbm, query_gain_hbm, key_gain_hbm,
    query_rot_ref, query_scaled_ref, query_scale_ref,
    key_rot_ref, key_scaled_ref, key_turned_ref, key_scale_ref, cos_ref, sin_ref, bias_ref,
    value_ref, out_grad_ref, gains_ref,
    lengths_ref, query_ref, key_ref, sems,
):
    moves = [
        pltpu.make_async_copy(source, target, sems.at[place])
        for place, (source, target) in enumerate(
            (
                (lengths_hbm, lengths_ref),
                (query_gain_hbm, gains_ref.at[0:1]),
                (key_gain_hbm, gains_ref.at[1:2]),
                (key_hbm, key_ref),
                (query_hbm, query_ref),
                (out_grad_hbm, out_grad_ref),
                (value_hbm, value_ref),
            )
        )
    ]
    for move in moves:
        move.start()
    rows = query_ref.shape[0]
    keys = cos_ref.shape[0]
    base = own_index() * rows - (keys - rows)
    shape = (keys, HEAD)
    lane = lax.broadcasted_iota(jnp.int32, shape, 1)
    tokens = base + lax.broadcasted_iota(jnp.int32, shape, 0)
    frequency = frequencies()
    moves[0].wait()
    positions = tokens - doc_starts(tokens, lengths_ref)
    mixed = cos_sin_lanes(positions.astype(F32) * frequency, lane)
    turned = roll_half(mixed)
    cos = jnp.where(lane < HALF, mixed, turned)
    sin = jnp.where(lane < HALF, -turned, mixed)
    cos_ref[...] = cos
    sin_ref[...] = sin
    queries = base + (keys - rows) + lax.broadcasted_iota(jnp.int32, (1, rows), 1)
    lowest = jnp.maximum(doc_starts(queries, lengths_ref), queries - (WINDOW - 1))
    key_tokens = base + lax.broadcasted_iota(jnp.int32, (keys, rows), 0)
    visible = (key_tokens >= lowest) & (key_tokens <= queries)
    bias_ref[...] = jnp.where(visible, 0.0, MASKED)
    own_cos, own_sin = cos[keys - rows :], sin[keys - rows :]
    moves[1].wait()
    moves[2].wait()
    matrix = turning()
    for raw_ref, move, row, rot_ref, scaled_ref, scale_ref in (
        (key_ref, moves[3], 1, key_rot_ref, key_scaled_ref, key_scale_ref),
        (query_ref, moves[4], 0, query_rot_ref, query_scaled_ref, query_scale_ref),
    ):
        gain = gains_ref[row : row + 1]
        cos_gain = own_cos * gain
        sin_gain = own_sin * turned_gain(gain)
        move.wait()
        for head in range(raw_ref.shape[1] // HEAD):
            part = slice(head * rows, (head + 1) * rows)
            raw = raw_ref[:, head * HEAD : (head + 1) * HEAD]
            x = raw.astype(F32)
            scale = row_scale(x)
            scaled = x * scale
            turned = turned_rows(raw, matrix) * scale
            scale_ref[part, :] = scale
            scaled_ref[part, :] = scaled
            rot_ref[part, :HEAD] = (scaled * cos_gain + turned * sin_gain).astype(BF16)
            if raw_ref is key_ref:
                key_turned_ref[part, :] = turned
                rot_ref[part, HEAD:] = (
                    turned * roll_half(cos_gain) + scaled * roll_half(sin_gain)
                ).astype(BF16)
    moves[5].wait()
    moves[6].wait()


def stacked(ref, head, group):
    return jnp.concatenate(
        [ref[:, (head * group + one) * HEAD : (head * group + one + 1) * HEAD] for one in range(group)],
        0,
    )


def attend_keys_kernel(
    far_ref, near_ref, out_grad_ref, query_rot_ref, key_rot_ref, cos_ref, sin_ref, bias_ref,
    gains_ref,
    exps_ref, inverse_ref, halo_rot_ref, halo_scaled_ref, halo_turned_ref, far_value_ref, near_value_ref, own_value_ref,
):
    rows = far_ref.shape[0]
    heads = far_ref.shape[1] // HEAD
    group = out_grad_ref.shape[1] // far_ref.shape[1]
    halo = WINDOW
    keys = halo + rows
    key_gain = gains_ref[1:2]
    cos_gain = cos_ref[:halo] * key_gain
    sin_gain = sin_ref[:halo] * turned_gain(key_gain)
    cos_turned, sin_turned = roll_half(cos_gain), roll_half(sin_gain)
    matrix = turning()

    def scores_of(head):
        cols = slice(head * HEAD, (head + 1) * HEAD)
        raw = jnp.concatenate([far_ref[:, cols], near_ref[:, cols]], 0)
        x = raw.astype(F32)
        scale = row_scale(x)
        scaled = x * scale
        turned = turned_rows(raw, matrix) * scale
        part = slice(head * halo, (head + 1) * halo)
        halo_scaled_ref[part, :] = scaled
        halo_turned_ref[part, :] = turned
        rotated = (scaled * cos_gain + turned * sin_gain).astype(BF16)
        halo_rot_ref[part, :HEAD] = rotated
        halo_rot_ref[part, HEAD:] = (turned * cos_turned + scaled * sin_turned).astype(BF16)
        both = jnp.concatenate([rotated, key_rot_ref[head * rows : (head + 1) * rows, :HEAD]], 0)
        queries = query_rot_ref[head * group * rows : (head + 1) * group * rows, :]
        return lax.dot_general(
            both, queries, (((1,), (1,)), ((), ())), preferred_element_type=F32
        )

    later = scores_of(0)
    for head in range(heads):
        scores = later
        if head + 1 < heads:
            later = scores_of(head + 1)
        cols = slice(head * HEAD, (head + 1) * HEAD)
        low = []
        for one in range(group):
            place = (slice(head * keys, (head + 1) * keys), slice(one * rows, (one + 1) * rows))
            part = scores[:, place[1]] * (SCALE * math.log2(math.e)) + bias_ref[...]
            exps = jnp.exp2(part - jnp.max(part, axis=0, keepdims=True))
            exps_ref[place] = exps
            inverse = 1.0 / jnp.sum(exps, axis=0, keepdims=True)
            inverse_ref[head : head + 1, place[1]] = inverse
            low.append((exps_ref[place] * inverse).astype(BF16))
        value_term = jnp.dot(
            jnp.concatenate(low, 1), stacked(out_grad_ref, head, group), preferred_element_type=F32
        )
        far_value_ref[:, cols] = value_term[:rows].astype(BF16)
        near_value_ref[:, cols] = value_term[rows:halo].astype(BF16)
        own_value_ref[:, cols] = value_term[halo:]


def norm_backward(grad_rot, grad_turned, scaled, scale, gain, cos, sin):
    normed_grad = grad_rot * cos - grad_turned * sin
    part = normed_grad * scaled
    mean = row_sums(part * gain) * (1.0 / HEAD)
    return scale * (normed_grad * gain - scaled * mean), part


def attend_values_kernel(
    far_ref, near_ref, value_ref, out_grad_ref, exps_ref, inverse_ref, query_rot_ref, key_rot_ref,
    halo_rot_ref, halo_scaled_ref, halo_turned_ref, key_scaled_ref, key_turned_ref,
    query_scaled_ref, query_scale_ref, cos_ref, sin_ref, gains_ref,
    far_key_ref, near_key_ref, own_key_ref, grad_query_ref, gain_ref,
):
    rows = far_ref.shape[0]
    heads = far_ref.shape[1] // HEAD
    group = out_grad_ref.shape[1] // far_ref.shape[1]
    halo = WINDOW
    keys = halo + rows
    query_gain = gains_ref[0:1]
    own_cos, own_sin = cos_ref[halo:] * SCALE, sin_ref[halo:] * SCALE
    query_gain_acc = jnp.zeros((rows, HEAD), F32)
    key_acc = jnp.zeros((keys, HEAD), F32)
    key_acc_turned = jnp.zeros((keys, HEAD), F32)

    def prob_grad_of(head):
        cols = slice(head * HEAD, (head + 1) * HEAD)
        values = jnp.concatenate([far_ref[:, cols], near_ref[:, cols], value_ref[:, cols]], 0)
        return lax.dot_general(
            values, stacked(out_grad_ref, head, group), (((1,), (1,)), ((), ())),
            preferred_element_type=F32,
        )

    later = prob_grad_of(0)
    for head in range(heads):
        prob_grad = later
        if head + 1 < heads:
            later = prob_grad_of(head + 1)
        cols = slice(head * HEAD, (head + 1) * HEAD)
        halo_part = slice(head * halo, (head + 1) * halo)
        own_part = slice(head * rows, (head + 1) * rows)
        group_part = slice(head * group * rows, (head + 1) * group * rows)
        score_grads = []
        for one in range(group):
            place = (slice(head * keys, (head + 1) * keys), slice(one * rows, (one + 1) * rows))
            part = prob_grad[:, place[1]]
            inverse = inverse_ref[head : head + 1, place[1]]
            delta = jnp.sum(exps_ref[place] * part, axis=0, keepdims=True) * inverse
            score_grads.append((exps_ref[place] * inverse * (part - delta)).astype(BF16))
        score_grad = jnp.concatenate(score_grads, 1)
        key_term = (
            jnp.dot(score_grad, query_rot_ref[group_part, :], preferred_element_type=F32) * SCALE
        )
        keys_rot = jnp.concatenate([halo_rot_ref[halo_part, :], key_rot_ref[own_part, :]], 0)
        query_term = lax.dot_general(
            score_grad, keys_rot, (((0,), (0,)), ((), ())), preferred_element_type=F32
        )
        halo_key = key_term[:halo].astype(BF16)
        far_key_ref[:, cols] = halo_key[:rows]
        near_key_ref[:, cols] = halo_key[rows:]
        own_key_ref[:, cols] = key_term[halo:]
        term = jnp.concatenate([halo_key.astype(F32), key_term[halo:]], 0)
        scaled = jnp.concatenate([halo_scaled_ref[halo_part, :], key_scaled_ref[own_part, :]], 0)
        key_acc = key_acc + term * scaled
        turned = jnp.concatenate([halo_turned_ref[halo_part, :], key_turned_ref[own_part, :]], 0)
        key_acc_turned = key_acc_turned + term * turned
        for one in range(group):
            index = head * group + one
            part = slice(index * rows, (index + 1) * rows)
            term = query_term[one * rows : (one + 1) * rows]
            grad, gain_part = norm_backward(
                term[:, :HEAD], term[:, HEAD:],
                query_scaled_ref[part, :], query_scale_ref[part, :], query_gain, own_cos, own_sin,
            )
            grad_query_ref[:, index * HEAD : (index + 1) * HEAD] = grad.astype(BF16)
            query_gain_acc = query_gain_acc + gain_part
    query_sum = jnp.sum(query_gain_acc, axis=0, keepdims=True)
    key_sum = jnp.sum(key_acc * cos_ref[...], axis=0, keepdims=True)
    turned_sum = jnp.sum(key_acc_turned * sin_ref[...], axis=0, keepdims=True)
    gain_ref[...] = jnp.concatenate([query_sum, key_sum + turned_gain(turned_sum)], 0)


def finish_values_kernel(own_ref, near_ref, far_ref, gain_ref, grad_value_ref, copies_ref):
    total = own_ref[...] + near_ref[...].astype(F32) + far_ref[...].astype(F32)
    grad_value_ref[...] = total.astype(BF16)
    copies_ref[...] = jnp.broadcast_to(gain_ref[...][None], copies_ref.shape)


def finish_keys_kernel(
    own_ref, near_ref, far_ref, key_scaled_ref, key_scale_ref, cos_ref, sin_ref, gains_ref, parts_ref,
    grad_key_ref, query_gain_ref, key_gain_ref,
):
    rows = own_ref.shape[0]
    cos, sin = cos_ref[WINDOW:], sin_ref[WINDOW:]
    gain = gains_ref[1:2]
    for head in range(own_ref.shape[1] // HEAD):
        cols = slice(head * HEAD, (head + 1) * HEAD)
        part = slice(head * rows, (head + 1) * rows)
        total = own_ref[:, cols] + near_ref[:, cols].astype(F32) + far_ref[:, cols].astype(F32)
        grad, _ = norm_backward(
            total, roll_half(total), key_scaled_ref[part, :], key_scale_ref[part, :], gain, cos, sin
        )
        grad_key_ref[:, cols] = grad.astype(BF16)
    sums = jnp.sum(parts_ref[...], axis=0)
    query_gain_ref[...] = sums[:1]
    key_gain_ref[...] = sums[1:]


def call(kernel, name, outs, operands, cost=None, space=pltpu.VMEM, scratch=()):
    return pl.pallas_call(
        kernel,
        out_shape=outs,
        in_specs=[pl.BlockSpec(memory_space=space)] * len(operands),
        out_specs=[pl.BlockSpec(memory_space=pltpu.VMEM)] * len(outs),
        scratch_shapes=scratch,
        compiler_params=pltpu.CompilerParams(vmem_limit_bytes=VMEM_LIMIT),
        cost_estimate=cost,
        name=name,
    )(*operands)


def cost(flops, size, exps=0):
    return pl.CostEstimate(flops=flops, bytes_accessed=size, transcendentals=exps)


def shape(dims, dtype):
    return jax.ShapeDtypeStruct(dims, dtype)


def on_device(doc_lengths, query_raw, key_raw, value_matrix, out_grad, query_gain, key_gain):
    rows, query_width = query_raw.shape
    width = key_raw.shape[1]
    heads = width // HEAD
    query_heads = query_width // HEAD
    keys = WINDOW + rows
    devices = lax.axis_size(AXES)
    query_gain = query_gain.reshape(1, HEAD)
    key_gain = key_gain.reshape(1, HEAD)
    near_key, far_key = shift(key_raw, 1), shift(key_raw, 2)
    term = shape((rows, width), BF16)
    own = shape((rows, width), F32)
    (
        query_rot, query_scaled, query_scale, key_rot, key_scaled, key_turned, key_scale, cos, sin, bias,
        values, grads_out, gains,
    ) = call(
        prepare_kernel,
        "prepare",
        [
            shape((query_heads * rows, HEAD), BF16),
            shape((query_heads * rows, HEAD), F32),
            shape((query_heads * rows, HEAD), F32),
            shape((heads * rows, 2 * HEAD), BF16),
            shape((heads * rows, HEAD), F32),
            shape((heads * rows, HEAD), F32),
            shape((heads * rows, HEAD), F32),
            shape((keys, HEAD), F32),
            shape((keys, HEAD), F32),
            shape((keys, rows), F32),
            term,
            shape((rows, query_width), BF16),
            shape((8, HEAD), F32),
        ],
        [
            pltpu.with_memory_space_constraint(x, pltpu.HBM)
            for x in (doc_lengths, query_raw, key_raw, value_matrix, out_grad, query_gain, key_gain)
        ],
        cost(4_000_000, 6_000_000),
        space=pltpu.HBM,
        scratch=[
            pltpu.SMEM(doc_lengths.shape, jnp.int32),
            pltpu.VMEM((rows, query_width), BF16),
            pltpu.VMEM((rows, width), BF16),
            pltpu.SemaphoreType.DMA((7,)),
        ],
    )
    near_value, far_value = shift(values, 1), shift(values, 2)
    exps, inverse, halo_rot, halo_scaled, halo_turned, far_value_term, near_value_term, own_value = call(
        attend_keys_kernel,
        "attend_keys",
        [
            shape((heads * keys, query_heads // heads * rows), F32),
            shape((heads, query_heads // heads * rows), F32),
            shape((heads * WINDOW, 2 * HEAD), BF16),
            shape((heads * WINDOW, HEAD), F32),
            shape((heads * WINDOW, HEAD), F32),
            term,
            term,
            own,
        ],
        (far_key, near_key, grads_out, query_rot, key_rot, cos, sin, bias, gains),
        cost(400_000_000, 4_000_000, 800_000),
    )
    near_value_back, far_value_back = shift(near_value_term, -1), shift(far_value_term, -2)
    far_key_term, near_key_term, own_key, grad_query, gain_part = call(
        attend_values_kernel,
        "attend_values",
        [term, term, own, shape((rows, query_width), BF16), shape((2, HEAD), F32)],
        (
            far_value, near_value, values, grads_out, exps, inverse, query_rot, key_rot,
            halo_rot, halo_scaled, halo_turned, key_scaled, key_turned,
            query_scaled, query_scale, cos, sin, gains,
        ),
        cost(600_000_000, 4_000_000),
    )
    near_key_back, far_key_back = shift(near_key_term, -1), shift(far_key_term, -2)
    grad_value, copies = call(
        finish_values_kernel,
        "finish_values",
        [term, shape((devices, 2, HEAD), F32)],
        (own_value, near_value_back, far_value_back, gain_part),
        cost(1_000_000, 2_000_000),
    )
    parts = lax.all_to_all(copies, AXES, 0, 0)
    grad_key, grad_query_gain, grad_key_gain = call(
        finish_keys_kernel,
        "finish_keys",
        [term, shape((1, HEAD), F32), shape((1, HEAD), F32)],
        (own_key, near_key_back, far_key_back, key_scaled, key_scale, cos, sin, gains, parts),
        cost(4_000_000, 3_000_000),
    )
    return (
        grad_query, grad_key, grad_value, grad_query_gain.reshape(HEAD), grad_key_gain.reshape(HEAD)
    )


def solution(mesh):
    rows = P(AXES, None)
    return jax.shard_map(
        on_device,
        mesh=mesh,
        in_specs=(P(), rows, rows, rows, rows, P(), P()),
        out_specs=(rows, rows, rows, P(), P()),
        check_vma=False,
    )
```

```python
import math

import jax
import jax.numpy as jnp
import numpy as np
from jax import lax
from jax.experimental import pallas as pl
from jax.experimental.pallas import tpu as pltpu
from jax.sharding import PartitionSpec as P

HEAD = 128
HALF = HEAD // 2
WINDOW = 256
EPS = 1e-06
SCALE = 168.0 ** (-0.5)
ROPE_BASE = 10000.0
MASKED = -1e30
AXES = ("ctx", "grp")
F32 = jnp.float32
BF16 = jnp.bfloat16
VMEM_LIMIT = 40 * 1024 * 1024


def frequencies():
    lane = lax.broadcasted_iota(jnp.int32, (1, HEAD), 1) % HALF
    values = jnp.zeros((1, HEAD), F32)
    for m in range(HALF):
        values = jnp.where(lane == m, np.float32(ROPE_BASE ** (-2.0 * m / HEAD)), values)
    return values


def shift(value, steps):
    count = lax.axis_size(AXES)
    return lax.ppermute(value, AXES, [(s, (s + steps) % count) for s in range(count)])


def own_index():
    return lax.axis_index("ctx") * lax.axis_size("grp") + lax.axis_index("grp")


def roll_half(x):
    return pltpu.roll(x, HALF, 1)


def doc_starts(tokens, lengths_ref):
    def step(doc, carry):
        end, starts = carry
        end = end + lengths_ref[doc]
        return end, jnp.where(tokens >= end, end, starts)

    count = lengths_ref.shape[0]
    return lax.fori_loop(
        0, count, step, (jnp.int32(0), jnp.zeros_like(tokens)), unroll=count if count <= 8 else 1
    )[1]


def cos_sin_lanes(angle, lane):
    turns = jnp.floor(angle * (2.0 / math.pi) + 0.5)
    r = angle - turns * 1.5703125
    r = r - turns * 4.837512969970703125e-4
    r = r - turns * 7.549789948768648e-8
    z = r * r
    sin_r = r + r * z * (-1.6666654611e-1 + z * (8.3321608736e-3 + z * -1.9515295891e-4))
    cos_r = 1.0 - 0.5 * z + z * z * (
        4.166664568298827e-2 + z * (-1.388731625493765e-3 + z * 2.443315711809948e-5)
    )
    quadrant = turns.astype(jnp.int32) - jnp.where(lane >= HALF, 1, 0)
    odd = (quadrant & 1) == 1
    value = jnp.where(odd, sin_r, cos_r)
    negative = ((quadrant + 1) & 2) == 2
    return jnp.where(negative, -value, value)


def ones(rows, columns):
    return jnp.ones((rows, columns), BF16)


def split(x):
    high = x.astype(BF16)
    low = (x - high.astype(F32)).astype(BF16)
    return jnp.concatenate([high, low], 1)


def row_sums(x):
    return jnp.dot(split(x), ones(2 * HEAD, HEAD), preferred_element_type=F32)


def scale_of(sums):
    return lax.rsqrt(sums * (1.0 / HEAD) + EPS)


def row_scale(x):
    return scale_of(row_sums(x * x))


def turning():
    source = lax.broadcasted_iota(jnp.int32, (HEAD, HEAD), 0)
    target = lax.broadcasted_iota(jnp.int32, (HEAD, HEAD), 1)
    return jnp.where(target == (source + HALF) % HEAD, 1.0, 0.0).astype(BF16)


def turned_rows(raw, matrix):
    return jnp.dot(raw, matrix, preferred_element_type=F32)


def turned_gain(gain):
    return roll_half(jnp.broadcast_to(gain, (8, HEAD)))[:1]


def prepare_kernel(
    lengths_hbm, query_hbm, key_hbm, value_hbm, out_grad_hbm, query_gain_hbm, key_gain_hbm,
    query_rot_ref, query_scaled_ref, query_scale_ref, key_rot_ref, key_across_ref,
    key_scaled_ref, key_turned_ref, key_scale_ref, cos_ref, sin_ref, across_ref, bias_ref,
    value_ref, out_grad_ref, gains_ref,
    lengths_ref, query_ref, key_ref, sems,
):
    moves = [
        pltpu.make_async_copy(source, target, sems.at[place])
        for place, (source, target) in enumerate(
            (
                (lengths_hbm, lengths_ref),
                (query_gain_hbm, gains_ref.at[0:1]),
                (key_gain_hbm, gains_ref.at[1:2]),
                (key_hbm, key_ref),
                (query_hbm, query_ref),
                (out_grad_hbm, out_grad_ref),
                (value_hbm, value_ref),
            )
        )
    ]
    for move in moves:
        move.start()
    rows = query_ref.shape[0]
    keys = cos_ref.shape[0]
    base = own_index() * rows - (keys - rows)
    shape = (keys, HEAD)
    lane = lax.broadcasted_iota(jnp.int32, shape, 1)
    tokens = base + lax.broadcasted_iota(jnp.int32, shape, 0)
    frequency = frequencies()
    moves[0].wait()
    positions = tokens - doc_starts(tokens, lengths_ref)
    mixed = cos_sin_lanes(positions.astype(F32) * frequency, lane)
    turned = roll_half(mixed)
    cos = jnp.where(lane < HALF, mixed, turned)
    sin = jnp.where(lane < HALF, -turned, mixed)
    cos_ref[...] = cos
    sin_ref[...] = sin
    queries = base + (keys - rows) + lax.broadcasted_iota(jnp.int32, (1, rows), 1)
    lowest = jnp.maximum(doc_starts(queries, lengths_ref), queries - (WINDOW - 1))
    key_tokens = base + lax.broadcasted_iota(jnp.int32, (keys, rows), 0)
    visible = (key_tokens >= lowest) & (key_tokens <= queries)
    bias_ref[...] = jnp.where(visible, 0.0, MASKED)
    own_cos, own_sin = cos[keys - rows :], sin[keys - rows :]
    moves[1].wait()
    moves[2].wait()
    across_ref[0] = own_cos.T
    across_ref[1] = own_sin.T
    across_ref[2] = jnp.broadcast_to(gains_ref[0:1], (HEAD, HEAD)).T
    matrix = turning()
    for raw_ref, move, row, rot_ref in (
        (key_ref, moves[3], 1, key_rot_ref),
        (query_ref, moves[4], 0, query_rot_ref),
    ):
        gain = gains_ref[row : row + 1]
        cos_gain = own_cos * gain
        sin_gain = own_sin * turned_gain(gain)
        move.wait()
        for head in range(raw_ref.shape[1] // HEAD):
            part = slice(head * rows, (head + 1) * rows)
            across = slice(head * HEAD, (head + 1) * HEAD)
            raw = raw_ref[:, across]
            x = raw.astype(F32)
            parts = split(x * x)
            scale = scale_of(jnp.dot(parts, ones(2 * HEAD, HEAD), preferred_element_type=F32))
            scaled = x * scale
            turned = turned_rows(raw, matrix) * scale
            rotated = scaled * cos_gain + turned * sin_gain
            rot_ref[part, :] = rotated.astype(BF16)
            if raw_ref is key_ref:
                key_scale_ref[part, :] = scale
                key_scaled_ref[part, :] = scaled
                key_turned_ref[part, :] = turned
                key_across_ref[across, :] = rotated.T.astype(BF16)
            else:
                query_scaled_ref[across, :] = scaled.T
                sums = lax.dot_general(
                    ones(8, 2 * HEAD), parts, (((1,), (1,)), ((), ())), preferred_element_type=F32
                )
                query_scale_ref[head : head + 1, :] = scale_of(sums[:1])
    moves[5].wait()
    moves[6].wait()


def stacked(ref, head, group):
    return jnp.concatenate(
        [ref[:, (head * group + one) * HEAD : (head * group + one + 1) * HEAD] for one in range(group)],
        0,
    )


def attend_keys_kernel(
    far_ref, near_ref, out_grad_ref, query_rot_ref, key_rot_ref, cos_ref, sin_ref, bias_ref,
    gains_ref,
    exps_ref, inverse_ref, halo_across_ref, halo_scaled_ref, halo_turned_ref, far_value_ref, near_value_ref, own_value_ref,
):
    rows = far_ref.shape[0]
    heads = far_ref.shape[1] // HEAD
    group = out_grad_ref.shape[1] // far_ref.shape[1]
    halo = WINDOW
    keys = halo + rows
    key_gain = gains_ref[1:2]
    cos_gain = cos_ref[:halo] * key_gain
    sin_gain = sin_ref[:halo] * turned_gain(key_gain)
    matrix = turning()

    def scores_of(head):
        cols = slice(head * HEAD, (head + 1) * HEAD)
        raw = jnp.concatenate([far_ref[:, cols], near_ref[:, cols]], 0)
        x = raw.astype(F32)
        scale = row_scale(x)
        scaled = x * scale
        turned = turned_rows(raw, matrix) * scale
        part = slice(head * halo, (head + 1) * halo)
        halo_scaled_ref[part, :] = scaled
        halo_turned_ref[part, :] = turned
        rotated = scaled * cos_gain + turned * sin_gain
        halo_across_ref[cols, :] = rotated.T.astype(BF16)
        both = jnp.concatenate(
            [rotated.astype(BF16), key_rot_ref[head * rows : (head + 1) * rows, :]], 0
        )
        queries = query_rot_ref[head * group * rows : (head + 1) * group * rows, :]
        return lax.dot_general(
            both, queries, (((1,), (1,)), ((), ())), preferred_element_type=F32
        )

    later = scores_of(0)
    for head in range(heads):
        scores = later
        if head + 1 < heads:
            later = scores_of(head + 1)
        cols = slice(head * HEAD, (head + 1) * HEAD)
        low = []
        for one in range(group):
            place = (slice(head * keys, (head + 1) * keys), slice(one * rows, (one + 1) * rows))
            part = scores[:, place[1]] * (SCALE * math.log2(math.e)) + bias_ref[...]
            exps = jnp.exp2(part - jnp.max(part, axis=0, keepdims=True))
            exps_ref[place] = exps
            inverse = 1.0 / jnp.sum(exps, axis=0, keepdims=True)
            inverse_ref[head : head + 1, place[1]] = inverse
            low.append((exps_ref[place] * inverse).astype(BF16))
        value_term = jnp.dot(
            jnp.concatenate(low, 1), stacked(out_grad_ref, head, group), preferred_element_type=F32
        )
        far_value_ref[:, cols] = value_term[:rows].astype(BF16)
        near_value_ref[:, cols] = value_term[rows:halo].astype(BF16)
        own_value_ref[:, cols] = value_term[halo:]


def norm_backward(grad_rot, grad_turned, scaled, scale, gain, cos, sin):
    normed_grad = grad_rot * cos - grad_turned * sin
    part = normed_grad * scaled
    mean = row_sums(part * gain) * (1.0 / HEAD)
    return scale * (normed_grad * gain - scaled * mean), part


def attend_values_kernel(
    far_ref, near_ref, value_ref, out_grad_ref, exps_ref, inverse_ref, query_rot_ref,
    halo_across_ref, key_across_ref, halo_scaled_ref, halo_turned_ref, key_scaled_ref,
    key_turned_ref, query_scaled_ref, cos_ref, sin_ref, across_ref,
    far_key_ref, near_key_ref, own_key_ref, query_grad_ref, gain_ref,
):
    rows = far_ref.shape[0]
    heads = far_ref.shape[1] // HEAD
    group = out_grad_ref.shape[1] // far_ref.shape[1]
    halo = WINDOW
    keys = halo + rows
    cos_across, sin_across = across_ref[0] * SCALE, across_ref[1] * SCALE
    query_acc = jnp.zeros((HEAD, rows), F32)
    key_acc = jnp.zeros((keys, HEAD), F32)
    key_acc_turned = jnp.zeros((keys, HEAD), F32)

    def prob_grad_of(head):
        cols = slice(head * HEAD, (head + 1) * HEAD)
        values = jnp.concatenate([far_ref[:, cols], near_ref[:, cols], value_ref[:, cols]], 0)
        return lax.dot_general(
            values, stacked(out_grad_ref, head, group), (((1,), (1,)), ((), ())),
            preferred_element_type=F32,
        )

    later = prob_grad_of(0)
    for head in range(heads):
        prob_grad = later
        if head + 1 < heads:
            later = prob_grad_of(head + 1)
        cols = slice(head * HEAD, (head + 1) * HEAD)
        halo_part = slice(head * halo, (head + 1) * halo)
        own_part = slice(head * rows, (head + 1) * rows)
        group_part = slice(head * group * rows, (head + 1) * group * rows)
        score_grads = []
        for one in range(group):
            place = (slice(head * keys, (head + 1) * keys), slice(one * rows, (one + 1) * rows))
            part = prob_grad[:, place[1]]
            inverse = inverse_ref[head : head + 1, place[1]]
            delta = jnp.sum(exps_ref[place] * part, axis=0, keepdims=True) * inverse
            score_grads.append((exps_ref[place] * inverse * (part - delta)).astype(BF16))
        score_grad = jnp.concatenate(score_grads, 1)
        key_term = (
            jnp.dot(score_grad, query_rot_ref[group_part, :], preferred_element_type=F32) * SCALE
        )
        keys_across = jnp.concatenate([halo_across_ref[cols, :], key_across_ref[cols, :]], 1)
        query_term = jnp.dot(keys_across, score_grad, preferred_element_type=F32)
        halo_key = key_term[:halo].astype(BF16)
        far_key_ref[:, cols] = halo_key[:rows]
        near_key_ref[:, cols] = halo_key[rows:]
        own_key_ref[:, cols] = key_term[halo:]
        term = jnp.concatenate([halo_key.astype(F32), key_term[halo:]], 0)
        scaled = jnp.concatenate([halo_scaled_ref[halo_part, :], key_scaled_ref[own_part, :]], 0)
        key_acc = key_acc + term * scaled
        turned = jnp.concatenate([halo_turned_ref[halo_part, :], key_turned_ref[own_part, :]], 0)
        key_acc_turned = key_acc_turned + term * turned
        for one in range(group):
            index = head * group + one
            across = slice(index * HEAD, (index + 1) * HEAD)
            grad = query_term[:, one * rows : (one + 1) * rows]
            turned = jnp.concatenate([grad[HALF:], grad[:HALF]], 0)
            normed_grad = grad * cos_across - turned * sin_across
            query_grad_ref[across, :] = normed_grad
            query_acc = query_acc + normed_grad * query_scaled_ref[across, :]
    query_sum = jnp.sum(query_acc.T, axis=0, keepdims=True)
    key_sum = jnp.sum(key_acc * cos_ref[...], axis=0, keepdims=True)
    turned_sum = jnp.sum(key_acc_turned * sin_ref[...], axis=0, keepdims=True)
    both = jnp.concatenate([query_sum, key_sum + turned_gain(turned_sum)], 0)
    gain_ref[...] = jnp.broadcast_to(both[None], gain_ref.shape)


def finish_queries_kernel(query_grad_ref, query_scaled_ref, query_scale_ref, across_ref, out_ref):
    gain = across_ref[2]
    for head in range(out_ref.shape[1] // HEAD):
        across = slice(head * HEAD, (head + 1) * HEAD)
        scaled = query_scaled_ref[across, :]
        weighted = query_grad_ref[across, :] * gain
        mean = jnp.sum(weighted * scaled, axis=0, keepdims=True) * (1.0 / HEAD)
        grad = query_scale_ref[head : head + 1, :] * (weighted - scaled * mean)
        out_ref[:, across] = grad.T.astype(BF16)


def finish_values_kernel(own_ref, near_ref, far_ref, grad_value_ref):
    total = own_ref[...] + near_ref[...].astype(F32) + far_ref[...].astype(F32)
    grad_value_ref[...] = total.astype(BF16)


def finish_keys_kernel(
    own_ref, near_ref, far_ref, key_scaled_ref, key_scale_ref, cos_ref, sin_ref, gains_ref, parts_ref,
    grad_key_ref, query_gain_ref, key_gain_ref,
):
    rows = own_ref.shape[0]
    cos, sin = cos_ref[WINDOW:], sin_ref[WINDOW:]
    gain = gains_ref[1:2]
    for head in range(own_ref.shape[1] // HEAD):
        cols = slice(head * HEAD, (head + 1) * HEAD)
        part = slice(head * rows, (head + 1) * rows)
        total = own_ref[:, cols] + near_ref[:, cols].astype(F32) + far_ref[:, cols].astype(F32)
        grad, _ = norm_backward(
            total, roll_half(total), key_scaled_ref[part, :], key_scale_ref[part, :], gain, cos, sin
        )
        grad_key_ref[:, cols] = grad.astype(BF16)
    sums = jnp.sum(parts_ref[...], axis=0)
    query_gain_ref[...] = sums[:1]
    key_gain_ref[...] = sums[1:]


def call(kernel, name, outs, operands, cost=None, space=pltpu.VMEM, scratch=()):
    return pl.pallas_call(
        kernel,
        out_shape=outs,
        in_specs=[pl.BlockSpec(memory_space=space)] * len(operands),
        out_specs=[pl.BlockSpec(memory_space=pltpu.VMEM)] * len(outs),
        scratch_shapes=scratch,
        compiler_params=pltpu.CompilerParams(vmem_limit_bytes=VMEM_LIMIT),
        cost_estimate=cost,
        name=name,
    )(*operands)


def cost(flops, size, exps=0):
    return pl.CostEstimate(flops=flops, bytes_accessed=size, transcendentals=exps)


def shape(dims, dtype):
    return jax.ShapeDtypeStruct(dims, dtype)


def on_device(doc_lengths, query_raw, key_raw, value_matrix, out_grad, query_gain, key_gain):
    rows, query_width = query_raw.shape
    width = key_raw.shape[1]
    heads = width // HEAD
    query_heads = query_width // HEAD
    keys = WINDOW + rows
    devices = lax.axis_size(AXES)
    query_gain = query_gain.reshape(1, HEAD)
    key_gain = key_gain.reshape(1, HEAD)
    near_key, far_key = shift(key_raw, 1), shift(key_raw, 2)
    term = shape((rows, width), BF16)
    own = shape((rows, width), F32)
    (
        query_rot, query_scaled, query_scale, key_rot, key_across, key_scaled, key_turned, key_scale,
        cos, sin, across, bias, values, grads_out, gains,
    ) = call(
        prepare_kernel,
        "prepare",
        [
            shape((query_heads * rows, HEAD), BF16),
            shape((query_width, rows), F32),
            shape((query_heads, rows), F32),
            shape((heads * rows, HEAD), BF16),
            shape((width, rows), BF16),
            shape((heads * rows, HEAD), F32),
            shape((heads * rows, HEAD), F32),
            shape((heads * rows, HEAD), F32),
            shape((keys, HEAD), F32),
            shape((keys, HEAD), F32),
            shape((3, HEAD, rows), F32),
            shape((keys, rows), F32),
            term,
            shape((rows, query_width), BF16),
            shape((8, HEAD), F32),
        ],
        [
            pltpu.with_memory_space_constraint(x, pltpu.HBM)
            for x in (doc_lengths, query_raw, key_raw, value_matrix, out_grad, query_gain, key_gain)
        ],
        cost(4_000_000, 6_000_000),
        space=pltpu.HBM,
        scratch=[
            pltpu.SMEM(doc_lengths.shape, jnp.int32),
            pltpu.VMEM((rows, query_width), BF16),
            pltpu.VMEM((rows, width), BF16),
            pltpu.SemaphoreType.DMA((7,)),
        ],
    )
    near_value, far_value = shift(values, 1), shift(values, 2)
    exps, inverse, halo_across, halo_scaled, halo_turned, far_value_term, near_value_term, own_value = call(
        attend_keys_kernel,
        "attend_keys",
        [
            shape((heads * keys, query_heads // heads * rows), F32),
            shape((heads, query_heads // heads * rows), F32),
            shape((width, WINDOW), BF16),
            shape((heads * WINDOW, HEAD), F32),
            shape((heads * WINDOW, HEAD), F32),
            term,
            term,
            own,
        ],
        (far_key, near_key, grads_out, query_rot, key_rot, cos, sin, bias, gains),
        cost(400_000_000, 4_000_000, 800_000),
    )
    near_value_back, far_value_back = shift(near_value_term, -1), shift(far_value_term, -2)
    far_key_term, near_key_term, own_key, query_grad, copies = call(
        attend_values_kernel,
        "attend_values",
        [term, term, own, shape((query_width, rows), F32), shape((devices, 2, HEAD), F32)],
        (
            far_value, near_value, values, grads_out, exps, inverse, query_rot,
            halo_across, key_across, halo_scaled, halo_turned, key_scaled,
            key_turned, query_scaled, cos, sin, across,
        ),
        cost(600_000_000, 4_000_000),
    )
    parts = lax.all_to_all(copies, AXES, 0, 0)
    near_key_term, far_key_term, near_value_back, far_value_back = lax.optimization_barrier(
        (near_key_term, far_key_term, near_value_back, far_value_back)
    )
    near_key_back, far_key_back = shift(near_key_term, -1), shift(far_key_term, -2)
    (grad_value,) = call(
        finish_values_kernel,
        "finish_values",
        [term],
        (own_value, near_value_back, far_value_back),
        cost(1_000_000, 2_000_000),
    )
    (grad_query,) = call(
        finish_queries_kernel,
        "finish_queries",
        [shape((rows, query_width), BF16)],
        (query_grad, query_scaled, query_scale, across),
        cost(4_000_000, 4_000_000),
    )
    grad_key, grad_query_gain, grad_key_gain = call(
        finish_keys_kernel,
        "finish_keys",
        [term, shape((1, HEAD), F32), shape((1, HEAD), F32)],
        (own_key, near_key_back, far_key_back, key_scaled, key_scale, cos, sin, gains, parts),
        cost(4_000_000, 3_000_000),
    )
    return (
        grad_query, grad_key, grad_value, grad_query_gain.reshape(HEAD), grad_key_gain.reshape(HEAD)
    )


def solution(mesh):
    rows = P(AXES, None)
    return jax.shard_map(
        on_device,
        mesh=mesh,
        in_specs=(P(), rows, rows, rows, rows, P(), P()),
        out_specs=(rows, rows, rows, P(), P()),
        check_vma=False,
    )
```

```python
import math

import jax
import jax.numpy as jnp
import numpy as np
from jax import lax
from jax.experimental import pallas as pl
from jax.experimental.pallas import tpu as pltpu
from jax.sharding import PartitionSpec as P

HEAD = 128
HALF = HEAD // 2
WINDOW = 256
EPS = 1e-06
SCALE = 168.0 ** (-0.5)
ROPE_BASE = 10000.0
MASKED = -1e30
AXES = ("ctx", "grp")
F32 = jnp.float32
BF16 = jnp.bfloat16
VMEM_LIMIT = 16 * 1024 * 1024


def frequencies():
    lane = lax.broadcasted_iota(jnp.int32, (1, HEAD), 1) % HALF
    values = jnp.zeros((1, HEAD), F32)
    for m in range(HALF):
        values = jnp.where(lane == m, np.float32(ROPE_BASE ** (-2.0 * m / HEAD)), values)
    return values


def shift(value, steps):
    count = lax.axis_size(AXES)
    return lax.ppermute(value, AXES, [(s, (s + steps) % count) for s in range(count)])


def own_index():
    return lax.axis_index("ctx") * lax.axis_size("grp") + lax.axis_index("grp")


def roll_half(x):
    return pltpu.roll(x, HALF, 1)


def doc_starts(tokens, lengths_ref):
    def step(doc, carry):
        end, starts = carry
        end = end + lengths_ref[doc]
        return end, jnp.where(tokens >= end, end, starts)

    count = lengths_ref.shape[0]
    return lax.fori_loop(
        0, count, step, (jnp.int32(0), jnp.zeros_like(tokens)), unroll=count if count <= 8 else 1
    )[1]


def cos_sin_lanes(angle, lane):
    turns = jnp.floor(angle * (2.0 / math.pi) + 0.5)
    r = angle - turns * 1.5703125
    r = r - turns * 4.837512969970703125e-4
    r = r - turns * 7.549789948768648e-8
    z = r * r
    sin_r = r + r * z * (-1.6666654611e-1 + z * (8.3321608736e-3 + z * -1.9515295891e-4))
    cos_r = 1.0 - 0.5 * z + z * z * (
        4.166664568298827e-2 + z * (-1.388731625493765e-3 + z * 2.443315711809948e-5)
    )
    quadrant = turns.astype(jnp.int32) - jnp.where(lane >= HALF, 1, 0)
    odd = (quadrant & 1) == 1
    value = jnp.where(odd, sin_r, cos_r)
    negative = ((quadrant + 1) & 2) == 2
    return jnp.where(negative, -value, value)


def ones(rows, columns):
    return jnp.ones((rows, columns), BF16)


def split(x):
    high = x.astype(BF16)
    low = (x - high.astype(F32)).astype(BF16)
    return jnp.concatenate([high, low], 1)


def row_sums(x):
    return jnp.dot(split(x), ones(2 * HEAD, HEAD), preferred_element_type=F32)


def scale_of(sums):
    return lax.rsqrt(sums * (1.0 / HEAD) + EPS)


def row_scale(x):
    return scale_of(row_sums(x * x))


def turning():
    source = lax.broadcasted_iota(jnp.int32, (HEAD, HEAD), 0)
    target = lax.broadcasted_iota(jnp.int32, (HEAD, HEAD), 1)
    return jnp.where(target == (source + HALF) % HEAD, 1.0, 0.0).astype(BF16)


def turned_rows(raw, matrix):
    return jnp.dot(raw, matrix, preferred_element_type=F32)


def turned_gain(gain):
    return roll_half(jnp.broadcast_to(gain, (8, HEAD)))[:1]


def prepare_kernel(
    lengths_hbm, query_hbm, key_hbm, value_hbm, out_grad_hbm, query_gain_hbm, key_gain_hbm,
    query_rot_ref, query_scaled_ref, query_scale_ref, key_rot_ref, key_across_ref,
    key_scaled_ref, key_turned_ref, key_scale_ref, cos_ref, sin_ref, across_ref, bias_ref,
    value_ref, out_grad_ref, gains_ref,
    lengths_ref, query_ref, key_ref, sems,
):
    moves = [
        pltpu.make_async_copy(source, target, sems.at[place])
        for place, (source, target) in enumerate(
            (
                (lengths_hbm, lengths_ref),
                (query_gain_hbm, gains_ref.at[0:1]),
                (key_gain_hbm, gains_ref.at[1:2]),
                (key_hbm, key_ref),
                (query_hbm, query_ref),
                (out_grad_hbm, out_grad_ref),
                (value_hbm, value_ref),
            )
        )
    ]
    for move in moves:
        move.start()
    rows = query_ref.shape[0]
    keys = cos_ref.shape[0]
    base = own_index() * rows - (keys - rows)
    shape = (keys, HEAD)
    lane = lax.broadcasted_iota(jnp.int32, shape, 1)
    tokens = base + lax.broadcasted_iota(jnp.int32, shape, 0)
    frequency = frequencies()
    moves[0].wait()
    positions = tokens - doc_starts(tokens, lengths_ref)
    mixed = cos_sin_lanes(positions.astype(F32) * frequency, lane)
    turned = roll_half(mixed)
    cos = jnp.where(lane < HALF, mixed, turned)
    sin = jnp.where(lane < HALF, -turned, mixed)
    cos_ref[...] = cos
    sin_ref[...] = sin
    queries = base + (keys - rows) + lax.broadcasted_iota(jnp.int32, (1, rows), 1)
    lowest = jnp.maximum(doc_starts(queries, lengths_ref), queries - (WINDOW - 1))
    key_tokens = base + lax.broadcasted_iota(jnp.int32, (keys, rows), 0)
    visible = (key_tokens >= lowest) & (key_tokens <= queries)
    bias_ref[...] = jnp.where(visible, 0.0, MASKED)
    own_cos, own_sin = cos[keys - rows :], sin[keys - rows :]
    moves[1].wait()
    moves[2].wait()
    across_ref[0] = own_cos.T
    across_ref[1] = own_sin.T
    across_ref[2] = jnp.broadcast_to(gains_ref[0:1], (HEAD, HEAD)).T
    matrix = turning()
    for raw_ref, move, row, rot_ref in (
        (key_ref, moves[3], 1, key_rot_ref),
        (query_ref, moves[4], 0, query_rot_ref),
    ):
        gain = gains_ref[row : row + 1]
        cos_gain = own_cos * gain
        sin_gain = own_sin * turned_gain(gain)
        move.wait()
        for head in range(raw_ref.shape[1] // HEAD):
            part = slice(head * rows, (head + 1) * rows)
            across = slice(head * HEAD, (head + 1) * HEAD)
            raw = raw_ref[:, across]
            x = raw.astype(F32)
            parts = split(x * x)
            scale = scale_of(jnp.dot(parts, ones(2 * HEAD, HEAD), preferred_element_type=F32))
            scaled = x * scale
            turned = turned_rows(raw, matrix) * scale
            rotated = scaled * cos_gain + turned * sin_gain
            rot_ref[part, :] = rotated.astype(BF16)
            if raw_ref is key_ref:
                key_scale_ref[part, :] = scale
                key_scaled_ref[part, :] = scaled
                key_turned_ref[part, :] = turned
                key_across_ref[across, :] = rotated.T.astype(BF16)
            else:
                query_scaled_ref[across, :] = scaled.T
                sums = lax.dot_general(
                    ones(8, 2 * HEAD), parts, (((1,), (1,)), ((), ())), preferred_element_type=F32
                )
                query_scale_ref[head : head + 1, :] = scale_of(sums[:1])
    moves[5].wait()
    moves[6].wait()


def stacked(ref, head, group):
    return jnp.concatenate(
        [ref[:, (head * group + one) * HEAD : (head * group + one + 1) * HEAD] for one in range(group)],
        0,
    )


def attend_keys_kernel(
    far_ref, near_ref, out_grad_ref, query_rot_ref, key_rot_ref, cos_ref, sin_ref, bias_ref,
    gains_ref,
    exps_ref, inverse_ref, halo_across_ref, halo_scaled_ref, halo_turned_ref, far_value_ref, near_value_ref, own_value_ref,
):
    rows = far_ref.shape[0]
    heads = far_ref.shape[1] // HEAD
    group = out_grad_ref.shape[1] // far_ref.shape[1]
    halo = WINDOW
    keys = halo + rows
    key_gain = gains_ref[1:2]
    cos_gain = cos_ref[:halo] * key_gain
    sin_gain = sin_ref[:halo] * turned_gain(key_gain)
    matrix = turning()

    def scores_of(head):
        cols = slice(head * HEAD, (head + 1) * HEAD)
        raw = jnp.concatenate([far_ref[:, cols], near_ref[:, cols]], 0)
        x = raw.astype(F32)
        scale = row_scale(x)
        scaled = x * scale
        turned = turned_rows(raw, matrix) * scale
        part = slice(head * halo, (head + 1) * halo)
        halo_scaled_ref[part, :] = scaled
        halo_turned_ref[part, :] = turned
        rotated = scaled * cos_gain + turned * sin_gain
        halo_across_ref[cols, :] = rotated.T.astype(BF16)
        both = jnp.concatenate(
            [rotated.astype(BF16), key_rot_ref[head * rows : (head + 1) * rows, :]], 0
        )
        queries = query_rot_ref[head * group * rows : (head + 1) * group * rows, :]
        return lax.dot_general(
            both, queries, (((1,), (1,)), ((), ())), preferred_element_type=F32
        )

    later = scores_of(0)
    for head in range(heads):
        scores = later
        if head + 1 < heads:
            later = scores_of(head + 1)
        cols = slice(head * HEAD, (head + 1) * HEAD)
        low = []
        for one in range(group):
            place = (slice(head * keys, (head + 1) * keys), slice(one * rows, (one + 1) * rows))
            part = scores[:, place[1]] * (SCALE * math.log2(math.e)) + bias_ref[...]
            exps = jnp.exp2(part - jnp.max(part, axis=0, keepdims=True))
            exps_ref[place] = exps
            inverse = 1.0 / jnp.sum(exps, axis=0, keepdims=True)
            inverse_ref[head : head + 1, place[1]] = inverse
            low.append((exps_ref[place] * inverse).astype(BF16))
        value_term = jnp.dot(
            jnp.concatenate(low, 1), stacked(out_grad_ref, head, group), preferred_element_type=F32
        )
        far_value_ref[:, cols] = value_term[:rows].astype(BF16)
        near_value_ref[:, cols] = value_term[rows:halo].astype(BF16)
        own_value_ref[:, cols] = value_term[halo:]


def norm_backward(grad_rot, grad_turned, scaled, scale, gain, cos, sin):
    normed_grad = grad_rot * cos - grad_turned * sin
    part = normed_grad * scaled
    mean = row_sums(part * gain) * (1.0 / HEAD)
    return scale * (normed_grad * gain - scaled * mean), part


def attend_values_kernel(
    far_ref, near_ref, value_ref, out_grad_ref, exps_ref, inverse_ref, query_rot_ref,
    halo_across_ref, key_across_ref, halo_scaled_ref, halo_turned_ref, key_scaled_ref,
    key_turned_ref, query_scaled_ref, cos_ref, sin_ref, across_ref,
    far_key_ref, near_key_ref, own_key_ref, query_grad_ref, gain_ref,
):
    rows = far_ref.shape[0]
    heads = far_ref.shape[1] // HEAD
    group = out_grad_ref.shape[1] // far_ref.shape[1]
    halo = WINDOW
    keys = halo + rows
    cos_across, sin_across = across_ref[0] * SCALE, across_ref[1] * SCALE
    query_acc = jnp.zeros((HEAD, rows), F32)
    key_acc = jnp.zeros((keys, HEAD), F32)
    key_acc_turned = jnp.zeros((keys, HEAD), F32)

    def prob_grad_of(head):
        cols = slice(head * HEAD, (head + 1) * HEAD)
        values = jnp.concatenate([far_ref[:, cols], near_ref[:, cols], value_ref[:, cols]], 0)
        return lax.dot_general(
            values, stacked(out_grad_ref, head, group), (((1,), (1,)), ((), ())),
            preferred_element_type=F32,
        )

    later = prob_grad_of(0)
    for head in range(heads):
        prob_grad = later
        if head + 1 < heads:
            later = prob_grad_of(head + 1)
        cols = slice(head * HEAD, (head + 1) * HEAD)
        halo_part = slice(head * halo, (head + 1) * halo)
        own_part = slice(head * rows, (head + 1) * rows)
        group_part = slice(head * group * rows, (head + 1) * group * rows)
        score_grads = []
        for one in range(group):
            place = (slice(head * keys, (head + 1) * keys), slice(one * rows, (one + 1) * rows))
            part = prob_grad[:, place[1]]
            inverse = inverse_ref[head : head + 1, place[1]]
            delta = jnp.sum(exps_ref[place] * part, axis=0, keepdims=True) * inverse
            score_grads.append((exps_ref[place] * inverse * (part - delta)).astype(BF16))
        score_grad = jnp.concatenate(score_grads, 1)
        key_term = (
            jnp.dot(score_grad, query_rot_ref[group_part, :], preferred_element_type=F32) * SCALE
        )
        keys_across = jnp.concatenate([halo_across_ref[cols, :], key_across_ref[cols, :]], 1)
        query_term = jnp.dot(keys_across, score_grad, preferred_element_type=F32)
        halo_key = key_term[:halo].astype(BF16)
        far_key_ref[:, cols] = halo_key[:rows]
        near_key_ref[:, cols] = halo_key[rows:]
        own_key_ref[:, cols] = key_term[halo:]
        term = jnp.concatenate([halo_key.astype(F32), key_term[halo:]], 0)
        scaled = jnp.concatenate([halo_scaled_ref[halo_part, :], key_scaled_ref[own_part, :]], 0)
        key_acc = key_acc + term * scaled
        turned = jnp.concatenate([halo_turned_ref[halo_part, :], key_turned_ref[own_part, :]], 0)
        key_acc_turned = key_acc_turned + term * turned
        for one in range(group):
            index = head * group + one
            across = slice(index * HEAD, (index + 1) * HEAD)
            grad = query_term[:, one * rows : (one + 1) * rows]
            turned = jnp.concatenate([grad[HALF:], grad[:HALF]], 0)
            normed_grad = grad * cos_across - turned * sin_across
            query_grad_ref[across, :] = normed_grad
            query_acc = query_acc + normed_grad * query_scaled_ref[across, :]
    query_sum = jnp.sum(query_acc.T, axis=0, keepdims=True)
    key_sum = jnp.sum(key_acc * cos_ref[...], axis=0, keepdims=True)
    turned_sum = jnp.sum(key_acc_turned * sin_ref[...], axis=0, keepdims=True)
    gain_ref[...] = jnp.concatenate([query_sum, key_sum + turned_gain(turned_sum)], 0)


def spread_kernel(gain_ref, near_value_ref, far_value_ref, copies_ref):
    copies_ref[...] = jnp.broadcast_to(gain_ref[...][None], copies_ref.shape)


def finish_queries_kernel(query_grad_ref, query_scaled_ref, query_scale_ref, across_ref, out_ref):
    gain = across_ref[2]
    for head in range(out_ref.shape[1] // HEAD):
        across = slice(head * HEAD, (head + 1) * HEAD)
        scaled = query_scaled_ref[across, :]
        weighted = query_grad_ref[across, :] * gain
        mean = jnp.sum(weighted * scaled, axis=0, keepdims=True) * (1.0 / HEAD)
        grad = query_scale_ref[head : head + 1, :] * (weighted - scaled * mean)
        out_ref[:, across] = grad.T.astype(BF16)


def finish_values_kernel(own_ref, near_ref, far_ref, grad_value_ref):
    total = own_ref[...] + near_ref[...].astype(F32) + far_ref[...].astype(F32)
    grad_value_ref[...] = total.astype(BF16)


def finish_keys_kernel(
    own_ref, near_ref, far_ref, key_scaled_ref, key_scale_ref, cos_ref, sin_ref, gains_ref, parts_ref,
    grad_key_ref, query_gain_ref, key_gain_ref,
):
    rows = own_ref.shape[0]
    cos, sin = cos_ref[WINDOW:], sin_ref[WINDOW:]
    gain = gains_ref[1:2]
    for head in range(own_ref.shape[1] // HEAD):
        cols = slice(head * HEAD, (head + 1) * HEAD)
        part = slice(head * rows, (head + 1) * rows)
        total = own_ref[:, cols] + near_ref[:, cols].astype(F32) + far_ref[:, cols].astype(F32)
        grad, _ = norm_backward(
            total, roll_half(total), key_scaled_ref[part, :], key_scale_ref[part, :], gain, cos, sin
        )
        grad_key_ref[:, cols] = grad.astype(BF16)
    sums = jnp.sum(parts_ref[...], axis=0)
    query_gain_ref[...] = sums[:1]
    key_gain_ref[...] = sums[1:]


def call(kernel, name, outs, operands, cost=None, space=pltpu.VMEM, scratch=()):
    return pl.pallas_call(
        kernel,
        out_shape=outs,
        in_specs=[pl.BlockSpec(memory_space=space)] * len(operands),
        out_specs=[pl.BlockSpec(memory_space=pltpu.VMEM)] * len(outs),
        scratch_shapes=scratch,
        compiler_params=pltpu.CompilerParams(vmem_limit_bytes=VMEM_LIMIT),
        cost_estimate=cost,
        name=name,
    )(*operands)


def cost(flops, size, exps=0):
    return pl.CostEstimate(flops=flops, bytes_accessed=size, transcendentals=exps)


def shape(dims, dtype):
    return jax.ShapeDtypeStruct(dims, dtype)


def on_device(doc_lengths, query_raw, key_raw, value_matrix, out_grad, query_gain, key_gain):
    rows, query_width = query_raw.shape
    width = key_raw.shape[1]
    heads = width // HEAD
    query_heads = query_width // HEAD
    keys = WINDOW + rows
    devices = lax.axis_size(AXES)
    query_gain = query_gain.reshape(1, HEAD)
    key_gain = key_gain.reshape(1, HEAD)
    near_key, far_key = shift(key_raw, 1), shift(key_raw, 2)
    term = shape((rows, width), BF16)
    own = shape((rows, width), F32)
    (
        query_rot, query_scaled, query_scale, key_rot, key_across, key_scaled, key_turned, key_scale,
        cos, sin, across, bias, values, grads_out, gains,
    ) = call(
        prepare_kernel,
        "prepare",
        [
            shape((query_heads * rows, HEAD), BF16),
            shape((query_width, rows), F32),
            shape((query_heads, rows), F32),
            shape((heads * rows, HEAD), BF16),
            shape((width, rows), BF16),
            shape((heads * rows, HEAD), F32),
            shape((heads * rows, HEAD), F32),
            shape((heads * rows, HEAD), F32),
            shape((keys, HEAD), F32),
            shape((keys, HEAD), F32),
            shape((3, HEAD, rows), F32),
            shape((keys, rows), F32),
            term,
            shape((rows, query_width), BF16),
            shape((8, HEAD), F32),
        ],
        [
            pltpu.with_memory_space_constraint(x, pltpu.HBM)
            for x in (doc_lengths, query_raw, key_raw, value_matrix, out_grad, query_gain, key_gain)
        ],
        cost(4_000_000, 6_000_000),
        space=pltpu.HBM,
        scratch=[
            pltpu.SMEM(doc_lengths.shape, jnp.int32),
            pltpu.VMEM((rows, query_width), BF16),
            pltpu.VMEM((rows, width), BF16),
            pltpu.SemaphoreType.DMA((7,)),
        ],
    )
    near_value, far_value = shift(values, 1), shift(values, 2)
    exps, inverse, halo_across, halo_scaled, halo_turned, far_value_term, near_value_term, own_value = call(
        attend_keys_kernel,
        "attend_keys",
        [
            shape((heads * keys, query_heads // heads * rows), F32),
            shape((heads, query_heads // heads * rows), F32),
            shape((width, WINDOW), BF16),
            shape((heads * WINDOW, HEAD), F32),
            shape((heads * WINDOW, HEAD), F32),
            term,
            term,
            own,
        ],
        (far_key, near_key, grads_out, query_rot, key_rot, cos, sin, bias, gains),
        cost(400_000_000, 4_000_000, 800_000),
    )
    near_value_back, far_value_back = shift(near_value_term, -1), shift(far_value_term, -2)
    far_key_term, near_key_term, own_key, query_grad, gain_part = call(
        attend_values_kernel,
        "attend_values",
        [term, term, own, shape((query_width, rows), F32), shape((2, HEAD), F32)],
        (
            far_value, near_value, values, grads_out, exps, inverse, query_rot,
            halo_across, key_across, halo_scaled, halo_turned, key_scaled,
            key_turned, query_scaled, cos, sin, across,
        ),
        cost(600_000_000, 4_000_000),
    )
    near_key_back, far_key_back = shift(near_key_term, -1), shift(far_key_term, -2)
    copies = pl.pallas_call(
        spread_kernel,
        out_shape=shape((devices, 2, HEAD), F32),
        in_specs=[pl.BlockSpec(memory_space=pltpu.VMEM)] + [pl.BlockSpec(memory_space=pl.ANY)] * 2,
        out_specs=pl.BlockSpec(memory_space=pltpu.VMEM),
        name="spread_gains",
    )(gain_part, near_value_back, far_value_back)
    parts = lax.all_to_all(copies, AXES, 0, 0)
    (grad_value,) = call(
        finish_values_kernel,
        "finish_values",
        [term],
        (own_value, near_value_back, far_value_back),
        cost(1_000_000, 2_000_000),
    )
    (grad_query,) = call(
        finish_queries_kernel,
        "finish_queries",
        [shape((rows, query_width), BF16)],
        (query_grad, query_scaled, query_scale, across),
        cost(4_000_000, 4_000_000),
    )
    grad_key, grad_query_gain, grad_key_gain = call(
        finish_keys_kernel,
        "finish_keys",
        [term, shape((1, HEAD), F32), shape((1, HEAD), F32)],
        (own_key, near_key_back, far_key_back, key_scaled, key_scale, cos, sin, gains, parts),
        cost(4_000_000, 3_000_000),
    )
    return (
        grad_query, grad_key, grad_value, grad_query_gain.reshape(HEAD), grad_key_gain.reshape(HEAD)
    )


def solution(mesh):
    rows = P(AXES, None)
    return jax.shard_map(
        on_device,
        mesh=mesh,
        in_specs=(P(), rows, rows, rows, rows, P(), P()),
        out_specs=(rows, rows, rows, P(), P()),
        check_vma=False,
    )
```

```python
import math

import jax
import jax.numpy as jnp
import numpy as np
from jax import lax
from jax.experimental import pallas as pl
from jax.experimental.pallas import tpu as pltpu
from jax.sharding import PartitionSpec as P

HEAD = 128
HALF = HEAD // 2
WINDOW = 256
EPS = 1e-06
SCALE = 168.0 ** (-0.5)
ROPE_BASE = 10000.0
MASKED = -1e30
AXES = ("ctx", "grp")
F32 = jnp.float32
BF16 = jnp.bfloat16
VMEM_LIMIT = 16 * 1024 * 1024


def frequencies():
    lane = lax.broadcasted_iota(jnp.int32, (1, HEAD), 1) % HALF
    values = jnp.zeros((1, HEAD), F32)
    for m in range(HALF):
        values = jnp.where(lane == m, np.float32(ROPE_BASE ** (-2.0 * m / HEAD)), values)
    return values


def shift(value, steps):
    count = lax.axis_size(AXES)
    return lax.ppermute(value, AXES, [(s, (s + steps) % count) for s in range(count)])


def own_index():
    return lax.axis_index("ctx") * lax.axis_size("grp") + lax.axis_index("grp")


def roll_half(x):
    return pltpu.roll(x, HALF, 1)


def doc_starts(tokens, lengths_ref):
    def step(doc, carry):
        end, starts = carry
        end = end + lengths_ref[doc]
        return end, jnp.where(tokens >= end, end, starts)

    count = lengths_ref.shape[0]
    return lax.fori_loop(
        0, count, step, (jnp.int32(0), jnp.zeros_like(tokens)), unroll=count if count <= 8 else 1
    )[1]


def cos_sin_lanes(angle, lane):
    turns = jnp.floor(angle * (2.0 / math.pi) + 0.5)
    r = angle - turns * 1.5703125
    r = r - turns * 4.837512969970703125e-4
    r = r - turns * 7.549789948768648e-8
    z = r * r
    sin_r = r + r * z * (-1.6666654611e-1 + z * (8.3321608736e-3 + z * -1.9515295891e-4))
    cos_r = 1.0 - 0.5 * z + z * z * (
        4.166664568298827e-2 + z * (-1.388731625493765e-3 + z * 2.443315711809948e-5)
    )
    quadrant = turns.astype(jnp.int32) - jnp.where(lane >= HALF, 1, 0)
    odd = (quadrant & 1) == 1
    value = jnp.where(odd, sin_r, cos_r)
    negative = ((quadrant + 1) & 2) == 2
    return jnp.where(negative, -value, value)


def ones(rows, columns):
    return jnp.ones((rows, columns), BF16)


def split(x):
    high = x.astype(BF16)
    low = (x - high.astype(F32)).astype(BF16)
    return jnp.concatenate([high, low], 1)


def row_sums(x):
    return jnp.dot(split(x), ones(2 * HEAD, HEAD), preferred_element_type=F32)


def scale_of(sums):
    return lax.rsqrt(sums * (1.0 / HEAD) + EPS)


def row_scale(x):
    return scale_of(row_sums(x * x))


def turning():
    source = lax.broadcasted_iota(jnp.int32, (HEAD, HEAD), 0)
    target = lax.broadcasted_iota(jnp.int32, (HEAD, HEAD), 1)
    return jnp.where(target == (source + HALF) % HEAD, 1.0, 0.0).astype(BF16)


def turned_rows(raw, matrix):
    return jnp.dot(raw, matrix, preferred_element_type=F32)


def turned_gain(gain):
    return roll_half(jnp.broadcast_to(gain, (8, HEAD)))[:1]


def prepare_kernel(
    lengths_hbm, query_hbm, key_hbm, value_hbm, out_grad_hbm, query_gain_hbm, key_gain_hbm,
    query_rot_ref, query_scaled_ref, query_scale_ref, key_rot_ref, key_across_ref,
    key_scaled_ref, key_scale_ref, cos_ref, sin_ref, across_ref, bias_ref,
    value_ref, out_grad_ref, gains_ref,
    lengths_ref, query_ref, key_ref, sems,
):
    moves = [
        pltpu.make_async_copy(source, target, sems.at[place])
        for place, (source, target) in enumerate(
            (
                (lengths_hbm, lengths_ref),
                (query_gain_hbm, gains_ref.at[0:1]),
                (key_gain_hbm, gains_ref.at[1:2]),
                (key_hbm, key_ref),
                (query_hbm, query_ref),
                (out_grad_hbm, out_grad_ref),
                (value_hbm, value_ref),
            )
        )
    ]
    for move in moves:
        move.start()
    rows = query_ref.shape[0]
    keys = cos_ref.shape[0]
    base = own_index() * rows - (keys - rows)
    shape = (keys, HEAD)
    lane = lax.broadcasted_iota(jnp.int32, shape, 1)
    tokens = base + lax.broadcasted_iota(jnp.int32, shape, 0)
    frequency = frequencies()
    moves[0].wait()
    positions = tokens - doc_starts(tokens, lengths_ref)
    mixed = cos_sin_lanes(positions.astype(F32) * frequency, lane)
    turned = roll_half(mixed)
    cos = jnp.where(lane < HALF, mixed, turned)
    sin = jnp.where(lane < HALF, -turned, mixed)
    cos_ref[...] = cos
    sin_ref[...] = sin
    queries = base + (keys - rows) + lax.broadcasted_iota(jnp.int32, (1, rows), 1)
    lowest = jnp.maximum(doc_starts(queries, lengths_ref), queries - (WINDOW - 1))
    key_tokens = base + lax.broadcasted_iota(jnp.int32, (keys, rows), 0)
    visible = (key_tokens >= lowest) & (key_tokens <= queries)
    bias_ref[...] = jnp.where(visible, 0.0, MASKED)
    own_cos, own_sin = cos[keys - rows :], sin[keys - rows :]
    moves[1].wait()
    moves[2].wait()
    across_ref[0] = own_cos.T
    across_ref[1] = own_sin.T
    across_ref[2] = jnp.broadcast_to(gains_ref[0:1], (HEAD, HEAD)).T
    matrix = turning()
    for raw_ref, move, row, rot_ref in (
        (key_ref, moves[3], 1, key_rot_ref),
        (query_ref, moves[4], 0, query_rot_ref),
    ):
        gain = gains_ref[row : row + 1]
        cos_gain = own_cos * gain
        sin_gain = own_sin * turned_gain(gain)
        move.wait()
        for head in range(raw_ref.shape[1] // HEAD):
            part = slice(head * rows, (head + 1) * rows)
            across = slice(head * HEAD, (head + 1) * HEAD)
            raw = raw_ref[:, across]
            x = raw.astype(F32)
            parts = split(x * x)
            scale = scale_of(jnp.dot(parts, ones(2 * HEAD, HEAD), preferred_element_type=F32))
            scaled = x * scale
            turned = turned_rows(raw, matrix) * scale
            rotated = scaled * cos_gain + turned * sin_gain
            rot_ref[part, :] = rotated.astype(BF16)
            if raw_ref is key_ref:
                key_scale_ref[part, :] = scale
                key_scaled_ref[part, :] = scaled
                key_across_ref[across, :] = rotated.T.astype(BF16)
            else:
                query_scaled_ref[across, :] = scaled.T
                sums = lax.dot_general(
                    ones(8, 2 * HEAD), parts, (((1,), (1,)), ((), ())), preferred_element_type=F32
                )
                query_scale_ref[head : head + 1, :] = scale_of(sums[:1])
    moves[5].wait()
    moves[6].wait()


def stacked(ref, head, group):
    return jnp.concatenate(
        [ref[:, (head * group + one) * HEAD : (head * group + one + 1) * HEAD] for one in range(group)],
        0,
    )


def attend_keys_kernel(
    far_ref, near_ref, out_grad_ref, query_rot_ref, key_rot_ref, cos_ref, sin_ref, bias_ref,
    gains_ref,
    exps_ref, inverse_ref, halo_across_ref, halo_scaled_ref, far_value_ref, near_value_ref, own_value_ref,
):
    rows = far_ref.shape[0]
    heads = far_ref.shape[1] // HEAD
    group = out_grad_ref.shape[1] // far_ref.shape[1]
    halo = WINDOW
    keys = halo + rows
    key_gain = gains_ref[1:2]
    cos_gain = cos_ref[:halo] * key_gain
    sin_gain = sin_ref[:halo] * turned_gain(key_gain)
    matrix = turning()

    def scores_of(head):
        cols = slice(head * HEAD, (head + 1) * HEAD)
        raw = jnp.concatenate([far_ref[:, cols], near_ref[:, cols]], 0)
        x = raw.astype(F32)
        scale = row_scale(x)
        scaled = x * scale
        turned = turned_rows(raw, matrix) * scale
        part = slice(head * halo, (head + 1) * halo)
        halo_scaled_ref[part, :] = scaled
        rotated = scaled * cos_gain + turned * sin_gain
        halo_across_ref[cols, :] = rotated.T.astype(BF16)
        both = jnp.concatenate(
            [rotated.astype(BF16), key_rot_ref[head * rows : (head + 1) * rows, :]], 0
        )
        queries = query_rot_ref[head * group * rows : (head + 1) * group * rows, :]
        return lax.dot_general(
            both, queries, (((1,), (1,)), ((), ())), preferred_element_type=F32
        )

    later = scores_of(0)
    for head in range(heads):
        scores = later
        if head + 1 < heads:
            later = scores_of(head + 1)
        cols = slice(head * HEAD, (head + 1) * HEAD)
        low = []
        for one in range(group):
            place = (slice(head * keys, (head + 1) * keys), slice(one * rows, (one + 1) * rows))
            part = scores[:, place[1]] * (SCALE * math.log2(math.e)) + bias_ref[...]
            exps = jnp.exp2(part - jnp.max(part, axis=0, keepdims=True))
            exps_ref[place] = exps
            inverse = 1.0 / jnp.sum(exps, axis=0, keepdims=True)
            inverse_ref[head : head + 1, place[1]] = inverse
            low.append((exps_ref[place] * inverse).astype(BF16))
        value_term = jnp.dot(
            jnp.concatenate(low, 1), stacked(out_grad_ref, head, group), preferred_element_type=F32
        )
        far_value_ref[:, cols] = value_term[:rows].astype(BF16)
        near_value_ref[:, cols] = value_term[rows:halo].astype(BF16)
        own_value_ref[:, cols] = value_term[halo:]


def norm_backward(grad_rot, grad_turned, scaled, scale, gain, cos, sin):
    normed_grad = grad_rot * cos - grad_turned * sin
    part = normed_grad * scaled
    mean = row_sums(part * gain) * (1.0 / HEAD)
    return scale * (normed_grad * gain - scaled * mean), part


def attend_values_kernel(
    far_ref, near_ref, value_ref, out_grad_ref, exps_ref, inverse_ref, query_rot_ref,
    halo_across_ref, key_across_ref, halo_scaled_ref, key_scaled_ref,
    query_scaled_ref, cos_ref, sin_ref, across_ref,
    far_key_ref, near_key_ref, own_key_ref, query_grad_ref, gain_ref,
):
    rows = far_ref.shape[0]
    heads = far_ref.shape[1] // HEAD
    group = out_grad_ref.shape[1] // far_ref.shape[1]
    halo = WINDOW
    keys = halo + rows
    cos_across, sin_across = across_ref[0] * SCALE, across_ref[1] * SCALE
    query_acc = jnp.zeros((HEAD, rows), F32)
    key_acc = jnp.zeros((keys, HEAD), F32)
    key_acc_turned = jnp.zeros((keys, HEAD), F32)

    def prob_grad_of(head):
        cols = slice(head * HEAD, (head + 1) * HEAD)
        values = jnp.concatenate([far_ref[:, cols], near_ref[:, cols], value_ref[:, cols]], 0)
        return lax.dot_general(
            values, stacked(out_grad_ref, head, group), (((1,), (1,)), ((), ())),
            preferred_element_type=F32,
        )

    later = prob_grad_of(0)
    for head in range(heads):
        prob_grad = later
        if head + 1 < heads:
            later = prob_grad_of(head + 1)
        cols = slice(head * HEAD, (head + 1) * HEAD)
        halo_part = slice(head * halo, (head + 1) * halo)
        own_part = slice(head * rows, (head + 1) * rows)
        group_part = slice(head * group * rows, (head + 1) * group * rows)
        score_grads = []
        for one in range(group):
            place = (slice(head * keys, (head + 1) * keys), slice(one * rows, (one + 1) * rows))
            part = prob_grad[:, place[1]]
            inverse = inverse_ref[head : head + 1, place[1]]
            delta = jnp.sum(exps_ref[place] * part, axis=0, keepdims=True) * inverse
            score_grads.append((exps_ref[place] * inverse * (part - delta)).astype(BF16))
        score_grad = jnp.concatenate(score_grads, 1)
        key_term = (
            jnp.dot(score_grad, query_rot_ref[group_part, :], preferred_element_type=F32) * SCALE
        )
        keys_across = jnp.concatenate([halo_across_ref[cols, :], key_across_ref[cols, :]], 1)
        query_term = jnp.dot(keys_across, score_grad, preferred_element_type=F32)
        halo_key = key_term[:halo].astype(BF16)
        far_key_ref[:, cols] = halo_key[:rows]
        near_key_ref[:, cols] = halo_key[rows:]
        own_key_ref[:, cols] = key_term[halo:]
        term = jnp.concatenate([halo_key.astype(F32), key_term[halo:]], 0)
        scaled = jnp.concatenate([halo_scaled_ref[halo_part, :], key_scaled_ref[own_part, :]], 0)
        key_acc = key_acc + term * scaled
        key_acc_turned = key_acc_turned + term * roll_half(scaled)
        for one in range(group):
            index = head * group + one
            across = slice(index * HEAD, (index + 1) * HEAD)
            grad = query_term[:, one * rows : (one + 1) * rows]
            turned = jnp.concatenate([grad[HALF:], grad[:HALF]], 0)
            normed_grad = grad * cos_across - turned * sin_across
            query_grad_ref[across, :] = normed_grad
            query_acc = query_acc + normed_grad * query_scaled_ref[across, :]
    query_sum = jnp.sum(query_acc.T, axis=0, keepdims=True)
    key_sum = jnp.sum(key_acc * cos_ref[...], axis=0, keepdims=True)
    turned_sum = jnp.sum(key_acc_turned * sin_ref[...], axis=0, keepdims=True)
    gain_ref[...] = jnp.concatenate([query_sum, key_sum + turned_gain(turned_sum)], 0)


def finish_queries_kernel(query_grad_ref, query_scaled_ref, query_scale_ref, across_ref, out_ref):
    gain = across_ref[2]
    for head in range(out_ref.shape[1] // HEAD):
        across = slice(head * HEAD, (head + 1) * HEAD)
        scaled = query_scaled_ref[across, :]
        weighted = query_grad_ref[across, :] * gain
        mean = jnp.sum(weighted * scaled, axis=0, keepdims=True) * (1.0 / HEAD)
        grad = query_scale_ref[head : head + 1, :] * (weighted - scaled * mean)
        out_ref[:, across] = grad.T.astype(BF16)


def finish_values_kernel(own_ref, near_ref, far_ref, gain_ref, grad_value_ref, copies_ref):
    total = own_ref[...] + near_ref[...].astype(F32) + far_ref[...].astype(F32)
    grad_value_ref[...] = total.astype(BF16)
    copies_ref[...] = jnp.broadcast_to(gain_ref[...][None], copies_ref.shape)


def finish_keys_kernel(
    own_ref, near_ref, far_ref, key_scaled_ref, key_scale_ref, cos_ref, sin_ref, gains_ref, parts_ref,
    grad_key_ref, query_gain_ref, key_gain_ref,
):
    rows = own_ref.shape[0]
    cos, sin = cos_ref[WINDOW:], sin_ref[WINDOW:]
    gain = gains_ref[1:2]
    for head in range(own_ref.shape[1] // HEAD):
        cols = slice(head * HEAD, (head + 1) * HEAD)
        part = slice(head * rows, (head + 1) * rows)
        total = own_ref[:, cols] + near_ref[:, cols].astype(F32) + far_ref[:, cols].astype(F32)
        grad, _ = norm_backward(
            total, roll_half(total), key_scaled_ref[part, :], key_scale_ref[part, :], gain, cos, sin
        )
        grad_key_ref[:, cols] = grad.astype(BF16)
    sums = jnp.sum(parts_ref[...], axis=0)
    query_gain_ref[...] = sums[:1]
    key_gain_ref[...] = sums[1:]


def call(kernel, name, outs, operands, cost=None, space=pltpu.VMEM, scratch=()):
    return pl.pallas_call(
        kernel,
        out_shape=outs,
        in_specs=[pl.BlockSpec(memory_space=space)] * len(operands),
        out_specs=[pl.BlockSpec(memory_space=pltpu.VMEM)] * len(outs),
        scratch_shapes=scratch,
        compiler_params=pltpu.CompilerParams(vmem_limit_bytes=VMEM_LIMIT),
        cost_estimate=cost,
        name=name,
    )(*operands)


def cost(flops, size, exps=0):
    return pl.CostEstimate(flops=flops, bytes_accessed=size, transcendentals=exps)


def shape(dims, dtype):
    return jax.ShapeDtypeStruct(dims, dtype)


def on_device(doc_lengths, query_raw, key_raw, value_matrix, out_grad, query_gain, key_gain):
    rows, query_width = query_raw.shape
    width = key_raw.shape[1]
    heads = width // HEAD
    query_heads = query_width // HEAD
    keys = WINDOW + rows
    devices = lax.axis_size(AXES)
    query_gain = query_gain.reshape(1, HEAD)
    key_gain = key_gain.reshape(1, HEAD)
    near_key, far_key = shift(key_raw, 1), shift(key_raw, 2)
    term = shape((rows, width), BF16)
    own = shape((rows, width), F32)
    (
        query_rot, query_scaled, query_scale, key_rot, key_across, key_scaled, key_scale,
        cos, sin, across, bias, values, grads_out, gains,
    ) = call(
        prepare_kernel,
        "prepare",
        [
            shape((query_heads * rows, HEAD), BF16),
            shape((query_width, rows), F32),
            shape((query_heads, rows), F32),
            shape((heads * rows, HEAD), BF16),
            shape((width, rows), BF16),
            shape((heads * rows, HEAD), F32),
            shape((heads * rows, HEAD), F32),
            shape((keys, HEAD), F32),
            shape((keys, HEAD), F32),
            shape((3, HEAD, rows), F32),
            shape((keys, rows), F32),
            term,
            shape((rows, query_width), BF16),
            shape((8, HEAD), F32),
        ],
        [
            pltpu.with_memory_space_constraint(x, pltpu.HBM)
            for x in (doc_lengths, query_raw, key_raw, value_matrix, out_grad, query_gain, key_gain)
        ],
        cost(4_000_000, 6_000_000),
        space=pltpu.HBM,
        scratch=[
            pltpu.SMEM(doc_lengths.shape, jnp.int32),
            pltpu.VMEM((rows, query_width), BF16),
            pltpu.VMEM((rows, width), BF16),
            pltpu.SemaphoreType.DMA((7,)),
        ],
    )
    near_value, far_value = shift(values, 1), shift(values, 2)
    exps, inverse, halo_across, halo_scaled, far_value_term, near_value_term, own_value = call(
        attend_keys_kernel,
        "attend_keys",
        [
            shape((heads * keys, query_heads // heads * rows), F32),
            shape((heads, query_heads // heads * rows), F32),
            shape((width, WINDOW), BF16),
            shape((heads * WINDOW, HEAD), F32),
            term,
            term,
            own,
        ],
        (far_key, near_key, grads_out, query_rot, key_rot, cos, sin, bias, gains),
        cost(400_000_000, 4_000_000, 800_000),
    )
    near_value_back, far_value_back = shift(near_value_term, -1), shift(far_value_term, -2)
    far_key_term, near_key_term, own_key, query_grad, gain_part = call(
        attend_values_kernel,
        "attend_values",
        [term, term, own, shape((query_width, rows), F32), shape((2, HEAD), F32)],
        (
            far_value, near_value, values, grads_out, exps, inverse, query_rot,
            halo_across, key_across, halo_scaled, key_scaled, query_scaled, cos, sin, across,
        ),
        cost(600_000_000, 4_000_000),
    )
    near_key_back, far_key_back = shift(near_key_term, -1), shift(far_key_term, -2)
    grad_value, copies = call(
        finish_values_kernel,
        "finish_values",
        [term, shape((devices, 2, HEAD), F32)],
        (own_value, near_value_back, far_value_back, gain_part),
        cost(1_000_000, 2_000_000),
    )
    parts = lax.all_to_all(copies, AXES, 0, 0)
    (grad_query,) = call(
        finish_queries_kernel,
        "finish_queries",
        [shape((rows, query_width), BF16)],
        (query_grad, query_scaled, query_scale, across),
        cost(4_000_000, 4_000_000),
    )
    grad_key, grad_query_gain, grad_key_gain = call(
        finish_keys_kernel,
        "finish_keys",
        [term, shape((1, HEAD), F32), shape((1, HEAD), F32)],
        (own_key, near_key_back, far_key_back, key_scaled, key_scale, cos, sin, gains, parts),
        cost(4_000_000, 3_000_000),
    )
    return (
        grad_query, grad_key, grad_value, grad_query_gain.reshape(HEAD), grad_key_gain.reshape(HEAD)
    )


def solution(mesh):
    rows = P(AXES, None)
    return jax.shard_map(
        on_device,
        mesh=mesh,
        in_specs=(P(), rows, rows, rows, rows, P(), P()),
        out_specs=(rows, rows, rows, P(), P()),
        check_vma=False,
    )
```

```python
import math

import jax
import jax.numpy as jnp
import numpy as np
from jax import lax
from jax.experimental import pallas as pl
from jax.experimental.pallas import tpu as pltpu
from jax.sharding import PartitionSpec as P

HEAD = 128
HALF = HEAD // 2
WINDOW = 256
EPS = 1e-06
SCALE = 168.0 ** (-0.5)
ROPE_BASE = 10000.0
MASKED = -1e30
AXES = ("ctx", "grp")
F32 = jnp.float32
BF16 = jnp.bfloat16
VMEM_LIMIT = 16 * 1024 * 1024


def frequencies():
    lane = lax.broadcasted_iota(jnp.int32, (1, HEAD), 1) % HALF
    values = jnp.zeros((1, HEAD), F32)
    for m in range(HALF):
        values = jnp.where(lane == m, np.float32(ROPE_BASE ** (-2.0 * m / HEAD)), values)
    return values


def shift(value, steps):
    count = lax.axis_size(AXES)
    return lax.ppermute(value, AXES, [(s, (s + steps) % count) for s in range(count)])


def own_index():
    return lax.axis_index("ctx") * lax.axis_size("grp") + lax.axis_index("grp")


def roll_half(x):
    return pltpu.roll(x, HALF, 1)


def doc_starts(tokens, lengths_ref):
    def step(doc, carry):
        end, starts = carry
        end = end + lengths_ref[doc]
        return end, jnp.where(tokens >= end, end, starts)

    count = lengths_ref.shape[0]
    return lax.fori_loop(
        0, count, step, (jnp.int32(0), jnp.zeros_like(tokens)), unroll=count if count <= 8 else 1
    )[1]


def cos_sin_lanes(angle, lane):
    turns = jnp.floor(angle * (2.0 / math.pi) + 0.5)
    r = angle - turns * 1.5703125
    r = r - turns * 4.837512969970703125e-4
    r = r - turns * 7.549789948768648e-8
    z = r * r
    sin_r = r + r * z * (-1.6666654611e-1 + z * (8.3321608736e-3 + z * -1.9515295891e-4))
    cos_r = 1.0 - 0.5 * z + z * z * (
        4.166664568298827e-2 + z * (-1.388731625493765e-3 + z * 2.443315711809948e-5)
    )
    quadrant = turns.astype(jnp.int32) - jnp.where(lane >= HALF, 1, 0)
    odd = (quadrant & 1) == 1
    value = jnp.where(odd, sin_r, cos_r)
    negative = ((quadrant + 1) & 2) == 2
    return jnp.where(negative, -value, value)


def ones(rows, columns):
    return jnp.ones((rows, columns), BF16)


def split(x):
    high = x.astype(BF16)
    low = (x - high.astype(F32)).astype(BF16)
    return jnp.concatenate([high, low], 1)


def row_sums(x):
    return jnp.dot(split(x), ones(2 * HEAD, HEAD), preferred_element_type=F32)


def scale_of(sums):
    return lax.rsqrt(sums * (1.0 / HEAD) + EPS)


def row_scale(x):
    return scale_of(row_sums(x * x))


def turning():
    source = lax.broadcasted_iota(jnp.int32, (HEAD, HEAD), 0)
    target = lax.broadcasted_iota(jnp.int32, (HEAD, HEAD), 1)
    return jnp.where(target == (source + HALF) % HEAD, 1.0, 0.0).astype(BF16)


def turned_rows(raw, matrix):
    return jnp.dot(raw, matrix, preferred_element_type=F32)


def turned_gain(gain):
    return roll_half(jnp.broadcast_to(gain, (8, HEAD)))[:1]


def prepare_kernel(
    lengths_hbm, query_hbm, key_hbm, value_hbm, out_grad_hbm, query_gain_hbm, key_gain_hbm,
    query_rot_ref, query_scaled_ref, query_scale_ref, key_rot_ref, key_across_ref,
    key_scaled_ref, key_scale_ref, cos_ref, sin_ref, across_ref, gain_across_ref, bias_ref,
    value_ref, out_grad_ref, gains_ref, query_scaled_hbm,
    lengths_ref, query_ref, key_ref, sems, out_sems,
):
    moves = [
        pltpu.make_async_copy(source, target, sems.at[place])
        for place, (source, target) in enumerate(
            (
                (lengths_hbm, lengths_ref),
                (query_gain_hbm, gains_ref.at[0:1]),
                (key_gain_hbm, gains_ref.at[1:2]),
                (key_hbm, key_ref),
                (query_hbm, query_ref),
                (out_grad_hbm, out_grad_ref),
                (value_hbm, value_ref),
            )
        )
    ]
    for move in moves:
        move.start()
    rows = query_ref.shape[0]
    keys = cos_ref.shape[0]
    base = own_index() * rows - (keys - rows)
    shape = (keys, HEAD)
    lane = lax.broadcasted_iota(jnp.int32, shape, 1)
    tokens = base + lax.broadcasted_iota(jnp.int32, shape, 0)
    frequency = frequencies()
    moves[0].wait()
    positions = tokens - doc_starts(tokens, lengths_ref)
    mixed = cos_sin_lanes(positions.astype(F32) * frequency, lane)
    turned = roll_half(mixed)
    cos = jnp.where(lane < HALF, mixed, turned)
    sin = jnp.where(lane < HALF, -turned, mixed)
    cos_ref[...] = cos
    sin_ref[...] = sin
    queries = base + (keys - rows) + lax.broadcasted_iota(jnp.int32, (1, rows), 1)
    lowest = jnp.maximum(doc_starts(queries, lengths_ref), queries - (WINDOW - 1))
    key_tokens = base + lax.broadcasted_iota(jnp.int32, (keys, rows), 0)
    visible = (key_tokens >= lowest) & (key_tokens <= queries)
    bias_ref[...] = jnp.where(visible, 0.0, MASKED)
    own_cos, own_sin = cos[keys - rows :], sin[keys - rows :]
    moves[1].wait()
    moves[2].wait()
    across_ref[0] = own_cos.T
    across_ref[1] = own_sin.T
    gain_across_ref[...] = jnp.broadcast_to(gains_ref[0:1], (HEAD, HEAD)).T
    saves = []
    matrix = turning()
    for raw_ref, move, row, rot_ref in (
        (key_ref, moves[3], 1, key_rot_ref),
        (query_ref, moves[4], 0, query_rot_ref),
    ):
        gain = gains_ref[row : row + 1]
        cos_gain = own_cos * gain
        sin_gain = own_sin * turned_gain(gain)
        move.wait()
        for head in range(raw_ref.shape[1] // HEAD):
            part = slice(head * rows, (head + 1) * rows)
            across = slice(head * HEAD, (head + 1) * HEAD)
            raw = raw_ref[:, across]
            x = raw.astype(F32)
            parts = split(x * x)
            scale = scale_of(jnp.dot(parts, ones(2 * HEAD, HEAD), preferred_element_type=F32))
            scaled = x * scale
            turned = turned_rows(raw, matrix) * scale
            rotated = scaled * cos_gain + turned * sin_gain
            rot_ref[part, :] = rotated.astype(BF16)
            if raw_ref is key_ref:
                key_scale_ref[part, :] = scale
                key_scaled_ref[part, :] = scaled
                key_across_ref[across, :] = rotated.T.astype(BF16)
            else:
                query_scaled_ref[across, :] = scaled.T
                saves.append(
                    pltpu.make_async_copy(
                        query_scaled_ref.at[across], query_scaled_hbm.at[across], out_sems.at[head]
                    )
                )
                saves[-1].start()
                sums = lax.dot_general(
                    ones(8, 2 * HEAD), parts, (((1,), (1,)), ((), ())), preferred_element_type=F32
                )
                query_scale_ref[head : head + 1, :] = scale_of(sums[:1])
    for move in moves[5:] + saves:
        move.wait()


def stacked(ref, head, group):
    return jnp.concatenate(
        [ref[:, (head * group + one) * HEAD : (head * group + one + 1) * HEAD] for one in range(group)],
        0,
    )


def attend_keys_kernel(
    far_ref, near_ref, out_grad_ref, query_rot_ref, key_rot_ref, cos_ref, sin_ref, bias_ref,
    gains_ref,
    exps_ref, inverse_ref, halo_across_ref, halo_scaled_ref, far_value_ref, near_value_ref, own_value_ref,
):
    rows = far_ref.shape[0]
    heads = far_ref.shape[1] // HEAD
    group = out_grad_ref.shape[1] // far_ref.shape[1]
    halo = WINDOW
    keys = halo + rows
    key_gain = gains_ref[1:2]
    cos_gain = cos_ref[:halo] * key_gain
    sin_gain = sin_ref[:halo] * turned_gain(key_gain)
    matrix = turning()

    def scores_of(head):
        cols = slice(head * HEAD, (head + 1) * HEAD)
        raw = jnp.concatenate([far_ref[:, cols], near_ref[:, cols]], 0)
        x = raw.astype(F32)
        scale = row_scale(x)
        scaled = x * scale
        turned = turned_rows(raw, matrix) * scale
        part = slice(head * halo, (head + 1) * halo)
        halo_scaled_ref[part, :] = scaled
        rotated = scaled * cos_gain + turned * sin_gain
        halo_across_ref[cols, :] = rotated.T.astype(BF16)
        both = jnp.concatenate(
            [rotated.astype(BF16), key_rot_ref[head * rows : (head + 1) * rows, :]], 0
        )
        queries = query_rot_ref[head * group * rows : (head + 1) * group * rows, :]
        return lax.dot_general(
            both, queries, (((1,), (1,)), ((), ())), preferred_element_type=F32
        )

    later = scores_of(0)
    for head in range(heads):
        scores = later
        if head + 1 < heads:
            later = scores_of(head + 1)
        cols = slice(head * HEAD, (head + 1) * HEAD)
        low = []
        for one in range(group):
            place = (slice(head * keys, (head + 1) * keys), slice(one * rows, (one + 1) * rows))
            part = scores[:, place[1]] * (SCALE * math.log2(math.e)) + bias_ref[...]
            exps = jnp.exp2(part - jnp.max(part, axis=0, keepdims=True))
            exps_ref[place] = exps
            inverse = 1.0 / jnp.sum(exps, axis=0, keepdims=True)
            inverse_ref[head : head + 1, place[1]] = inverse
            low.append((exps_ref[place] * inverse).astype(BF16))
        value_term = jnp.dot(
            jnp.concatenate(low, 1), stacked(out_grad_ref, head, group), preferred_element_type=F32
        )
        far_value_ref[:, cols] = value_term[:rows].astype(BF16)
        near_value_ref[:, cols] = value_term[rows:halo].astype(BF16)
        own_value_ref[:, cols] = value_term[halo:]


def norm_backward(grad_rot, grad_turned, scaled, scale, gain, cos, sin):
    normed_grad = grad_rot * cos - grad_turned * sin
    part = normed_grad * scaled
    mean = row_sums(part * gain) * (1.0 / HEAD)
    return scale * (normed_grad * gain - scaled * mean), part


def attend_values_kernel(
    far_ref, near_ref, value_ref, out_grad_ref, exps_ref, inverse_ref, query_rot_ref,
    halo_across_ref, key_across_ref, halo_scaled_ref, key_scaled_ref,
    query_scaled_ref, cos_ref, sin_ref, across_ref,
    far_key_ref, near_key_ref, own_key_ref, gain_ref, query_grad_hbm,
    query_grad_ref, sems,
):
    rows = far_ref.shape[0]
    heads = far_ref.shape[1] // HEAD
    group = out_grad_ref.shape[1] // far_ref.shape[1]
    halo = WINDOW
    keys = halo + rows
    cos_across, sin_across = across_ref[0] * SCALE, across_ref[1] * SCALE
    query_acc = jnp.zeros((HEAD, rows), F32)
    saves = []
    key_acc = jnp.zeros((keys, HEAD), F32)
    key_acc_turned = jnp.zeros((keys, HEAD), F32)

    def prob_grad_of(head):
        cols = slice(head * HEAD, (head + 1) * HEAD)
        values = jnp.concatenate([far_ref[:, cols], near_ref[:, cols], value_ref[:, cols]], 0)
        return lax.dot_general(
            values, stacked(out_grad_ref, head, group), (((1,), (1,)), ((), ())),
            preferred_element_type=F32,
        )

    later = prob_grad_of(0)
    for head in range(heads):
        prob_grad = later
        if head + 1 < heads:
            later = prob_grad_of(head + 1)
        cols = slice(head * HEAD, (head + 1) * HEAD)
        halo_part = slice(head * halo, (head + 1) * halo)
        own_part = slice(head * rows, (head + 1) * rows)
        group_part = slice(head * group * rows, (head + 1) * group * rows)
        score_grads = []
        for one in range(group):
            place = (slice(head * keys, (head + 1) * keys), slice(one * rows, (one + 1) * rows))
            part = prob_grad[:, place[1]]
            inverse = inverse_ref[head : head + 1, place[1]]
            delta = jnp.sum(exps_ref[place] * part, axis=0, keepdims=True) * inverse
            score_grads.append((exps_ref[place] * inverse * (part - delta)).astype(BF16))
        score_grad = jnp.concatenate(score_grads, 1)
        key_term = (
            jnp.dot(score_grad, query_rot_ref[group_part, :], preferred_element_type=F32) * SCALE
        )
        keys_across = jnp.concatenate([halo_across_ref[cols, :], key_across_ref[cols, :]], 1)
        query_term = jnp.dot(keys_across, score_grad, preferred_element_type=F32)
        halo_key = key_term[:halo].astype(BF16)
        far_key_ref[:, cols] = halo_key[:rows]
        near_key_ref[:, cols] = halo_key[rows:]
        own_key_ref[:, cols] = key_term[halo:]
        term = jnp.concatenate([halo_key.astype(F32), key_term[halo:]], 0)
        scaled = jnp.concatenate([halo_scaled_ref[halo_part, :], key_scaled_ref[own_part, :]], 0)
        key_acc = key_acc + term * scaled
        key_acc_turned = key_acc_turned + term * roll_half(scaled)
        for one in range(group):
            index = head * group + one
            across = slice(index * HEAD, (index + 1) * HEAD)
            grad = query_term[:, one * rows : (one + 1) * rows]
            turned = jnp.concatenate([grad[HALF:], grad[:HALF]], 0)
            normed_grad = grad * cos_across - turned * sin_across
            query_grad_ref[across, :] = normed_grad
            query_acc = query_acc + normed_grad * query_scaled_ref[across, :]
        both = slice(head * group * HEAD, (head + 1) * group * HEAD)
        saves.append(
            pltpu.make_async_copy(
                query_grad_ref.at[both], query_grad_hbm.at[both], sems.at[head]
            )
        )
        saves[-1].start()
    query_sum = jnp.sum(query_acc.T, axis=0, keepdims=True)
    key_sum = jnp.sum(key_acc * cos_ref[...], axis=0, keepdims=True)
    turned_sum = jnp.sum(key_acc_turned * sin_ref[...], axis=0, keepdims=True)
    gain_ref[...] = jnp.concatenate([query_sum, key_sum + turned_gain(turned_sum)], 0)
    for save in saves:
        save.wait()


def finish_queries_kernel(
    query_grad_hbm, query_scaled_hbm, query_scale_ref, gain_across_ref,
    out_ref,
    query_grad_ref, query_scaled_ref, sems,
):
    heads = out_ref.shape[1] // HEAD
    pieces = [slice(head * HEAD, (head + 1) * HEAD) for head in range(heads)]
    loads = []
    for head, across in enumerate(pieces):
        for place, (source, target) in enumerate(
            ((query_grad_hbm, query_grad_ref), (query_scaled_hbm, query_scaled_ref))
        ):
            loads.append(
                pltpu.make_async_copy(source.at[across], target.at[across], sems.at[2 * head + place])
            )
            loads[-1].start()
    gain = gain_across_ref[...]
    for head, across in enumerate(pieces):
        loads[2 * head].wait()
        loads[2 * head + 1].wait()
        scaled = query_scaled_ref[across, :]
        weighted = query_grad_ref[across, :] * gain
        mean = jnp.sum(weighted * scaled, axis=0, keepdims=True) * (1.0 / HEAD)
        grad = query_scale_ref[head : head + 1, :] * (weighted - scaled * mean)
        out_ref[:, across] = grad.T.astype(BF16)


def finish_values_kernel(own_ref, near_ref, far_ref, gain_ref, grad_value_ref, copies_ref):
    total = own_ref[...] + near_ref[...].astype(F32) + far_ref[...].astype(F32)
    grad_value_ref[...] = total.astype(BF16)
    copies_ref[...] = jnp.broadcast_to(gain_ref[...][None], copies_ref.shape)


def finish_keys_kernel(
    own_ref, near_ref, far_ref, key_scaled_ref, key_scale_ref, cos_ref, sin_ref, gains_ref, parts_ref,
    grad_key_ref, query_gain_ref, key_gain_ref,
):
    rows = own_ref.shape[0]
    cos, sin = cos_ref[WINDOW:], sin_ref[WINDOW:]
    gain = gains_ref[1:2]
    for head in range(own_ref.shape[1] // HEAD):
        cols = slice(head * HEAD, (head + 1) * HEAD)
        part = slice(head * rows, (head + 1) * rows)
        total = own_ref[:, cols] + near_ref[:, cols].astype(F32) + far_ref[:, cols].astype(F32)
        grad, _ = norm_backward(
            total, roll_half(total), key_scaled_ref[part, :], key_scale_ref[part, :], gain, cos, sin
        )
        grad_key_ref[:, cols] = grad.astype(BF16)
    sums = jnp.sum(parts_ref[...], axis=0)
    query_gain_ref[...] = sums[:1]
    key_gain_ref[...] = sums[1:]


def call(kernel, name, outs, operands, cost=None, far=0, far_outs=0, scratch=()):
    spaces = [pltpu.HBM] * far + [pltpu.VMEM] * (len(operands) - far)
    out_spaces = [pltpu.VMEM] * (len(outs) - far_outs) + [pltpu.HBM] * far_outs
    return pl.pallas_call(
        kernel,
        out_shape=outs,
        in_specs=[pl.BlockSpec(memory_space=space) for space in spaces],
        out_specs=[pl.BlockSpec(memory_space=space) for space in out_spaces],
        scratch_shapes=scratch,
        compiler_params=pltpu.CompilerParams(vmem_limit_bytes=VMEM_LIMIT),
        cost_estimate=cost,
        name=name,
    )(*[pltpu.with_memory_space_constraint(x, pltpu.HBM) for x in operands[:far]], *operands[far:])


def cost(flops, size, exps=0):
    return pl.CostEstimate(flops=flops, bytes_accessed=size, transcendentals=exps)


def shape(dims, dtype):
    return jax.ShapeDtypeStruct(dims, dtype)


def on_device(doc_lengths, query_raw, key_raw, value_matrix, out_grad, query_gain, key_gain):
    rows, query_width = query_raw.shape
    width = key_raw.shape[1]
    heads = width // HEAD
    query_heads = query_width // HEAD
    keys = WINDOW + rows
    devices = lax.axis_size(AXES)
    query_gain = query_gain.reshape(1, HEAD)
    key_gain = key_gain.reshape(1, HEAD)
    near_key, far_key = shift(key_raw, 1), shift(key_raw, 2)
    term = shape((rows, width), BF16)
    own = shape((rows, width), F32)
    (
        query_rot, query_scaled, query_scale, key_rot, key_across, key_scaled, key_scale,
        cos, sin, across, gain_across, bias, values, grads_out, gains, query_scaled_far,
    ) = call(
        prepare_kernel,
        "prepare",
        [
            shape((query_heads * rows, HEAD), BF16),
            shape((query_width, rows), F32),
            shape((query_heads, rows), F32),
            shape((heads * rows, HEAD), BF16),
            shape((width, rows), BF16),
            shape((heads * rows, HEAD), F32),
            shape((heads * rows, HEAD), F32),
            shape((keys, HEAD), F32),
            shape((keys, HEAD), F32),
            shape((2, HEAD, rows), F32),
            shape((HEAD, rows), F32),
            shape((keys, rows), F32),
            term,
            shape((rows, query_width), BF16),
            shape((8, HEAD), F32),
            shape((query_width, rows), F32),
        ],
        (doc_lengths, query_raw, key_raw, value_matrix, out_grad, query_gain, key_gain),
        cost(4_000_000, 6_000_000),
        far=7,
        far_outs=1,
        scratch=[
            pltpu.SMEM(doc_lengths.shape, jnp.int32),
            pltpu.VMEM((rows, query_width), BF16),
            pltpu.VMEM((rows, width), BF16),
            pltpu.SemaphoreType.DMA((7,)),
            pltpu.SemaphoreType.DMA((query_heads,)),
        ],
    )
    near_value, far_value = shift(values, 1), shift(values, 2)
    exps, inverse, halo_across, halo_scaled, far_value_term, near_value_term, own_value = call(
        attend_keys_kernel,
        "attend_keys",
        [
            shape((heads * keys, query_heads // heads * rows), F32),
            shape((heads, query_heads // heads * rows), F32),
            shape((width, WINDOW), BF16),
            shape((heads * WINDOW, HEAD), F32),
            term,
            term,
            own,
        ],
        (far_key, near_key, grads_out, query_rot, key_rot, cos, sin, bias, gains),
        cost(400_000_000, 4_000_000, 800_000),
    )
    near_value_back, far_value_back = shift(near_value_term, -1), shift(far_value_term, -2)
    far_key_term, near_key_term, own_key, gain_part, query_grad = call(
        attend_values_kernel,
        "attend_values",
        [term, term, own, shape((2, HEAD), F32), shape((query_width, rows), F32)],
        (
            far_value, near_value, values, grads_out, exps, inverse, query_rot,
            halo_across, key_across, halo_scaled, key_scaled, query_scaled, cos, sin, across,
        ),
        cost(600_000_000, 4_000_000),
        far_outs=1,
        scratch=[pltpu.VMEM((query_width, rows), F32), pltpu.SemaphoreType.DMA((heads,))],
    )
    near_key_back, far_key_back = shift(near_key_term, -1), shift(far_key_term, -2)
    grad_value, copies = call(
        finish_values_kernel,
        "finish_values",
        [term, shape((devices, 2, HEAD), F32)],
        (own_value, near_value_back, far_value_back, gain_part),
        cost(1_000_000, 2_000_000),
    )
    parts = lax.all_to_all(copies, AXES, 0, 0)
    (grad_query,) = call(
        finish_queries_kernel,
        "finish_queries",
        [shape((rows, query_width), BF16)],
        (query_grad, query_scaled_far, query_scale, gain_across),
        cost(4_000_000, 4_000_000),
        far=2,
        scratch=[
            pltpu.VMEM((query_width, rows), F32),
            pltpu.VMEM((query_width, rows), F32),
            pltpu.SemaphoreType.DMA((2 * query_heads,)),
        ],
    )
    grad_key, grad_query_gain, grad_key_gain = call(
        finish_keys_kernel,
        "finish_keys",
        [term, shape((1, HEAD), F32), shape((1, HEAD), F32)],
        (own_key, near_key_back, far_key_back, key_scaled, key_scale, cos, sin, gains, parts),
        cost(4_000_000, 3_000_000),
    )
    return (
        grad_query, grad_key, grad_value, grad_query_gain.reshape(HEAD), grad_key_gain.reshape(HEAD)
    )


def solution(mesh):
    rows = P(AXES, None)
    return jax.shard_map(
        on_device,
        mesh=mesh,
        in_specs=(P(), rows, rows, rows, rows, P(), P()),
        out_specs=(rows, rows, rows, P(), P()),
        check_vma=False,
    )
```

```python
import math

import jax
import jax.numpy as jnp
import numpy as np
from jax import lax
from jax.experimental import pallas as pl
from jax.experimental.pallas import tpu as pltpu
from jax.sharding import PartitionSpec as P

HEAD = 128
HALF = HEAD // 2
WINDOW = 256
EPS = 1e-06
SCALE = 168.0 ** (-0.5)
ROPE_BASE = 10000.0
MASKED = -1e30
AXES = ("ctx", "grp")
F32 = jnp.float32
BF16 = jnp.bfloat16
VMEM_LIMIT = 32 * 1024 * 1024


def frequencies():
    lane = lax.broadcasted_iota(jnp.int32, (1, HEAD), 1) % HALF
    values = jnp.zeros((1, HEAD), F32)
    for m in range(HALF):
        values = jnp.where(lane == m, np.float32(ROPE_BASE ** (-2.0 * m / HEAD)), values)
    return values


def shift(value, steps):
    count = lax.axis_size(AXES)
    return lax.ppermute(value, AXES, [(s, (s + steps) % count) for s in range(count)])


def own_index():
    return lax.axis_index("ctx") * lax.axis_size("grp") + lax.axis_index("grp")


def roll_half(x):
    return pltpu.roll(x, HALF, 1)


def doc_starts(tokens, lengths_ref):
    def step(doc, carry):
        end, starts = carry
        end = end + lengths_ref[doc]
        return end, jnp.where(tokens >= end, end, starts)

    count = lengths_ref.shape[0]
    return lax.fori_loop(
        0, count, step, (jnp.int32(0), jnp.zeros_like(tokens)), unroll=count if count <= 8 else 1
    )[1]


def cos_sin_lanes(angle, lane):
    turns = jnp.floor(angle * (2.0 / math.pi) + 0.5)
    r = angle - turns * 1.5703125
    r = r - turns * 4.837512969970703125e-4
    r = r - turns * 7.549789948768648e-8
    z = r * r
    sin_r = r + r * z * (-1.6666654611e-1 + z * (8.3321608736e-3 + z * -1.9515295891e-4))
    cos_r = 1.0 - 0.5 * z + z * z * (
        4.166664568298827e-2 + z * (-1.388731625493765e-3 + z * 2.443315711809948e-5)
    )
    quadrant = turns.astype(jnp.int32) - jnp.where(lane >= HALF, 1, 0)
    odd = (quadrant & 1) == 1
    value = jnp.where(odd, sin_r, cos_r)
    negative = ((quadrant + 1) & 2) == 2
    return jnp.where(negative, -value, value)


def ones(rows, columns):
    return jnp.ones((rows, columns), BF16)


def split(x):
    high = x.astype(BF16)
    low = (x - high.astype(F32)).astype(BF16)
    return jnp.concatenate([high, low], 1)


def row_sums(x):
    return jnp.dot(split(x), ones(2 * HEAD, HEAD), preferred_element_type=F32)


def scale_of(sums):
    return lax.rsqrt(sums * (1.0 / HEAD) + EPS)


def row_scale(x):
    return scale_of(row_sums(x * x))


def turning():
    source = lax.broadcasted_iota(jnp.int32, (HEAD, HEAD), 0)
    target = lax.broadcasted_iota(jnp.int32, (HEAD, HEAD), 1)
    return jnp.where(target == (source + HALF) % HEAD, 1.0, 0.0).astype(BF16)


def turned_rows(raw, matrix):
    return jnp.dot(raw, matrix, preferred_element_type=F32)


def turned_gain(gain):
    return roll_half(jnp.broadcast_to(gain, (8, HEAD)))[:1]


def prepare_kernel(
    lengths_hbm, query_hbm, key_hbm, value_hbm, out_grad_hbm, query_gain_hbm, key_gain_hbm,
    query_rot_ref, query_scaled_ref, query_scale_ref, key_rot_ref, key_across_ref,
    key_scaled_ref, key_scale_ref, cos_ref, sin_ref, across_ref, bias_ref,
    value_ref, out_grad_ref, gains_ref,
    lengths_ref, query_ref, key_ref, sems,
):
    moves = [
        pltpu.make_async_copy(source, target, sems.at[place])
        for place, (source, target) in enumerate(
            (
                (lengths_hbm, lengths_ref),
                (query_gain_hbm, gains_ref.at[0:1]),
                (key_gain_hbm, gains_ref.at[1:2]),
                (key_hbm, key_ref),
                (query_hbm, query_ref),
                (out_grad_hbm, out_grad_ref),
                (value_hbm, value_ref),
            )
        )
    ]
    for move in moves:
        move.start()
    rows = query_ref.shape[0]
    keys = cos_ref.shape[0]
    base = own_index() * rows - (keys - rows)
    shape = (keys, HEAD)
    lane = lax.broadcasted_iota(jnp.int32, shape, 1)
    tokens = base + lax.broadcasted_iota(jnp.int32, shape, 0)
    frequency = frequencies()
    moves[0].wait()
    positions = tokens - doc_starts(tokens, lengths_ref)
    mixed = cos_sin_lanes(positions.astype(F32) * frequency, lane)
    turned = roll_half(mixed)
    cos = jnp.where(lane < HALF, mixed, turned)
    sin = jnp.where(lane < HALF, -turned, mixed)
    cos_ref[...] = cos
    sin_ref[...] = sin
    queries = base + (keys - rows) + lax.broadcasted_iota(jnp.int32, (1, rows), 1)
    lowest = jnp.maximum(doc_starts(queries, lengths_ref), queries - (WINDOW - 1))
    key_tokens = base + lax.broadcasted_iota(jnp.int32, (keys, rows), 0)
    visible = (key_tokens >= lowest) & (key_tokens <= queries)
    bias_ref[...] = jnp.where(visible, 0.0, MASKED)
    own_cos, own_sin = cos[keys - rows :], sin[keys - rows :]
    moves[1].wait()
    moves[2].wait()
    across_ref[0] = own_cos.T
    across_ref[1] = own_sin.T
    across_ref[2] = jnp.broadcast_to(gains_ref[0:1], (HEAD, HEAD)).T
    matrix = turning()
    for raw_ref, move, row, rot_ref in (
        (key_ref, moves[3], 1, key_rot_ref),
        (query_ref, moves[4], 0, query_rot_ref),
    ):
        gain = gains_ref[row : row + 1]
        cos_gain = own_cos * gain
        sin_gain = own_sin * turned_gain(gain)
        move.wait()
        for head in range(raw_ref.shape[1] // HEAD):
            part = slice(head * rows, (head + 1) * rows)
            across = slice(head * HEAD, (head + 1) * HEAD)
            raw = raw_ref[:, across]
            x = raw.astype(F32)
            parts = split(x * x)
            scale = scale_of(jnp.dot(parts, ones(2 * HEAD, HEAD), preferred_element_type=F32))
            scaled = x * scale
            turned = turned_rows(raw, matrix) * scale
            rotated = scaled * cos_gain + turned * sin_gain
            rot_ref[part, :] = rotated.astype(BF16)
            if raw_ref is key_ref:
                key_scale_ref[part, :] = scale
                key_scaled_ref[part, :] = scaled
                key_across_ref[across, :] = rotated.T.astype(BF16)
            else:
                query_scaled_ref[across, :] = scaled.T
                sums = lax.dot_general(
                    ones(8, 2 * HEAD), parts, (((1,), (1,)), ((), ())), preferred_element_type=F32
                )
                query_scale_ref[head : head + 1, :] = scale_of(sums[:1])
    moves[5].wait()
    moves[6].wait()


def stacked(ref, head, group):
    return jnp.concatenate(
        [ref[:, (head * group + one) * HEAD : (head * group + one + 1) * HEAD] for one in range(group)],
        0,
    )


def attend_keys_kernel(
    far_ref, near_ref, out_grad_ref, query_rot_ref, key_rot_ref, cos_ref, sin_ref, bias_ref,
    gains_ref,
    exps_ref, inverse_ref, halo_across_ref, halo_scaled_ref, far_value_ref, near_value_ref, own_value_ref,
):
    rows = far_ref.shape[0]
    heads = far_ref.shape[1] // HEAD
    group = out_grad_ref.shape[1] // far_ref.shape[1]
    halo = WINDOW
    keys = halo + rows
    key_gain = gains_ref[1:2]
    cos_gain = cos_ref[:halo] * key_gain
    sin_gain = sin_ref[:halo] * turned_gain(key_gain)
    matrix = turning()

    def scores_of(head):
        cols = slice(head * HEAD, (head + 1) * HEAD)
        raw = jnp.concatenate([far_ref[:, cols], near_ref[:, cols]], 0)
        x = raw.astype(F32)
        scale = row_scale(x)
        scaled = x * scale
        turned = turned_rows(raw, matrix) * scale
        part = slice(head * halo, (head + 1) * halo)
        halo_scaled_ref[part, :] = scaled
        rotated = scaled * cos_gain + turned * sin_gain
        halo_across_ref[cols, :] = rotated.T.astype(BF16)
        both = jnp.concatenate(
            [rotated.astype(BF16), key_rot_ref[head * rows : (head + 1) * rows, :]], 0
        )
        queries = query_rot_ref[head * group * rows : (head + 1) * group * rows, :]
        return lax.dot_general(
            both, queries, (((1,), (1,)), ((), ())), preferred_element_type=F32
        )

    later = scores_of(0)
    for head in range(heads):
        scores = later
        if head + 1 < heads:
            later = scores_of(head + 1)
        cols = slice(head * HEAD, (head + 1) * HEAD)
        low = []
        for one in range(group):
            place = (slice(head * keys, (head + 1) * keys), slice(one * rows, (one + 1) * rows))
            part = scores[:, place[1]] * (SCALE * math.log2(math.e)) + bias_ref[...]
            exps = jnp.exp2(part - jnp.max(part, axis=0, keepdims=True))
            exps_ref[place] = exps
            inverse = 1.0 / jnp.sum(exps, axis=0, keepdims=True)
            inverse_ref[head : head + 1, place[1]] = inverse
            low.append((exps_ref[place] * inverse).astype(BF16))
        value_term = jnp.dot(
            jnp.concatenate(low, 1), stacked(out_grad_ref, head, group), preferred_element_type=F32
        )
        far_value_ref[:, cols] = value_term[:rows].astype(BF16)
        near_value_ref[:, cols] = value_term[rows:halo].astype(BF16)
        own_value_ref[:, cols] = value_term[halo:]


def norm_backward(grad_rot, grad_turned, scaled, scale, gain, cos, sin):
    normed_grad = grad_rot * cos - grad_turned * sin
    part = normed_grad * scaled
    mean = row_sums(part * gain) * (1.0 / HEAD)
    return scale * (normed_grad * gain - scaled * mean), part


def attend_values_kernel(
    far_ref, near_ref, value_ref, out_grad_ref, exps_ref, inverse_ref, query_rot_ref,
    halo_across_ref, key_across_ref, halo_scaled_ref, key_scaled_ref,
    query_scaled_ref, query_scale_ref, cos_ref, sin_ref, across_ref,
    far_key_ref, near_key_ref, own_key_ref, grad_query_ref, gain_ref,
):
    rows = far_ref.shape[0]
    heads = far_ref.shape[1] // HEAD
    group = out_grad_ref.shape[1] // far_ref.shape[1]
    halo = WINDOW
    keys = halo + rows
    cos_across, sin_across = across_ref[0] * SCALE, across_ref[1] * SCALE
    query_gain = across_ref[2]
    query_acc = jnp.zeros((HEAD, rows), F32)
    key_acc = jnp.zeros((keys, HEAD), F32)
    key_acc_turned = jnp.zeros((keys, HEAD), F32)

    def prob_grad_of(head):
        cols = slice(head * HEAD, (head + 1) * HEAD)
        values = jnp.concatenate([far_ref[:, cols], near_ref[:, cols], value_ref[:, cols]], 0)
        return lax.dot_general(
            values, stacked(out_grad_ref, head, group), (((1,), (1,)), ((), ())),
            preferred_element_type=F32,
        )

    later = prob_grad_of(0)
    for head in range(heads):
        prob_grad = later
        if head + 1 < heads:
            later = prob_grad_of(head + 1)
        cols = slice(head * HEAD, (head + 1) * HEAD)
        halo_part = slice(head * halo, (head + 1) * halo)
        own_part = slice(head * rows, (head + 1) * rows)
        group_part = slice(head * group * rows, (head + 1) * group * rows)
        score_grads = []
        for one in range(group):
            place = (slice(head * keys, (head + 1) * keys), slice(one * rows, (one + 1) * rows))
            part = prob_grad[:, place[1]]
            inverse = inverse_ref[head : head + 1, place[1]]
            delta = jnp.sum(exps_ref[place] * part, axis=0, keepdims=True) * inverse
            score_grads.append((exps_ref[place] * inverse * (part - delta)).astype(BF16))
        score_grad = jnp.concatenate(score_grads, 1)
        key_term = (
            jnp.dot(score_grad, query_rot_ref[group_part, :], preferred_element_type=F32) * SCALE
        )
        keys_across = jnp.concatenate([halo_across_ref[cols, :], key_across_ref[cols, :]], 1)
        query_term = jnp.dot(keys_across, score_grad, preferred_element_type=F32)
        halo_key = key_term[:halo].astype(BF16)
        far_key_ref[:, cols] = halo_key[:rows]
        near_key_ref[:, cols] = halo_key[rows:]
        own_key_ref[:, cols] = key_term[halo:]
        term = jnp.concatenate([halo_key.astype(F32), key_term[halo:]], 0)
        scaled = jnp.concatenate([halo_scaled_ref[halo_part, :], key_scaled_ref[own_part, :]], 0)
        key_acc = key_acc + term * scaled
        key_acc_turned = key_acc_turned + term * roll_half(scaled)
        for one in range(group):
            index = head * group + one
            across = slice(index * HEAD, (index + 1) * HEAD)
            grad = query_term[:, one * rows : (one + 1) * rows]
            turned = jnp.concatenate([grad[HALF:], grad[:HALF]], 0)
            normed_grad = grad * cos_across - turned * sin_across
            scaled = query_scaled_ref[across, :]
            query_acc = query_acc + normed_grad * scaled
            weighted = normed_grad * query_gain
            mean = jnp.sum(weighted * scaled, axis=0, keepdims=True) * (1.0 / HEAD)
            raw_grad = query_scale_ref[index : index + 1, :] * (weighted - scaled * mean)
            grad_query_ref[:, across] = raw_grad.T.astype(BF16)
    query_sum = jnp.sum(query_acc.T, axis=0, keepdims=True)
    key_sum = jnp.sum(key_acc * cos_ref[...], axis=0, keepdims=True)
    turned_sum = jnp.sum(key_acc_turned * sin_ref[...], axis=0, keepdims=True)
    gain_ref[...] = jnp.concatenate([query_sum, key_sum + turned_gain(turned_sum)], 0)


def finish_values_kernel(own_ref, near_ref, far_ref, gain_ref, grad_value_ref, copies_ref):
    total = own_ref[...] + near_ref[...].astype(F32) + far_ref[...].astype(F32)
    grad_value_ref[...] = total.astype(BF16)
    copies_ref[...] = jnp.broadcast_to(gain_ref[...][None], copies_ref.shape)


def finish_keys_kernel(
    own_ref, near_ref, far_ref, key_scaled_ref, key_scale_ref, cos_ref, sin_ref, gains_ref, parts_ref,
    grad_key_ref, query_gain_ref, key_gain_ref,
):
    rows = own_ref.shape[0]
    cos, sin = cos_ref[WINDOW:], sin_ref[WINDOW:]
    gain = gains_ref[1:2]
    for head in range(own_ref.shape[1] // HEAD):
        cols = slice(head * HEAD, (head + 1) * HEAD)
        part = slice(head * rows, (head + 1) * rows)
        total = own_ref[:, cols] + near_ref[:, cols].astype(F32) + far_ref[:, cols].astype(F32)
        grad, _ = norm_backward(
            total, roll_half(total), key_scaled_ref[part, :], key_scale_ref[part, :], gain, cos, sin
        )
        grad_key_ref[:, cols] = grad.astype(BF16)
    sums = jnp.sum(parts_ref[...], axis=0)
    query_gain_ref[...] = sums[:1]
    key_gain_ref[...] = sums[1:]


def call(kernel, name, outs, operands, cost=None, space=pltpu.VMEM, scratch=()):
    return pl.pallas_call(
        kernel,
        out_shape=outs,
        in_specs=[pl.BlockSpec(memory_space=space)] * len(operands),
        out_specs=[pl.BlockSpec(memory_space=pltpu.VMEM)] * len(outs),
        scratch_shapes=scratch,
        compiler_params=pltpu.CompilerParams(vmem_limit_bytes=VMEM_LIMIT),
        cost_estimate=cost,
        name=name,
    )(*operands)


def cost(flops, size, exps=0):
    return pl.CostEstimate(flops=flops, bytes_accessed=size, transcendentals=exps)


def shape(dims, dtype):
    return jax.ShapeDtypeStruct(dims, dtype)


def on_device(doc_lengths, query_raw, key_raw, value_matrix, out_grad, query_gain, key_gain):
    rows, query_width = query_raw.shape
    width = key_raw.shape[1]
    heads = width // HEAD
    query_heads = query_width // HEAD
    keys = WINDOW + rows
    devices = lax.axis_size(AXES)
    query_gain = query_gain.reshape(1, HEAD)
    key_gain = key_gain.reshape(1, HEAD)
    near_key, far_key = shift(key_raw, 1), shift(key_raw, 2)
    term = shape((rows, width), BF16)
    own = shape((rows, width), F32)
    (
        query_rot, query_scaled, query_scale, key_rot, key_across, key_scaled, key_scale,
        cos, sin, across, bias, values, grads_out, gains,
    ) = call(
        prepare_kernel,
        "prepare",
        [
            shape((query_heads * rows, HEAD), BF16),
            shape((query_width, rows), F32),
            shape((query_heads, rows), F32),
            shape((heads * rows, HEAD), BF16),
            shape((width, rows), BF16),
            shape((heads * rows, HEAD), F32),
            shape((heads * rows, HEAD), F32),
            shape((keys, HEAD), F32),
            shape((keys, HEAD), F32),
            shape((3, HEAD, rows), F32),
            shape((keys, rows), F32),
            term,
            shape((rows, query_width), BF16),
            shape((8, HEAD), F32),
        ],
        [
            pltpu.with_memory_space_constraint(x, pltpu.HBM)
            for x in (doc_lengths, query_raw, key_raw, value_matrix, out_grad, query_gain, key_gain)
        ],
        cost(4_000_000, 6_000_000),
        space=pltpu.HBM,
        scratch=[
            pltpu.SMEM(doc_lengths.shape, jnp.int32),
            pltpu.VMEM((rows, query_width), BF16),
            pltpu.VMEM((rows, width), BF16),
            pltpu.SemaphoreType.DMA((7,)),
        ],
    )
    near_value, far_value = shift(values, 1), shift(values, 2)
    exps, inverse, halo_across, halo_scaled, far_value_term, near_value_term, own_value = call(
        attend_keys_kernel,
        "attend_keys",
        [
            shape((heads * keys, query_heads // heads * rows), F32),
            shape((heads, query_heads // heads * rows), F32),
            shape((width, WINDOW), BF16),
            shape((heads * WINDOW, HEAD), F32),
            term,
            term,
            own,
        ],
        (far_key, near_key, grads_out, query_rot, key_rot, cos, sin, bias, gains),
        cost(400_000_000, 4_000_000, 800_000),
    )
    near_value_back, far_value_back = shift(near_value_term, -1), shift(far_value_term, -2)
    far_key_term, near_key_term, own_key, grad_query, gain_part = call(
        attend_values_kernel,
        "attend_values",
        [term, term, own, shape((rows, query_width), BF16), shape((2, HEAD), F32)],
        (
            far_value, near_value, values, grads_out, exps, inverse, query_rot,
            halo_across, key_across, halo_scaled, key_scaled, query_scaled, query_scale, cos, sin, across,
        ),
        cost(600_000_000, 4_000_000),
    )
    near_key_back, far_key_back = shift(near_key_term, -1), shift(far_key_term, -2)
    grad_value, copies = call(
        finish_values_kernel,
        "finish_values",
        [term, shape((devices, 2, HEAD), F32)],
        (own_value, near_value_back, far_value_back, gain_part),
        cost(1_000_000, 2_000_000),
    )
    parts = lax.all_to_all(copies, AXES, 0, 0)
    grad_key, grad_query_gain, grad_key_gain = call(
        finish_keys_kernel,
        "finish_keys",
        [term, shape((1, HEAD), F32), shape((1, HEAD), F32)],
        (own_key, near_key_back, far_key_back, key_scaled, key_scale, cos, sin, gains, parts),
        cost(4_000_000, 3_000_000),
    )
    return (
        grad_query, grad_key, grad_value, grad_query_gain.reshape(HEAD), grad_key_gain.reshape(HEAD)
    )


def solution(mesh):
    rows = P(AXES, None)
    return jax.shard_map(
        on_device,
        mesh=mesh,
        in_specs=(P(), rows, rows, rows, rows, P(), P()),
        out_specs=(rows, rows, rows, P(), P()),
        check_vma=False,
    )
```

```python
import math

import jax
import jax.numpy as jnp
import numpy as np
from jax import lax
from jax.experimental import pallas as pl
from jax.experimental.pallas import tpu as pltpu
from jax.sharding import PartitionSpec as P

HEAD = 128
HALF = HEAD // 2
WINDOW = 256
EPS = 1e-06
SCALE = 168.0 ** (-0.5)
ROPE_BASE = 10000.0
MASKED = -1e30
AXES = ("ctx", "grp")
F32 = jnp.float32
BF16 = jnp.bfloat16
VMEM_LIMIT = 32 * 1024 * 1024


def frequencies():
    lane = lax.broadcasted_iota(jnp.int32, (1, HEAD), 1) % HALF
    values = jnp.zeros((1, HEAD), F32)
    for m in range(HALF):
        values = jnp.where(lane == m, np.float32(ROPE_BASE ** (-2.0 * m / HEAD)), values)
    return values


def shift(value, steps, cyclic=True):
    count = lax.axis_size(AXES)
    pairs = [(s, (s + steps) % count) for s in range(count)]
    if not cyclic:
        pairs = [(s, t) for s, t in pairs if t - s == steps]
    return lax.ppermute(value, AXES, pairs)


def own_index():
    return lax.axis_index("ctx") * lax.axis_size("grp") + lax.axis_index("grp")


def roll_half(x):
    return pltpu.roll(x, HALF, 1)


def doc_starts(tokens, lengths_ref):
    def step(doc, carry):
        end, starts = carry
        end = end + lengths_ref[doc]
        return end, jnp.where(tokens >= end, end, starts)

    count = lengths_ref.shape[0]
    return lax.fori_loop(
        0, count, step, (jnp.int32(0), jnp.zeros_like(tokens)), unroll=count if count <= 8 else 1
    )[1]


def cos_sin_lanes(angle, lane):
    turns = jnp.floor(angle * (2.0 / math.pi) + 0.5)
    r = angle - turns * 1.5703125
    r = r - turns * 4.837512969970703125e-4
    r = r - turns * 7.549789948768648e-8
    z = r * r
    sin_r = r + r * z * (-1.6666654611e-1 + z * (8.3321608736e-3 + z * -1.9515295891e-4))
    cos_r = 1.0 - 0.5 * z + z * z * (
        4.166664568298827e-2 + z * (-1.388731625493765e-3 + z * 2.443315711809948e-5)
    )
    quadrant = turns.astype(jnp.int32) - jnp.where(lane >= HALF, 1, 0)
    odd = (quadrant & 1) == 1
    value = jnp.where(odd, sin_r, cos_r)
    negative = ((quadrant + 1) & 2) == 2
    return jnp.where(negative, -value, value)


def ones(rows, columns):
    return jnp.ones((rows, columns), BF16)


def split(x):
    high = x.astype(BF16)
    low = (x - high.astype(F32)).astype(BF16)
    return jnp.concatenate([high, low], 1)


def row_sums(x):
    return jnp.dot(split(x), ones(2 * HEAD, HEAD), preferred_element_type=F32)


def scale_of(sums):
    return lax.rsqrt(sums * (1.0 / HEAD) + EPS)


def row_scale(x):
    return scale_of(row_sums(x * x))


def turning():
    source = lax.broadcasted_iota(jnp.int32, (HEAD, HEAD), 0)
    target = lax.broadcasted_iota(jnp.int32, (HEAD, HEAD), 1)
    return jnp.where(target == (source + HALF) % HEAD, 1.0, 0.0).astype(BF16)


def turned_rows(raw, matrix):
    return jnp.dot(raw, matrix, preferred_element_type=F32)


def turned_gain(gain):
    return roll_half(jnp.broadcast_to(gain, (8, HEAD)))[:1]


def prepare_kernel(
    lengths_hbm, query_hbm, key_hbm, value_hbm, out_grad_hbm, query_gain_hbm, key_gain_hbm,
    query_rot_ref, query_scaled_ref, query_scale_ref, key_rot_ref, key_across_ref,
    key_scaled_ref, key_scale_ref, cos_ref, sin_ref, across_ref, bias_ref,
    value_ref, out_grad_ref, gains_ref,
    lengths_ref, query_ref, key_ref, sems,
):
    moves = [
        pltpu.make_async_copy(source, target, sems.at[place])
        for place, (source, target) in enumerate(
            (
                (lengths_hbm, lengths_ref),
                (query_gain_hbm, gains_ref.at[0:1]),
                (key_gain_hbm, gains_ref.at[1:2]),
                (key_hbm, key_ref),
                (query_hbm, query_ref),
                (out_grad_hbm, out_grad_ref),
                (value_hbm, value_ref),
            )
        )
    ]
    for move in moves:
        move.start()
    rows = query_ref.shape[0]
    keys = cos_ref.shape[0]
    base = own_index() * rows - (keys - rows)
    shape = (keys, HEAD)
    lane = lax.broadcasted_iota(jnp.int32, shape, 1)
    tokens = base + lax.broadcasted_iota(jnp.int32, shape, 0)
    frequency = frequencies()
    moves[0].wait()
    positions = tokens - doc_starts(tokens, lengths_ref)
    mixed = cos_sin_lanes(positions.astype(F32) * frequency, lane)
    turned = roll_half(mixed)
    cos = jnp.where(lane < HALF, mixed, turned)
    sin = jnp.where(lane < HALF, -turned, mixed)
    cos_ref[...] = cos
    sin_ref[...] = sin
    queries = base + (keys - rows) + lax.broadcasted_iota(jnp.int32, (1, rows), 1)
    lowest = jnp.maximum(doc_starts(queries, lengths_ref), queries - (WINDOW - 1))
    key_tokens = base + lax.broadcasted_iota(jnp.int32, (keys, rows), 0)
    visible = (key_tokens >= lowest) & (key_tokens <= queries)
    bias_ref[...] = jnp.where(visible, 0.0, MASKED)
    own_cos, own_sin = cos[keys - rows :], sin[keys - rows :]
    moves[1].wait()
    moves[2].wait()
    across_ref[0] = own_cos.T
    across_ref[1] = own_sin.T
    across_ref[2] = jnp.broadcast_to(gains_ref[0:1], (HEAD, HEAD)).T
    matrix = turning()
    for raw_ref, move, row, rot_ref in (
        (key_ref, moves[3], 1, key_rot_ref),
        (query_ref, moves[4], 0, query_rot_ref),
    ):
        gain = gains_ref[row : row + 1]
        cos_gain = own_cos * gain
        sin_gain = own_sin * turned_gain(gain)
        move.wait()
        for head in range(raw_ref.shape[1] // HEAD):
            part = slice(head * rows, (head + 1) * rows)
            across = slice(head * HEAD, (head + 1) * HEAD)
            raw = raw_ref[:, across]
            x = raw.astype(F32)
            parts = split(x * x)
            scale = scale_of(jnp.dot(parts, ones(2 * HEAD, HEAD), preferred_element_type=F32))
            scaled = x * scale
            turned = turned_rows(raw, matrix) * scale
            rotated = scaled * cos_gain + turned * sin_gain
            rot_ref[part, :] = rotated.astype(BF16)
            if raw_ref is key_ref:
                key_scale_ref[part, :] = scale
                key_scaled_ref[part, :] = scaled
                key_across_ref[across, :] = rotated.T.astype(BF16)
            else:
                query_scaled_ref[across, :] = scaled.T
                sums = lax.dot_general(
                    ones(8, 2 * HEAD), parts, (((1,), (1,)), ((), ())), preferred_element_type=F32
                )
                query_scale_ref[head : head + 1, :] = scale_of(sums[:1])
    moves[5].wait()
    moves[6].wait()


def stacked(ref, head, group):
    return jnp.concatenate(
        [ref[:, (head * group + one) * HEAD : (head * group + one + 1) * HEAD] for one in range(group)],
        0,
    )


def attend_keys_kernel(
    far_ref, near_ref, out_grad_ref, query_rot_ref, key_rot_ref, cos_ref, sin_ref, bias_ref,
    gains_ref,
    exps_ref, inverse_ref, halo_across_ref, halo_scaled_ref, far_value_ref, near_value_ref, own_value_ref,
):
    rows = far_ref.shape[0]
    heads = far_ref.shape[1] // HEAD
    group = out_grad_ref.shape[1] // far_ref.shape[1]
    halo = WINDOW
    keys = halo + rows
    key_gain = gains_ref[1:2]
    cos_gain = cos_ref[:halo] * key_gain
    sin_gain = sin_ref[:halo] * turned_gain(key_gain)
    matrix = turning()

    def scores_of(head):
        cols = slice(head * HEAD, (head + 1) * HEAD)
        raw = jnp.concatenate([far_ref[:, cols], near_ref[:, cols]], 0)
        x = raw.astype(F32)
        scale = row_scale(x)
        scaled = x * scale
        turned = turned_rows(raw, matrix) * scale
        part = slice(head * halo, (head + 1) * halo)
        halo_scaled_ref[part, :] = scaled
        rotated = scaled * cos_gain + turned * sin_gain
        halo_across_ref[cols, :] = rotated.T.astype(BF16)
        both = jnp.concatenate(
            [rotated.astype(BF16), key_rot_ref[head * rows : (head + 1) * rows, :]], 0
        )
        queries = query_rot_ref[head * group * rows : (head + 1) * group * rows, :]
        return lax.dot_general(
            both, queries, (((1,), (1,)), ((), ())), preferred_element_type=F32
        )

    later = scores_of(0)
    for head in range(heads):
        scores = later
        if head + 1 < heads:
            later = scores_of(head + 1)
        cols = slice(head * HEAD, (head + 1) * HEAD)
        low = []
        for one in range(group):
            place = (slice(head * keys, (head + 1) * keys), slice(one * rows, (one + 1) * rows))
            part = scores[:, place[1]] * (SCALE * math.log2(math.e)) + bias_ref[...]
            exps = jnp.exp2(part - jnp.max(part, axis=0, keepdims=True))
            exps_ref[place] = exps
            inverse = 1.0 / jnp.sum(exps, axis=0, keepdims=True)
            inverse_ref[head : head + 1, place[1]] = inverse
            low.append((exps_ref[place] * inverse).astype(BF16))
        value_term = jnp.dot(
            jnp.concatenate(low, 1), stacked(out_grad_ref, head, group), preferred_element_type=F32
        )
        far_value_ref[:, cols] = value_term[:rows].astype(BF16)
        near_value_ref[:, cols] = value_term[rows:halo].astype(BF16)
        own_value_ref[:, cols] = value_term[halo:]


def norm_backward(grad_rot, grad_turned, scaled, scale, gain, cos, sin):
    normed_grad = grad_rot * cos - grad_turned * sin
    part = normed_grad * scaled
    mean = row_sums(part * gain) * (1.0 / HEAD)
    return scale * (normed_grad * gain - scaled * mean), part


def attend_values_kernel(
    far_ref, near_ref, value_ref, out_grad_ref, exps_ref, inverse_ref, query_rot_ref,
    halo_across_ref, key_across_ref, halo_scaled_ref, key_scaled_ref,
    query_scaled_ref, query_scale_ref, cos_ref, sin_ref, across_ref,
    far_key_ref, near_key_ref, own_key_ref, grad_query_ref, gain_ref,
):
    rows = far_ref.shape[0]
    heads = far_ref.shape[1] // HEAD
    group = out_grad_ref.shape[1] // far_ref.shape[1]
    halo = WINDOW
    keys = halo + rows
    cos_across, sin_across = across_ref[0] * SCALE, across_ref[1] * SCALE
    query_gain = across_ref[2]
    query_acc = jnp.zeros((HEAD, rows), F32)
    key_acc = jnp.zeros((keys, HEAD), F32)
    key_acc_turned = jnp.zeros((keys, HEAD), F32)

    def prob_grad_of(head):
        cols = slice(head * HEAD, (head + 1) * HEAD)
        values = jnp.concatenate([far_ref[:, cols], near_ref[:, cols], value_ref[:, cols]], 0)
        return lax.dot_general(
            values, stacked(out_grad_ref, head, group), (((1,), (1,)), ((), ())),
            preferred_element_type=F32,
        )

    later = prob_grad_of(0)
    for head in range(heads):
        prob_grad = later
        if head + 1 < heads:
            later = prob_grad_of(head + 1)
        cols = slice(head * HEAD, (head + 1) * HEAD)
        halo_part = slice(head * halo, (head + 1) * halo)
        own_part = slice(head * rows, (head + 1) * rows)
        group_part = slice(head * group * rows, (head + 1) * group * rows)
        score_grads = []
        for one in range(group):
            place = (slice(head * keys, (head + 1) * keys), slice(one * rows, (one + 1) * rows))
            part = prob_grad[:, place[1]]
            inverse = inverse_ref[head : head + 1, place[1]]
            delta = jnp.sum(exps_ref[place] * part, axis=0, keepdims=True) * inverse
            score_grads.append((exps_ref[place] * inverse * (part - delta)).astype(BF16))
        score_grad = jnp.concatenate(score_grads, 1)
        key_term = (
            jnp.dot(score_grad, query_rot_ref[group_part, :], preferred_element_type=F32) * SCALE
        )
        keys_across = jnp.concatenate([halo_across_ref[cols, :], key_across_ref[cols, :]], 1)
        query_term = jnp.dot(keys_across, score_grad, preferred_element_type=F32)
        halo_key = key_term[:halo].astype(BF16)
        far_key_ref[:, cols] = halo_key[:rows]
        near_key_ref[:, cols] = halo_key[rows:]
        own_key_ref[:, cols] = key_term[halo:]
        term = jnp.concatenate([halo_key.astype(F32), key_term[halo:]], 0)
        scaled = jnp.concatenate([halo_scaled_ref[halo_part, :], key_scaled_ref[own_part, :]], 0)
        key_acc = key_acc + term * scaled
        key_acc_turned = key_acc_turned + term * roll_half(scaled)
        for one in range(group):
            index = head * group + one
            across = slice(index * HEAD, (index + 1) * HEAD)
            grad = query_term[:, one * rows : (one + 1) * rows]
            turned = jnp.concatenate([grad[HALF:], grad[:HALF]], 0)
            normed_grad = grad * cos_across - turned * sin_across
            scaled = query_scaled_ref[across, :]
            query_acc = query_acc + normed_grad * scaled
            weighted = normed_grad * query_gain
            mean = jnp.sum(weighted * scaled, axis=0, keepdims=True) * (1.0 / HEAD)
            raw_grad = query_scale_ref[index : index + 1, :] * (weighted - scaled * mean)
            grad_query_ref[:, across] = raw_grad.T.astype(BF16)
    query_sum = jnp.sum(query_acc.T, axis=0, keepdims=True)
    key_sum = jnp.sum(key_acc * cos_ref[...], axis=0, keepdims=True)
    turned_sum = jnp.sum(key_acc_turned * sin_ref[...], axis=0, keepdims=True)
    gain_ref[...] = jnp.concatenate([query_sum, key_sum + turned_gain(turned_sum)], 0)


def finish_values_kernel(own_ref, near_ref, far_ref, gain_ref, grad_value_ref, copies_ref):
    total = own_ref[...] + near_ref[...].astype(F32) + far_ref[...].astype(F32)
    grad_value_ref[...] = total.astype(BF16)
    copies_ref[...] = jnp.broadcast_to(gain_ref[...][None], copies_ref.shape)


def finish_keys_kernel(
    own_ref, near_ref, far_ref, key_scaled_ref, key_scale_ref, cos_ref, sin_ref, gains_ref, parts_ref,
    grad_key_ref, query_gain_ref, key_gain_ref,
):
    rows = own_ref.shape[0]
    cos, sin = cos_ref[WINDOW:], sin_ref[WINDOW:]
    gain = gains_ref[1:2]
    for head in range(own_ref.shape[1] // HEAD):
        cols = slice(head * HEAD, (head + 1) * HEAD)
        part = slice(head * rows, (head + 1) * rows)
        total = own_ref[:, cols] + near_ref[:, cols].astype(F32) + far_ref[:, cols].astype(F32)
        grad, _ = norm_backward(
            total, roll_half(total), key_scaled_ref[part, :], key_scale_ref[part, :], gain, cos, sin
        )
        grad_key_ref[:, cols] = grad.astype(BF16)
    sums = jnp.sum(parts_ref[...], axis=0)
    query_gain_ref[...] = sums[:1]
    key_gain_ref[...] = sums[1:]


def call(kernel, name, outs, operands, cost=None, space=pltpu.VMEM, scratch=()):
    return pl.pallas_call(
        kernel,
        out_shape=outs,
        in_specs=[pl.BlockSpec(memory_space=space)] * len(operands),
        out_specs=[pl.BlockSpec(memory_space=pltpu.VMEM)] * len(outs),
        scratch_shapes=scratch,
        compiler_params=pltpu.CompilerParams(vmem_limit_bytes=VMEM_LIMIT),
        cost_estimate=cost,
        name=name,
    )(*operands)


def cost(flops, size, exps=0):
    return pl.CostEstimate(flops=flops, bytes_accessed=size, transcendentals=exps)


def shape(dims, dtype):
    return jax.ShapeDtypeStruct(dims, dtype)


def on_device(doc_lengths, query_raw, key_raw, value_matrix, out_grad, query_gain, key_gain):
    rows, query_width = query_raw.shape
    width = key_raw.shape[1]
    heads = width // HEAD
    query_heads = query_width // HEAD
    keys = WINDOW + rows
    devices = lax.axis_size(AXES)
    query_gain = query_gain.reshape(1, HEAD)
    key_gain = key_gain.reshape(1, HEAD)
    near_key, far_key = shift(key_raw, 1), shift(key_raw, 2, False)
    term = shape((rows, width), BF16)
    own = shape((rows, width), F32)
    (
        query_rot, query_scaled, query_scale, key_rot, key_across, key_scaled, key_scale,
        cos, sin, across, bias, values, grads_out, gains,
    ) = call(
        prepare_kernel,
        "prepare",
        [
            shape((query_heads * rows, HEAD), BF16),
            shape((query_width, rows), F32),
            shape((query_heads, rows), F32),
            shape((heads * rows, HEAD), BF16),
            shape((width, rows), BF16),
            shape((heads * rows, HEAD), F32),
            shape((heads * rows, HEAD), F32),
            shape((keys, HEAD), F32),
            shape((keys, HEAD), F32),
            shape((3, HEAD, rows), F32),
            shape((keys, rows), F32),
            term,
            shape((rows, query_width), BF16),
            shape((8, HEAD), F32),
        ],
        [
            pltpu.with_memory_space_constraint(x, pltpu.HBM)
            for x in (doc_lengths, query_raw, key_raw, value_matrix, out_grad, query_gain, key_gain)
        ],
        cost(4_000_000, 6_000_000),
        space=pltpu.HBM,
        scratch=[
            pltpu.SMEM(doc_lengths.shape, jnp.int32),
            pltpu.VMEM((rows, query_width), BF16),
            pltpu.VMEM((rows, width), BF16),
            pltpu.SemaphoreType.DMA((7,)),
        ],
    )
    near_value, far_value = shift(values, 1), shift(values, 2, False)
    exps, inverse, halo_across, halo_scaled, far_value_term, near_value_term, own_value = call(
        attend_keys_kernel,
        "attend_keys",
        [
            shape((heads * keys, query_heads // heads * rows), F32),
            shape((heads, query_heads // heads * rows), F32),
            shape((width, WINDOW), BF16),
            shape((heads * WINDOW, HEAD), F32),
            term,
            term,
            own,
        ],
        (far_key, near_key, grads_out, query_rot, key_rot, cos, sin, bias, gains),
        cost(400_000_000, 4_000_000, 800_000),
    )
    near_value_back, far_value_back = shift(near_value_term, -1), shift(far_value_term, -2, False)
    far_key_term, near_key_term, own_key, grad_query, gain_part = call(
        attend_values_kernel,
        "attend_values",
        [term, term, own, shape((rows, query_width), BF16), shape((2, HEAD), F32)],
        (
            far_value, near_value, values, grads_out, exps, inverse, query_rot,
            halo_across, key_across, halo_scaled, key_scaled, query_scaled, query_scale, cos, sin, across,
        ),
        cost(600_000_000, 4_000_000),
    )
    near_key_back, far_key_back = shift(near_key_term, -1), shift(far_key_term, -2, False)
    grad_value, copies = call(
        finish_values_kernel,
        "finish_values",
        [term, shape((devices, 2, HEAD), F32)],
        (own_value, near_value_back, far_value_back, gain_part),
        cost(1_000_000, 2_000_000),
    )
    parts = lax.all_to_all(copies, AXES, 0, 0)
    grad_key, grad_query_gain, grad_key_gain = call(
        finish_keys_kernel,
        "finish_keys",
        [term, shape((1, HEAD), F32), shape((1, HEAD), F32)],
        (own_key, near_key_back, far_key_back, key_scaled, key_scale, cos, sin, gains, parts),
        cost(4_000_000, 3_000_000),
    )
    return (
        grad_query, grad_key, grad_value, grad_query_gain.reshape(HEAD), grad_key_gain.reshape(HEAD)
    )


def solution(mesh):
    rows = P(AXES, None)
    return jax.shard_map(
        on_device,
        mesh=mesh,
        in_specs=(P(), rows, rows, rows, rows, P(), P()),
        out_specs=(rows, rows, rows, P(), P()),
        check_vma=False,
    )
```

```python
import math

import jax
import jax.numpy as jnp
import numpy as np
from jax import lax
from jax.experimental import pallas as pl
from jax.experimental.pallas import tpu as pltpu
from jax.sharding import PartitionSpec as P

HEAD = 128
HALF = HEAD // 2
WINDOW = 256
EPS = 1e-06
SCALE = 168.0 ** (-0.5)
ROPE_BASE = 10000.0
MASKED = -1e30
AXES = ("ctx", "grp")
F32 = jnp.float32
BF16 = jnp.bfloat16
VMEM_LIMIT = 32 * 1024 * 1024


def frequencies():
    lane = lax.broadcasted_iota(jnp.int32, (1, HEAD), 1) % HALF
    values = jnp.zeros((1, HEAD), F32)
    for m in range(HALF):
        values = jnp.where(lane == m, np.float32(ROPE_BASE ** (-2.0 * m / HEAD)), values)
    return values


def shift(value, steps):
    count = lax.axis_size(AXES)
    return lax.ppermute(value, AXES, [(s, (s + steps) % count) for s in range(count)])


def own_index():
    return lax.axis_index("ctx") * lax.axis_size("grp") + lax.axis_index("grp")


def roll_half(x):
    return pltpu.roll(x, HALF, 1)


def doc_starts(tokens, lengths_ref):
    def step(doc, carry):
        end, starts = carry
        end = end + lengths_ref[doc]
        return end, jnp.where(tokens >= end, end, starts)

    count = lengths_ref.shape[0]
    return lax.fori_loop(
        0, count, step, (jnp.int32(0), jnp.zeros_like(tokens)), unroll=count if count <= 8 else 1
    )[1]


def cos_sin_lanes(angle, lane):
    turns = jnp.floor(angle * (2.0 / math.pi) + 0.5)
    r = angle - turns * 1.5703125
    r = r - turns * 4.837512969970703125e-4
    r = r - turns * 7.549789948768648e-8
    z = r * r
    sin_r = r + r * z * (-1.6666654611e-1 + z * (8.3321608736e-3 + z * -1.9515295891e-4))
    cos_r = 1.0 - 0.5 * z + z * z * (
        4.166664568298827e-2 + z * (-1.388731625493765e-3 + z * 2.443315711809948e-5)
    )
    quadrant = turns.astype(jnp.int32) - jnp.where(lane >= HALF, 1, 0)
    odd = (quadrant & 1) == 1
    value = jnp.where(odd, sin_r, cos_r)
    negative = ((quadrant + 1) & 2) == 2
    return jnp.where(negative, -value, value)


def ones(rows, columns):
    return jnp.ones((rows, columns), BF16)


def split(x):
    high = x.astype(BF16)
    low = (x - high.astype(F32)).astype(BF16)
    return jnp.concatenate([high, low], 1)


def row_sums(x):
    return jnp.dot(split(x), ones(2 * HEAD, HEAD), preferred_element_type=F32)


def scale_of(sums):
    return lax.rsqrt(sums * (1.0 / HEAD) + EPS)


def row_scale(x):
    return scale_of(row_sums(x * x))


def turning():
    source = lax.broadcasted_iota(jnp.int32, (HEAD, HEAD), 0)
    target = lax.broadcasted_iota(jnp.int32, (HEAD, HEAD), 1)
    return jnp.where(target == (source + HALF) % HEAD, 1.0, 0.0).astype(BF16)


def turned_rows(raw, matrix):
    return jnp.dot(raw, matrix, preferred_element_type=F32)


def turned_gain(gain):
    return roll_half(jnp.broadcast_to(gain, (8, HEAD)))[:1]


def prepare_kernel(
    lengths_hbm, query_hbm, key_hbm, value_hbm, out_grad_hbm, query_gain_hbm, key_gain_hbm,
    query_rot_ref, query_scaled_ref, query_scale_ref, key_rot_ref, key_across_ref,
    key_scaled_ref, cos_ref, sin_ref, own_tables_ref, across_ref, bias_ref,
    value_ref, out_grad_ref, gains_ref,
    lengths_ref, query_ref, key_ref, sems,
):
    moves = [
        pltpu.make_async_copy(source, target, sems.at[place])
        for place, (source, target) in enumerate(
            (
                (lengths_hbm, lengths_ref),
                (query_gain_hbm, gains_ref.at[0:1]),
                (key_gain_hbm, gains_ref.at[1:2]),
                (key_hbm, key_ref),
                (query_hbm, query_ref),
                (out_grad_hbm, out_grad_ref),
                (value_hbm, value_ref),
            )
        )
    ]
    for move in moves:
        move.start()
    rows = query_ref.shape[0]
    keys = cos_ref.shape[0]
    base = own_index() * rows - (keys - rows)
    shape = (keys, HEAD)
    lane = lax.broadcasted_iota(jnp.int32, shape, 1)
    tokens = base + lax.broadcasted_iota(jnp.int32, shape, 0)
    frequency = frequencies()
    moves[0].wait()
    positions = tokens - doc_starts(tokens, lengths_ref)
    mixed = cos_sin_lanes(positions.astype(F32) * frequency, lane)
    turned = roll_half(mixed)
    cos = jnp.where(lane < HALF, mixed, turned)
    sin = jnp.where(lane < HALF, -turned, mixed)
    cos_ref[...] = cos
    sin_ref[...] = sin
    queries = base + (keys - rows) + lax.broadcasted_iota(jnp.int32, (1, rows), 1)
    lowest = jnp.maximum(doc_starts(queries, lengths_ref), queries - (WINDOW - 1))
    key_tokens = base + lax.broadcasted_iota(jnp.int32, (keys, rows), 0)
    visible = (key_tokens >= lowest) & (key_tokens <= queries)
    bias_ref[...] = jnp.where(visible, 0.0, MASKED)
    own_cos, own_sin = cos[keys - rows :], sin[keys - rows :]
    moves[1].wait()
    moves[2].wait()
    own_tables_ref[0] = own_cos
    own_tables_ref[1] = own_sin
    across_ref[0] = own_cos.T
    across_ref[1] = own_sin.T
    across_ref[2] = jnp.broadcast_to(gains_ref[0:1], (HEAD, HEAD)).T
    matrix = turning()
    for raw_ref, move, row, rot_ref in (
        (key_ref, moves[3], 1, key_rot_ref),
        (query_ref, moves[4], 0, query_rot_ref),
    ):
        gain = gains_ref[row : row + 1]
        cos_gain = own_cos * gain
        sin_gain = own_sin * turned_gain(gain)
        move.wait()
        for head in range(raw_ref.shape[1] // HEAD):
            part = slice(head * rows, (head + 1) * rows)
            across = slice(head * HEAD, (head + 1) * HEAD)
            raw = raw_ref[:, across]
            x = raw.astype(F32)
            parts = split(x * x)
            scale = scale_of(jnp.dot(parts, ones(2 * HEAD, HEAD), preferred_element_type=F32))
            scaled = x * scale
            turned = turned_rows(raw, matrix) * scale
            rotated = scaled * cos_gain + turned * sin_gain
            rot_ref[part, :] = rotated.astype(BF16)
            if raw_ref is key_ref:
                key_scaled_ref[part, :] = scaled
                key_across_ref[across, :] = rotated.T.astype(BF16)
            else:
                query_scaled_ref[across, :] = scaled.T
                sums = lax.dot_general(
                    ones(8, 2 * HEAD), parts, (((1,), (1,)), ((), ())), preferred_element_type=F32
                )
                query_scale_ref[head : head + 1, :] = scale_of(sums[:1])
    moves[5].wait()
    moves[6].wait()


def stacked(ref, head, group):
    return jnp.concatenate(
        [ref[:, (head * group + one) * HEAD : (head * group + one + 1) * HEAD] for one in range(group)],
        0,
    )


def attend_keys_kernel(
    far_ref, near_ref, out_grad_ref, query_rot_ref, key_rot_ref, cos_ref, sin_ref, bias_ref,
    gains_ref,
    exps_ref, inverse_ref, halo_across_ref, halo_scaled_ref, far_value_ref, near_value_ref, own_value_ref,
):
    rows = far_ref.shape[0]
    heads = far_ref.shape[1] // HEAD
    group = out_grad_ref.shape[1] // far_ref.shape[1]
    halo = WINDOW
    keys = halo + rows
    key_gain = gains_ref[1:2]
    cos_gain = cos_ref[:halo] * key_gain
    sin_gain = sin_ref[:halo] * turned_gain(key_gain)
    matrix = turning()

    def scores_of(head):
        cols = slice(head * HEAD, (head + 1) * HEAD)
        raw = jnp.concatenate([far_ref[:, cols], near_ref[:, cols]], 0)
        x = raw.astype(F32)
        scale = row_scale(x)
        scaled = x * scale
        turned = turned_rows(raw, matrix) * scale
        part = slice(head * halo, (head + 1) * halo)
        halo_scaled_ref[part, :] = scaled
        rotated = scaled * cos_gain + turned * sin_gain
        halo_across_ref[cols, :] = rotated.T.astype(BF16)
        both = jnp.concatenate(
            [rotated.astype(BF16), key_rot_ref[head * rows : (head + 1) * rows, :]], 0
        )
        queries = query_rot_ref[head * group * rows : (head + 1) * group * rows, :]
        return lax.dot_general(
            both, queries, (((1,), (1,)), ((), ())), preferred_element_type=F32
        )

    later = scores_of(0)
    for head in range(heads):
        scores = later
        if head + 1 < heads:
            later = scores_of(head + 1)
        cols = slice(head * HEAD, (head + 1) * HEAD)
        low = []
        for one in range(group):
            place = (slice(head * keys, (head + 1) * keys), slice(one * rows, (one + 1) * rows))
            part = scores[:, place[1]] * (SCALE * math.log2(math.e)) + bias_ref[...]
            exps = jnp.exp2(part - jnp.max(part, axis=0, keepdims=True))
            exps_ref[place] = exps
            inverse = 1.0 / jnp.sum(exps, axis=0, keepdims=True)
            inverse_ref[head : head + 1, place[1]] = inverse
            low.append((exps_ref[place] * inverse).astype(BF16))
        value_term = jnp.dot(
            jnp.concatenate(low, 1), stacked(out_grad_ref, head, group), preferred_element_type=F32
        )
        far_value_ref[:, cols] = value_term[:rows].astype(BF16)
        near_value_ref[:, cols] = value_term[rows:halo].astype(BF16)
        own_value_ref[:, cols] = value_term[halo:]


def norm_backward(grad_rot, grad_turned, scaled, scale, gain, cos, sin):
    normed_grad = grad_rot * cos - grad_turned * sin
    part = normed_grad * scaled
    mean = row_sums(part * gain) * (1.0 / HEAD)
    return scale * (normed_grad * gain - scaled * mean), part


def attend_values_kernel(
    far_ref, near_ref, value_ref, out_grad_ref, exps_ref, inverse_ref, query_rot_ref,
    halo_across_ref, key_across_ref, halo_scaled_ref, key_scaled_ref,
    query_scaled_ref, query_scale_ref, cos_ref, sin_ref, across_ref,
    far_key_ref, near_key_ref, own_key_ref, grad_query_ref, gain_ref,
):
    rows = far_ref.shape[0]
    heads = far_ref.shape[1] // HEAD
    group = out_grad_ref.shape[1] // far_ref.shape[1]
    halo = WINDOW
    keys = halo + rows
    cos_across, sin_across = across_ref[0] * SCALE, across_ref[1] * SCALE
    query_gain = across_ref[2]
    query_acc = jnp.zeros((HEAD, rows), F32)
    key_acc = jnp.zeros((keys, HEAD), F32)
    key_acc_turned = jnp.zeros((keys, HEAD), F32)

    def prob_grad_of(head):
        cols = slice(head * HEAD, (head + 1) * HEAD)
        values = jnp.concatenate([far_ref[:, cols], near_ref[:, cols], value_ref[:, cols]], 0)
        return lax.dot_general(
            values, stacked(out_grad_ref, head, group), (((1,), (1,)), ((), ())),
            preferred_element_type=F32,
        )

    later = prob_grad_of(0)
    for head in range(heads):
        prob_grad = later
        if head + 1 < heads:
            later = prob_grad_of(head + 1)
        cols = slice(head * HEAD, (head + 1) * HEAD)
        halo_part = slice(head * halo, (head + 1) * halo)
        own_part = slice(head * rows, (head + 1) * rows)
        group_part = slice(head * group * rows, (head + 1) * group * rows)
        score_grads = []
        for one in range(group):
            place = (slice(head * keys, (head + 1) * keys), slice(one * rows, (one + 1) * rows))
            part = prob_grad[:, place[1]]
            inverse = inverse_ref[head : head + 1, place[1]]
            delta = jnp.sum(exps_ref[place] * part, axis=0, keepdims=True) * inverse
            score_grads.append((exps_ref[place] * inverse * (part - delta)).astype(BF16))
        score_grad = jnp.concatenate(score_grads, 1)
        key_term = (
            jnp.dot(score_grad, query_rot_ref[group_part, :], preferred_element_type=F32) * SCALE
        )
        keys_across = jnp.concatenate([halo_across_ref[cols, :], key_across_ref[cols, :]], 1)
        query_term = jnp.dot(keys_across, score_grad, preferred_element_type=F32)
        halo_key = key_term[:halo].astype(BF16)
        far_key_ref[:, cols] = halo_key[:rows]
        near_key_ref[:, cols] = halo_key[rows:]
        own_key_ref[:, cols] = key_term[halo:]
        term = jnp.concatenate([halo_key.astype(F32), key_term[halo:]], 0)
        scaled = jnp.concatenate([halo_scaled_ref[halo_part, :], key_scaled_ref[own_part, :]], 0)
        key_acc = key_acc + term * scaled
        key_acc_turned = key_acc_turned + term * roll_half(scaled)
        for one in range(group):
            index = head * group + one
            across = slice(index * HEAD, (index + 1) * HEAD)
            grad = query_term[:, one * rows : (one + 1) * rows]
            turned = jnp.concatenate([grad[HALF:], grad[:HALF]], 0)
            normed_grad = grad * cos_across - turned * sin_across
            scaled = query_scaled_ref[across, :]
            query_acc = query_acc + normed_grad * scaled
            weighted = normed_grad * query_gain
            mean = jnp.sum(weighted * scaled, axis=0, keepdims=True) * (1.0 / HEAD)
            raw_grad = query_scale_ref[index : index + 1, :] * (weighted - scaled * mean)
            grad_query_ref[:, across] = raw_grad.T.astype(BF16)
    query_sum = jnp.sum(query_acc.T, axis=0, keepdims=True)
    key_sum = jnp.sum(key_acc * cos_ref[...], axis=0, keepdims=True)
    turned_sum = jnp.sum(key_acc_turned * sin_ref[...], axis=0, keepdims=True)
    gain_ref[...] = jnp.concatenate([query_sum, key_sum + turned_gain(turned_sum)], 0)


def spread_kernel(gain_ref, near_value_ref, copies_ref):
    copies_ref[...] = jnp.broadcast_to(gain_ref[...][None], copies_ref.shape)


def finish_values_kernel(own_ref, near_ref, far_ref, grad_value_ref):
    total = own_ref[...] + near_ref[...].astype(F32) + far_ref[...].astype(F32)
    grad_value_ref[...] = total.astype(BF16)


def finish_keys_kernel(
    key_hbm, own_ref, near_ref, far_ref, tables_ref, gains_ref, grad_key_ref, key_ref, sem
):
    load = pltpu.make_async_copy(key_hbm, key_ref, sem)
    load.start()
    cos, sin = tables_ref[0], tables_ref[1]
    gain = gains_ref[1:2]
    load.wait()
    for head in range(own_ref.shape[1] // HEAD):
        cols = slice(head * HEAD, (head + 1) * HEAD)
        x = key_ref[:, cols].astype(F32)
        scale = row_scale(x)
        total = own_ref[:, cols] + near_ref[:, cols].astype(F32) + far_ref[:, cols].astype(F32)
        grad, _ = norm_backward(total, roll_half(total), x * scale, scale, gain, cos, sin)
        grad_key_ref[:, cols] = grad.astype(BF16)


def sum_kernel(parts_ref, query_gain_ref, key_gain_ref):
    sums = jnp.sum(parts_ref[...], axis=0)
    query_gain_ref[...] = sums[:1]
    key_gain_ref[...] = sums[1:]


def call(kernel, name, outs, operands, cost=None, far=0, scratch=()):
    spaces = [pltpu.HBM] * far + [pltpu.VMEM] * (len(operands) - far)
    return pl.pallas_call(
        kernel,
        out_shape=outs,
        in_specs=[pl.BlockSpec(memory_space=space) for space in spaces],
        out_specs=[pl.BlockSpec(memory_space=pltpu.VMEM)] * len(outs),
        scratch_shapes=scratch,
        compiler_params=pltpu.CompilerParams(vmem_limit_bytes=VMEM_LIMIT),
        cost_estimate=cost,
        name=name,
    )(*[pltpu.with_memory_space_constraint(x, pltpu.HBM) for x in operands[:far]], *operands[far:])


def cost(flops, size, exps=0):
    return pl.CostEstimate(flops=flops, bytes_accessed=size, transcendentals=exps)


def shape(dims, dtype):
    return jax.ShapeDtypeStruct(dims, dtype)


def on_device(doc_lengths, query_raw, key_raw, value_matrix, out_grad, query_gain, key_gain):
    rows, query_width = query_raw.shape
    width = key_raw.shape[1]
    heads = width // HEAD
    query_heads = query_width // HEAD
    keys = WINDOW + rows
    devices = lax.axis_size(AXES)
    query_gain = query_gain.reshape(1, HEAD)
    key_gain = key_gain.reshape(1, HEAD)
    near_key, far_key = shift(key_raw, 1), shift(key_raw, 2)
    term = shape((rows, width), BF16)
    own = shape((rows, width), F32)
    (
        query_rot, query_scaled, query_scale, key_rot, key_across, key_scaled,
        cos, sin, own_tables, across, bias, values, grads_out, gains,
    ) = call(
        prepare_kernel,
        "prepare",
        [
            shape((query_heads * rows, HEAD), BF16),
            shape((query_width, rows), F32),
            shape((query_heads, rows), F32),
            shape((heads * rows, HEAD), BF16),
            shape((width, rows), BF16),
            shape((heads * rows, HEAD), F32),
            shape((keys, HEAD), F32),
            shape((keys, HEAD), F32),
            shape((2, rows, HEAD), F32),
            shape((3, HEAD, rows), F32),
            shape((keys, rows), F32),
            term,
            shape((rows, query_width), BF16),
            shape((8, HEAD), F32),
        ],
        (doc_lengths, query_raw, key_raw, value_matrix, out_grad, query_gain, key_gain),
        cost(4_000_000, 6_000_000),
        far=7,
        scratch=[
            pltpu.SMEM(doc_lengths.shape, jnp.int32),
            pltpu.VMEM((rows, query_width), BF16),
            pltpu.VMEM((rows, width), BF16),
            pltpu.SemaphoreType.DMA((7,)),
        ],
    )
    near_value, far_value = shift(values, 1), shift(values, 2)
    exps, inverse, halo_across, halo_scaled, far_value_term, near_value_term, own_value = call(
        attend_keys_kernel,
        "attend_keys",
        [
            shape((heads * keys, query_heads // heads * rows), F32),
            shape((heads, query_heads // heads * rows), F32),
            shape((width, WINDOW), BF16),
            shape((heads * WINDOW, HEAD), F32),
            term,
            term,
            own,
        ],
        (far_key, near_key, grads_out, query_rot, key_rot, cos, sin, bias, gains),
        cost(400_000_000, 4_000_000, 800_000),
    )
    near_value_back, far_value_back = shift(near_value_term, -1), shift(far_value_term, -2)
    far_key_term, near_key_term, own_key, grad_query, gain_part = call(
        attend_values_kernel,
        "attend_values",
        [term, term, own, shape((rows, query_width), BF16), shape((2, HEAD), F32)],
        (
            far_value, near_value, values, grads_out, exps, inverse, query_rot,
            halo_across, key_across, halo_scaled, key_scaled, query_scaled, query_scale, cos, sin, across,
        ),
        cost(600_000_000, 4_000_000),
    )
    near_key_back, far_key_back = shift(near_key_term, -1), shift(far_key_term, -2)
    (copies,) = call(
        spread_kernel, "spread_gains", [shape((devices, 2, HEAD), F32)], (gain_part, near_value_back)
    )
    parts = lax.all_to_all(copies, AXES, 0, 0)
    (grad_value,) = call(
        finish_values_kernel,
        "finish_values",
        [term],
        (own_value, near_value_back, far_value_back),
        cost(1_000_000, 2_000_000),
    )
    (grad_key,) = call(
        finish_keys_kernel,
        "finish_keys",
        [term],
        (key_raw, own_key, near_key_back, far_key_back, own_tables, gains),
        cost(4_000_000, 3_000_000),
        far=1,
        scratch=[pltpu.VMEM((rows, width), BF16), pltpu.SemaphoreType.DMA],
    )
    grad_query_gain, grad_key_gain = call(
        sum_kernel, "sum_gains", [shape((1, HEAD), F32), shape((1, HEAD), F32)], (parts,)
    )
    return (
        grad_query, grad_key, grad_value, grad_query_gain.reshape(HEAD), grad_key_gain.reshape(HEAD)
    )


def solution(mesh):
    rows = P(AXES, None)
    return jax.shard_map(
        on_device,
        mesh=mesh,
        in_specs=(P(), rows, rows, rows, rows, P(), P()),
        out_specs=(rows, rows, rows, P(), P()),
        check_vma=False,
    )
```

```python
import math

import jax
import jax.numpy as jnp
import numpy as np
from jax import lax
from jax.experimental import pallas as pl
from jax.experimental.pallas import tpu as pltpu
from jax.sharding import PartitionSpec as P

HEAD = 128
HALF = HEAD // 2
WINDOW = 256
EPS = 1e-06
SCALE = 168.0 ** (-0.5)
ROPE_BASE = 10000.0
MASKED = -1e30
AXES = ("ctx", "grp")
F32 = jnp.float32
BF16 = jnp.bfloat16
VMEM_LIMIT = 32 * 1024 * 1024


def frequencies():
    lane = lax.broadcasted_iota(jnp.int32, (1, HEAD), 1) % HALF
    values = jnp.zeros((1, HEAD), F32)
    for m in range(HALF):
        values = jnp.where(lane == m, np.float32(ROPE_BASE ** (-2.0 * m / HEAD)), values)
    return values


def shift(value, steps):
    count = lax.axis_size(AXES)
    return lax.ppermute(value, AXES, [(s, (s + steps) % count) for s in range(count)])


def own_index():
    return lax.axis_index("ctx") * lax.axis_size("grp") + lax.axis_index("grp")


def roll_half(x):
    return pltpu.roll(x, HALF, 1)


def doc_starts(tokens, lengths_ref):
    def step(doc, carry):
        end, starts = carry
        end = end + lengths_ref[doc]
        return end, jnp.where(tokens >= end, end, starts)

    count = lengths_ref.shape[0]
    return lax.fori_loop(
        0, count, step, (jnp.int32(0), jnp.zeros_like(tokens)), unroll=count if count <= 8 else 1
    )[1]


def cos_sin_lanes(angle, lane):
    turns = jnp.floor(angle * (2.0 / math.pi) + 0.5)
    r = angle - turns * 1.5703125
    r = r - turns * 4.837512969970703125e-4
    r = r - turns * 7.549789948768648e-8
    z = r * r
    sin_r = r + r * z * (-1.6666654611e-1 + z * (8.3321608736e-3 + z * -1.9515295891e-4))
    cos_r = 1.0 - 0.5 * z + z * z * (
        4.166664568298827e-2 + z * (-1.388731625493765e-3 + z * 2.443315711809948e-5)
    )
    quadrant = turns.astype(jnp.int32) - jnp.where(lane >= HALF, 1, 0)
    odd = (quadrant & 1) == 1
    value = jnp.where(odd, sin_r, cos_r)
    negative = ((quadrant + 1) & 2) == 2
    return jnp.where(negative, -value, value)


def ones(rows, columns):
    return jnp.ones((rows, columns), BF16)


def split(x):
    high = x.astype(BF16)
    low = (x - high.astype(F32)).astype(BF16)
    return jnp.concatenate([high, low], 1)


def row_sums(x):
    return jnp.dot(split(x), ones(2 * HEAD, HEAD), preferred_element_type=F32)


def scale_of(sums):
    return lax.rsqrt(sums * (1.0 / HEAD) + EPS)


def row_scale(x):
    return scale_of(row_sums(x * x))


def turning():
    source = lax.broadcasted_iota(jnp.int32, (HEAD, HEAD), 0)
    target = lax.broadcasted_iota(jnp.int32, (HEAD, HEAD), 1)
    return jnp.where(target == (source + HALF) % HEAD, 1.0, 0.0).astype(BF16)


def turned_rows(raw, matrix):
    return jnp.dot(raw, matrix, preferred_element_type=F32)


def turned_gain(gain):
    return roll_half(jnp.broadcast_to(gain, (8, HEAD)))[:1]


def prepare_kernel(
    lengths_hbm, query_hbm, key_hbm, value_hbm, out_grad_hbm, query_gain_hbm, key_gain_hbm,
    query_rot_ref, query_scaled_ref, query_scale_ref, key_rot_ref, key_across_ref,
    key_scaled_ref, cos_ref, sin_ref, own_tables_ref, across_ref, bias_ref,
    value_ref, out_grad_ref, gains_ref,
    lengths_ref, query_ref, key_ref, sems,
):
    moves = [
        pltpu.make_async_copy(source, target, sems.at[place])
        for place, (source, target) in enumerate(
            (
                (lengths_hbm, lengths_ref),
                (query_gain_hbm, gains_ref.at[0:1]),
                (key_gain_hbm, gains_ref.at[1:2]),
                (key_hbm, key_ref),
                (query_hbm, query_ref),
                (out_grad_hbm, out_grad_ref),
                (value_hbm, value_ref),
            )
        )
    ]
    for move in moves:
        move.start()
    rows = query_ref.shape[0]
    keys = cos_ref.shape[0]
    base = own_index() * rows - (keys - rows)
    shape = (keys, HEAD)
    lane = lax.broadcasted_iota(jnp.int32, shape, 1)
    tokens = base + lax.broadcasted_iota(jnp.int32, shape, 0)
    frequency = frequencies()
    moves[0].wait()
    positions = tokens - doc_starts(tokens, lengths_ref)
    mixed = cos_sin_lanes(positions.astype(F32) * frequency, lane)
    turned = roll_half(mixed)
    cos = jnp.where(lane < HALF, mixed, turned)
    sin = jnp.where(lane < HALF, -turned, mixed)
    cos_ref[...] = cos
    sin_ref[...] = sin
    queries = base + (keys - rows) + lax.broadcasted_iota(jnp.int32, (1, rows), 1)
    lowest = jnp.maximum(doc_starts(queries, lengths_ref), queries - (WINDOW - 1))
    key_tokens = base + lax.broadcasted_iota(jnp.int32, (keys, rows), 0)
    visible = (key_tokens >= lowest) & (key_tokens <= queries)
    bias_ref[...] = jnp.where(visible, 0.0, MASKED)
    own_cos, own_sin = cos[keys - rows :], sin[keys - rows :]
    moves[1].wait()
    moves[2].wait()
    own_tables_ref[0] = own_cos
    own_tables_ref[1] = own_sin
    across_ref[0] = own_cos.T
    across_ref[1] = own_sin.T
    across_ref[2] = jnp.broadcast_to(gains_ref[0:1], (HEAD, HEAD)).T
    matrix = turning()
    for raw_ref, move, row, rot_ref in (
        (key_ref, moves[3], 1, key_rot_ref),
        (query_ref, moves[4], 0, query_rot_ref),
    ):
        gain = gains_ref[row : row + 1]
        cos_gain = own_cos * gain
        sin_gain = own_sin * turned_gain(gain)
        move.wait()
        for head in range(raw_ref.shape[1] // HEAD):
            part = slice(head * rows, (head + 1) * rows)
            across = slice(head * HEAD, (head + 1) * HEAD)
            raw = raw_ref[:, across]
            x = raw.astype(F32)
            parts = split(x * x)
            scale = scale_of(jnp.dot(parts, ones(2 * HEAD, HEAD), preferred_element_type=F32))
            scaled = x * scale
            turned = turned_rows(raw, matrix) * scale
            rotated = scaled * cos_gain + turned * sin_gain
            rot_ref[part, :] = rotated.astype(BF16)
            if raw_ref is key_ref:
                key_scaled_ref[part, :] = scaled
                key_across_ref[across, :] = rotated.T.astype(BF16)
            else:
                query_scaled_ref[across, :] = scaled.T
                sums = lax.dot_general(
                    ones(8, 2 * HEAD), parts, (((1,), (1,)), ((), ())), preferred_element_type=F32
                )
                query_scale_ref[head : head + 1, :] = scale_of(sums[:1])
    moves[5].wait()
    moves[6].wait()


def stacked(ref, head, group):
    return jnp.concatenate(
        [ref[:, (head * group + one) * HEAD : (head * group + one + 1) * HEAD] for one in range(group)],
        0,
    )


def attend_keys_kernel(
    near_ref, far_ref, out_grad_ref, query_rot_ref, key_rot_ref, cos_ref, sin_ref, bias_ref,
    gains_ref,
    exps_ref, inverse_ref, halo_across_ref, halo_scaled_ref, far_value_ref, near_value_ref, own_value_ref,
):
    rows = far_ref.shape[0]
    heads = far_ref.shape[1] // HEAD
    group = out_grad_ref.shape[1] // far_ref.shape[1]
    halo = WINDOW
    keys = halo + rows
    key_gain = gains_ref[1:2]
    cos_gain = cos_ref[:halo] * key_gain
    sin_gain = sin_ref[:halo] * turned_gain(key_gain)
    matrix = turning()

    def scores_of(head):
        cols = slice(head * HEAD, (head + 1) * HEAD)
        raw = jnp.concatenate([far_ref[:, cols], near_ref[:, cols]], 0)
        x = raw.astype(F32)
        scale = row_scale(x)
        scaled = x * scale
        turned = turned_rows(raw, matrix) * scale
        part = slice(head * halo, (head + 1) * halo)
        halo_scaled_ref[part, :] = scaled
        rotated = scaled * cos_gain + turned * sin_gain
        halo_across_ref[cols, :] = rotated.T.astype(BF16)
        both = jnp.concatenate(
            [rotated.astype(BF16), key_rot_ref[head * rows : (head + 1) * rows, :]], 0
        )
        queries = query_rot_ref[head * group * rows : (head + 1) * group * rows, :]
        return lax.dot_general(
            both, queries, (((1,), (1,)), ((), ())), preferred_element_type=F32
        )

    later = scores_of(0)
    for head in range(heads):
        scores = later
        if head + 1 < heads:
            later = scores_of(head + 1)
        cols = slice(head * HEAD, (head + 1) * HEAD)
        low = []
        for one in range(group):
            place = (slice(head * keys, (head + 1) * keys), slice(one * rows, (one + 1) * rows))
            part = scores[:, place[1]] * (SCALE * math.log2(math.e)) + bias_ref[...]
            exps = jnp.exp2(part - jnp.max(part, axis=0, keepdims=True))
            exps_ref[place] = exps
            inverse = 1.0 / jnp.sum(exps, axis=0, keepdims=True)
            inverse_ref[head : head + 1, place[1]] = inverse
            low.append((exps_ref[place] * inverse).astype(BF16))
        value_term = jnp.dot(
            jnp.concatenate(low, 1), stacked(out_grad_ref, head, group), preferred_element_type=F32
        )
        far_value_ref[:, cols] = value_term[:rows].astype(BF16)
        near_value_ref[:, cols] = value_term[rows:halo].astype(BF16)
        own_value_ref[:, cols] = value_term[halo:]


def norm_backward(grad_rot, grad_turned, scaled, scale, gain, cos, sin):
    normed_grad = grad_rot * cos - grad_turned * sin
    part = normed_grad * scaled
    mean = row_sums(part * gain) * (1.0 / HEAD)
    return scale * (normed_grad * gain - scaled * mean), part


def attend_values_kernel(
    far_ref, near_ref, value_ref, out_grad_ref, exps_ref, inverse_ref, query_rot_ref,
    halo_across_ref, key_across_ref, halo_scaled_ref, key_scaled_ref,
    query_scaled_ref, query_scale_ref, cos_ref, sin_ref, across_ref,
    far_key_ref, near_key_ref, own_key_ref, grad_query_ref, gain_ref,
):
    rows = far_ref.shape[0]
    heads = far_ref.shape[1] // HEAD
    group = out_grad_ref.shape[1] // far_ref.shape[1]
    halo = WINDOW
    keys = halo + rows
    cos_across, sin_across = across_ref[0] * SCALE, across_ref[1] * SCALE
    query_gain = across_ref[2]
    query_acc = jnp.zeros((HEAD, rows), F32)
    key_acc = jnp.zeros((keys, HEAD), F32)
    key_acc_turned = jnp.zeros((keys, HEAD), F32)

    def prob_grad_of(head):
        cols = slice(head * HEAD, (head + 1) * HEAD)
        values = jnp.concatenate([far_ref[:, cols], near_ref[:, cols], value_ref[:, cols]], 0)
        return lax.dot_general(
            values, stacked(out_grad_ref, head, group), (((1,), (1,)), ((), ())),
            preferred_element_type=F32,
        )

    later = prob_grad_of(0)
    for head in range(heads):
        prob_grad = later
        if head + 1 < heads:
            later = prob_grad_of(head + 1)
        cols = slice(head * HEAD, (head + 1) * HEAD)
        halo_part = slice(head * halo, (head + 1) * halo)
        own_part = slice(head * rows, (head + 1) * rows)
        group_part = slice(head * group * rows, (head + 1) * group * rows)
        score_grads = []
        for one in range(group):
            place = (slice(head * keys, (head + 1) * keys), slice(one * rows, (one + 1) * rows))
            part = prob_grad[:, place[1]]
            inverse = inverse_ref[head : head + 1, place[1]]
            delta = jnp.sum(exps_ref[place] * part, axis=0, keepdims=True) * inverse
            score_grads.append((exps_ref[place] * inverse * (part - delta)).astype(BF16))
        score_grad = jnp.concatenate(score_grads, 1)
        key_term = (
            jnp.dot(score_grad, query_rot_ref[group_part, :], preferred_element_type=F32) * SCALE
        )
        keys_across = jnp.concatenate([halo_across_ref[cols, :], key_across_ref[cols, :]], 1)
        query_term = jnp.dot(keys_across, score_grad, preferred_element_type=F32)
        halo_key = key_term[:halo].astype(BF16)
        far_key_ref[:, cols] = halo_key[:rows]
        near_key_ref[:, cols] = halo_key[rows:]
        own_key_ref[:, cols] = key_term[halo:]
        term = jnp.concatenate([halo_key.astype(F32), key_term[halo:]], 0)
        scaled = jnp.concatenate([halo_scaled_ref[halo_part, :], key_scaled_ref[own_part, :]], 0)
        key_acc = key_acc + term * scaled
        key_acc_turned = key_acc_turned + term * roll_half(scaled)
        for one in range(group):
            index = head * group + one
            across = slice(index * HEAD, (index + 1) * HEAD)
            grad = query_term[:, one * rows : (one + 1) * rows]
            turned = jnp.concatenate([grad[HALF:], grad[:HALF]], 0)
            normed_grad = grad * cos_across - turned * sin_across
            scaled = query_scaled_ref[across, :]
            query_acc = query_acc + normed_grad * scaled
            weighted = normed_grad * query_gain
            mean = jnp.sum(weighted * scaled, axis=0, keepdims=True) * (1.0 / HEAD)
            raw_grad = query_scale_ref[index : index + 1, :] * (weighted - scaled * mean)
            grad_query_ref[:, across] = raw_grad.T.astype(BF16)
    query_sum = jnp.sum(query_acc.T, axis=0, keepdims=True)
    key_sum = jnp.sum(key_acc * cos_ref[...], axis=0, keepdims=True)
    turned_sum = jnp.sum(key_acc_turned * sin_ref[...], axis=0, keepdims=True)
    gain_ref[...] = jnp.concatenate([query_sum, key_sum + turned_gain(turned_sum)], 0)


def spread_kernel(gain_ref, near_value_ref, copies_ref):
    copies_ref[...] = jnp.broadcast_to(gain_ref[...][None], copies_ref.shape)


def finish_values_kernel(own_ref, near_ref, far_ref, grad_value_ref):
    total = own_ref[...] + near_ref[...].astype(F32) + far_ref[...].astype(F32)
    grad_value_ref[...] = total.astype(BF16)


def finish_keys_kernel(
    key_hbm, own_ref, near_ref, far_ref, tables_ref, gains_ref, grad_key_ref, key_ref, sem
):
    load = pltpu.make_async_copy(key_hbm, key_ref, sem)
    load.start()
    cos, sin = tables_ref[0], tables_ref[1]
    gain = gains_ref[1:2]
    load.wait()
    for head in range(own_ref.shape[1] // HEAD):
        cols = slice(head * HEAD, (head + 1) * HEAD)
        x = key_ref[:, cols].astype(F32)
        scale = row_scale(x)
        total = own_ref[:, cols] + near_ref[:, cols].astype(F32) + far_ref[:, cols].astype(F32)
        grad, _ = norm_backward(total, roll_half(total), x * scale, scale, gain, cos, sin)
        grad_key_ref[:, cols] = grad.astype(BF16)


def sum_kernel(parts_ref, query_gain_ref, key_gain_ref):
    sums = jnp.sum(parts_ref[...], axis=0)
    query_gain_ref[...] = sums[:1]
    key_gain_ref[...] = sums[1:]


def call(kernel, name, outs, operands, cost=None, far=0, scratch=()):
    spaces = [pltpu.HBM] * far + [pltpu.VMEM] * (len(operands) - far)
    return pl.pallas_call(
        kernel,
        out_shape=outs,
        in_specs=[pl.BlockSpec(memory_space=space) for space in spaces],
        out_specs=[pl.BlockSpec(memory_space=pltpu.VMEM)] * len(outs),
        scratch_shapes=scratch,
        compiler_params=pltpu.CompilerParams(vmem_limit_bytes=VMEM_LIMIT),
        cost_estimate=cost,
        name=name,
    )(*[pltpu.with_memory_space_constraint(x, pltpu.HBM) for x in operands[:far]], *operands[far:])


def cost(flops, size, exps=0):
    return pl.CostEstimate(flops=flops, bytes_accessed=size, transcendentals=exps)


def shape(dims, dtype):
    return jax.ShapeDtypeStruct(dims, dtype)


def on_device(doc_lengths, query_raw, key_raw, value_matrix, out_grad, query_gain, key_gain):
    rows, query_width = query_raw.shape
    width = key_raw.shape[1]
    heads = width // HEAD
    query_heads = query_width // HEAD
    keys = WINDOW + rows
    devices = lax.axis_size(AXES)
    query_gain = query_gain.reshape(1, HEAD)
    key_gain = key_gain.reshape(1, HEAD)
    near_key, far_key = shift(key_raw, 1), shift(key_raw, 2)
    term = shape((rows, width), BF16)
    own = shape((rows, width), F32)
    (
        query_rot, query_scaled, query_scale, key_rot, key_across, key_scaled,
        cos, sin, own_tables, across, bias, values, grads_out, gains,
    ) = call(
        prepare_kernel,
        "prepare",
        [
            shape((query_heads * rows, HEAD), BF16),
            shape((query_width, rows), F32),
            shape((query_heads, rows), F32),
            shape((heads * rows, HEAD), BF16),
            shape((width, rows), BF16),
            shape((heads * rows, HEAD), F32),
            shape((keys, HEAD), F32),
            shape((keys, HEAD), F32),
            shape((2, rows, HEAD), F32),
            shape((3, HEAD, rows), F32),
            shape((keys, rows), F32),
            term,
            shape((rows, query_width), BF16),
            shape((8, HEAD), F32),
        ],
        (doc_lengths, query_raw, key_raw, value_matrix, out_grad, query_gain, key_gain),
        cost(4_000_000, 6_000_000),
        far=7,
        scratch=[
            pltpu.SMEM(doc_lengths.shape, jnp.int32),
            pltpu.VMEM((rows, query_width), BF16),
            pltpu.VMEM((rows, width), BF16),
            pltpu.SemaphoreType.DMA((7,)),
        ],
    )
    near_value, far_value = shift(values, 1), shift(values, 2)
    exps, inverse, halo_across, halo_scaled, far_value_term, near_value_term, own_value = call(
        attend_keys_kernel,
        "attend_keys",
        [
            shape((heads * keys, query_heads // heads * rows), F32),
            shape((heads, query_heads // heads * rows), F32),
            shape((width, WINDOW), BF16),
            shape((heads * WINDOW, HEAD), F32),
            term,
            term,
            own,
        ],
        (near_key, far_key, grads_out, query_rot, key_rot, cos, sin, bias, gains),
        cost(400_000_000, 4_000_000, 800_000),
    )
    near_value_back, far_value_back = shift(near_value_term, -1), shift(far_value_term, -2)
    far_key_term, near_key_term, own_key, grad_query, gain_part = call(
        attend_values_kernel,
        "attend_values",
        [term, term, own, shape((rows, query_width), BF16), shape((2, HEAD), F32)],
        (
            far_value, near_value, values, grads_out, exps, inverse, query_rot,
            halo_across, key_across, halo_scaled, key_scaled, query_scaled, query_scale, cos, sin, across,
        ),
        cost(600_000_000, 4_000_000),
    )
    near_key_back, far_key_back = shift(near_key_term, -1), shift(far_key_term, -2)
    (copies,) = call(
        spread_kernel, "spread_gains", [shape((devices, 2, HEAD), F32)], (gain_part, near_value_back)
    )
    parts = lax.all_to_all(copies, AXES, 0, 0)
    (grad_value,) = call(
        finish_values_kernel,
        "finish_values",
        [term],
        (own_value, near_value_back, far_value_back),
        cost(1_000_000, 2_000_000),
    )
    (grad_key,) = call(
        finish_keys_kernel,
        "finish_keys",
        [term],
        (key_raw, own_key, near_key_back, far_key_back, own_tables, gains),
        cost(4_000_000, 3_000_000),
        far=1,
        scratch=[pltpu.VMEM((rows, width), BF16), pltpu.SemaphoreType.DMA],
    )
    grad_query_gain, grad_key_gain = call(
        sum_kernel, "sum_gains", [shape((1, HEAD), F32), shape((1, HEAD), F32)], (parts,)
    )
    return (
        grad_query, grad_key, grad_value, grad_query_gain.reshape(HEAD), grad_key_gain.reshape(HEAD)
    )


def solution(mesh):
    rows = P(AXES, None)
    return jax.shard_map(
        on_device,
        mesh=mesh,
        in_specs=(P(), rows, rows, rows, rows, P(), P()),
        out_specs=(rows, rows, rows, P(), P()),
        check_vma=False,
    )
```

```python
import math

import jax
import jax.numpy as jnp
import numpy as np
from jax import lax
from jax.experimental import pallas as pl
from jax.experimental.pallas import tpu as pltpu
from jax.sharding import PartitionSpec as P

HEAD = 128
HALF = HEAD // 2
WINDOW = 256
EPS = 1e-06
SCALE = 168.0 ** (-0.5)
ROPE_BASE = 10000.0
MASKED = -1e30
AXES = ("ctx", "grp")
F32 = jnp.float32
BF16 = jnp.bfloat16
VMEM_LIMIT = 32 * 1024 * 1024


def frequencies():
    lane = lax.broadcasted_iota(jnp.int32, (1, HEAD), 1) % HALF
    values = jnp.zeros((1, HEAD), F32)
    for m in range(HALF):
        values = jnp.where(lane == m, np.float32(ROPE_BASE ** (-2.0 * m / HEAD)), values)
    return values


def shift(value, steps):
    count = lax.axis_size(AXES)
    return lax.ppermute(value, AXES, [(s, (s + steps) % count) for s in range(count)])


def own_index():
    return lax.axis_index("ctx") * lax.axis_size("grp") + lax.axis_index("grp")


def roll_half(x):
    return pltpu.roll(x, HALF, 1)


def doc_starts(tokens, lengths_ref):
    def step(doc, carry):
        end, starts = carry
        end = end + lengths_ref[doc]
        return end, jnp.where(tokens >= end, end, starts)

    count = lengths_ref.shape[0]
    return lax.fori_loop(
        0, count, step, (jnp.int32(0), jnp.zeros_like(tokens)), unroll=count if count <= 8 else 1
    )[1]


def cos_sin_lanes(angle, lane):
    turns = jnp.floor(angle * (2.0 / math.pi) + 0.5)
    r = angle - turns * 1.5703125
    r = r - turns * 4.837512969970703125e-4
    r = r - turns * 7.549789948768648e-8
    z = r * r
    sin_r = r + r * z * (-1.6666654611e-1 + z * (8.3321608736e-3 + z * -1.9515295891e-4))
    cos_r = 1.0 - 0.5 * z + z * z * (
        4.166664568298827e-2 + z * (-1.388731625493765e-3 + z * 2.443315711809948e-5)
    )
    quadrant = turns.astype(jnp.int32) - jnp.where(lane >= HALF, 1, 0)
    odd = (quadrant & 1) == 1
    value = jnp.where(odd, sin_r, cos_r)
    negative = ((quadrant + 1) & 2) == 2
    return jnp.where(negative, -value, value)


def ones(rows, columns):
    return jnp.ones((rows, columns), BF16)


def split(x):
    high = x.astype(BF16)
    low = (x - high.astype(F32)).astype(BF16)
    return jnp.concatenate([high, low], 1)


def row_sums(x):
    return jnp.dot(split(x), ones(2 * HEAD, HEAD), preferred_element_type=F32)


def scale_of(sums):
    return lax.rsqrt(sums * (1.0 / HEAD) + EPS)


def row_scale(x):
    return scale_of(row_sums(x * x))


def turning():
    source = lax.broadcasted_iota(jnp.int32, (HEAD, HEAD), 0)
    target = lax.broadcasted_iota(jnp.int32, (HEAD, HEAD), 1)
    return jnp.where(target == (source + HALF) % HEAD, 1.0, 0.0).astype(BF16)


def turned_rows(raw, matrix):
    return jnp.dot(raw, matrix, preferred_element_type=F32)


def turned_gain(gain):
    return roll_half(jnp.broadcast_to(gain, (8, HEAD)))[:1]


def prepare_kernel(
    lengths_hbm, query_hbm, key_hbm, value_hbm, out_grad_hbm, query_gain_hbm, key_gain_hbm,
    query_rot_ref, query_scaled_ref, query_scale_ref, key_rot_ref, key_across_ref,
    key_scaled_ref, cos_ref, sin_ref, own_tables_ref, across_ref, bias_ref,
    value_ref, out_grad_ref, gains_ref,
    lengths_ref, query_ref, key_ref, sems,
):
    moves = [
        pltpu.make_async_copy(source, target, sems.at[place])
        for place, (source, target) in enumerate(
            (
                (lengths_hbm, lengths_ref),
                (query_gain_hbm, gains_ref.at[0:1]),
                (key_gain_hbm, gains_ref.at[1:2]),
                (key_hbm, key_ref),
                (query_hbm, query_ref),
                (out_grad_hbm, out_grad_ref),
                (value_hbm, value_ref),
            )
        )
    ]
    for move in moves:
        move.start()
    rows = query_ref.shape[0]
    keys = cos_ref.shape[0]
    base = own_index() * rows - (keys - rows)
    shape = (keys, HEAD)
    lane = lax.broadcasted_iota(jnp.int32, shape, 1)
    tokens = base + lax.broadcasted_iota(jnp.int32, shape, 0)
    frequency = frequencies()
    moves[0].wait()
    positions = tokens - doc_starts(tokens, lengths_ref)
    mixed = cos_sin_lanes(positions.astype(F32) * frequency, lane)
    turned = roll_half(mixed)
    cos = jnp.where(lane < HALF, mixed, turned)
    sin = jnp.where(lane < HALF, -turned, mixed)
    cos_ref[...] = cos
    sin_ref[...] = sin
    queries = base + (keys - rows) + lax.broadcasted_iota(jnp.int32, (1, rows), 1)
    lowest = jnp.maximum(doc_starts(queries, lengths_ref), queries - (WINDOW - 1))
    key_tokens = base + lax.broadcasted_iota(jnp.int32, (keys, rows), 0)
    visible = (key_tokens >= lowest) & (key_tokens <= queries)
    bias_ref[...] = jnp.where(visible, 0.0, MASKED)
    own_cos, own_sin = cos[keys - rows :], sin[keys - rows :]
    moves[1].wait()
    moves[2].wait()
    own_tables_ref[0] = own_cos
    own_tables_ref[1] = own_sin
    across_ref[0] = own_cos.T
    across_ref[1] = own_sin.T
    across_ref[2] = jnp.broadcast_to(gains_ref[0:1], (HEAD, HEAD)).T
    matrix = turning()
    for raw_ref, move, row, rot_ref in (
        (key_ref, moves[3], 1, key_rot_ref),
        (query_ref, moves[4], 0, query_rot_ref),
    ):
        gain = gains_ref[row : row + 1]
        cos_gain = own_cos * gain
        sin_gain = own_sin * turned_gain(gain)
        move.wait()
        for head in range(raw_ref.shape[1] // HEAD):
            part = slice(head * rows, (head + 1) * rows)
            across = slice(head * HEAD, (head + 1) * HEAD)
            raw = raw_ref[:, across]
            x = raw.astype(F32)
            parts = split(x * x)
            scale = scale_of(jnp.dot(parts, ones(2 * HEAD, HEAD), preferred_element_type=F32))
            scaled = x * scale
            turned = turned_rows(raw, matrix) * scale
            rotated = scaled * cos_gain + turned * sin_gain
            rot_ref[part, :] = rotated.astype(BF16)
            if raw_ref is key_ref:
                key_scaled_ref[part, :] = scaled
                key_across_ref[across, :] = rotated.T.astype(BF16)
            else:
                query_scaled_ref[across, :] = scaled.T
                sums = lax.dot_general(
                    ones(8, 2 * HEAD), parts, (((1,), (1,)), ((), ())), preferred_element_type=F32
                )
                query_scale_ref[head : head + 1, :] = scale_of(sums[:1])
    moves[5].wait()
    moves[6].wait()


def stacked(ref, head, group):
    return jnp.concatenate(
        [ref[:, (head * group + one) * HEAD : (head * group + one + 1) * HEAD] for one in range(group)],
        0,
    )


def attend_keys_kernel(
    near_ref, far_ref, out_grad_ref, query_rot_ref, key_rot_ref, cos_ref, sin_ref, bias_ref,
    gains_ref,
    exps_ref, inverse_ref, halo_across_ref, halo_scaled_ref, far_value_ref, near_value_ref, own_value_ref,
):
    rows = far_ref.shape[0]
    heads = far_ref.shape[1] // HEAD
    group = out_grad_ref.shape[1] // far_ref.shape[1]
    halo = WINDOW
    keys = halo + rows
    key_gain = gains_ref[1:2]
    cos_gain = cos_ref[:halo] * key_gain
    sin_gain = sin_ref[:halo] * turned_gain(key_gain)
    matrix = turning()

    def scores_of(head):
        cols = slice(head * HEAD, (head + 1) * HEAD)
        raw = jnp.concatenate([far_ref[:, cols], near_ref[:, cols]], 0)
        x = raw.astype(F32)
        scale = row_scale(x)
        scaled = x * scale
        turned = turned_rows(raw, matrix) * scale
        part = slice(head * halo, (head + 1) * halo)
        halo_scaled_ref[part, :] = scaled
        rotated = scaled * cos_gain + turned * sin_gain
        halo_across_ref[cols, :] = rotated.T.astype(BF16)
        both = jnp.concatenate(
            [rotated.astype(BF16), key_rot_ref[head * rows : (head + 1) * rows, :]], 0
        )
        queries = query_rot_ref[head * group * rows : (head + 1) * group * rows, :]
        return lax.dot_general(
            both, queries, (((1,), (1,)), ((), ())), preferred_element_type=F32
        )

    later = scores_of(0)
    for head in range(heads):
        scores = later
        if head + 1 < heads:
            later = scores_of(head + 1)
        cols = slice(head * HEAD, (head + 1) * HEAD)
        low = []
        for one in range(group):
            place = (slice(head * keys, (head + 1) * keys), slice(one * rows, (one + 1) * rows))
            part = scores[:, place[1]] * (SCALE * math.log2(math.e)) + bias_ref[...]
            exps = jnp.exp2(part - jnp.max(part, axis=0, keepdims=True))
            exps_ref[place] = exps
            inverse = 1.0 / jnp.sum(exps, axis=0, keepdims=True)
            inverse_ref[head : head + 1, place[1]] = inverse
            low.append((exps_ref[place] * inverse).astype(BF16))
        value_term = jnp.dot(
            jnp.concatenate(low, 1), stacked(out_grad_ref, head, group), preferred_element_type=F32
        )
        far_value_ref[:, cols] = value_term[:rows].astype(BF16)
        near_value_ref[:, cols] = value_term[rows:halo].astype(BF16)
        own_value_ref[:, cols] = value_term[halo:]


def norm_backward(grad_rot, grad_turned, scaled, scale, gain, cos, sin):
    normed_grad = grad_rot * cos - grad_turned * sin
    part = normed_grad * scaled
    mean = row_sums(part * gain) * (1.0 / HEAD)
    return scale * (normed_grad * gain - scaled * mean), part


def attend_values_kernel(
    far_ref, near_ref, value_ref, out_grad_ref, exps_ref, inverse_ref, query_rot_ref,
    halo_across_ref, key_across_ref, halo_scaled_ref, key_scaled_ref,
    query_scaled_ref, query_scale_ref, cos_ref, sin_ref, across_ref,
    far_key_ref, near_key_ref, own_key_ref, grad_query_ref, gain_ref,
):
    rows = far_ref.shape[0]
    heads = far_ref.shape[1] // HEAD
    group = out_grad_ref.shape[1] // far_ref.shape[1]
    halo = WINDOW
    keys = halo + rows
    cos_across, sin_across = across_ref[0] * SCALE, across_ref[1] * SCALE
    query_gain = across_ref[2]
    query_acc = jnp.zeros((HEAD, rows), F32)
    key_acc = jnp.zeros((keys, HEAD), F32)
    key_acc_turned = jnp.zeros((keys, HEAD), F32)

    def prob_grad_of(head):
        cols = slice(head * HEAD, (head + 1) * HEAD)
        values = jnp.concatenate([far_ref[:, cols], near_ref[:, cols], value_ref[:, cols]], 0)
        return lax.dot_general(
            values, stacked(out_grad_ref, head, group), (((1,), (1,)), ((), ())),
            preferred_element_type=F32,
        )

    later = prob_grad_of(0)
    for head in range(heads):
        prob_grad = later
        if head + 1 < heads:
            later = prob_grad_of(head + 1)
        cols = slice(head * HEAD, (head + 1) * HEAD)
        halo_part = slice(head * halo, (head + 1) * halo)
        own_part = slice(head * rows, (head + 1) * rows)
        group_part = slice(head * group * rows, (head + 1) * group * rows)
        score_grads = []
        for one in range(group):
            place = (slice(head * keys, (head + 1) * keys), slice(one * rows, (one + 1) * rows))
            part = prob_grad[:, place[1]]
            inverse = inverse_ref[head : head + 1, place[1]]
            delta = jnp.sum(exps_ref[place] * part, axis=0, keepdims=True) * inverse
            score_grads.append((exps_ref[place] * inverse * (part - delta)).astype(BF16))
        score_grad = jnp.concatenate(score_grads, 1)
        key_term = (
            jnp.dot(score_grad, query_rot_ref[group_part, :], preferred_element_type=F32) * SCALE
        )
        keys_across = jnp.concatenate([halo_across_ref[cols, :], key_across_ref[cols, :]], 1)
        query_term = jnp.dot(keys_across, score_grad, preferred_element_type=F32)
        halo_key = key_term[:halo].astype(BF16)
        far_key_ref[:, cols] = halo_key[:rows]
        near_key_ref[:, cols] = halo_key[rows:]
        own_key_ref[:, cols] = key_term[halo:]
        term = jnp.concatenate([halo_key.astype(F32), key_term[halo:]], 0)
        scaled = jnp.concatenate([halo_scaled_ref[halo_part, :], key_scaled_ref[own_part, :]], 0)
        key_acc = key_acc + term * scaled
        key_acc_turned = key_acc_turned + term * roll_half(scaled)
        for one in range(group):
            index = head * group + one
            across = slice(index * HEAD, (index + 1) * HEAD)
            grad = query_term[:, one * rows : (one + 1) * rows]
            turned = jnp.concatenate([grad[HALF:], grad[:HALF]], 0)
            normed_grad = grad * cos_across - turned * sin_across
            scaled = query_scaled_ref[across, :]
            query_acc = query_acc + normed_grad * scaled
            weighted = normed_grad * query_gain
            mean = jnp.sum(weighted * scaled, axis=0, keepdims=True) * (1.0 / HEAD)
            raw_grad = query_scale_ref[index : index + 1, :] * (weighted - scaled * mean)
            grad_query_ref[:, across] = raw_grad.T.astype(BF16)
    query_sum = jnp.sum(query_acc.T, axis=0, keepdims=True)
    key_sum = jnp.sum(key_acc * cos_ref[...], axis=0, keepdims=True)
    turned_sum = jnp.sum(key_acc_turned * sin_ref[...], axis=0, keepdims=True)
    gain_ref[...] = jnp.concatenate([query_sum, key_sum + turned_gain(turned_sum)], 0)


def spread_kernel(gain_ref, far_value_ref, copies_ref):
    copies_ref[...] = jnp.broadcast_to(gain_ref[...][None], copies_ref.shape)


def finish_values_kernel(own_ref, far_ref, near_ref, grad_value_ref):
    total = own_ref[...] + near_ref[...].astype(F32) + far_ref[...].astype(F32)
    grad_value_ref[...] = total.astype(BF16)


def finish_keys_kernel(
    key_hbm, own_ref, far_ref, near_ref, tables_ref, gains_ref, grad_key_ref, key_ref, sem
):
    load = pltpu.make_async_copy(key_hbm, key_ref, sem)
    load.start()
    cos, sin = tables_ref[0], tables_ref[1]
    gain = gains_ref[1:2]
    load.wait()
    for head in range(own_ref.shape[1] // HEAD):
        cols = slice(head * HEAD, (head + 1) * HEAD)
        x = key_ref[:, cols].astype(F32)
        scale = row_scale(x)
        total = own_ref[:, cols] + near_ref[:, cols].astype(F32) + far_ref[:, cols].astype(F32)
        grad, _ = norm_backward(total, roll_half(total), x * scale, scale, gain, cos, sin)
        grad_key_ref[:, cols] = grad.astype(BF16)


def sum_kernel(parts_ref, query_gain_ref, key_gain_ref):
    sums = jnp.sum(parts_ref[...], axis=0)
    query_gain_ref[...] = sums[:1]
    key_gain_ref[...] = sums[1:]


def call(kernel, name, outs, operands, cost=None, far=0, scratch=()):
    spaces = [pltpu.HBM] * far + [pltpu.VMEM] * (len(operands) - far)
    return pl.pallas_call(
        kernel,
        out_shape=outs,
        in_specs=[pl.BlockSpec(memory_space=space) for space in spaces],
        out_specs=[pl.BlockSpec(memory_space=pltpu.VMEM)] * len(outs),
        scratch_shapes=scratch,
        compiler_params=pltpu.CompilerParams(vmem_limit_bytes=VMEM_LIMIT),
        cost_estimate=cost,
        name=name,
    )(*[pltpu.with_memory_space_constraint(x, pltpu.HBM) for x in operands[:far]], *operands[far:])


def cost(flops, size, exps=0):
    return pl.CostEstimate(flops=flops, bytes_accessed=size, transcendentals=exps)


def shape(dims, dtype):
    return jax.ShapeDtypeStruct(dims, dtype)


def on_device(doc_lengths, query_raw, key_raw, value_matrix, out_grad, query_gain, key_gain):
    rows, query_width = query_raw.shape
    width = key_raw.shape[1]
    heads = width // HEAD
    query_heads = query_width // HEAD
    keys = WINDOW + rows
    devices = lax.axis_size(AXES)
    query_gain = query_gain.reshape(1, HEAD)
    key_gain = key_gain.reshape(1, HEAD)
    near_key, far_key = shift(key_raw, 1), shift(key_raw, 2)
    term = shape((rows, width), BF16)
    own = shape((rows, width), F32)
    (
        query_rot, query_scaled, query_scale, key_rot, key_across, key_scaled,
        cos, sin, own_tables, across, bias, values, grads_out, gains,
    ) = call(
        prepare_kernel,
        "prepare",
        [
            shape((query_heads * rows, HEAD), BF16),
            shape((query_width, rows), F32),
            shape((query_heads, rows), F32),
            shape((heads * rows, HEAD), BF16),
            shape((width, rows), BF16),
            shape((heads * rows, HEAD), F32),
            shape((keys, HEAD), F32),
            shape((keys, HEAD), F32),
            shape((2, rows, HEAD), F32),
            shape((3, HEAD, rows), F32),
            shape((keys, rows), F32),
            term,
            shape((rows, query_width), BF16),
            shape((8, HEAD), F32),
        ],
        (doc_lengths, query_raw, key_raw, value_matrix, out_grad, query_gain, key_gain),
        cost(4_000_000, 6_000_000),
        far=7,
        scratch=[
            pltpu.SMEM(doc_lengths.shape, jnp.int32),
            pltpu.VMEM((rows, query_width), BF16),
            pltpu.VMEM((rows, width), BF16),
            pltpu.SemaphoreType.DMA((7,)),
        ],
    )
    near_value, far_value = shift(values, 1), shift(values, 2)
    exps, inverse, halo_across, halo_scaled, far_value_term, near_value_term, own_value = call(
        attend_keys_kernel,
        "attend_keys",
        [
            shape((heads * keys, query_heads // heads * rows), F32),
            shape((heads, query_heads // heads * rows), F32),
            shape((width, WINDOW), BF16),
            shape((heads * WINDOW, HEAD), F32),
            term,
            term,
            own,
        ],
        (near_key, far_key, grads_out, query_rot, key_rot, cos, sin, bias, gains),
        cost(400_000_000, 4_000_000, 800_000),
    )
    near_value_back, far_value_back = shift(near_value_term, -1), shift(far_value_term, -2)
    far_key_term, near_key_term, own_key, grad_query, gain_part = call(
        attend_values_kernel,
        "attend_values",
        [term, term, own, shape((rows, query_width), BF16), shape((2, HEAD), F32)],
        (
            far_value, near_value, values, grads_out, exps, inverse, query_rot,
            halo_across, key_across, halo_scaled, key_scaled, query_scaled, query_scale, cos, sin, across,
        ),
        cost(600_000_000, 4_000_000),
    )
    near_key_back, far_key_back = shift(near_key_term, -1), shift(far_key_term, -2)
    (copies,) = call(
        spread_kernel, "spread_gains", [shape((devices, 2, HEAD), F32)], (gain_part, far_value_back)
    )
    parts = lax.all_to_all(copies, AXES, 0, 0)
    (grad_value,) = call(
        finish_values_kernel,
        "finish_values",
        [term],
        (own_value, far_value_back, near_value_back),
        cost(1_000_000, 2_000_000),
    )
    (grad_key,) = call(
        finish_keys_kernel,
        "finish_keys",
        [term],
        (key_raw, own_key, far_key_back, near_key_back, own_tables, gains),
        cost(4_000_000, 3_000_000),
        far=1,
        scratch=[pltpu.VMEM((rows, width), BF16), pltpu.SemaphoreType.DMA],
    )
    grad_query_gain, grad_key_gain = call(
        sum_kernel, "sum_gains", [shape((1, HEAD), F32), shape((1, HEAD), F32)], (parts,)
    )
    return (
        grad_query, grad_key, grad_value, grad_query_gain.reshape(HEAD), grad_key_gain.reshape(HEAD)
    )


def solution(mesh):
    rows = P(AXES, None)
    return jax.shard_map(
        on_device,
        mesh=mesh,
        in_specs=(P(), rows, rows, rows, rows, P(), P()),
        out_specs=(rows, rows, rows, P(), P()),
        check_vma=False,
    )
```

```python
import math

import jax
import jax.numpy as jnp
import numpy as np
from jax import lax
from jax.experimental import pallas as pl
from jax.experimental.pallas import tpu as pltpu
from jax.sharding import PartitionSpec as P

HEAD = 128
HALF = HEAD // 2
WINDOW = 256
EPS = 1e-06
SCALE = 168.0 ** (-0.5)
ROPE_BASE = 10000.0
MASKED = -1e30
AXES = ("ctx", "grp")
F32 = jnp.float32
BF16 = jnp.bfloat16
VMEM_LIMIT = 32 * 1024 * 1024


def frequencies():
    lane = lax.broadcasted_iota(jnp.int32, (1, HEAD), 1) % HALF
    values = jnp.zeros((1, HEAD), F32)
    for m in range(HALF):
        values = jnp.where(lane == m, np.float32(ROPE_BASE ** (-2.0 * m / HEAD)), values)
    return values


def shift(value, steps):
    count = lax.axis_size(AXES)
    return lax.ppermute(value, AXES, [(s, (s + steps) % count) for s in range(count)])


def own_index():
    return lax.axis_index("ctx") * lax.axis_size("grp") + lax.axis_index("grp")


def roll_half(x):
    return pltpu.roll(x, HALF, 1)


def doc_starts(tokens, lengths_ref):
    def step(doc, carry):
        end, starts = carry
        end = end + lengths_ref[doc]
        return end, jnp.where(tokens >= end, end, starts)

    count = lengths_ref.shape[0]
    return lax.fori_loop(
        0, count, step, (jnp.int32(0), jnp.zeros_like(tokens)), unroll=count if count <= 8 else 1
    )[1]


def cos_sin_lanes(angle, lane):
    turns = jnp.floor(angle * (2.0 / math.pi) + 0.5)
    r = angle - turns * 1.5703125
    r = r - turns * 4.837512969970703125e-4
    r = r - turns * 7.549789948768648e-8
    z = r * r
    sin_r = r + r * z * (-1.6666654611e-1 + z * (8.3321608736e-3 + z * -1.9515295891e-4))
    cos_r = 1.0 - 0.5 * z + z * z * (
        4.166664568298827e-2 + z * (-1.388731625493765e-3 + z * 2.443315711809948e-5)
    )
    quadrant = turns.astype(jnp.int32) - jnp.where(lane >= HALF, 1, 0)
    odd = (quadrant & 1) == 1
    value = jnp.where(odd, sin_r, cos_r)
    negative = ((quadrant + 1) & 2) == 2
    return jnp.where(negative, -value, value)


def ones(rows, columns):
    return jnp.ones((rows, columns), BF16)


def split(x):
    high = x.astype(BF16)
    low = (x - high.astype(F32)).astype(BF16)
    return jnp.concatenate([high, low], 1)


def row_sums(x):
    return jnp.dot(split(x), ones(2 * HEAD, HEAD), preferred_element_type=F32)


def row_scale(x):
    return lax.rsqrt(row_sums(x * x) * (1.0 / HEAD) + EPS)


def turning():
    source = lax.broadcasted_iota(jnp.int32, (HEAD, HEAD), 0)
    target = lax.broadcasted_iota(jnp.int32, (HEAD, HEAD), 1)
    return jnp.where(target == (source + HALF) % HEAD, 1.0, 0.0).astype(BF16)


def turned_rows(raw, matrix):
    return jnp.dot(raw, matrix, preferred_element_type=F32)


def turned_gain(gain):
    return roll_half(jnp.broadcast_to(gain, (8, HEAD)))[:1]


def prepare_kernel(
    lengths_hbm, query_hbm, key_hbm, value_hbm, out_grad_hbm, query_gain_hbm, key_gain_hbm,
    query_rot_ref, query_scaled_ref, key_rot_ref, key_across_ref,
    key_scaled_ref, cos_ref, sin_ref, own_tables_ref, across_ref, bias_ref,
    value_ref, out_grad_ref, gains_ref,
    lengths_ref, query_ref, key_ref, sems,
):
    moves = [
        pltpu.make_async_copy(source, target, sems.at[place])
        for place, (source, target) in enumerate(
            (
                (lengths_hbm, lengths_ref),
                (query_gain_hbm, gains_ref.at[0:1]),
                (key_gain_hbm, gains_ref.at[1:2]),
                (key_hbm, key_ref),
                (query_hbm, query_ref),
                (out_grad_hbm, out_grad_ref),
                (value_hbm, value_ref),
            )
        )
    ]
    for move in moves:
        move.start()
    rows = query_ref.shape[0]
    keys = cos_ref.shape[0]
    base = own_index() * rows - (keys - rows)
    shape = (keys, HEAD)
    lane = lax.broadcasted_iota(jnp.int32, shape, 1)
    tokens = base + lax.broadcasted_iota(jnp.int32, shape, 0)
    frequency = frequencies()
    moves[0].wait()
    positions = tokens - doc_starts(tokens, lengths_ref)
    mixed = cos_sin_lanes(positions.astype(F32) * frequency, lane)
    turned = roll_half(mixed)
    cos = jnp.where(lane < HALF, mixed, turned)
    sin = jnp.where(lane < HALF, -turned, mixed)
    cos_ref[...] = cos
    sin_ref[...] = sin
    queries = base + (keys - rows) + lax.broadcasted_iota(jnp.int32, (1, rows), 1)
    lowest = jnp.maximum(doc_starts(queries, lengths_ref), queries - (WINDOW - 1))
    key_tokens = base + lax.broadcasted_iota(jnp.int32, (keys, rows), 0)
    visible = (key_tokens >= lowest) & (key_tokens <= queries)
    bias_ref[...] = jnp.where(visible, 0.0, MASKED)
    own_cos, own_sin = cos[keys - rows :], sin[keys - rows :]
    moves[1].wait()
    moves[2].wait()
    own_tables_ref[0] = own_cos
    own_tables_ref[1] = own_sin
    across_ref[0] = own_cos.T
    across_ref[1] = own_sin.T
    matrix = turning()
    for raw_ref, move, row, rot_ref in (
        (key_ref, moves[3], 1, key_rot_ref),
        (query_ref, moves[4], 0, query_rot_ref),
    ):
        gain = gains_ref[row : row + 1]
        cos_gain = own_cos * gain
        sin_gain = own_sin * turned_gain(gain)
        move.wait()
        for head in range(raw_ref.shape[1] // HEAD):
            part = slice(head * rows, (head + 1) * rows)
            across = slice(head * HEAD, (head + 1) * HEAD)
            raw = raw_ref[:, across]
            x = raw.astype(F32)
            scale = row_scale(x)
            scaled = x * scale
            turned = turned_rows(raw, matrix) * scale
            rotated = scaled * cos_gain + turned * sin_gain
            rot_ref[part, :] = rotated.astype(BF16)
            if raw_ref is key_ref:
                key_scaled_ref[part, :] = scaled
                key_across_ref[across, :] = rotated.T.astype(BF16)
            else:
                query_scaled_ref[across, :] = scaled.T
    moves[5].wait()
    moves[6].wait()


def stacked(ref, head, group):
    return jnp.concatenate(
        [ref[:, (head * group + one) * HEAD : (head * group + one + 1) * HEAD] for one in range(group)],
        0,
    )


def attend_keys_kernel(
    near_ref, far_ref, out_grad_ref, query_rot_ref, key_rot_ref, cos_ref, sin_ref, bias_ref,
    gains_ref,
    exps_ref, inverse_ref, halo_across_ref, halo_scaled_ref, far_value_ref, near_value_ref, own_value_ref,
):
    rows = far_ref.shape[0]
    heads = far_ref.shape[1] // HEAD
    group = out_grad_ref.shape[1] // far_ref.shape[1]
    halo = WINDOW
    keys = halo + rows
    key_gain = gains_ref[1:2]
    cos_gain = cos_ref[:halo] * key_gain
    sin_gain = sin_ref[:halo] * turned_gain(key_gain)
    matrix = turning()

    def scores_of(head):
        cols = slice(head * HEAD, (head + 1) * HEAD)
        raw = jnp.concatenate([far_ref[:, cols], near_ref[:, cols]], 0)
        x = raw.astype(F32)
        scale = row_scale(x)
        scaled = x * scale
        turned = turned_rows(raw, matrix) * scale
        part = slice(head * halo, (head + 1) * halo)
        halo_scaled_ref[part, :] = scaled
        rotated = scaled * cos_gain + turned * sin_gain
        halo_across_ref[cols, :] = rotated.T.astype(BF16)
        both = jnp.concatenate(
            [rotated.astype(BF16), key_rot_ref[head * rows : (head + 1) * rows, :]], 0
        )
        queries = query_rot_ref[head * group * rows : (head + 1) * group * rows, :]
        return lax.dot_general(
            both, queries, (((1,), (1,)), ((), ())), preferred_element_type=F32
        )

    later = scores_of(0)
    for head in range(heads):
        scores = later
        if head + 1 < heads:
            later = scores_of(head + 1)
        cols = slice(head * HEAD, (head + 1) * HEAD)
        low = []
        for one in range(group):
            place = (slice(head * keys, (head + 1) * keys), slice(one * rows, (one + 1) * rows))
            part = scores[:, place[1]] * (SCALE * math.log2(math.e)) + bias_ref[...]
            exps = jnp.exp2(part - jnp.max(part, axis=0, keepdims=True))
            exps_ref[place] = exps
            inverse = 1.0 / jnp.sum(exps, axis=0, keepdims=True)
            inverse_ref[head : head + 1, place[1]] = inverse
            low.append((exps_ref[place] * inverse).astype(BF16))
        value_term = jnp.dot(
            jnp.concatenate(low, 1), stacked(out_grad_ref, head, group), preferred_element_type=F32
        )
        far_value_ref[:, cols] = value_term[:rows].astype(BF16)
        near_value_ref[:, cols] = value_term[rows:halo].astype(BF16)
        own_value_ref[:, cols] = value_term[halo:]


def norm_backward(normed_grad, scaled, scale, gain):
    weighted = normed_grad * gain
    mean = row_sums(weighted * scaled) * (1.0 / HEAD)
    return scale * (weighted - scaled * mean)


def attend_values_kernel(
    far_ref, near_ref, value_ref, out_grad_ref, exps_ref, inverse_ref, query_rot_ref,
    halo_across_ref, key_across_ref, halo_scaled_ref, key_scaled_ref,
    query_scaled_ref, cos_ref, sin_ref, across_ref,
    far_key_ref, near_key_ref, own_key_ref, query_grad_ref, gain_ref,
):
    rows = far_ref.shape[0]
    heads = far_ref.shape[1] // HEAD
    group = out_grad_ref.shape[1] // far_ref.shape[1]
    halo = WINDOW
    keys = halo + rows
    cos_across, sin_across = across_ref[0] * SCALE, across_ref[1] * SCALE
    query_acc = jnp.zeros((HEAD, rows), F32)
    key_acc = jnp.zeros((keys, HEAD), F32)
    key_acc_turned = jnp.zeros((keys, HEAD), F32)

    def prob_grad_of(head):
        cols = slice(head * HEAD, (head + 1) * HEAD)
        values = jnp.concatenate([far_ref[:, cols], near_ref[:, cols], value_ref[:, cols]], 0)
        return lax.dot_general(
            values, stacked(out_grad_ref, head, group), (((1,), (1,)), ((), ())),
            preferred_element_type=F32,
        )

    later = prob_grad_of(0)
    for head in range(heads):
        prob_grad = later
        if head + 1 < heads:
            later = prob_grad_of(head + 1)
        cols = slice(head * HEAD, (head + 1) * HEAD)
        halo_part = slice(head * halo, (head + 1) * halo)
        own_part = slice(head * rows, (head + 1) * rows)
        group_part = slice(head * group * rows, (head + 1) * group * rows)
        score_grads = []
        for one in range(group):
            place = (slice(head * keys, (head + 1) * keys), slice(one * rows, (one + 1) * rows))
            part = prob_grad[:, place[1]]
            inverse = inverse_ref[head : head + 1, place[1]]
            delta = jnp.sum(exps_ref[place] * part, axis=0, keepdims=True) * inverse
            score_grads.append((exps_ref[place] * inverse * (part - delta)).astype(BF16))
        score_grad = jnp.concatenate(score_grads, 1)
        key_term = (
            jnp.dot(score_grad, query_rot_ref[group_part, :], preferred_element_type=F32) * SCALE
        )
        keys_across = jnp.concatenate([halo_across_ref[cols, :], key_across_ref[cols, :]], 1)
        query_term = jnp.dot(keys_across, score_grad, preferred_element_type=F32)
        halo_key = key_term[:halo].astype(BF16)
        far_key_ref[:, cols] = halo_key[:rows]
        near_key_ref[:, cols] = halo_key[rows:]
        own_key_ref[:, cols] = key_term[halo:]
        term = jnp.concatenate([halo_key.astype(F32), key_term[halo:]], 0)
        scaled = jnp.concatenate([halo_scaled_ref[halo_part, :], key_scaled_ref[own_part, :]], 0)
        key_acc = key_acc + term * scaled
        key_acc_turned = key_acc_turned + term * roll_half(scaled)
        for one in range(group):
            index = head * group + one
            across = slice(index * HEAD, (index + 1) * HEAD)
            grad = query_term[:, one * rows : (one + 1) * rows]
            turned = jnp.concatenate([grad[HALF:], grad[:HALF]], 0)
            normed_grad = grad * cos_across - turned * sin_across
            query_acc = query_acc + normed_grad * query_scaled_ref[across, :]
            query_grad_ref[across, :] = normed_grad.astype(BF16)
    query_sum = jnp.sum(query_acc.T, axis=0, keepdims=True)
    key_sum = jnp.sum(key_acc * cos_ref[...], axis=0, keepdims=True)
    turned_sum = jnp.sum(key_acc_turned * sin_ref[...], axis=0, keepdims=True)
    gain_ref[...] = jnp.concatenate([query_sum, key_sum + turned_gain(turned_sum)], 0)


def spread_kernel(gain_ref, far_value_ref, copies_ref):
    copies_ref[...] = jnp.broadcast_to(gain_ref[...][None], copies_ref.shape)


def finish_values_kernel(own_ref, far_ref, near_ref, grad_value_ref):
    total = own_ref[...] + near_ref[...].astype(F32) + far_ref[...].astype(F32)
    grad_value_ref[...] = total.astype(BF16)


def finish_queries_kernel(
    query_hbm, key_hbm, query_grad_ref, gains_ref,
    grad_query_ref, key_scaled_ref, key_scale_ref,
    query_ref, key_ref, sems,
):
    rows = query_ref.shape[0]
    loads = [
        pltpu.make_async_copy(query_hbm, query_ref, sems.at[0]),
        pltpu.make_async_copy(key_hbm, key_ref, sems.at[1]),
    ]
    for load in loads:
        load.start()
    gain = gains_ref[0:1]
    loads[0].wait()
    for head in range(query_ref.shape[1] // HEAD):
        cols = slice(head * HEAD, (head + 1) * HEAD)
        x = query_ref[:, cols].astype(F32)
        scale = row_scale(x)
        normed_grad = query_grad_ref[cols, :].astype(F32).T
        grad_query_ref[:, cols] = norm_backward(normed_grad, x * scale, scale, gain).astype(BF16)
    loads[1].wait()
    for head in range(key_ref.shape[1] // HEAD):
        part = slice(head * rows, (head + 1) * rows)
        x = key_ref[:, head * HEAD : (head + 1) * HEAD].astype(F32)
        scale = row_scale(x)
        key_scale_ref[part, :] = scale
        key_scaled_ref[part, :] = x * scale


def finish_keys_kernel(
    own_ref, far_ref, near_ref, key_scaled_ref, key_scale_ref, tables_ref, gains_ref, grad_key_ref
):
    rows = own_ref.shape[0]
    cos, sin = tables_ref[0], tables_ref[1]
    gain = gains_ref[1:2]
    for head in range(own_ref.shape[1] // HEAD):
        cols = slice(head * HEAD, (head + 1) * HEAD)
        part = slice(head * rows, (head + 1) * rows)
        total = own_ref[:, cols] + near_ref[:, cols].astype(F32) + far_ref[:, cols].astype(F32)
        normed_grad = total * cos - roll_half(total) * sin
        grad = norm_backward(normed_grad, key_scaled_ref[part, :], key_scale_ref[part, :], gain)
        grad_key_ref[:, cols] = grad.astype(BF16)


def sum_kernel(parts_ref, query_gain_ref, key_gain_ref):
    sums = jnp.sum(parts_ref[...], axis=0)
    query_gain_ref[...] = sums[:1]
    key_gain_ref[...] = sums[1:]


def call(kernel, name, outs, operands, cost=None, far=0, scratch=()):
    spaces = [pltpu.HBM] * far + [pltpu.VMEM] * (len(operands) - far)
    return pl.pallas_call(
        kernel,
        out_shape=outs,
        in_specs=[pl.BlockSpec(memory_space=space) for space in spaces],
        out_specs=[pl.BlockSpec(memory_space=pltpu.VMEM)] * len(outs),
        scratch_shapes=scratch,
        compiler_params=pltpu.CompilerParams(vmem_limit_bytes=VMEM_LIMIT),
        cost_estimate=cost,
        name=name,
    )(*[pltpu.with_memory_space_constraint(x, pltpu.HBM) for x in operands[:far]], *operands[far:])


def cost(flops, size, exps=0):
    return pl.CostEstimate(flops=flops, bytes_accessed=size, transcendentals=exps)


def shape(dims, dtype):
    return jax.ShapeDtypeStruct(dims, dtype)


def on_device(doc_lengths, query_raw, key_raw, value_matrix, out_grad, query_gain, key_gain):
    rows, query_width = query_raw.shape
    width = key_raw.shape[1]
    heads = width // HEAD
    query_heads = query_width // HEAD
    keys = WINDOW + rows
    devices = lax.axis_size(AXES)
    query_gain = query_gain.reshape(1, HEAD)
    key_gain = key_gain.reshape(1, HEAD)
    near_key, far_key = shift(key_raw, 1), shift(key_raw, 2)
    term = shape((rows, width), BF16)
    own = shape((rows, width), F32)
    (
        query_rot, query_scaled, key_rot, key_across, key_scaled,
        cos, sin, own_tables, across, bias, values, grads_out, gains,
    ) = call(
        prepare_kernel,
        "prepare",
        [
            shape((query_heads * rows, HEAD), BF16),
            shape((query_width, rows), F32),
            shape((heads * rows, HEAD), BF16),
            shape((width, rows), BF16),
            shape((heads * rows, HEAD), F32),
            shape((keys, HEAD), F32),
            shape((keys, HEAD), F32),
            shape((2, rows, HEAD), F32),
            shape((2, HEAD, rows), F32),
            shape((keys, rows), F32),
            term,
            shape((rows, query_width), BF16),
            shape((8, HEAD), F32),
        ],
        (doc_lengths, query_raw, key_raw, value_matrix, out_grad, query_gain, key_gain),
        cost(4_000_000, 6_000_000),
        far=7,
        scratch=[
            pltpu.SMEM(doc_lengths.shape, jnp.int32),
            pltpu.VMEM((rows, query_width), BF16),
            pltpu.VMEM((rows, width), BF16),
            pltpu.SemaphoreType.DMA((7,)),
        ],
    )
    near_value, far_value = shift(values, 1), shift(values, 2)
    exps, inverse, halo_across, halo_scaled, far_value_term, near_value_term, own_value = call(
        attend_keys_kernel,
        "attend_keys",
        [
            shape((heads * keys, query_heads // heads * rows), F32),
            shape((heads, query_heads // heads * rows), F32),
            shape((width, WINDOW), BF16),
            shape((heads * WINDOW, HEAD), F32),
            term,
            term,
            own,
        ],
        (near_key, far_key, grads_out, query_rot, key_rot, cos, sin, bias, gains),
        cost(400_000_000, 4_000_000, 800_000),
    )
    near_value_back, far_value_back = shift(near_value_term, -1), shift(far_value_term, -2)
    far_key_term, near_key_term, own_key, query_grad, gain_part = call(
        attend_values_kernel,
        "attend_values",
        [term, term, own, shape((query_width, rows), BF16), shape((2, HEAD), F32)],
        (
            far_value, near_value, values, grads_out, exps, inverse, query_rot,
            halo_across, key_across, halo_scaled, key_scaled, query_scaled, cos, sin, across,
        ),
        cost(600_000_000, 4_000_000),
    )
    near_key_back, far_key_back = shift(near_key_term, -1), shift(far_key_term, -2)
    (copies,) = call(
        spread_kernel, "spread_gains", [shape((devices, 2, HEAD), F32)], (gain_part, far_value_back)
    )
    parts = lax.all_to_all(copies, AXES, 0, 0)
    (grad_value,) = call(
        finish_values_kernel,
        "finish_values",
        [term],
        (own_value, far_value_back, near_value_back),
        cost(1_000_000, 2_000_000),
    )
    grad_query, key_scaled, key_scale = call(
        finish_queries_kernel,
        "finish_queries",
        [
            shape((rows, query_width), BF16),
            shape((heads * rows, HEAD), F32),
            shape((heads * rows, HEAD), F32),
        ],
        (query_raw, key_raw, query_grad, gains),
        cost(4_000_000, 4_000_000),
        far=2,
        scratch=[
            pltpu.VMEM((rows, query_width), BF16),
            pltpu.VMEM((rows, width), BF16),
            pltpu.SemaphoreType.DMA((2,)),
        ],
    )
    (grad_key,) = call(
        finish_keys_kernel,
        "finish_keys",
        [term],
        (own_key, far_key_back, near_key_back, key_scaled, key_scale, own_tables, gains),
        cost(4_000_000, 3_000_000),
    )
    grad_query_gain, grad_key_gain = call(
        sum_kernel, "sum_gains", [shape((1, HEAD), F32), shape((1, HEAD), F32)], (parts,)
    )
    return (
        grad_query, grad_key, grad_value, grad_query_gain.reshape(HEAD), grad_key_gain.reshape(HEAD)
    )


def solution(mesh):
    rows = P(AXES, None)
    return jax.shard_map(
        on_device,
        mesh=mesh,
        in_specs=(P(), rows, rows, rows, rows, P(), P()),
        out_specs=(rows, rows, rows, P(), P()),
        check_vma=False,
    )
```

```python
import math

import jax
import jax.numpy as jnp
import numpy as np
from jax import lax
from jax.experimental import pallas as pl
from jax.experimental.pallas import tpu as pltpu
from jax.sharding import PartitionSpec as P

HEAD = 128
HALF = HEAD // 2
WINDOW = 256
EPS = 1e-06
SCALE = 168.0 ** (-0.5)
ROPE_BASE = 10000.0
MASKED = -1e30
AXES = ("ctx", "grp")
F32 = jnp.float32
BF16 = jnp.bfloat16
VMEM_LIMIT = 32 * 1024 * 1024


def frequencies():
    lane = lax.broadcasted_iota(jnp.int32, (1, HEAD), 1) % HALF
    values = jnp.zeros((1, HEAD), F32)
    for m in range(HALF):
        values = jnp.where(lane == m, np.float32(ROPE_BASE ** (-2.0 * m / HEAD)), values)
    return values


def shift(value, steps):
    count = lax.axis_size(AXES)
    return lax.ppermute(value, AXES, [(s, (s + steps) % count) for s in range(count)])


def own_index():
    return lax.axis_index("ctx") * lax.axis_size("grp") + lax.axis_index("grp")


def roll_half(x):
    return pltpu.roll(x, HALF, 1)


def doc_starts(tokens, lengths_ref):
    def step(doc, carry):
        end, starts = carry
        end = end + lengths_ref[doc]
        return end, jnp.where(tokens >= end, end, starts)

    count = lengths_ref.shape[0]
    return lax.fori_loop(
        0, count, step, (jnp.int32(0), jnp.zeros_like(tokens)), unroll=count if count <= 8 else 1
    )[1]


def cos_sin_lanes(angle, lane):
    turns = jnp.floor(angle * (2.0 / math.pi) + 0.5)
    r = angle - turns * 1.5703125
    r = r - turns * 4.837512969970703125e-4
    r = r - turns * 7.549789948768648e-8
    z = r * r
    sin_r = r + r * z * (-1.6666654611e-1 + z * (8.3321608736e-3 + z * -1.9515295891e-4))
    cos_r = 1.0 - 0.5 * z + z * z * (
        4.166664568298827e-2 + z * (-1.388731625493765e-3 + z * 2.443315711809948e-5)
    )
    quadrant = turns.astype(jnp.int32) - jnp.where(lane >= HALF, 1, 0)
    odd = (quadrant & 1) == 1
    value = jnp.where(odd, sin_r, cos_r)
    negative = ((quadrant + 1) & 2) == 2
    return jnp.where(negative, -value, value)


def ones(rows, columns):
    return jnp.ones((rows, columns), BF16)


def split(x):
    high = x.astype(BF16)
    low = (x - high.astype(F32)).astype(BF16)
    return jnp.concatenate([high, low], 1)


def row_sums(x):
    return jnp.dot(split(x), ones(2 * HEAD, HEAD), preferred_element_type=F32)


def row_scale(x):
    return lax.rsqrt(row_sums(x * x) * (1.0 / HEAD) + EPS)


def turning():
    source = lax.broadcasted_iota(jnp.int32, (HEAD, HEAD), 0)
    target = lax.broadcasted_iota(jnp.int32, (HEAD, HEAD), 1)
    return jnp.where(target == (source + HALF) % HEAD, 1.0, 0.0).astype(BF16)


def turned_rows(raw, matrix):
    return jnp.dot(raw, matrix, preferred_element_type=F32)


def turned_gain(gain):
    return roll_half(jnp.broadcast_to(gain, (8, HEAD)))[:1]


def prepare_kernel(
    lengths_hbm, query_hbm, key_hbm, value_hbm, out_grad_hbm, query_gain_hbm, key_gain_hbm,
    query_rot_ref, query_scaled_ref, key_rot_ref, key_across_ref,
    key_scaled_ref, cos_ref, sin_ref, own_tables_ref, across_ref, bias_ref,
    value_ref, out_grad_ref, gains_ref,
    lengths_ref, query_ref, key_ref, sems,
):
    moves = [
        pltpu.make_async_copy(source, target, sems.at[place])
        for place, (source, target) in enumerate(
            (
                (lengths_hbm, lengths_ref),
                (query_gain_hbm, gains_ref.at[0:1]),
                (key_gain_hbm, gains_ref.at[1:2]),
                (key_hbm, key_ref),
                (query_hbm, query_ref),
                (out_grad_hbm, out_grad_ref),
                (value_hbm, value_ref),
            )
        )
    ]
    for move in moves:
        move.start()
    rows = query_ref.shape[0]
    keys = cos_ref.shape[0]
    base = own_index() * rows - (keys - rows)
    shape = (keys, HEAD)
    lane = lax.broadcasted_iota(jnp.int32, shape, 1)
    tokens = base + lax.broadcasted_iota(jnp.int32, shape, 0)
    frequency = frequencies()
    moves[0].wait()
    positions = tokens - doc_starts(tokens, lengths_ref)
    mixed = cos_sin_lanes(positions.astype(F32) * frequency, lane)
    turned = roll_half(mixed)
    cos = jnp.where(lane < HALF, mixed, turned)
    sin = jnp.where(lane < HALF, -turned, mixed)
    cos_ref[...] = cos
    sin_ref[...] = sin
    queries = base + (keys - rows) + lax.broadcasted_iota(jnp.int32, (1, rows), 1)
    lowest = jnp.maximum(doc_starts(queries, lengths_ref), queries - (WINDOW - 1))
    key_tokens = base + lax.broadcasted_iota(jnp.int32, (keys, rows), 0)
    visible = (key_tokens >= lowest) & (key_tokens <= queries)
    bias_ref[...] = jnp.where(visible, 0.0, MASKED)
    own_cos, own_sin = cos[keys - rows :], sin[keys - rows :]
    moves[1].wait()
    moves[2].wait()
    own_tables_ref[0] = own_cos
    own_tables_ref[1] = own_sin
    across_ref[0] = own_cos.T
    across_ref[1] = own_sin.T
    matrix = turning()
    for raw_ref, move, row, rot_ref in (
        (key_ref, moves[3], 1, key_rot_ref),
        (query_ref, moves[4], 0, query_rot_ref),
    ):
        gain = gains_ref[row : row + 1]
        cos_gain = own_cos * gain
        sin_gain = own_sin * turned_gain(gain)
        move.wait()
        for head in range(raw_ref.shape[1] // HEAD):
            part = slice(head * rows, (head + 1) * rows)
            across = slice(head * HEAD, (head + 1) * HEAD)
            raw = raw_ref[:, across]
            x = raw.astype(F32)
            scale = row_scale(x)
            scaled = x * scale
            turned = turned_rows(raw, matrix) * scale
            rotated = scaled * cos_gain + turned * sin_gain
            rot_ref[part, :] = rotated.astype(BF16)
            if raw_ref is key_ref:
                key_scaled_ref[part, :] = scaled
                key_across_ref[across, :] = rotated.T.astype(BF16)
            else:
                query_scaled_ref[across, :] = scaled.T
    moves[5].wait()
    moves[6].wait()


def stacked(ref, head, group):
    return jnp.concatenate(
        [ref[:, (head * group + one) * HEAD : (head * group + one + 1) * HEAD] for one in range(group)],
        0,
    )


def attend_keys_kernel(
    near_ref, far_ref, out_grad_ref, query_rot_ref, key_rot_ref, cos_ref, sin_ref, bias_ref,
    gains_ref,
    exps_ref, inverse_ref, halo_across_ref, halo_scaled_ref, far_value_ref, near_value_ref, own_value_ref,
):
    rows = far_ref.shape[0]
    heads = far_ref.shape[1] // HEAD
    group = out_grad_ref.shape[1] // far_ref.shape[1]
    halo = WINDOW
    keys = halo + rows
    key_gain = gains_ref[1:2]
    cos_gain = cos_ref[:halo] * key_gain
    sin_gain = sin_ref[:halo] * turned_gain(key_gain)
    matrix = turning()

    def scores_of(head):
        cols = slice(head * HEAD, (head + 1) * HEAD)
        raw = jnp.concatenate([far_ref[:, cols], near_ref[:, cols]], 0)
        x = raw.astype(F32)
        scale = row_scale(x)
        scaled = x * scale
        turned = turned_rows(raw, matrix) * scale
        part = slice(head * halo, (head + 1) * halo)
        halo_scaled_ref[part, :] = scaled
        rotated = scaled * cos_gain + turned * sin_gain
        halo_across_ref[cols, :] = rotated.T.astype(BF16)
        both = jnp.concatenate(
            [rotated.astype(BF16), key_rot_ref[head * rows : (head + 1) * rows, :]], 0
        )
        queries = query_rot_ref[head * group * rows : (head + 1) * group * rows, :]
        return lax.dot_general(
            both, queries, (((1,), (1,)), ((), ())), preferred_element_type=F32
        )

    later = scores_of(0)
    for head in range(heads):
        scores = later
        if head + 1 < heads:
            later = scores_of(head + 1)
        cols = slice(head * HEAD, (head + 1) * HEAD)
        low = []
        for one in range(group):
            place = (slice(head * keys, (head + 1) * keys), slice(one * rows, (one + 1) * rows))
            part = scores[:, place[1]] * (SCALE * math.log2(math.e)) + bias_ref[...]
            exps = jnp.exp2(part - jnp.max(part, axis=0, keepdims=True))
            exps_ref[place] = exps
            inverse = 1.0 / jnp.sum(exps, axis=0, keepdims=True)
            inverse_ref[head : head + 1, place[1]] = inverse
            low.append((exps_ref[place] * inverse).astype(BF16))
        value_term = jnp.dot(
            jnp.concatenate(low, 1), stacked(out_grad_ref, head, group), preferred_element_type=F32
        )
        far_value_ref[:, cols] = value_term[:rows].astype(BF16)
        near_value_ref[:, cols] = value_term[rows:halo].astype(BF16)
        own_value_ref[:, cols] = value_term[halo:]


def norm_backward(normed_grad, scaled, scale, gain):
    weighted = normed_grad * gain
    mean = row_sums(weighted * scaled) * (1.0 / HEAD)
    return scale * (weighted - scaled * mean)


def attend_values_kernel(
    far_ref, near_ref, value_ref, out_grad_ref, exps_ref, inverse_ref, query_rot_ref,
    halo_across_ref, key_across_ref, halo_scaled_ref, key_scaled_ref,
    query_scaled_ref, cos_ref, sin_ref, across_ref, held_ref,
    far_key_ref, near_key_ref, own_key_ref, query_grad_ref, gain_ref, far_value_ref,
):
    far_value_ref[...] = held_ref[...]
    rows = far_ref.shape[0]
    heads = far_ref.shape[1] // HEAD
    group = out_grad_ref.shape[1] // far_ref.shape[1]
    halo = WINDOW
    keys = halo + rows
    cos_across, sin_across = across_ref[0] * SCALE, across_ref[1] * SCALE
    query_acc = jnp.zeros((HEAD, rows), F32)
    key_acc = jnp.zeros((keys, HEAD), F32)
    key_acc_turned = jnp.zeros((keys, HEAD), F32)

    def prob_grad_of(head):
        cols = slice(head * HEAD, (head + 1) * HEAD)
        values = jnp.concatenate([far_ref[:, cols], near_ref[:, cols], value_ref[:, cols]], 0)
        return lax.dot_general(
            values, stacked(out_grad_ref, head, group), (((1,), (1,)), ((), ())),
            preferred_element_type=F32,
        )

    later = prob_grad_of(0)
    for head in range(heads):
        prob_grad = later
        if head + 1 < heads:
            later = prob_grad_of(head + 1)
        cols = slice(head * HEAD, (head + 1) * HEAD)
        halo_part = slice(head * halo, (head + 1) * halo)
        own_part = slice(head * rows, (head + 1) * rows)
        group_part = slice(head * group * rows, (head + 1) * group * rows)
        score_grads = []
        for one in range(group):
            place = (slice(head * keys, (head + 1) * keys), slice(one * rows, (one + 1) * rows))
            part = prob_grad[:, place[1]]
            inverse = inverse_ref[head : head + 1, place[1]]
            delta = jnp.sum(exps_ref[place] * part, axis=0, keepdims=True) * inverse
            score_grads.append((exps_ref[place] * inverse * (part - delta)).astype(BF16))
        score_grad = jnp.concatenate(score_grads, 1)
        key_term = (
            jnp.dot(score_grad, query_rot_ref[group_part, :], preferred_element_type=F32) * SCALE
        )
        keys_across = jnp.concatenate([halo_across_ref[cols, :], key_across_ref[cols, :]], 1)
        query_term = jnp.dot(keys_across, score_grad, preferred_element_type=F32)
        halo_key = key_term[:halo].astype(BF16)
        far_key_ref[:, cols] = halo_key[:rows]
        near_key_ref[:, cols] = halo_key[rows:]
        own_key_ref[:, cols] = key_term[halo:]
        term = jnp.concatenate([halo_key.astype(F32), key_term[halo:]], 0)
        scaled = jnp.concatenate([halo_scaled_ref[halo_part, :], key_scaled_ref[own_part, :]], 0)
        key_acc = key_acc + term * scaled
        key_acc_turned = key_acc_turned + term * roll_half(scaled)
        for one in range(group):
            index = head * group + one
            across = slice(index * HEAD, (index + 1) * HEAD)
            grad = query_term[:, one * rows : (one + 1) * rows]
            turned = jnp.concatenate([grad[HALF:], grad[:HALF]], 0)
            normed_grad = grad * cos_across - turned * sin_across
            query_acc = query_acc + normed_grad * query_scaled_ref[across, :]
            query_grad_ref[across, :] = normed_grad.astype(BF16)
    query_sum = jnp.sum(query_acc.T, axis=0, keepdims=True)
    key_sum = jnp.sum(key_acc * cos_ref[...], axis=0, keepdims=True)
    turned_sum = jnp.sum(key_acc_turned * sin_ref[...], axis=0, keepdims=True)
    gain_ref[...] = jnp.concatenate([query_sum, key_sum + turned_gain(turned_sum)], 0)


def spread_kernel(gain_ref, near_value_ref, copies_ref):
    copies_ref[...] = jnp.broadcast_to(gain_ref[...][None], copies_ref.shape)


def finish_values_kernel(own_ref, far_ref, near_ref, grad_value_ref):
    total = own_ref[...] + near_ref[...].astype(F32) + far_ref[...].astype(F32)
    grad_value_ref[...] = total.astype(BF16)


def finish_queries_kernel(
    query_hbm, key_hbm, query_grad_ref, gains_ref,
    grad_query_ref, key_scaled_ref, key_scale_ref,
    query_ref, key_ref, sems,
):
    rows = query_ref.shape[0]
    loads = [
        pltpu.make_async_copy(query_hbm, query_ref, sems.at[0]),
        pltpu.make_async_copy(key_hbm, key_ref, sems.at[1]),
    ]
    for load in loads:
        load.start()
    gain = gains_ref[0:1]
    loads[0].wait()
    for head in range(query_ref.shape[1] // HEAD):
        cols = slice(head * HEAD, (head + 1) * HEAD)
        x = query_ref[:, cols].astype(F32)
        scale = row_scale(x)
        normed_grad = query_grad_ref[cols, :].astype(F32).T
        grad_query_ref[:, cols] = norm_backward(normed_grad, x * scale, scale, gain).astype(BF16)
    loads[1].wait()
    for head in range(key_ref.shape[1] // HEAD):
        part = slice(head * rows, (head + 1) * rows)
        x = key_ref[:, head * HEAD : (head + 1) * HEAD].astype(F32)
        scale = row_scale(x)
        key_scale_ref[part, :] = scale
        key_scaled_ref[part, :] = x * scale


def finish_keys_kernel(
    own_ref, far_ref, near_ref, key_scaled_ref, key_scale_ref, tables_ref, gains_ref, grad_key_ref
):
    rows = own_ref.shape[0]
    cos, sin = tables_ref[0], tables_ref[1]
    gain = gains_ref[1:2]
    for head in range(own_ref.shape[1] // HEAD):
        cols = slice(head * HEAD, (head + 1) * HEAD)
        part = slice(head * rows, (head + 1) * rows)
        total = own_ref[:, cols] + near_ref[:, cols].astype(F32) + far_ref[:, cols].astype(F32)
        normed_grad = total * cos - roll_half(total) * sin
        grad = norm_backward(normed_grad, key_scaled_ref[part, :], key_scale_ref[part, :], gain)
        grad_key_ref[:, cols] = grad.astype(BF16)


def sum_kernel(parts_ref, query_gain_ref, key_gain_ref):
    sums = jnp.sum(parts_ref[...], axis=0)
    query_gain_ref[...] = sums[:1]
    key_gain_ref[...] = sums[1:]


def call(kernel, name, outs, operands, cost=None, far=0, scratch=()):
    spaces = [pltpu.HBM] * far + [pltpu.VMEM] * (len(operands) - far)
    return pl.pallas_call(
        kernel,
        out_shape=outs,
        in_specs=[pl.BlockSpec(memory_space=space) for space in spaces],
        out_specs=[pl.BlockSpec(memory_space=pltpu.VMEM)] * len(outs),
        scratch_shapes=scratch,
        compiler_params=pltpu.CompilerParams(vmem_limit_bytes=VMEM_LIMIT),
        cost_estimate=cost,
        name=name,
    )(*[pltpu.with_memory_space_constraint(x, pltpu.HBM) for x in operands[:far]], *operands[far:])


def cost(flops, size, exps=0):
    return pl.CostEstimate(flops=flops, bytes_accessed=size, transcendentals=exps)


def shape(dims, dtype):
    return jax.ShapeDtypeStruct(dims, dtype)


def on_device(doc_lengths, query_raw, key_raw, value_matrix, out_grad, query_gain, key_gain):
    rows, query_width = query_raw.shape
    width = key_raw.shape[1]
    heads = width // HEAD
    query_heads = query_width // HEAD
    keys = WINDOW + rows
    devices = lax.axis_size(AXES)
    query_gain = query_gain.reshape(1, HEAD)
    key_gain = key_gain.reshape(1, HEAD)
    near_key, far_key = shift(key_raw, 1), shift(key_raw, 2)
    term = shape((rows, width), BF16)
    own = shape((rows, width), F32)
    (
        query_rot, query_scaled, key_rot, key_across, key_scaled,
        cos, sin, own_tables, across, bias, values, grads_out, gains,
    ) = call(
        prepare_kernel,
        "prepare",
        [
            shape((query_heads * rows, HEAD), BF16),
            shape((query_width, rows), F32),
            shape((heads * rows, HEAD), BF16),
            shape((width, rows), BF16),
            shape((heads * rows, HEAD), F32),
            shape((keys, HEAD), F32),
            shape((keys, HEAD), F32),
            shape((2, rows, HEAD), F32),
            shape((2, HEAD, rows), F32),
            shape((keys, rows), F32),
            term,
            shape((rows, query_width), BF16),
            shape((8, HEAD), F32),
        ],
        (doc_lengths, query_raw, key_raw, value_matrix, out_grad, query_gain, key_gain),
        cost(4_000_000, 6_000_000),
        far=7,
        scratch=[
            pltpu.SMEM(doc_lengths.shape, jnp.int32),
            pltpu.VMEM((rows, query_width), BF16),
            pltpu.VMEM((rows, width), BF16),
            pltpu.SemaphoreType.DMA((7,)),
        ],
    )
    near_value, far_value = shift(values, 1), shift(values, 2)
    exps, inverse, halo_across, halo_scaled, held, near_value_term, own_value = call(
        attend_keys_kernel,
        "attend_keys",
        [
            shape((heads * keys, query_heads // heads * rows), F32),
            shape((heads, query_heads // heads * rows), F32),
            shape((width, WINDOW), BF16),
            shape((heads * WINDOW, HEAD), F32),
            term,
            term,
            own,
        ],
        (near_key, far_key, grads_out, query_rot, key_rot, cos, sin, bias, gains),
        cost(400_000_000, 4_000_000, 800_000),
    )
    near_value_back = shift(near_value_term, -1)
    far_key_term, near_key_term, own_key, query_grad, gain_part, far_value_term = call(
        attend_values_kernel,
        "attend_values",
        [term, term, own, shape((query_width, rows), BF16), shape((2, HEAD), F32), term],
        (
            far_value, near_value, values, grads_out, exps, inverse, query_rot,
            halo_across, key_across, halo_scaled, key_scaled, query_scaled, cos, sin, across,
            held,
        ),
        cost(600_000_000, 4_000_000),
    )
    near_key_back, far_key_back = shift(near_key_term, -1), shift(far_key_term, -2)
    far_value_back = shift(far_value_term, -2)
    (copies,) = call(
        spread_kernel, "spread_gains", [shape((devices, 2, HEAD), F32)], (gain_part, near_value_back)
    )
    parts = lax.all_to_all(copies, AXES, 0, 0)
    (grad_value,) = call(
        finish_values_kernel,
        "finish_values",
        [term],
        (own_value, far_value_back, near_value_back),
        cost(1_000_000, 2_000_000),
    )
    grad_query, key_scaled, key_scale = call(
        finish_queries_kernel,
        "finish_queries",
        [
            shape((rows, query_width), BF16),
            shape((heads * rows, HEAD), F32),
            shape((heads * rows, HEAD), F32),
        ],
        (query_raw, key_raw, query_grad, gains),
        cost(4_000_000, 4_000_000),
        far=2,
        scratch=[
            pltpu.VMEM((rows, query_width), BF16),
            pltpu.VMEM((rows, width), BF16),
            pltpu.SemaphoreType.DMA((2,)),
        ],
    )
    (grad_key,) = call(
        finish_keys_kernel,
        "finish_keys",
        [term],
        (own_key, far_key_back, near_key_back, key_scaled, key_scale, own_tables, gains),
        cost(4_000_000, 3_000_000),
    )
    grad_query_gain, grad_key_gain = call(
        sum_kernel, "sum_gains", [shape((1, HEAD), F32), shape((1, HEAD), F32)], (parts,)
    )
    return (
        grad_query, grad_key, grad_value, grad_query_gain.reshape(HEAD), grad_key_gain.reshape(HEAD)
    )


def solution(mesh):
    rows = P(AXES, None)
    return jax.shard_map(
        on_device,
        mesh=mesh,
        in_specs=(P(), rows, rows, rows, rows, P(), P()),
        out_specs=(rows, rows, rows, P(), P()),
        check_vma=False,
    )
```

```python
import math

import jax
import jax.numpy as jnp
import numpy as np
from jax import lax
from jax.experimental import pallas as pl
from jax.experimental.pallas import tpu as pltpu
from jax.sharding import PartitionSpec as P

HEAD = 128
HALF = HEAD // 2
WINDOW = 256
EPS = 1e-06
SCALE = 168.0 ** (-0.5)
ROPE_BASE = 10000.0
MASKED = -1e30
AXES = ("ctx", "grp")
F32 = jnp.float32
BF16 = jnp.bfloat16
VMEM_LIMIT = 32 * 1024 * 1024


def frequencies():
    lane = lax.broadcasted_iota(jnp.int32, (1, HEAD), 1) % HALF
    values = jnp.zeros((1, HEAD), F32)
    for m in range(HALF):
        values = jnp.where(lane == m, np.float32(ROPE_BASE ** (-2.0 * m / HEAD)), values)
    return values


def shift(value, steps):
    count = lax.axis_size(AXES)
    return lax.ppermute(value, AXES, [(s, (s + steps) % count) for s in range(count)])


def own_index():
    return lax.axis_index("ctx") * lax.axis_size("grp") + lax.axis_index("grp")


def roll_half(x):
    return pltpu.roll(x, HALF, 1)


def doc_starts(tokens, lengths_ref):
    def step(doc, carry):
        end, starts = carry
        end = end + lengths_ref[doc]
        return end, jnp.where(tokens >= end, end, starts)

    count = lengths_ref.shape[0]
    return lax.fori_loop(
        0, count, step, (jnp.int32(0), jnp.zeros_like(tokens)), unroll=count if count <= 8 else 1
    )[1]


def cos_sin_lanes(angle, lane):
    turns = jnp.floor(angle * (2.0 / math.pi) + 0.5)
    r = angle - turns * 1.5703125
    r = r - turns * 4.837512969970703125e-4
    r = r - turns * 7.549789948768648e-8
    z = r * r
    sin_r = r + r * z * (-1.6666654611e-1 + z * (8.3321608736e-3 + z * -1.9515295891e-4))
    cos_r = 1.0 - 0.5 * z + z * z * (
        4.166664568298827e-2 + z * (-1.388731625493765e-3 + z * 2.443315711809948e-5)
    )
    quadrant = turns.astype(jnp.int32) - jnp.where(lane >= HALF, 1, 0)
    odd = (quadrant & 1) == 1
    value = jnp.where(odd, sin_r, cos_r)
    negative = ((quadrant + 1) & 2) == 2
    return jnp.where(negative, -value, value)


def ones(rows, columns):
    return jnp.ones((rows, columns), BF16)


def split(x):
    high = x.astype(BF16)
    low = (x - high.astype(F32)).astype(BF16)
    return jnp.concatenate([high, low], 1)


def row_sums(x):
    return jnp.dot(split(x), ones(2 * HEAD, HEAD), preferred_element_type=F32)


def row_scale(x):
    return lax.rsqrt(row_sums(x * x) * (1.0 / HEAD) + EPS)


def turning():
    source = lax.broadcasted_iota(jnp.int32, (HEAD, HEAD), 0)
    target = lax.broadcasted_iota(jnp.int32, (HEAD, HEAD), 1)
    return jnp.where(target == (source + HALF) % HEAD, 1.0, 0.0).astype(BF16)


def turned_rows(raw, matrix):
    return jnp.dot(raw, matrix, preferred_element_type=F32)


def turned_gain(gain):
    return roll_half(jnp.broadcast_to(gain, (8, HEAD)))[:1]


def prepare_kernel(
    lengths_hbm, query_hbm, key_hbm, value_hbm, out_grad_hbm, query_gain_hbm, key_gain_hbm,
    query_rot_ref, query_scaled_ref, key_rot_ref, key_across_ref,
    key_scaled_ref, cos_ref, sin_ref, own_tables_ref, across_ref, bias_ref,
    value_ref, out_grad_ref, gains_ref,
    lengths_ref, query_ref, key_ref, sems,
):
    moves = [
        pltpu.make_async_copy(source, target, sems.at[place])
        for place, (source, target) in enumerate(
            (
                (lengths_hbm, lengths_ref),
                (query_gain_hbm, gains_ref.at[0:1]),
                (key_gain_hbm, gains_ref.at[1:2]),
                (key_hbm, key_ref),
                (query_hbm, query_ref),
                (out_grad_hbm, out_grad_ref),
                (value_hbm, value_ref),
            )
        )
    ]
    for move in moves:
        move.start()
    rows = query_ref.shape[0]
    keys = cos_ref.shape[0]
    base = own_index() * rows - (keys - rows)
    shape = (keys, HEAD)
    lane = lax.broadcasted_iota(jnp.int32, shape, 1)
    tokens = base + lax.broadcasted_iota(jnp.int32, shape, 0)
    frequency = frequencies()
    moves[0].wait()
    positions = tokens - doc_starts(tokens, lengths_ref)
    mixed = cos_sin_lanes(positions.astype(F32) * frequency, lane)
    turned = roll_half(mixed)
    cos = jnp.where(lane < HALF, mixed, turned)
    sin = jnp.where(lane < HALF, -turned, mixed)
    cos_ref[...] = cos
    sin_ref[...] = sin
    queries = base + (keys - rows) + lax.broadcasted_iota(jnp.int32, (1, rows), 1)
    lowest = jnp.maximum(doc_starts(queries, lengths_ref), queries - (WINDOW - 1))
    key_tokens = base + lax.broadcasted_iota(jnp.int32, (keys, rows), 0)
    visible = (key_tokens >= lowest) & (key_tokens <= queries)
    bias_ref[...] = jnp.where(visible, 0.0, MASKED)
    own_cos, own_sin = cos[keys - rows :], sin[keys - rows :]
    moves[1].wait()
    moves[2].wait()
    own_tables_ref[0] = own_cos
    own_tables_ref[1] = own_sin
    across_ref[0] = own_cos.T
    across_ref[1] = own_sin.T
    matrix = turning()
    for raw_ref, move, row, rot_ref in (
        (key_ref, moves[3], 1, key_rot_ref),
        (query_ref, moves[4], 0, query_rot_ref),
    ):
        gain = gains_ref[row : row + 1]
        cos_gain = own_cos * gain
        sin_gain = own_sin * turned_gain(gain)
        move.wait()
        for head in range(raw_ref.shape[1] // HEAD):
            part = slice(head * rows, (head + 1) * rows)
            across = slice(head * HEAD, (head + 1) * HEAD)
            raw = raw_ref[:, across]
            x = raw.astype(F32)
            scale = row_scale(x)
            scaled = x * scale
            turned = turned_rows(raw, matrix) * scale
            rotated = scaled * cos_gain + turned * sin_gain
            rot_ref[part, :] = rotated.astype(BF16)
            if raw_ref is key_ref:
                key_scaled_ref[part, :] = scaled
                key_across_ref[across, :] = rotated.T.astype(BF16)
            else:
                query_scaled_ref[across, :] = scaled.T
    moves[5].wait()
    moves[6].wait()


def stacked(ref, head, group):
    return jnp.concatenate(
        [ref[:, (head * group + one) * HEAD : (head * group + one + 1) * HEAD] for one in range(group)],
        0,
    )


def attend_keys_kernel(
    near_ref, far_ref, out_grad_ref, query_rot_ref, key_rot_ref, cos_ref, sin_ref, bias_ref,
    gains_ref,
    exps_ref, inverse_ref, halo_across_ref, halo_scaled_ref, far_value_ref, near_value_ref, own_value_ref,
):
    rows = far_ref.shape[0]
    heads = far_ref.shape[1] // HEAD
    group = out_grad_ref.shape[1] // far_ref.shape[1]
    halo = WINDOW
    keys = halo + rows
    key_gain = gains_ref[1:2]
    cos_gain = cos_ref[:halo] * key_gain
    sin_gain = sin_ref[:halo] * turned_gain(key_gain)
    matrix = turning()

    def scores_of(head):
        cols = slice(head * HEAD, (head + 1) * HEAD)
        raw = jnp.concatenate([far_ref[:, cols], near_ref[:, cols]], 0)
        x = raw.astype(F32)
        scale = row_scale(x)
        scaled = x * scale
        turned = turned_rows(raw, matrix) * scale
        part = slice(head * halo, (head + 1) * halo)
        halo_scaled_ref[part, :] = scaled
        rotated = scaled * cos_gain + turned * sin_gain
        halo_across_ref[cols, :] = rotated.T.astype(BF16)
        both = jnp.concatenate(
            [rotated.astype(BF16), key_rot_ref[head * rows : (head + 1) * rows, :]], 0
        )
        queries = query_rot_ref[head * group * rows : (head + 1) * group * rows, :]
        return lax.dot_general(
            both, queries, (((1,), (1,)), ((), ())), preferred_element_type=F32
        )

    later = scores_of(0)
    for head in range(heads):
        scores = later
        if head + 1 < heads:
            later = scores_of(head + 1)
        cols = slice(head * HEAD, (head + 1) * HEAD)
        low = []
        for one in range(group):
            place = (slice(head * keys, (head + 1) * keys), slice(one * rows, (one + 1) * rows))
            part = scores[:, place[1]] * (SCALE * math.log2(math.e)) + bias_ref[...]
            exps = jnp.exp2(part - jnp.max(part, axis=0, keepdims=True))
            exps_ref[place] = exps
            inverse = 1.0 / jnp.sum(exps, axis=0, keepdims=True)
            inverse_ref[head : head + 1, place[1]] = inverse
            low.append((exps_ref[place] * inverse).astype(BF16))
        value_term = jnp.dot(
            jnp.concatenate(low, 1), stacked(out_grad_ref, head, group), preferred_element_type=F32
        )
        far_value_ref[:, cols] = value_term[:rows].astype(BF16)
        near_value_ref[:, cols] = value_term[rows:halo].astype(BF16)
        own_value_ref[:, cols] = value_term[halo:]


def norm_backward(normed_grad, scaled, scale, gain):
    weighted = normed_grad * gain
    mean = row_sums(weighted * scaled) * (1.0 / HEAD)
    return scale * (weighted - scaled * mean)


def attend_values_kernel(
    far_ref, near_ref, value_ref, out_grad_ref, exps_ref, inverse_ref, query_rot_ref,
    halo_across_ref, key_across_ref, halo_scaled_ref, key_scaled_ref,
    query_scaled_ref, cos_ref, sin_ref, across_ref,
    far_key_ref, near_key_ref, own_key_ref, query_grad_ref, copies_ref,
):
    rows = far_ref.shape[0]
    heads = far_ref.shape[1] // HEAD
    group = out_grad_ref.shape[1] // far_ref.shape[1]
    halo = WINDOW
    keys = halo + rows
    cos_across, sin_across = across_ref[0] * SCALE, across_ref[1] * SCALE
    query_acc = jnp.zeros((HEAD, rows), F32)
    key_acc = jnp.zeros((keys, HEAD), F32)
    key_acc_turned = jnp.zeros((keys, HEAD), F32)

    def prob_grad_of(head):
        cols = slice(head * HEAD, (head + 1) * HEAD)
        values = jnp.concatenate([far_ref[:, cols], near_ref[:, cols], value_ref[:, cols]], 0)
        return lax.dot_general(
            values, stacked(out_grad_ref, head, group), (((1,), (1,)), ((), ())),
            preferred_element_type=F32,
        )

    later = prob_grad_of(0)
    for head in range(heads):
        prob_grad = later
        if head + 1 < heads:
            later = prob_grad_of(head + 1)
        cols = slice(head * HEAD, (head + 1) * HEAD)
        halo_part = slice(head * halo, (head + 1) * halo)
        own_part = slice(head * rows, (head + 1) * rows)
        group_part = slice(head * group * rows, (head + 1) * group * rows)
        score_grads = []
        for one in range(group):
            place = (slice(head * keys, (head + 1) * keys), slice(one * rows, (one + 1) * rows))
            part = prob_grad[:, place[1]]
            inverse = inverse_ref[head : head + 1, place[1]]
            delta = jnp.sum(exps_ref[place] * part, axis=0, keepdims=True) * inverse
            score_grads.append((exps_ref[place] * inverse * (part - delta)).astype(BF16))
        score_grad = jnp.concatenate(score_grads, 1)
        key_term = (
            jnp.dot(score_grad, query_rot_ref[group_part, :], preferred_element_type=F32) * SCALE
        )
        keys_across = jnp.concatenate([halo_across_ref[cols, :], key_across_ref[cols, :]], 1)
        query_term = jnp.dot(keys_across, score_grad, preferred_element_type=F32)
        halo_key = key_term[:halo].astype(BF16)
        far_key_ref[:, cols] = halo_key[:rows]
        near_key_ref[:, cols] = halo_key[rows:]
        own_key_ref[:, cols] = key_term[halo:]
        term = jnp.concatenate([halo_key.astype(F32), key_term[halo:]], 0)
        scaled = jnp.concatenate([halo_scaled_ref[halo_part, :], key_scaled_ref[own_part, :]], 0)
        key_acc = key_acc + term * scaled
        key_acc_turned = key_acc_turned + term * roll_half(scaled)
        for one in range(group):
            index = head * group + one
            across = slice(index * HEAD, (index + 1) * HEAD)
            grad = query_term[:, one * rows : (one + 1) * rows]
            turned = jnp.concatenate([grad[HALF:], grad[:HALF]], 0)
            normed_grad = grad * cos_across - turned * sin_across
            query_acc = query_acc + normed_grad * query_scaled_ref[across, :]
            query_grad_ref[across, :] = normed_grad.astype(BF16)
    query_sum = jnp.sum(query_acc.T, axis=0, keepdims=True)
    key_sum = jnp.sum(key_acc * cos_ref[...], axis=0, keepdims=True)
    turned_sum = jnp.sum(key_acc_turned * sin_ref[...], axis=0, keepdims=True)
    both = jnp.concatenate([query_sum, key_sum + turned_gain(turned_sum)], 0)
    copies_ref[...] = jnp.broadcast_to(both[None], copies_ref.shape)


def finish_values_kernel(own_ref, far_ref, near_ref, grad_value_ref):
    total = own_ref[...] + near_ref[...].astype(F32) + far_ref[...].astype(F32)
    grad_value_ref[...] = total.astype(BF16)


def finish_queries_kernel(
    query_hbm, key_hbm, query_grad_ref, gains_ref,
    grad_query_ref, key_scaled_ref, key_scale_ref,
    query_ref, key_ref, sems,
):
    rows = query_ref.shape[0]
    loads = [
        pltpu.make_async_copy(query_hbm, query_ref, sems.at[0]),
        pltpu.make_async_copy(key_hbm, key_ref, sems.at[1]),
    ]
    for load in loads:
        load.start()
    gain = gains_ref[0:1]
    loads[0].wait()
    for head in range(query_ref.shape[1] // HEAD):
        cols = slice(head * HEAD, (head + 1) * HEAD)
        x = query_ref[:, cols].astype(F32)
        scale = row_scale(x)
        normed_grad = query_grad_ref[cols, :].astype(F32).T
        grad_query_ref[:, cols] = norm_backward(normed_grad, x * scale, scale, gain).astype(BF16)
    loads[1].wait()
    for head in range(key_ref.shape[1] // HEAD):
        part = slice(head * rows, (head + 1) * rows)
        x = key_ref[:, head * HEAD : (head + 1) * HEAD].astype(F32)
        scale = row_scale(x)
        key_scale_ref[part, :] = scale
        key_scaled_ref[part, :] = x * scale


def finish_keys_kernel(
    own_ref, far_ref, near_ref, key_scaled_ref, key_scale_ref, tables_ref, gains_ref, grad_key_ref
):
    rows = own_ref.shape[0]
    cos, sin = tables_ref[0], tables_ref[1]
    gain = gains_ref[1:2]
    for head in range(own_ref.shape[1] // HEAD):
        cols = slice(head * HEAD, (head + 1) * HEAD)
        part = slice(head * rows, (head + 1) * rows)
        total = own_ref[:, cols] + near_ref[:, cols].astype(F32) + far_ref[:, cols].astype(F32)
        normed_grad = total * cos - roll_half(total) * sin
        grad = norm_backward(normed_grad, key_scaled_ref[part, :], key_scale_ref[part, :], gain)
        grad_key_ref[:, cols] = grad.astype(BF16)


def sum_kernel(parts_ref, query_gain_ref, key_gain_ref):
    sums = jnp.sum(parts_ref[...], axis=0)
    query_gain_ref[...] = sums[:1]
    key_gain_ref[...] = sums[1:]


def call(kernel, name, outs, operands, cost=None, far=0, scratch=()):
    spaces = [pltpu.HBM] * far + [pltpu.VMEM] * (len(operands) - far)
    return pl.pallas_call(
        kernel,
        out_shape=outs,
        in_specs=[pl.BlockSpec(memory_space=space) for space in spaces],
        out_specs=[pl.BlockSpec(memory_space=pltpu.VMEM)] * len(outs),
        scratch_shapes=scratch,
        compiler_params=pltpu.CompilerParams(vmem_limit_bytes=VMEM_LIMIT),
        cost_estimate=cost,
        name=name,
    )(*[pltpu.with_memory_space_constraint(x, pltpu.HBM) for x in operands[:far]], *operands[far:])


def cost(flops, size, exps=0):
    return pl.CostEstimate(flops=flops, bytes_accessed=size, transcendentals=exps)


def shape(dims, dtype):
    return jax.ShapeDtypeStruct(dims, dtype)


def on_device(doc_lengths, query_raw, key_raw, value_matrix, out_grad, query_gain, key_gain):
    rows, query_width = query_raw.shape
    width = key_raw.shape[1]
    heads = width // HEAD
    query_heads = query_width // HEAD
    keys = WINDOW + rows
    devices = lax.axis_size(AXES)
    query_gain = query_gain.reshape(1, HEAD)
    key_gain = key_gain.reshape(1, HEAD)
    near_key, far_key = shift(key_raw, 1), shift(key_raw, 2)
    term = shape((rows, width), BF16)
    own = shape((rows, width), F32)
    (
        query_rot, query_scaled, key_rot, key_across, key_scaled,
        cos, sin, own_tables, across, bias, values, grads_out, gains,
    ) = call(
        prepare_kernel,
        "prepare",
        [
            shape((query_heads * rows, HEAD), BF16),
            shape((query_width, rows), F32),
            shape((heads * rows, HEAD), BF16),
            shape((width, rows), BF16),
            shape((heads * rows, HEAD), F32),
            shape((keys, HEAD), F32),
            shape((keys, HEAD), F32),
            shape((2, rows, HEAD), F32),
            shape((2, HEAD, rows), F32),
            shape((keys, rows), F32),
            term,
            shape((rows, query_width), BF16),
            shape((8, HEAD), F32),
        ],
        (doc_lengths, query_raw, key_raw, value_matrix, out_grad, query_gain, key_gain),
        cost(4_000_000, 6_000_000),
        far=7,
        scratch=[
            pltpu.SMEM(doc_lengths.shape, jnp.int32),
            pltpu.VMEM((rows, query_width), BF16),
            pltpu.VMEM((rows, width), BF16),
            pltpu.SemaphoreType.DMA((7,)),
        ],
    )
    near_value, far_value = shift(values, 1), shift(values, 2)
    exps, inverse, halo_across, halo_scaled, far_value_term, near_value_term, own_value = call(
        attend_keys_kernel,
        "attend_keys",
        [
            shape((heads * keys, query_heads // heads * rows), F32),
            shape((heads, query_heads // heads * rows), F32),
            shape((width, WINDOW), BF16),
            shape((heads * WINDOW, HEAD), F32),
            term,
            term,
            own,
        ],
        (near_key, far_key, grads_out, query_rot, key_rot, cos, sin, bias, gains),
        cost(400_000_000, 4_000_000, 800_000),
    )
    near_value_back, far_value_back = shift(near_value_term, -1), shift(far_value_term, -2)
    far_key_term, near_key_term, own_key, query_grad, copies = call(
        attend_values_kernel,
        "attend_values",
        [term, term, own, shape((query_width, rows), BF16), shape((devices, 2, HEAD), F32)],
        (
            far_value, near_value, values, grads_out, exps, inverse, query_rot,
            halo_across, key_across, halo_scaled, key_scaled, query_scaled, cos, sin, across,
        ),
        cost(600_000_000, 4_000_000),
    )
    near_key_back, far_key_back = shift(near_key_term, -1), shift(far_key_term, -2)
    parts = lax.all_to_all(copies, AXES, 0, 0)
    (grad_value,) = call(
        finish_values_kernel,
        "finish_values",
        [term],
        (own_value, far_value_back, near_value_back),
        cost(1_000_000, 2_000_000),
    )
    grad_query, key_scaled, key_scale = call(
        finish_queries_kernel,
        "finish_queries",
        [
            shape((rows, query_width), BF16),
            shape((heads * rows, HEAD), F32),
            shape((heads * rows, HEAD), F32),
        ],
        (query_raw, key_raw, query_grad, gains),
        cost(4_000_000, 4_000_000),
        far=2,
        scratch=[
            pltpu.VMEM((rows, query_width), BF16),
            pltpu.VMEM((rows, width), BF16),
            pltpu.SemaphoreType.DMA((2,)),
        ],
    )
    (grad_key,) = call(
        finish_keys_kernel,
        "finish_keys",
        [term],
        (own_key, far_key_back, near_key_back, key_scaled, key_scale, own_tables, gains),
        cost(4_000_000, 3_000_000),
    )
    grad_query_gain, grad_key_gain = call(
        sum_kernel, "sum_gains", [shape((1, HEAD), F32), shape((1, HEAD), F32)], (parts,)
    )
    return (
        grad_query, grad_key, grad_value, grad_query_gain.reshape(HEAD), grad_key_gain.reshape(HEAD)
    )


def solution(mesh):
    rows = P(AXES, None)
    return jax.shard_map(
        on_device,
        mesh=mesh,
        in_specs=(P(), rows, rows, rows, rows, P(), P()),
        out_specs=(rows, rows, rows, P(), P()),
        check_vma=False,
    )
```

```python
import math

import jax
import jax.numpy as jnp
import numpy as np
from jax import lax
from jax.experimental import pallas as pl
from jax.experimental.pallas import tpu as pltpu
from jax.sharding import PartitionSpec as P

HEAD = 128
HALF = HEAD // 2
WINDOW = 256
EPS = 1e-06
SCALE = 168.0 ** (-0.5)
ROPE_BASE = 10000.0
MASKED = -1e30
AXES = ("ctx", "grp")
F32 = jnp.float32
BF16 = jnp.bfloat16
VMEM_LIMIT = 32 * 1024 * 1024


def frequencies():
    lane = lax.broadcasted_iota(jnp.int32, (1, HEAD), 1) % HALF
    values = jnp.zeros((1, HEAD), F32)
    for m in range(HALF):
        values = jnp.where(lane == m, np.float32(ROPE_BASE ** (-2.0 * m / HEAD)), values)
    return values


def shift(value, steps):
    count = lax.axis_size(AXES)
    return lax.ppermute(value, AXES, [(s, (s + steps) % count) for s in range(count)])


def own_index():
    return lax.axis_index("ctx") * lax.axis_size("grp") + lax.axis_index("grp")


def roll_half(x):
    return pltpu.roll(x, HALF, 1)


def doc_starts(tokens, lengths_ref):
    def step(doc, carry):
        end, starts = carry
        end = end + lengths_ref[doc]
        return end, jnp.where(tokens >= end, end, starts)

    count = lengths_ref.shape[0]
    return lax.fori_loop(
        0, count, step, (jnp.int32(0), jnp.zeros_like(tokens)), unroll=count if count <= 8 else 1
    )[1]


def cos_sin_lanes(angle, lane):
    turns = jnp.floor(angle * (2.0 / math.pi) + 0.5)
    r = angle - turns * 1.5703125
    r = r - turns * 4.837512969970703125e-4
    r = r - turns * 7.549789948768648e-8
    z = r * r
    sin_r = r + r * z * (-1.6666654611e-1 + z * (8.3321608736e-3 + z * -1.9515295891e-4))
    cos_r = 1.0 - 0.5 * z + z * z * (
        4.166664568298827e-2 + z * (-1.388731625493765e-3 + z * 2.443315711809948e-5)
    )
    quadrant = turns.astype(jnp.int32) - jnp.where(lane >= HALF, 1, 0)
    odd = (quadrant & 1) == 1
    value = jnp.where(odd, sin_r, cos_r)
    negative = ((quadrant + 1) & 2) == 2
    return jnp.where(negative, -value, value)


def ones(rows, columns):
    return jnp.ones((rows, columns), BF16)


def split(x):
    high = x.astype(BF16)
    low = (x - high.astype(F32)).astype(BF16)
    return jnp.concatenate([high, low], 1)


def row_sums(x):
    return jnp.dot(split(x), ones(2 * HEAD, HEAD), preferred_element_type=F32)


def row_scale(x):
    return lax.rsqrt(row_sums(x * x) * (1.0 / HEAD) + EPS)


def turning():
    source = lax.broadcasted_iota(jnp.int32, (HEAD, HEAD), 0)
    target = lax.broadcasted_iota(jnp.int32, (HEAD, HEAD), 1)
    return jnp.where(target == (source + HALF) % HEAD, 1.0, 0.0).astype(BF16)


def turned_rows(raw, matrix):
    return jnp.dot(raw, matrix, preferred_element_type=F32)


def turned_gain(gain):
    return roll_half(jnp.broadcast_to(gain, (8, HEAD)))[:1]


def prepare_kernel(
    lengths_hbm, query_hbm, key_hbm, value_hbm, out_grad_hbm, query_gain_hbm, key_gain_hbm,
    query_rot_ref, query_scaled_ref, key_rot_ref, key_across_ref,
    key_scaled_ref, cos_ref, sin_ref, own_tables_ref, across_ref, bias_ref,
    value_ref, out_grad_ref, gains_ref,
    lengths_ref, query_ref, key_ref, sems,
):
    moves = [
        pltpu.make_async_copy(source, target, sems.at[place])
        for place, (source, target) in enumerate(
            (
                (lengths_hbm, lengths_ref),
                (query_gain_hbm, gains_ref.at[0:1]),
                (key_gain_hbm, gains_ref.at[1:2]),
                (key_hbm, key_ref),
                (query_hbm, query_ref),
                (out_grad_hbm, out_grad_ref),
                (value_hbm, value_ref),
            )
        )
    ]
    for move in moves:
        move.start()
    rows = query_ref.shape[0]
    keys = cos_ref.shape[0]
    base = own_index() * rows - (keys - rows)
    shape = (keys, HEAD)
    lane = lax.broadcasted_iota(jnp.int32, shape, 1)
    tokens = base + lax.broadcasted_iota(jnp.int32, shape, 0)
    frequency = frequencies()
    moves[0].wait()
    positions = tokens - doc_starts(tokens, lengths_ref)
    mixed = cos_sin_lanes(positions.astype(F32) * frequency, lane)
    turned = roll_half(mixed)
    cos = jnp.where(lane < HALF, mixed, turned)
    sin = jnp.where(lane < HALF, -turned, mixed)
    cos_ref[...] = cos
    sin_ref[...] = sin
    queries = base + (keys - rows) + lax.broadcasted_iota(jnp.int32, (1, rows), 1)
    lowest = jnp.maximum(doc_starts(queries, lengths_ref), queries - (WINDOW - 1))
    key_tokens = base + lax.broadcasted_iota(jnp.int32, (keys, rows), 0)
    visible = (key_tokens >= lowest) & (key_tokens <= queries)
    bias_ref[...] = jnp.where(visible, 0.0, MASKED)
    own_cos, own_sin = cos[keys - rows :], sin[keys - rows :]
    moves[1].wait()
    moves[2].wait()
    own_tables_ref[0] = own_cos
    own_tables_ref[1] = own_sin
    across_ref[0] = own_cos.T
    across_ref[1] = own_sin.T
    matrix = turning()
    for raw_ref, move, row, rot_ref in (
        (key_ref, moves[3], 1, key_rot_ref),
        (query_ref, moves[4], 0, query_rot_ref),
    ):
        gain = gains_ref[row : row + 1]
        cos_gain = own_cos * gain
        sin_gain = own_sin * turned_gain(gain)
        move.wait()
        for head in range(raw_ref.shape[1] // HEAD):
            part = slice(head * rows, (head + 1) * rows)
            across = slice(head * HEAD, (head + 1) * HEAD)
            raw = raw_ref[:, across]
            x = raw.astype(F32)
            scale = row_scale(x)
            scaled = x * scale
            turned = turned_rows(raw, matrix) * scale
            rotated = scaled * cos_gain + turned * sin_gain
            rot_ref[part, :] = rotated.astype(BF16)
            if raw_ref is key_ref:
                key_scaled_ref[part, :] = scaled
                key_across_ref[across, :] = rotated.T.astype(BF16)
            else:
                query_scaled_ref[across, :] = scaled.T
    moves[5].wait()
    moves[6].wait()


def stacked(ref, head, group):
    return jnp.concatenate(
        [ref[:, (head * group + one) * HEAD : (head * group + one + 1) * HEAD] for one in range(group)],
        0,
    )


def attend_keys_kernel(
    near_ref, far_ref, out_grad_ref, query_rot_ref, key_rot_ref, cos_ref, sin_ref, bias_ref,
    gains_ref,
    exps_ref, inverse_ref, halo_across_ref, halo_scaled_ref, far_value_ref, near_value_ref, own_value_ref,
):
    rows = far_ref.shape[0]
    heads = far_ref.shape[1] // HEAD
    group = out_grad_ref.shape[1] // far_ref.shape[1]
    halo = WINDOW
    keys = halo + rows
    key_gain = gains_ref[1:2]
    cos_gain = cos_ref[:halo] * key_gain
    sin_gain = sin_ref[:halo] * turned_gain(key_gain)
    matrix = turning()

    def scores_of(head):
        cols = slice(head * HEAD, (head + 1) * HEAD)
        raw = jnp.concatenate([far_ref[:, cols], near_ref[:, cols]], 0)
        x = raw.astype(F32)
        scale = row_scale(x)
        scaled = x * scale
        turned = turned_rows(raw, matrix) * scale
        part = slice(head * halo, (head + 1) * halo)
        halo_scaled_ref[part, :] = scaled
        rotated = scaled * cos_gain + turned * sin_gain
        halo_across_ref[cols, :] = rotated.T.astype(BF16)
        both = jnp.concatenate(
            [rotated.astype(BF16), key_rot_ref[head * rows : (head + 1) * rows, :]], 0
        )
        queries = query_rot_ref[head * group * rows : (head + 1) * group * rows, :]
        return lax.dot_general(
            both, queries, (((1,), (1,)), ((), ())), preferred_element_type=F32
        )

    later = scores_of(0)
    for head in range(heads):
        scores = later
        if head + 1 < heads:
            later = scores_of(head + 1)
        cols = slice(head * HEAD, (head + 1) * HEAD)
        low = []
        for one in range(group):
            place = (slice(head * keys, (head + 1) * keys), slice(one * rows, (one + 1) * rows))
            part = scores[:, place[1]] * (SCALE * math.log2(math.e)) + bias_ref[...]
            exps = jnp.exp2(part - jnp.max(part, axis=0, keepdims=True))
            exps_ref[place] = exps
            inverse = 1.0 / jnp.sum(exps, axis=0, keepdims=True)
            inverse_ref[head : head + 1, place[1]] = inverse
            low.append((exps_ref[place] * inverse).astype(BF16))
        value_term = jnp.dot(
            jnp.concatenate(low, 1), stacked(out_grad_ref, head, group), preferred_element_type=F32
        )
        far_value_ref[:, cols] = value_term[:rows].astype(BF16)
        near_value_ref[:, cols] = value_term[rows:halo].astype(BF16)
        own_value_ref[:, cols] = value_term[halo:]


def norm_backward(normed_grad, scaled, scale, gain):
    weighted = normed_grad * gain
    mean = row_sums(weighted * scaled) * (1.0 / HEAD)
    return scale * (weighted - scaled * mean)


def attend_values_kernel(
    near_ref, far_ref, value_ref, out_grad_ref, exps_ref, inverse_ref, query_rot_ref,
    halo_across_ref, key_across_ref, halo_scaled_ref, key_scaled_ref,
    query_scaled_ref, cos_ref, sin_ref, across_ref,
    far_key_ref, near_key_ref, own_key_ref, query_grad_ref, copies_ref,
):
    rows = far_ref.shape[0]
    heads = far_ref.shape[1] // HEAD
    group = out_grad_ref.shape[1] // far_ref.shape[1]
    halo = WINDOW
    keys = halo + rows
    cos_across, sin_across = across_ref[0] * SCALE, across_ref[1] * SCALE
    query_acc = jnp.zeros((HEAD, rows), F32)
    key_acc = jnp.zeros((keys, HEAD), F32)
    key_acc_turned = jnp.zeros((keys, HEAD), F32)

    def prob_grad_of(head):
        cols = slice(head * HEAD, (head + 1) * HEAD)
        values = jnp.concatenate([far_ref[:, cols], near_ref[:, cols], value_ref[:, cols]], 0)
        return lax.dot_general(
            values, stacked(out_grad_ref, head, group), (((1,), (1,)), ((), ())),
            preferred_element_type=F32,
        )

    later = prob_grad_of(0)
    for head in range(heads):
        prob_grad = later
        if head + 1 < heads:
            later = prob_grad_of(head + 1)
        cols = slice(head * HEAD, (head + 1) * HEAD)
        halo_part = slice(head * halo, (head + 1) * halo)
        own_part = slice(head * rows, (head + 1) * rows)
        group_part = slice(head * group * rows, (head + 1) * group * rows)
        score_grads = []
        for one in range(group):
            place = (slice(head * keys, (head + 1) * keys), slice(one * rows, (one + 1) * rows))
            part = prob_grad[:, place[1]]
            inverse = inverse_ref[head : head + 1, place[1]]
            delta = jnp.sum(exps_ref[place] * part, axis=0, keepdims=True) * inverse
            score_grads.append((exps_ref[place] * inverse * (part - delta)).astype(BF16))
        score_grad = jnp.concatenate(score_grads, 1)
        key_term = (
            jnp.dot(score_grad, query_rot_ref[group_part, :], preferred_element_type=F32) * SCALE
        )
        keys_across = jnp.concatenate([halo_across_ref[cols, :], key_across_ref[cols, :]], 1)
        query_term = jnp.dot(keys_across, score_grad, preferred_element_type=F32)
        halo_key = key_term[:halo].astype(BF16)
        far_key_ref[:, cols] = halo_key[:rows]
        near_key_ref[:, cols] = halo_key[rows:]
        own_key_ref[:, cols] = key_term[halo:]
        term = jnp.concatenate([halo_key.astype(F32), key_term[halo:]], 0)
        scaled = jnp.concatenate([halo_scaled_ref[halo_part, :], key_scaled_ref[own_part, :]], 0)
        key_acc = key_acc + term * scaled
        key_acc_turned = key_acc_turned + term * roll_half(scaled)
        for one in range(group):
            index = head * group + one
            across = slice(index * HEAD, (index + 1) * HEAD)
            grad = query_term[:, one * rows : (one + 1) * rows]
            turned = jnp.concatenate([grad[HALF:], grad[:HALF]], 0)
            normed_grad = grad * cos_across - turned * sin_across
            query_acc = query_acc + normed_grad * query_scaled_ref[across, :]
            query_grad_ref[across, :] = normed_grad.astype(BF16)
    query_sum = jnp.sum(query_acc.T, axis=0, keepdims=True)
    key_sum = jnp.sum(key_acc * cos_ref[...], axis=0, keepdims=True)
    turned_sum = jnp.sum(key_acc_turned * sin_ref[...], axis=0, keepdims=True)
    both = jnp.concatenate([query_sum, key_sum + turned_gain(turned_sum)], 0)
    copies_ref[...] = jnp.broadcast_to(both[None], copies_ref.shape)


def finish_values_kernel(own_ref, far_ref, near_ref, grad_value_ref, mark_ref):
    mark_ref[...] = jnp.zeros_like(mark_ref)
    total = own_ref[...] + near_ref[...].astype(F32) + far_ref[...].astype(F32)
    grad_value_ref[...] = total.astype(BF16)


def finish_queries_kernel(
    query_hbm, key_hbm, query_grad_ref, gains_ref,
    grad_query_ref, key_scaled_ref, key_scale_ref,
    query_ref, key_ref, sems,
):
    rows = query_ref.shape[0]
    loads = [
        pltpu.make_async_copy(query_hbm, query_ref, sems.at[0]),
        pltpu.make_async_copy(key_hbm, key_ref, sems.at[1]),
    ]
    for load in loads:
        load.start()
    gain = gains_ref[0:1]
    loads[0].wait()
    for head in range(query_ref.shape[1] // HEAD):
        cols = slice(head * HEAD, (head + 1) * HEAD)
        x = query_ref[:, cols].astype(F32)
        scale = row_scale(x)
        normed_grad = query_grad_ref[cols, :].astype(F32).T
        grad_query_ref[:, cols] = norm_backward(normed_grad, x * scale, scale, gain).astype(BF16)
    loads[1].wait()
    for head in range(key_ref.shape[1] // HEAD):
        part = slice(head * rows, (head + 1) * rows)
        x = key_ref[:, head * HEAD : (head + 1) * HEAD].astype(F32)
        scale = row_scale(x)
        key_scale_ref[part, :] = scale
        key_scaled_ref[part, :] = x * scale


def finish_keys_kernel(
    own_ref, far_ref, near_ref, key_scaled_ref, key_scale_ref, tables_ref, gains_ref, mark_ref,
    grad_key_ref, next_ref,
):
    next_ref[...] = mark_ref[...]
    rows = own_ref.shape[0]
    cos, sin = tables_ref[0], tables_ref[1]
    gain = gains_ref[1:2]
    for head in range(own_ref.shape[1] // HEAD):
        cols = slice(head * HEAD, (head + 1) * HEAD)
        part = slice(head * rows, (head + 1) * rows)
        total = own_ref[:, cols] + near_ref[:, cols].astype(F32) + far_ref[:, cols].astype(F32)
        normed_grad = total * cos - roll_half(total) * sin
        grad = norm_backward(normed_grad, key_scaled_ref[part, :], key_scale_ref[part, :], gain)
        grad_key_ref[:, cols] = grad.astype(BF16)


def sum_kernel(parts_ref, mark_ref, query_gain_ref, key_gain_ref):
    sums = jnp.sum(parts_ref[...], axis=0)
    query_gain_ref[...] = sums[:1]
    key_gain_ref[...] = sums[1:]


def call(kernel, name, outs, operands, cost=None, far=0, scratch=()):
    spaces = [pltpu.HBM] * far + [pltpu.VMEM] * (len(operands) - far)
    return pl.pallas_call(
        kernel,
        out_shape=outs,
        in_specs=[pl.BlockSpec(memory_space=space) for space in spaces],
        out_specs=[pl.BlockSpec(memory_space=pltpu.VMEM)] * len(outs),
        scratch_shapes=scratch,
        compiler_params=pltpu.CompilerParams(vmem_limit_bytes=VMEM_LIMIT),
        cost_estimate=cost,
        name=name,
    )(*[pltpu.with_memory_space_constraint(x, pltpu.HBM) for x in operands[:far]], *operands[far:])


def cost(flops, size, exps=0):
    return pl.CostEstimate(flops=flops, bytes_accessed=size, transcendentals=exps)


def shape(dims, dtype):
    return jax.ShapeDtypeStruct(dims, dtype)


def on_device(doc_lengths, query_raw, key_raw, value_matrix, out_grad, query_gain, key_gain):
    rows, query_width = query_raw.shape
    width = key_raw.shape[1]
    heads = width // HEAD
    query_heads = query_width // HEAD
    keys = WINDOW + rows
    devices = lax.axis_size(AXES)
    query_gain = query_gain.reshape(1, HEAD)
    key_gain = key_gain.reshape(1, HEAD)
    near_key, far_key = shift(key_raw, 1), shift(key_raw, 2)
    term = shape((rows, width), BF16)
    own = shape((rows, width), F32)
    (
        query_rot, query_scaled, key_rot, key_across, key_scaled,
        cos, sin, own_tables, across, bias, values, grads_out, gains,
    ) = call(
        prepare_kernel,
        "prepare",
        [
            shape((query_heads * rows, HEAD), BF16),
            shape((query_width, rows), F32),
            shape((heads * rows, HEAD), BF16),
            shape((width, rows), BF16),
            shape((heads * rows, HEAD), F32),
            shape((keys, HEAD), F32),
            shape((keys, HEAD), F32),
            shape((2, rows, HEAD), F32),
            shape((2, HEAD, rows), F32),
            shape((keys, rows), F32),
            term,
            shape((rows, query_width), BF16),
            shape((8, HEAD), F32),
        ],
        (doc_lengths, query_raw, key_raw, value_matrix, out_grad, query_gain, key_gain),
        cost(4_000_000, 6_000_000),
        far=7,
        scratch=[
            pltpu.SMEM(doc_lengths.shape, jnp.int32),
            pltpu.VMEM((rows, query_width), BF16),
            pltpu.VMEM((rows, width), BF16),
            pltpu.SemaphoreType.DMA((7,)),
        ],
    )
    near_value, far_value = shift(values, 1), shift(values, 2)
    exps, inverse, halo_across, halo_scaled, far_value_term, near_value_term, own_value = call(
        attend_keys_kernel,
        "attend_keys",
        [
            shape((heads * keys, query_heads // heads * rows), F32),
            shape((heads, query_heads // heads * rows), F32),
            shape((width, WINDOW), BF16),
            shape((heads * WINDOW, HEAD), F32),
            term,
            term,
            own,
        ],
        (near_key, far_key, grads_out, query_rot, key_rot, cos, sin, bias, gains),
        cost(400_000_000, 4_000_000, 800_000),
    )
    near_value_back, far_value_back = shift(near_value_term, -1), shift(far_value_term, -2)
    far_key_term, near_key_term, own_key, query_grad, copies = call(
        attend_values_kernel,
        "attend_values",
        [term, term, own, shape((query_width, rows), BF16), shape((devices, 2, HEAD), F32)],
        (
            near_value, far_value, values, grads_out, exps, inverse, query_rot,
            halo_across, key_across, halo_scaled, key_scaled, query_scaled, cos, sin, across,
        ),
        cost(600_000_000, 4_000_000),
    )
    near_key_back, far_key_back = shift(near_key_term, -1), shift(far_key_term, -2)
    parts = lax.all_to_all(copies, AXES, 0, 0)
    mark = shape((8, HEAD), F32)
    grad_value, first_mark = call(
        finish_values_kernel,
        "finish_values",
        [term, mark],
        (own_value, far_value_back, near_value_back),
        cost(1_000_000, 2_000_000),
    )
    grad_query, key_scaled, key_scale = call(
        finish_queries_kernel,
        "finish_queries",
        [
            shape((rows, query_width), BF16),
            shape((heads * rows, HEAD), F32),
            shape((heads * rows, HEAD), F32),
        ],
        (query_raw, key_raw, query_grad, gains),
        cost(4_000_000, 4_000_000),
        far=2,
        scratch=[
            pltpu.VMEM((rows, query_width), BF16),
            pltpu.VMEM((rows, width), BF16),
            pltpu.SemaphoreType.DMA((2,)),
        ],
    )
    grad_key, second_mark = call(
        finish_keys_kernel,
        "finish_keys",
        [term, mark],
        (own_key, far_key_back, near_key_back, key_scaled, key_scale, own_tables, gains, first_mark),
        cost(4_000_000, 3_000_000),
    )
    grad_query_gain, grad_key_gain = call(
        sum_kernel, "sum_gains", [shape((1, HEAD), F32), shape((1, HEAD), F32)], (parts, second_mark)
    )
    return (
        grad_query, grad_key, grad_value, grad_query_gain.reshape(HEAD), grad_key_gain.reshape(HEAD)
    )


def solution(mesh):
    rows = P(AXES, None)
    return jax.shard_map(
        on_device,
        mesh=mesh,
        in_specs=(P(), rows, rows, rows, rows, P(), P()),
        out_specs=(rows, rows, rows, P(), P()),
        check_vma=False,
    )
```

```python
import math

import jax
import jax.numpy as jnp
import numpy as np
from jax import lax
from jax.experimental import pallas as pl
from jax.experimental.pallas import tpu as pltpu
from jax.sharding import PartitionSpec as P

HEAD = 128
HALF = HEAD // 2
WINDOW = 256
EPS = 1e-06
SCALE = 168.0 ** (-0.5)
ROPE_BASE = 10000.0
MASKED = -1e30
AXES = ("ctx", "grp")
F32 = jnp.float32
BF16 = jnp.bfloat16
VMEM_LIMIT = 32 * 1024 * 1024


def frequencies():
    lane = lax.broadcasted_iota(jnp.int32, (1, HEAD), 1) % HALF
    values = jnp.zeros((1, HEAD), F32)
    for m in range(HALF):
        values = jnp.where(lane == m, np.float32(ROPE_BASE ** (-2.0 * m / HEAD)), values)
    return values


def shift(value, steps):
    count = lax.axis_size(AXES)
    return lax.ppermute(value, AXES, [(s, (s + steps) % count) for s in range(count)])


def own_index():
    return lax.axis_index("ctx") * lax.axis_size("grp") + lax.axis_index("grp")


def roll_half(x):
    return pltpu.roll(x, HALF, 1)


def doc_starts(tokens, lengths_ref):
    def step(doc, carry):
        end, starts = carry
        end = end + lengths_ref[doc]
        return end, jnp.where(tokens >= end, end, starts)

    count = lengths_ref.shape[0]
    return lax.fori_loop(
        0, count, step, (jnp.int32(0), jnp.zeros_like(tokens)), unroll=count if count <= 8 else 1
    )[1]


def cos_sin_lanes(angle, lane):
    turns = jnp.floor(angle * (2.0 / math.pi) + 0.5)
    r = angle - turns * 1.5703125
    r = r - turns * 4.837512969970703125e-4
    r = r - turns * 7.549789948768648e-8
    z = r * r
    sin_r = r + r * z * (-1.6666654611e-1 + z * (8.3321608736e-3 + z * -1.9515295891e-4))
    cos_r = 1.0 - 0.5 * z + z * z * (
        4.166664568298827e-2 + z * (-1.388731625493765e-3 + z * 2.443315711809948e-5)
    )
    quadrant = turns.astype(jnp.int32) - jnp.where(lane >= HALF, 1, 0)
    odd = (quadrant & 1) == 1
    value = jnp.where(odd, sin_r, cos_r)
    negative = ((quadrant + 1) & 2) == 2
    return jnp.where(negative, -value, value)


def ones(rows, columns):
    return jnp.ones((rows, columns), BF16)


def split(x):
    high = x.astype(BF16)
    low = (x - high.astype(F32)).astype(BF16)
    return jnp.concatenate([high, low], 1)


def row_sums(x):
    return jnp.dot(split(x), ones(2 * HEAD, HEAD), preferred_element_type=F32)


def row_scale(x):
    return lax.rsqrt(row_sums(x * x) * (1.0 / HEAD) + EPS)


def turning():
    source = lax.broadcasted_iota(jnp.int32, (HEAD, HEAD), 0)
    target = lax.broadcasted_iota(jnp.int32, (HEAD, HEAD), 1)
    return jnp.where(target == (source + HALF) % HEAD, 1.0, 0.0).astype(BF16)


def turned_rows(raw, matrix):
    return jnp.dot(raw, matrix, preferred_element_type=F32)


def turned_gain(gain):
    return roll_half(jnp.broadcast_to(gain, (8, HEAD)))[:1]


def prepare_kernel(
    lengths_hbm, query_hbm, key_hbm, value_hbm, out_grad_hbm, query_gain_hbm, key_gain_hbm,
    query_rot_ref, query_scaled_ref, key_rot_ref, key_across_ref,
    key_scaled_ref, cos_ref, sin_ref, own_tables_ref, across_ref, bias_ref,
    value_ref, out_grad_ref, gains_ref,
    lengths_ref, query_ref, key_ref, sems,
):
    moves = [
        pltpu.make_async_copy(source, target, sems.at[place])
        for place, (source, target) in enumerate(
            (
                (lengths_hbm, lengths_ref),
                (query_gain_hbm, gains_ref.at[0:1]),
                (key_gain_hbm, gains_ref.at[1:2]),
                (key_hbm, key_ref),
                (query_hbm, query_ref),
                (out_grad_hbm, out_grad_ref),
                (value_hbm, value_ref),
            )
        )
    ]
    for move in moves:
        move.start()
    rows = query_ref.shape[0]
    keys = cos_ref.shape[0]
    base = own_index() * rows - (keys - rows)
    shape = (keys, HEAD)
    lane = lax.broadcasted_iota(jnp.int32, shape, 1)
    tokens = base + lax.broadcasted_iota(jnp.int32, shape, 0)
    frequency = frequencies()
    moves[0].wait()
    positions = tokens - doc_starts(tokens, lengths_ref)
    mixed = cos_sin_lanes(positions.astype(F32) * frequency, lane)
    turned = roll_half(mixed)
    cos = jnp.where(lane < HALF, mixed, turned)
    sin = jnp.where(lane < HALF, -turned, mixed)
    cos_ref[...] = cos
    sin_ref[...] = sin
    queries = base + (keys - rows) + lax.broadcasted_iota(jnp.int32, (1, rows), 1)
    lowest = jnp.maximum(doc_starts(queries, lengths_ref), queries - (WINDOW - 1))
    key_tokens = base + lax.broadcasted_iota(jnp.int32, (keys, rows), 0)
    visible = (key_tokens >= lowest) & (key_tokens <= queries)
    bias_ref[...] = jnp.where(visible, 0.0, MASKED)
    own_cos, own_sin = cos[keys - rows :], sin[keys - rows :]
    moves[1].wait()
    moves[2].wait()
    own_tables_ref[0] = own_cos * SCALE
    own_tables_ref[1] = own_sin * SCALE
    across_ref[0] = own_cos.T
    across_ref[1] = own_sin.T
    matrix = turning()
    for raw_ref, move, row, rot_ref in (
        (key_ref, moves[3], 1, key_rot_ref),
        (query_ref, moves[4], 0, query_rot_ref),
    ):
        gain = gains_ref[row : row + 1]
        cos_gain = own_cos * gain
        sin_gain = own_sin * turned_gain(gain)
        move.wait()
        for head in range(raw_ref.shape[1] // HEAD):
            part = slice(head * rows, (head + 1) * rows)
            across = slice(head * HEAD, (head + 1) * HEAD)
            raw = raw_ref[:, across]
            x = raw.astype(F32)
            scale = row_scale(x)
            scaled = x * scale
            turned = turned_rows(raw, matrix) * scale
            rotated = scaled * cos_gain + turned * sin_gain
            rot_ref[part, :] = rotated.astype(BF16)
            if raw_ref is key_ref:
                key_scaled_ref[part, :] = scaled
                key_across_ref[across, :] = rotated.T.astype(BF16)
            else:
                query_scaled_ref[across, :] = scaled.T
    moves[5].wait()
    moves[6].wait()


def stacked(ref, head, group):
    return jnp.concatenate(
        [ref[:, (head * group + one) * HEAD : (head * group + one + 1) * HEAD] for one in range(group)],
        0,
    )


def attend_keys_kernel(
    near_ref, far_ref, out_grad_ref, query_rot_ref, key_rot_ref, cos_ref, sin_ref, bias_ref,
    gains_ref,
    exps_ref, inverse_ref, halo_across_ref, halo_scaled_ref, far_value_ref, near_value_ref, own_value_ref,
):
    rows = far_ref.shape[0]
    heads = far_ref.shape[1] // HEAD
    group = out_grad_ref.shape[1] // far_ref.shape[1]
    halo = WINDOW
    keys = halo + rows
    key_gain = gains_ref[1:2]
    cos_gain = cos_ref[:halo] * key_gain
    sin_gain = sin_ref[:halo] * turned_gain(key_gain)

    def scores_of(head):
        cols = slice(head * HEAD, (head + 1) * HEAD)
        raw = jnp.concatenate([far_ref[:, cols], near_ref[:, cols]], 0)
        x = raw.astype(F32)
        scale = row_scale(x)
        scaled = x * scale
        turned = roll_half(scaled)
        part = slice(head * halo, (head + 1) * halo)
        halo_scaled_ref[part, :] = scaled
        rotated = scaled * cos_gain + turned * sin_gain
        halo_across_ref[cols, :] = rotated.T.astype(BF16)
        both = jnp.concatenate(
            [rotated.astype(BF16), key_rot_ref[head * rows : (head + 1) * rows, :]], 0
        )
        queries = query_rot_ref[head * group * rows : (head + 1) * group * rows, :]
        return lax.dot_general(
            both, queries, (((1,), (1,)), ((), ())), preferred_element_type=F32
        )

    later = scores_of(0)
    for head in range(heads):
        scores = later
        if head + 1 < heads:
            later = scores_of(head + 1)
        cols = slice(head * HEAD, (head + 1) * HEAD)
        low = []
        for one in range(group):
            place = (slice(head * keys, (head + 1) * keys), slice(one * rows, (one + 1) * rows))
            part = scores[:, place[1]] * (SCALE * math.log2(math.e)) + bias_ref[...]
            exps = jnp.exp2(part - jnp.max(part, axis=0, keepdims=True))
            exps_ref[place] = exps
            inverse = 1.0 / jnp.sum(exps, axis=0, keepdims=True)
            inverse_ref[head : head + 1, place[1]] = inverse
            low.append((exps_ref[place] * inverse).astype(BF16))
        value_term = jnp.dot(
            jnp.concatenate(low, 1), stacked(out_grad_ref, head, group), preferred_element_type=F32
        )
        far_value_ref[:, cols] = value_term[:rows].astype(BF16)
        near_value_ref[:, cols] = value_term[rows:halo].astype(BF16)
        own_value_ref[:, cols] = value_term[halo:]


def norm_backward(normed_grad, scaled, scale, gain):
    weighted = normed_grad * gain
    mean = row_sums(weighted * scaled) * (1.0 / HEAD)
    return scale * (weighted - scaled * mean)


def attend_values_kernel(
    near_ref, far_ref, value_ref, out_grad_ref, exps_ref, inverse_ref, query_rot_ref,
    halo_across_ref, key_across_ref, halo_scaled_ref, key_scaled_ref,
    query_scaled_ref, cos_ref, sin_ref, across_ref,
    far_key_ref, near_key_ref, own_key_ref, query_grad_ref, copies_ref,
):
    rows = far_ref.shape[0]
    heads = far_ref.shape[1] // HEAD
    group = out_grad_ref.shape[1] // far_ref.shape[1]
    halo = WINDOW
    keys = halo + rows
    cos_across, sin_across = across_ref[0] * SCALE, across_ref[1] * SCALE
    query_acc = jnp.zeros((HEAD, rows), F32)
    key_acc = jnp.zeros((keys, HEAD), F32)
    key_acc_turned = jnp.zeros((keys, HEAD), F32)

    def prob_grad_of(head):
        cols = slice(head * HEAD, (head + 1) * HEAD)
        values = jnp.concatenate([far_ref[:, cols], near_ref[:, cols], value_ref[:, cols]], 0)
        return lax.dot_general(
            values, stacked(out_grad_ref, head, group), (((1,), (1,)), ((), ())),
            preferred_element_type=F32,
        )

    later = prob_grad_of(0)
    for head in range(heads):
        prob_grad = later
        if head + 1 < heads:
            later = prob_grad_of(head + 1)
        cols = slice(head * HEAD, (head + 1) * HEAD)
        halo_part = slice(head * halo, (head + 1) * halo)
        own_part = slice(head * rows, (head + 1) * rows)
        group_part = slice(head * group * rows, (head + 1) * group * rows)
        score_grads = []
        for one in range(group):
            place = (slice(head * keys, (head + 1) * keys), slice(one * rows, (one + 1) * rows))
            part = prob_grad[:, place[1]]
            inverse = inverse_ref[head : head + 1, place[1]]
            delta = jnp.sum(exps_ref[place] * part, axis=0, keepdims=True) * inverse
            score_grads.append((exps_ref[place] * inverse * (part - delta)).astype(BF16))
        score_grad = jnp.concatenate(score_grads, 1)
        key_term = jnp.dot(score_grad, query_rot_ref[group_part, :], preferred_element_type=F32)
        keys_across = jnp.concatenate([halo_across_ref[cols, :], key_across_ref[cols, :]], 1)
        query_term = jnp.dot(keys_across, score_grad, preferred_element_type=F32)
        halo_key = key_term[:halo].astype(BF16)
        far_key_ref[:, cols] = halo_key[:rows]
        near_key_ref[:, cols] = halo_key[rows:]
        own_key_ref[:, cols] = key_term[halo:]
        scaled = jnp.concatenate([halo_scaled_ref[halo_part, :], key_scaled_ref[own_part, :]], 0)
        key_acc = key_acc + key_term * scaled
        key_acc_turned = key_acc_turned + key_term * roll_half(scaled)
        for one in range(group):
            index = head * group + one
            across = slice(index * HEAD, (index + 1) * HEAD)
            grad = query_term[:, one * rows : (one + 1) * rows]
            turned = jnp.concatenate([grad[HALF:], grad[:HALF]], 0)
            normed_grad = grad * cos_across - turned * sin_across
            query_acc = query_acc + normed_grad * query_scaled_ref[across, :]
            query_grad_ref[across, :] = normed_grad.astype(BF16)
    query_sum = jnp.sum(query_acc.T, axis=0, keepdims=True)
    key_sum = jnp.sum(key_acc * cos_ref[...], axis=0, keepdims=True)
    turned_sum = jnp.sum(key_acc_turned * sin_ref[...], axis=0, keepdims=True)
    key_sum = (key_sum + turned_gain(turned_sum)) * SCALE
    both = jnp.concatenate([query_sum, key_sum], 0)
    copies_ref[...] = jnp.broadcast_to(both[None], copies_ref.shape)


def finish_values_kernel(own_ref, far_ref, near_ref, grad_value_ref, mark_ref):
    mark_ref[...] = jnp.zeros_like(mark_ref)
    total = own_ref[...] + near_ref[...].astype(F32) + far_ref[...].astype(F32)
    grad_value_ref[...] = total.astype(BF16)


def finish_queries_kernel(
    query_hbm, key_hbm, query_grad_ref, gains_ref,
    grad_query_ref, key_scaled_ref, key_scale_ref,
    query_ref, key_ref, sems,
):
    rows = query_ref.shape[0]
    loads = [
        pltpu.make_async_copy(query_hbm, query_ref, sems.at[0]),
        pltpu.make_async_copy(key_hbm, key_ref, sems.at[1]),
    ]
    for load in loads:
        load.start()
    gain = gains_ref[0:1]
    loads[0].wait()
    for head in range(query_ref.shape[1] // HEAD):
        cols = slice(head * HEAD, (head + 1) * HEAD)
        x = query_ref[:, cols].astype(F32)
        scale = row_scale(x)
        normed_grad = query_grad_ref[cols, :].astype(F32).T
        grad_query_ref[:, cols] = norm_backward(normed_grad, x * scale, scale, gain).astype(BF16)
    loads[1].wait()
    for head in range(key_ref.shape[1] // HEAD):
        part = slice(head * rows, (head + 1) * rows)
        x = key_ref[:, head * HEAD : (head + 1) * HEAD].astype(F32)
        scale = row_scale(x)
        key_scale_ref[part, :] = scale
        key_scaled_ref[part, :] = x * scale


def finish_keys_kernel(
    own_ref, far_ref, near_ref, key_scaled_ref, key_scale_ref, tables_ref, gains_ref, mark_ref,
    grad_key_ref, next_ref,
):
    next_ref[...] = mark_ref[...]
    rows = own_ref.shape[0]
    cos, sin = tables_ref[0], tables_ref[1]
    gain = gains_ref[1:2]
    for head in range(own_ref.shape[1] // HEAD):
        cols = slice(head * HEAD, (head + 1) * HEAD)
        part = slice(head * rows, (head + 1) * rows)
        total = own_ref[:, cols] + near_ref[:, cols].astype(F32) + far_ref[:, cols].astype(F32)
        normed_grad = total * cos - roll_half(total) * sin
        grad = norm_backward(normed_grad, key_scaled_ref[part, :], key_scale_ref[part, :], gain)
        grad_key_ref[:, cols] = grad.astype(BF16)


def sum_kernel(parts_ref, mark_ref, query_gain_ref, key_gain_ref):
    sums = jnp.sum(parts_ref[...], axis=0)
    query_gain_ref[...] = sums[:1]
    key_gain_ref[...] = sums[1:]


def call(kernel, name, outs, operands, cost=None, far=0, scratch=()):
    spaces = [pltpu.HBM] * far + [pltpu.VMEM] * (len(operands) - far)
    return pl.pallas_call(
        kernel,
        out_shape=outs,
        in_specs=[pl.BlockSpec(memory_space=space) for space in spaces],
        out_specs=[pl.BlockSpec(memory_space=pltpu.VMEM)] * len(outs),
        scratch_shapes=scratch,
        compiler_params=pltpu.CompilerParams(vmem_limit_bytes=VMEM_LIMIT),
        cost_estimate=cost,
        name=name,
    )(*[pltpu.with_memory_space_constraint(x, pltpu.HBM) for x in operands[:far]], *operands[far:])


def cost(flops, size, exps=0):
    return pl.CostEstimate(flops=flops, bytes_accessed=size, transcendentals=exps)


def shape(dims, dtype):
    return jax.ShapeDtypeStruct(dims, dtype)


def on_device(doc_lengths, query_raw, key_raw, value_matrix, out_grad, query_gain, key_gain):
    rows, query_width = query_raw.shape
    width = key_raw.shape[1]
    heads = width // HEAD
    query_heads = query_width // HEAD
    keys = WINDOW + rows
    devices = lax.axis_size(AXES)
    query_gain = query_gain.reshape(1, HEAD)
    key_gain = key_gain.reshape(1, HEAD)
    near_key, far_key = shift(key_raw, 1), shift(key_raw, 2)
    term = shape((rows, width), BF16)
    own = shape((rows, width), F32)
    (
        query_rot, query_scaled, key_rot, key_across, key_scaled,
        cos, sin, own_tables, across, bias, values, grads_out, gains,
    ) = call(
        prepare_kernel,
        "prepare",
        [
            shape((query_heads * rows, HEAD), BF16),
            shape((query_width, rows), F32),
            shape((heads * rows, HEAD), BF16),
            shape((width, rows), BF16),
            shape((heads * rows, HEAD), F32),
            shape((keys, HEAD), F32),
            shape((keys, HEAD), F32),
            shape((2, rows, HEAD), F32),
            shape((2, HEAD, rows), F32),
            shape((keys, rows), F32),
            term,
            shape((rows, query_width), BF16),
            shape((8, HEAD), F32),
        ],
        (doc_lengths, query_raw, key_raw, value_matrix, out_grad, query_gain, key_gain),
        cost(4_000_000, 6_000_000),
        far=7,
        scratch=[
            pltpu.SMEM(doc_lengths.shape, jnp.int32),
            pltpu.VMEM((rows, query_width), BF16),
            pltpu.VMEM((rows, width), BF16),
            pltpu.SemaphoreType.DMA((7,)),
        ],
    )
    near_value, far_value = shift(values, 1), shift(values, 2)
    exps, inverse, halo_across, halo_scaled, far_value_term, near_value_term, own_value = call(
        attend_keys_kernel,
        "attend_keys",
        [
            shape((heads * keys, query_heads // heads * rows), F32),
            shape((heads, query_heads // heads * rows), F32),
            shape((width, WINDOW), BF16),
            shape((heads * WINDOW, HEAD), F32),
            term,
            term,
            own,
        ],
        (near_key, far_key, grads_out, query_rot, key_rot, cos, sin, bias, gains),
        cost(400_000_000, 4_000_000, 800_000),
    )
    near_value_back, far_value_back = shift(near_value_term, -1), shift(far_value_term, -2)
    far_key_term, near_key_term, own_key, query_grad, copies = call(
        attend_values_kernel,
        "attend_values",
        [term, term, own, shape((query_width, rows), BF16), shape((devices, 2, HEAD), F32)],
        (
            near_value, far_value, values, grads_out, exps, inverse, query_rot,
            halo_across, key_across, halo_scaled, key_scaled, query_scaled, cos, sin, across,
        ),
        cost(600_000_000, 4_000_000),
    )
    near_key_back, far_key_back = shift(near_key_term, -1), shift(far_key_term, -2)
    parts = lax.all_to_all(copies, AXES, 0, 0)
    mark = shape((8, HEAD), F32)
    grad_value, first_mark = call(
        finish_values_kernel,
        "finish_values",
        [term, mark],
        (own_value, far_value_back, near_value_back),
        cost(1_000_000, 2_000_000),
    )
    grad_query, key_scaled, key_scale = call(
        finish_queries_kernel,
        "finish_queries",
        [
            shape((rows, query_width), BF16),
            shape((heads * rows, HEAD), F32),
            shape((heads * rows, HEAD), F32),
        ],
        (query_raw, key_raw, query_grad, gains),
        cost(4_000_000, 4_000_000),
        far=2,
        scratch=[
            pltpu.VMEM((rows, query_width), BF16),
            pltpu.VMEM((rows, width), BF16),
            pltpu.SemaphoreType.DMA((2,)),
        ],
    )
    grad_key, second_mark = call(
        finish_keys_kernel,
        "finish_keys",
        [term, mark],
        (own_key, far_key_back, near_key_back, key_scaled, key_scale, own_tables, gains, first_mark),
        cost(4_000_000, 3_000_000),
    )
    grad_query_gain, grad_key_gain = call(
        sum_kernel, "sum_gains", [shape((1, HEAD), F32), shape((1, HEAD), F32)], (parts, second_mark)
    )
    return (
        grad_query, grad_key, grad_value, grad_query_gain.reshape(HEAD), grad_key_gain.reshape(HEAD)
    )


def solution(mesh):
    rows = P(AXES, None)
    return jax.shard_map(
        on_device,
        mesh=mesh,
        in_specs=(P(), rows, rows, rows, rows, P(), P()),
        out_specs=(rows, rows, rows, P(), P()),
        check_vma=False,
    )
```

```python
import math

import jax
import jax.numpy as jnp
import numpy as np
from jax import lax
from jax.experimental import pallas as pl
from jax.experimental.pallas import tpu as pltpu
from jax.sharding import PartitionSpec as P

HEAD = 128
HALF = HEAD // 2
WINDOW = 256
EPS = 1e-06
SCALE = 168.0 ** (-0.5)
ROPE_BASE = 10000.0
MASKED = -1e30
AXES = ("ctx", "grp")
F32 = jnp.float32
BF16 = jnp.bfloat16
VMEM_LIMIT = 32 * 1024 * 1024


def frequencies():
    lane = lax.broadcasted_iota(jnp.int32, (1, HEAD), 1) % HALF
    values = jnp.zeros((1, HEAD), F32)
    for m in range(HALF):
        values = jnp.where(lane == m, np.float32(ROPE_BASE ** (-2.0 * m / HEAD)), values)
    return values


def shift(value, steps):
    count = lax.axis_size(AXES)
    return lax.ppermute(value, AXES, [(s, (s + steps) % count) for s in range(count)])


def own_index():
    return lax.axis_index("ctx") * lax.axis_size("grp") + lax.axis_index("grp")


def roll_half(x):
    return pltpu.roll(x, HALF, 1)


def doc_starts(tokens, lengths_ref):
    def step(doc, carry):
        end, starts = carry
        end = end + lengths_ref[doc]
        return end, jnp.where(tokens >= end, end, starts)

    count = lengths_ref.shape[0]
    return lax.fori_loop(
        0, count, step, (jnp.int32(0), jnp.zeros_like(tokens)), unroll=count if count <= 8 else 1
    )[1]


def cos_sin_lanes(angle, lane):
    turns = jnp.floor(angle * (2.0 / math.pi) + 0.5)
    r = angle - turns * 1.5703125
    r = r - turns * 4.837512969970703125e-4
    r = r - turns * 7.549789948768648e-8
    z = r * r
    sin_r = r + r * z * (-1.6666654611e-1 + z * (8.3321608736e-3 + z * -1.9515295891e-4))
    cos_r = 1.0 - 0.5 * z + z * z * (
        4.166664568298827e-2 + z * (-1.388731625493765e-3 + z * 2.443315711809948e-5)
    )
    quadrant = turns.astype(jnp.int32) - jnp.where(lane >= HALF, 1, 0)
    odd = (quadrant & 1) == 1
    value = jnp.where(odd, sin_r, cos_r)
    negative = ((quadrant + 1) & 2) == 2
    return jnp.where(negative, -value, value)


def ones(rows, columns):
    return jnp.ones((rows, columns), BF16)


def split(x):
    high = x.astype(BF16)
    low = (x - high.astype(F32)).astype(BF16)
    return jnp.concatenate([high, low], 1)


def row_sums(x):
    return jnp.dot(split(x), ones(2 * HEAD, HEAD), preferred_element_type=F32)


def row_scale(x):
    return lax.rsqrt(row_sums(x * x) * (1.0 / HEAD) + EPS)


def turning(steps=HALF):
    source = lax.broadcasted_iota(jnp.int32, (HEAD, HEAD), 0)
    target = lax.broadcasted_iota(jnp.int32, (HEAD, HEAD), 1)
    return jnp.where(target == (source + steps) % HEAD, 1.0, 0.0).astype(BF16)


def turned_rows(raw, matrix):
    return jnp.dot(raw, matrix, preferred_element_type=F32)


def turned_gain(gain):
    return roll_half(jnp.broadcast_to(gain, (8, HEAD)))[:1]


def prepare_kernel(
    lengths_hbm, query_hbm, key_hbm, value_hbm, out_grad_hbm, query_gain_hbm, key_gain_hbm,
    query_rot_ref, query_scaled_ref, key_rot_ref, key_across_ref,
    key_scaled_ref, cos_ref, sin_ref, own_tables_ref, across_ref, bias_ref,
    value_ref, out_grad_ref, gains_ref,
    lengths_ref, query_ref, key_ref, sems,
):
    moves = [
        pltpu.make_async_copy(source, target, sems.at[place])
        for place, (source, target) in enumerate(
            (
                (lengths_hbm, lengths_ref),
                (query_gain_hbm, gains_ref.at[0:1]),
                (key_gain_hbm, gains_ref.at[1:2]),
                (key_hbm, key_ref),
                (query_hbm, query_ref),
                (out_grad_hbm, out_grad_ref),
                (value_hbm, value_ref),
            )
        )
    ]
    for move in moves:
        move.start()
    rows = query_ref.shape[0]
    keys = cos_ref.shape[0]
    base = own_index() * rows - (keys - rows)
    shape = (keys, HEAD)
    lane = lax.broadcasted_iota(jnp.int32, shape, 1)
    tokens = base + lax.broadcasted_iota(jnp.int32, shape, 0)
    frequency = frequencies()
    moves[0].wait()
    positions = tokens - doc_starts(tokens, lengths_ref)
    mixed = cos_sin_lanes(positions.astype(F32) * frequency, lane)
    turned = roll_half(mixed)
    cos = jnp.where(lane < HALF, mixed, turned)
    sin = jnp.where(lane < HALF, -turned, mixed)
    cos_ref[...] = cos
    sin_ref[...] = sin
    queries = base + (keys - rows) + lax.broadcasted_iota(jnp.int32, (1, rows), 1)
    lowest = jnp.maximum(doc_starts(queries, lengths_ref), queries - (WINDOW - 1))
    key_tokens = base + lax.broadcasted_iota(jnp.int32, (keys, rows), 0)
    visible = (key_tokens >= lowest) & (key_tokens <= queries)
    bias_ref[...] = jnp.where(visible, 0.0, MASKED)
    own_cos, own_sin = cos[keys - rows :], sin[keys - rows :]
    moves[1].wait()
    moves[2].wait()
    own_tables_ref[0] = own_cos * SCALE
    own_tables_ref[1] = own_sin * SCALE
    across_ref[0] = own_cos.T
    across_ref[1] = own_sin.T
    matrix = turning()
    for raw_ref, move, row, rot_ref in (
        (key_ref, moves[3], 1, key_rot_ref),
        (query_ref, moves[4], 0, query_rot_ref),
    ):
        gain = gains_ref[row : row + 1]
        cos_gain = own_cos * gain
        sin_gain = own_sin * turned_gain(gain)
        move.wait()
        for head in range(raw_ref.shape[1] // HEAD):
            part = slice(head * rows, (head + 1) * rows)
            across = slice(head * HEAD, (head + 1) * HEAD)
            raw = raw_ref[:, across]
            x = raw.astype(F32)
            scale = row_scale(x)
            scaled = x * scale
            turned = turned_rows(raw, matrix) * scale
            rotated = scaled * cos_gain + turned * sin_gain
            rot_ref[part, :] = rotated.astype(BF16)
            if raw_ref is key_ref:
                key_scaled_ref[part, :] = scaled
                key_across_ref[across, :] = rotated.T.astype(BF16)
            else:
                query_scaled_ref[across, :] = scaled.T
    moves[5].wait()
    moves[6].wait()


def stacked(ref, head, group):
    return jnp.concatenate(
        [ref[:, (head * group + one) * HEAD : (head * group + one + 1) * HEAD] for one in range(group)],
        0,
    )


def attend_keys_kernel(
    near_ref, far_ref, out_grad_ref, query_rot_ref, key_rot_ref, cos_ref, sin_ref, bias_ref,
    gains_ref,
    exps_ref, inverse_ref, halo_across_ref, halo_scaled_ref, far_value_ref, near_value_ref, own_value_ref,
):
    rows = far_ref.shape[0]
    heads = far_ref.shape[1] // HEAD
    group = out_grad_ref.shape[1] // far_ref.shape[1]
    halo = WINDOW
    keys = halo + rows
    key_gain = gains_ref[1:2]
    cos_gain = cos_ref[:halo] * key_gain
    sin_gain = sin_ref[:halo] * turned_gain(key_gain)

    matrix, unit = turning(), turning(0)

    def scores_of(head):
        cols = slice(head * HEAD, (head + 1) * HEAD)
        raw = jnp.concatenate([far_ref[:, cols], near_ref[:, cols]], 0)
        x = raw.astype(F32)
        scale = row_scale(x)
        scaled = x * scale
        turned = turned_rows(raw, matrix) * scale
        part = slice(head * halo, (head + 1) * halo)
        halo_scaled_ref[part, :] = scaled
        rotated = (scaled * cos_gain + turned * sin_gain).astype(BF16)
        halo_across_ref[cols, :] = lax.dot_general(
            unit, rotated, (((1,), (1,)), ((), ())), preferred_element_type=F32
        ).astype(BF16)
        both = jnp.concatenate([rotated, key_rot_ref[head * rows : (head + 1) * rows, :]], 0)
        queries = query_rot_ref[head * group * rows : (head + 1) * group * rows, :]
        return lax.dot_general(
            both, queries, (((1,), (1,)), ((), ())), preferred_element_type=F32
        )

    later = scores_of(0)
    for head in range(heads):
        scores = later
        if head + 1 < heads:
            later = scores_of(head + 1)
        cols = slice(head * HEAD, (head + 1) * HEAD)
        low = []
        for one in range(group):
            place = (slice(head * keys, (head + 1) * keys), slice(one * rows, (one + 1) * rows))
            part = scores[:, place[1]] * (SCALE * math.log2(math.e)) + bias_ref[...]
            exps = jnp.exp2(part - jnp.max(part, axis=0, keepdims=True))
            exps_ref[place] = exps
            inverse = 1.0 / jnp.sum(exps, axis=0, keepdims=True)
            inverse_ref[head : head + 1, place[1]] = inverse
            low.append((exps_ref[place] * inverse).astype(BF16))
        value_term = jnp.dot(
            jnp.concatenate(low, 1), stacked(out_grad_ref, head, group), preferred_element_type=F32
        )
        far_value_ref[:, cols] = value_term[:rows].astype(BF16)
        near_value_ref[:, cols] = value_term[rows:halo].astype(BF16)
        own_value_ref[:, cols] = value_term[halo:]


def norm_backward(normed_grad, scaled, scale, gain):
    weighted = normed_grad * gain
    mean = row_sums(weighted * scaled) * (1.0 / HEAD)
    return scale * (weighted - scaled * mean)


def attend_values_kernel(
    near_ref, far_ref, value_ref, out_grad_ref, exps_ref, inverse_ref, query_rot_ref,
    halo_across_ref, key_across_ref, halo_scaled_ref, key_scaled_ref,
    query_scaled_ref, cos_ref, sin_ref, across_ref,
    far_key_ref, near_key_ref, own_key_ref, query_grad_ref, copies_ref,
):
    rows = far_ref.shape[0]
    heads = far_ref.shape[1] // HEAD
    group = out_grad_ref.shape[1] // far_ref.shape[1]
    halo = WINDOW
    keys = halo + rows
    cos_across, sin_across = across_ref[0] * SCALE, across_ref[1] * SCALE
    query_acc = jnp.zeros((HEAD, rows), F32)
    key_acc = jnp.zeros((keys, HEAD), F32)
    key_acc_turned = jnp.zeros((keys, HEAD), F32)

    def prob_grad_of(head):
        cols = slice(head * HEAD, (head + 1) * HEAD)
        values = jnp.concatenate([far_ref[:, cols], near_ref[:, cols], value_ref[:, cols]], 0)
        return lax.dot_general(
            values, stacked(out_grad_ref, head, group), (((1,), (1,)), ((), ())),
            preferred_element_type=F32,
        )

    later = prob_grad_of(0)
    for head in range(heads):
        prob_grad = later
        if head + 1 < heads:
            later = prob_grad_of(head + 1)
        cols = slice(head * HEAD, (head + 1) * HEAD)
        halo_part = slice(head * halo, (head + 1) * halo)
        own_part = slice(head * rows, (head + 1) * rows)
        group_part = slice(head * group * rows, (head + 1) * group * rows)
        score_grads = []
        for one in range(group):
            place = (slice(head * keys, (head + 1) * keys), slice(one * rows, (one + 1) * rows))
            part = prob_grad[:, place[1]]
            inverse = inverse_ref[head : head + 1, place[1]]
            delta = jnp.sum(exps_ref[place] * part, axis=0, keepdims=True) * inverse
            score_grads.append((exps_ref[place] * inverse * (part - delta)).astype(BF16))
        score_grad = jnp.concatenate(score_grads, 1)
        key_term = jnp.dot(score_grad, query_rot_ref[group_part, :], preferred_element_type=F32)
        keys_across = jnp.concatenate([halo_across_ref[cols, :], key_across_ref[cols, :]], 1)
        query_term = jnp.dot(keys_across, score_grad, preferred_element_type=F32)
        halo_key = key_term[:halo].astype(BF16)
        far_key_ref[:, cols] = halo_key[:rows]
        near_key_ref[:, cols] = halo_key[rows:]
        own_key_ref[:, cols] = key_term[halo:]
        scaled = jnp.concatenate([halo_scaled_ref[halo_part, :], key_scaled_ref[own_part, :]], 0)
        key_acc = key_acc + key_term * scaled
        key_acc_turned = key_acc_turned + key_term * roll_half(scaled)
        for one in range(group):
            index = head * group + one
            across = slice(index * HEAD, (index + 1) * HEAD)
            grad = query_term[:, one * rows : (one + 1) * rows]
            turned = jnp.concatenate([grad[HALF:], grad[:HALF]], 0)
            normed_grad = grad * cos_across - turned * sin_across
            query_acc = query_acc + normed_grad * query_scaled_ref[across, :]
            query_grad_ref[across, :] = normed_grad.astype(BF16)
    query_sum = jnp.sum(query_acc.T, axis=0, keepdims=True)
    key_sum = jnp.sum(key_acc * cos_ref[...], axis=0, keepdims=True)
    turned_sum = jnp.sum(key_acc_turned * sin_ref[...], axis=0, keepdims=True)
    key_sum = (key_sum + turned_gain(turned_sum)) * SCALE
    both = jnp.concatenate([query_sum, key_sum], 0)
    copies_ref[...] = jnp.broadcast_to(both[None], copies_ref.shape)


def finish_values_kernel(own_ref, far_ref, near_ref, grad_value_ref, mark_ref):
    mark_ref[...] = jnp.zeros_like(mark_ref)
    total = own_ref[...] + near_ref[...].astype(F32) + far_ref[...].astype(F32)
    grad_value_ref[...] = total.astype(BF16)


def finish_queries_kernel(
    query_hbm, key_hbm, query_grad_ref, gains_ref,
    grad_query_ref, key_scaled_ref, key_scale_ref,
    query_ref, key_ref, sems,
):
    rows = query_ref.shape[0]
    loads = [
        pltpu.make_async_copy(query_hbm, query_ref, sems.at[0]),
        pltpu.make_async_copy(key_hbm, key_ref, sems.at[1]),
    ]
    for load in loads:
        load.start()
    gain = gains_ref[0:1]
    loads[0].wait()
    for head in range(query_ref.shape[1] // HEAD):
        cols = slice(head * HEAD, (head + 1) * HEAD)
        x = query_ref[:, cols].astype(F32)
        scale = row_scale(x)
        normed_grad = query_grad_ref[cols, :].astype(F32).T
        grad_query_ref[:, cols] = norm_backward(normed_grad, x * scale, scale, gain).astype(BF16)
    loads[1].wait()
    for head in range(key_ref.shape[1] // HEAD):
        part = slice(head * rows, (head + 1) * rows)
        x = key_ref[:, head * HEAD : (head + 1) * HEAD].astype(F32)
        scale = row_scale(x)
        key_scale_ref[part, :] = scale
        key_scaled_ref[part, :] = x * scale


def finish_keys_kernel(
    own_ref, far_ref, near_ref, key_scaled_ref, key_scale_ref, tables_ref, gains_ref, mark_ref,
    grad_key_ref, next_ref,
):
    next_ref[...] = mark_ref[...]
    rows = own_ref.shape[0]
    cos, sin = tables_ref[0], tables_ref[1]
    gain = gains_ref[1:2]
    for head in range(own_ref.shape[1] // HEAD):
        cols = slice(head * HEAD, (head + 1) * HEAD)
        part = slice(head * rows, (head + 1) * rows)
        total = own_ref[:, cols] + near_ref[:, cols].astype(F32) + far_ref[:, cols].astype(F32)
        normed_grad = total * cos - roll_half(total) * sin
        grad = norm_backward(normed_grad, key_scaled_ref[part, :], key_scale_ref[part, :], gain)
        grad_key_ref[:, cols] = grad.astype(BF16)


def sum_kernel(parts_ref, mark_ref, query_gain_ref, key_gain_ref):
    sums = jnp.sum(parts_ref[...], axis=0)
    query_gain_ref[...] = sums[:1]
    key_gain_ref[...] = sums[1:]


def call(kernel, name, outs, operands, cost=None, far=0, scratch=()):
    spaces = [pltpu.HBM] * far + [pltpu.VMEM] * (len(operands) - far)
    return pl.pallas_call(
        kernel,
        out_shape=outs,
        in_specs=[pl.BlockSpec(memory_space=space) for space in spaces],
        out_specs=[pl.BlockSpec(memory_space=pltpu.VMEM)] * len(outs),
        scratch_shapes=scratch,
        compiler_params=pltpu.CompilerParams(vmem_limit_bytes=VMEM_LIMIT),
        cost_estimate=cost,
        name=name,
    )(*[pltpu.with_memory_space_constraint(x, pltpu.HBM) for x in operands[:far]], *operands[far:])


def cost(flops, size, exps=0):
    return pl.CostEstimate(flops=flops, bytes_accessed=size, transcendentals=exps)


def shape(dims, dtype):
    return jax.ShapeDtypeStruct(dims, dtype)


def on_device(doc_lengths, query_raw, key_raw, value_matrix, out_grad, query_gain, key_gain):
    rows, query_width = query_raw.shape
    width = key_raw.shape[1]
    heads = width // HEAD
    query_heads = query_width // HEAD
    keys = WINDOW + rows
    devices = lax.axis_size(AXES)
    query_gain = query_gain.reshape(1, HEAD)
    key_gain = key_gain.reshape(1, HEAD)
    near_key, far_key = shift(key_raw, 1), shift(key_raw, 2)
    term = shape((rows, width), BF16)
    own = shape((rows, width), F32)
    (
        query_rot, query_scaled, key_rot, key_across, key_scaled,
        cos, sin, own_tables, across, bias, values, grads_out, gains,
    ) = call(
        prepare_kernel,
        "prepare",
        [
            shape((query_heads * rows, HEAD), BF16),
            shape((query_width, rows), F32),
            shape((heads * rows, HEAD), BF16),
            shape((width, rows), BF16),
            shape((heads * rows, HEAD), F32),
            shape((keys, HEAD), F32),
            shape((keys, HEAD), F32),
            shape((2, rows, HEAD), F32),
            shape((2, HEAD, rows), F32),
            shape((keys, rows), F32),
            term,
            shape((rows, query_width), BF16),
            shape((8, HEAD), F32),
        ],
        (doc_lengths, query_raw, key_raw, value_matrix, out_grad, query_gain, key_gain),
        cost(4_000_000, 6_000_000),
        far=7,
        scratch=[
            pltpu.SMEM(doc_lengths.shape, jnp.int32),
            pltpu.VMEM((rows, query_width), BF16),
            pltpu.VMEM((rows, width), BF16),
            pltpu.SemaphoreType.DMA((7,)),
        ],
    )
    near_value, far_value = shift(values, 1), shift(values, 2)
    exps, inverse, halo_across, halo_scaled, far_value_term, near_value_term, own_value = call(
        attend_keys_kernel,
        "attend_keys",
        [
            shape((heads * keys, query_heads // heads * rows), F32),
            shape((heads, query_heads // heads * rows), F32),
            shape((width, WINDOW), BF16),
            shape((heads * WINDOW, HEAD), F32),
            term,
            term,
            own,
        ],
        (near_key, far_key, grads_out, query_rot, key_rot, cos, sin, bias, gains),
        cost(400_000_000, 4_000_000, 800_000),
    )
    near_value_back, far_value_back = shift(near_value_term, -1), shift(far_value_term, -2)
    far_key_term, near_key_term, own_key, query_grad, copies = call(
        attend_values_kernel,
        "attend_values",
        [term, term, own, shape((query_width, rows), BF16), shape((devices, 2, HEAD), F32)],
        (
            near_value, far_value, values, grads_out, exps, inverse, query_rot,
            halo_across, key_across, halo_scaled, key_scaled, query_scaled, cos, sin, across,
        ),
        cost(600_000_000, 4_000_000),
    )
    near_key_back, far_key_back = shift(near_key_term, -1), shift(far_key_term, -2)
    parts = lax.all_to_all(copies, AXES, 0, 0)
    mark = shape((8, HEAD), F32)
    grad_value, first_mark = call(
        finish_values_kernel,
        "finish_values",
        [term, mark],
        (own_value, far_value_back, near_value_back),
        cost(1_000_000, 2_000_000),
    )
    grad_query, key_scaled, key_scale = call(
        finish_queries_kernel,
        "finish_queries",
        [
            shape((rows, query_width), BF16),
            shape((heads * rows, HEAD), F32),
            shape((heads * rows, HEAD), F32),
        ],
        (query_raw, key_raw, query_grad, gains),
        cost(4_000_000, 4_000_000),
        far=2,
        scratch=[
            pltpu.VMEM((rows, query_width), BF16),
            pltpu.VMEM((rows, width), BF16),
            pltpu.SemaphoreType.DMA((2,)),
        ],
    )
    grad_key, second_mark = call(
        finish_keys_kernel,
        "finish_keys",
        [term, mark],
        (own_key, far_key_back, near_key_back, key_scaled, key_scale, own_tables, gains, first_mark),
        cost(4_000_000, 3_000_000),
    )
    grad_query_gain, grad_key_gain = call(
        sum_kernel, "sum_gains", [shape((1, HEAD), F32), shape((1, HEAD), F32)], (parts, second_mark)
    )
    return (
        grad_query, grad_key, grad_value, grad_query_gain.reshape(HEAD), grad_key_gain.reshape(HEAD)
    )


def solution(mesh):
    rows = P(AXES, None)
    return jax.shard_map(
        on_device,
        mesh=mesh,
        in_specs=(P(), rows, rows, rows, rows, P(), P()),
        out_specs=(rows, rows, rows, P(), P()),
        check_vma=False,
    )
```

```python
import math

import jax
import jax.numpy as jnp
import numpy as np
from jax import lax
from jax.experimental import pallas as pl
from jax.experimental.pallas import tpu as pltpu
from jax.sharding import PartitionSpec as P

HEAD = 128
HALF = HEAD // 2
WINDOW = 256
EPS = 1e-06
SCALE = 168.0 ** (-0.5)
ROPE_BASE = 10000.0
MASKED = -1e30
AXES = ("ctx", "grp")
F32 = jnp.float32
BF16 = jnp.bfloat16
VMEM_LIMIT = 32 * 1024 * 1024


def frequencies():
    lane = lax.broadcasted_iota(jnp.int32, (1, HEAD), 1) % HALF
    values = jnp.zeros((1, HEAD), F32)
    for m in range(HALF):
        values = jnp.where(lane == m, np.float32(ROPE_BASE ** (-2.0 * m / HEAD)), values)
    return values


def shift(value, steps):
    count = lax.axis_size(AXES)
    return lax.ppermute(value, AXES, [(s, (s + steps) % count) for s in range(count)])


def own_index():
    return lax.axis_index("ctx") * lax.axis_size("grp") + lax.axis_index("grp")


def roll_half(x):
    return pltpu.roll(x, HALF, 1)


def doc_starts(tokens, lengths_ref):
    def step(doc, carry):
        end, starts = carry
        end = end + lengths_ref[doc]
        return end, jnp.where(tokens >= end, end, starts)

    count = lengths_ref.shape[0]
    return lax.fori_loop(
        0, count, step, (jnp.int32(0), jnp.zeros_like(tokens)), unroll=count if count <= 8 else 1
    )[1]


def cos_sin_lanes(angle, lane):
    turns = jnp.floor(angle * (2.0 / math.pi) + 0.5)
    r = angle - turns * 1.5703125
    r = r - turns * 4.837512969970703125e-4
    r = r - turns * 7.549789948768648e-8
    z = r * r
    sin_r = r + r * z * (-1.6666654611e-1 + z * (8.3321608736e-3 + z * -1.9515295891e-4))
    cos_r = 1.0 - 0.5 * z + z * z * (
        4.166664568298827e-2 + z * (-1.388731625493765e-3 + z * 2.443315711809948e-5)
    )
    quadrant = turns.astype(jnp.int32) - jnp.where(lane >= HALF, 1, 0)
    odd = (quadrant & 1) == 1
    value = jnp.where(odd, sin_r, cos_r)
    negative = ((quadrant + 1) & 2) == 2
    return jnp.where(negative, -value, value)


def ones(rows, columns):
    return jnp.ones((rows, columns), BF16)


def split(x):
    high = x.astype(BF16)
    low = (x - high.astype(F32)).astype(BF16)
    return jnp.concatenate([high, low], 1)


def row_sums(x):
    return jnp.dot(split(x), ones(2 * HEAD, HEAD), preferred_element_type=F32)


def row_scale(x):
    return lax.rsqrt(row_sums(x * x) * (1.0 / HEAD) + EPS)


def turning():
    source = lax.broadcasted_iota(jnp.int32, (HEAD, HEAD), 0)
    target = lax.broadcasted_iota(jnp.int32, (HEAD, HEAD), 1)
    return jnp.where(target == (source + HALF) % HEAD, 1.0, 0.0).astype(BF16)


def turned_rows(raw, matrix):
    return jnp.dot(raw, matrix, preferred_element_type=F32)


def turned_gain(gain):
    return roll_half(jnp.broadcast_to(gain, (8, HEAD)))[:1]


def prepare_kernel(
    lengths_hbm, query_hbm, key_hbm, value_hbm, out_grad_hbm, query_gain_hbm, key_gain_hbm,
    query_rot_ref, query_scaled_ref, key_rot_ref, key_across_ref,
    key_scaled_ref, cos_ref, sin_ref, own_tables_ref, across_ref, bias_ref,
    value_ref, out_grad_ref, gains_ref,
    lengths_ref, query_ref, key_ref, sems,
):
    moves = [
        pltpu.make_async_copy(source, target, sems.at[place])
        for place, (source, target) in enumerate(
            (
                (lengths_hbm, lengths_ref),
                (query_gain_hbm, gains_ref.at[0:1]),
                (key_gain_hbm, gains_ref.at[1:2]),
                (key_hbm, key_ref),
                (query_hbm, query_ref),
                (out_grad_hbm, out_grad_ref),
                (value_hbm, value_ref),
            )
        )
    ]
    for move in moves:
        move.start()
    rows = query_ref.shape[0]
    keys = cos_ref.shape[0]
    base = own_index() * rows - (keys - rows)
    shape = (keys, HEAD)
    lane = lax.broadcasted_iota(jnp.int32, shape, 1)
    tokens = base + lax.broadcasted_iota(jnp.int32, shape, 0)
    frequency = frequencies()
    moves[0].wait()
    positions = tokens - doc_starts(tokens, lengths_ref)
    mixed = cos_sin_lanes(positions.astype(F32) * frequency, lane)
    turned = roll_half(mixed)
    cos = jnp.where(lane < HALF, mixed, turned)
    sin = jnp.where(lane < HALF, -turned, mixed)
    cos_ref[...] = cos
    sin_ref[...] = sin
    queries = base + (keys - rows) + lax.broadcasted_iota(jnp.int32, (1, rows), 1)
    lowest = jnp.maximum(doc_starts(queries, lengths_ref), queries - (WINDOW - 1))
    key_tokens = base + lax.broadcasted_iota(jnp.int32, (keys, rows), 0)
    visible = (key_tokens >= lowest) & (key_tokens <= queries)
    bias_ref[...] = jnp.where(visible, 0.0, MASKED)
    own_cos, own_sin = cos[keys - rows :], sin[keys - rows :]
    moves[1].wait()
    moves[2].wait()
    own_tables_ref[0] = own_cos * SCALE
    own_tables_ref[1] = own_sin * SCALE
    across_ref[0] = own_cos.T
    across_ref[1] = own_sin.T
    matrix = turning()
    for raw_ref, move, row, rot_ref in (
        (key_ref, moves[3], 1, key_rot_ref),
        (query_ref, moves[4], 0, query_rot_ref),
    ):
        gain = gains_ref[row : row + 1]
        cos_gain = own_cos * gain
        sin_gain = own_sin * turned_gain(gain)
        move.wait()
        for head in range(raw_ref.shape[1] // HEAD):
            part = slice(head * rows, (head + 1) * rows)
            across = slice(head * HEAD, (head + 1) * HEAD)
            raw = raw_ref[:, across]
            x = raw.astype(F32)
            scale = row_scale(x)
            scaled = x * scale
            turned = turned_rows(raw, matrix) * scale
            rotated = scaled * cos_gain + turned * sin_gain
            rot_ref[part, :] = rotated.astype(BF16)
            if raw_ref is key_ref:
                key_scaled_ref[part, :] = scaled
                key_across_ref[across, :] = rotated.T.astype(BF16)
            else:
                query_scaled_ref[across, :] = scaled.T
    moves[5].wait()
    moves[6].wait()


def stacked(ref, head, group):
    return jnp.concatenate(
        [ref[:, (head * group + one) * HEAD : (head * group + one + 1) * HEAD] for one in range(group)],
        0,
    )


def attend_keys_kernel(
    near_ref, far_ref, out_grad_ref, query_rot_ref, key_rot_ref, cos_ref, sin_ref, bias_ref,
    gains_ref,
    exps_ref, inverse_ref, halo_across_ref, halo_scaled_ref, far_value_ref, near_value_ref, own_value_ref,
):
    rows = far_ref.shape[0]
    heads = far_ref.shape[1] // HEAD
    group = out_grad_ref.shape[1] // far_ref.shape[1]
    halo = WINDOW
    keys = halo + rows
    key_gain = gains_ref[1:2]
    cos_gain = cos_ref[:halo] * key_gain
    sin_gain = sin_ref[:halo] * turned_gain(key_gain)
    matrix = turning()

    def scores_of(head):
        cols = slice(head * HEAD, (head + 1) * HEAD)
        raw = jnp.concatenate([far_ref[:, cols], near_ref[:, cols]], 0)
        x = raw.astype(F32)
        scale = row_scale(x)
        scaled = x * scale
        turned = turned_rows(raw, matrix) * scale
        part = slice(head * halo, (head + 1) * halo)
        halo_scaled_ref[part, :] = scaled
        rotated = scaled * cos_gain + turned * sin_gain
        halo_across_ref[cols, :] = rotated.T.astype(BF16)
        both = jnp.concatenate(
            [rotated.astype(BF16), key_rot_ref[head * rows : (head + 1) * rows, :]], 0
        )
        queries = query_rot_ref[head * group * rows : (head + 1) * group * rows, :]
        return lax.dot_general(
            both, queries, (((1,), (1,)), ((), ())), preferred_element_type=F32
        )

    later = scores_of(0)
    for head in range(heads):
        scores = later
        if head + 1 < heads:
            later = scores_of(head + 1)
        cols = slice(head * HEAD, (head + 1) * HEAD)
        low = []
        for one in range(group):
            place = (slice(head * keys, (head + 1) * keys), slice(one * rows, (one + 1) * rows))
            part = scores[:, place[1]] * (SCALE * math.log2(math.e)) + bias_ref[...]
            exps = jnp.exp2(part - jnp.max(part, axis=0, keepdims=True))
            exps_ref[place] = exps
            inverse = 1.0 / jnp.sum(exps, axis=0, keepdims=True)
            inverse_ref[head : head + 1, place[1]] = inverse
            low.append((exps_ref[place] * inverse).astype(BF16))
        value_term = jnp.dot(
            jnp.concatenate(low, 1), stacked(out_grad_ref, head, group), preferred_element_type=F32
        )
        far_value_ref[:, cols] = value_term[:rows].astype(BF16)
        near_value_ref[:, cols] = value_term[rows:halo].astype(BF16)
        own_value_ref[:, cols] = value_term[halo:]


def norm_backward(normed_grad, scaled, scale, gain):
    weighted = normed_grad * gain
    mean = row_sums(weighted * scaled) * (1.0 / HEAD)
    return scale * (weighted - scaled * mean)


def attend_values_kernel(
    far_ref, near_ref, value_ref, out_grad_ref, exps_ref, inverse_ref, query_rot_ref,
    halo_across_ref, key_across_ref, halo_scaled_ref, key_scaled_ref,
    query_scaled_ref, cos_ref, sin_ref, across_ref,
    far_key_ref, near_key_ref, own_key_ref, query_grad_ref, copies_ref,
):
    rows = far_ref.shape[0]
    heads = far_ref.shape[1] // HEAD
    group = out_grad_ref.shape[1] // far_ref.shape[1]
    halo = WINDOW
    keys = halo + rows
    cos_across, sin_across = across_ref[0] * SCALE, across_ref[1] * SCALE
    query_acc = jnp.zeros((HEAD, rows), F32)
    key_acc = jnp.zeros((keys, HEAD), F32)
    key_acc_turned = jnp.zeros((keys, HEAD), F32)

    def prob_grad_of(head):
        cols = slice(head * HEAD, (head + 1) * HEAD)
        values = jnp.concatenate([far_ref[:, cols], near_ref[:, cols], value_ref[:, cols]], 0)
        return lax.dot_general(
            values, stacked(out_grad_ref, head, group), (((1,), (1,)), ((), ())),
            preferred_element_type=F32,
        )

    later = prob_grad_of(0)
    for head in range(heads):
        prob_grad = later
        if head + 1 < heads:
            later = prob_grad_of(head + 1)
        cols = slice(head * HEAD, (head + 1) * HEAD)
        halo_part = slice(head * halo, (head + 1) * halo)
        own_part = slice(head * rows, (head + 1) * rows)
        group_part = slice(head * group * rows, (head + 1) * group * rows)
        score_grads = []
        for one in range(group):
            place = (slice(head * keys, (head + 1) * keys), slice(one * rows, (one + 1) * rows))
            part = prob_grad[:, place[1]]
            inverse = inverse_ref[head : head + 1, place[1]]
            delta = jnp.sum(exps_ref[place] * part, axis=0, keepdims=True) * inverse
            score_grads.append((exps_ref[place] * inverse * (part - delta)).astype(BF16))
        score_grad = jnp.concatenate(score_grads, 1)
        key_term = jnp.dot(score_grad, query_rot_ref[group_part, :], preferred_element_type=F32)
        keys_across = jnp.concatenate([halo_across_ref[cols, :], key_across_ref[cols, :]], 1)
        query_term = jnp.dot(keys_across, score_grad, preferred_element_type=F32)
        halo_key = key_term[:halo].astype(BF16)
        far_key_ref[:, cols] = halo_key[:rows]
        near_key_ref[:, cols] = halo_key[rows:]
        own_key_ref[:, cols] = key_term[halo:]
        scaled = jnp.concatenate([halo_scaled_ref[halo_part, :], key_scaled_ref[own_part, :]], 0)
        key_acc = key_acc + key_term * scaled
        key_acc_turned = key_acc_turned + key_term * roll_half(scaled)
        for one in range(group):
            index = head * group + one
            across = slice(index * HEAD, (index + 1) * HEAD)
            grad = query_term[:, one * rows : (one + 1) * rows]
            turned = jnp.concatenate([grad[HALF:], grad[:HALF]], 0)
            normed_grad = grad * cos_across - turned * sin_across
            query_acc = query_acc + normed_grad * query_scaled_ref[across, :]
            query_grad_ref[across, :] = normed_grad.astype(BF16)
    query_sum = jnp.sum(query_acc.T, axis=0, keepdims=True)
    key_sum = jnp.sum(key_acc * cos_ref[...], axis=0, keepdims=True)
    turned_sum = jnp.sum(key_acc_turned * sin_ref[...], axis=0, keepdims=True)
    key_sum = (key_sum + turned_gain(turned_sum)) * SCALE
    both = jnp.concatenate([query_sum, key_sum], 0)
    copies_ref[...] = jnp.broadcast_to(both[None], copies_ref.shape)


def finish_values_kernel(own_ref, far_ref, near_ref, grad_value_ref, mark_ref):
    mark_ref[...] = jnp.zeros_like(mark_ref)
    total = own_ref[...] + near_ref[...].astype(F32) + far_ref[...].astype(F32)
    grad_value_ref[...] = total.astype(BF16)


def finish_queries_kernel(
    query_hbm, key_hbm, query_grad_ref, gains_ref,
    grad_query_ref, key_scaled_ref, key_scale_ref,
    query_ref, key_ref, sems,
):
    rows = query_ref.shape[0]
    loads = [
        pltpu.make_async_copy(query_hbm, query_ref, sems.at[0]),
        pltpu.make_async_copy(key_hbm, key_ref, sems.at[1]),
    ]
    for load in loads:
        load.start()
    gain = gains_ref[0:1]
    loads[0].wait()
    for head in range(query_ref.shape[1] // HEAD):
        cols = slice(head * HEAD, (head + 1) * HEAD)
        x = query_ref[:, cols].astype(F32)
        scale = row_scale(x)
        normed_grad = query_grad_ref[cols, :].astype(F32).T
        grad_query_ref[:, cols] = norm_backward(normed_grad, x * scale, scale, gain).astype(BF16)
    loads[1].wait()
    for head in range(key_ref.shape[1] // HEAD):
        part = slice(head * rows, (head + 1) * rows)
        x = key_ref[:, head * HEAD : (head + 1) * HEAD].astype(F32)
        scale = row_scale(x)
        key_scale_ref[part, :] = scale
        key_scaled_ref[part, :] = x * scale


def finish_keys_kernel(
    own_ref, far_ref, near_ref, key_scaled_ref, key_scale_ref, tables_ref, gains_ref, mark_ref,
    grad_key_ref, next_ref,
):
    next_ref[...] = mark_ref[...]
    rows = own_ref.shape[0]
    cos, sin = tables_ref[0], tables_ref[1]
    gain = gains_ref[1:2]
    for head in range(own_ref.shape[1] // HEAD):
        cols = slice(head * HEAD, (head + 1) * HEAD)
        part = slice(head * rows, (head + 1) * rows)
        total = own_ref[:, cols] + near_ref[:, cols].astype(F32) + far_ref[:, cols].astype(F32)
        normed_grad = total * cos - roll_half(total) * sin
        grad = norm_backward(normed_grad, key_scaled_ref[part, :], key_scale_ref[part, :], gain)
        grad_key_ref[:, cols] = grad.astype(BF16)


def sum_kernel(parts_ref, mark_ref, query_gain_ref, key_gain_ref):
    sums = jnp.sum(parts_ref[...], axis=0)
    query_gain_ref[...] = sums[:1]
    key_gain_ref[...] = sums[1:]


def call(kernel, name, outs, operands, cost=None, far=0, scratch=()):
    spaces = [pltpu.HBM] * far + [pltpu.VMEM] * (len(operands) - far)
    return pl.pallas_call(
        kernel,
        out_shape=outs,
        in_specs=[pl.BlockSpec(memory_space=space) for space in spaces],
        out_specs=[pl.BlockSpec(memory_space=pltpu.VMEM)] * len(outs),
        scratch_shapes=scratch,
        compiler_params=pltpu.CompilerParams(vmem_limit_bytes=VMEM_LIMIT),
        cost_estimate=cost,
        name=name,
    )(*[pltpu.with_memory_space_constraint(x, pltpu.HBM) for x in operands[:far]], *operands[far:])


def cost(flops, size, exps=0):
    return pl.CostEstimate(flops=flops, bytes_accessed=size, transcendentals=exps)


def shape(dims, dtype):
    return jax.ShapeDtypeStruct(dims, dtype)


def on_device(doc_lengths, query_raw, key_raw, value_matrix, out_grad, query_gain, key_gain):
    rows, query_width = query_raw.shape
    width = key_raw.shape[1]
    heads = width // HEAD
    query_heads = query_width // HEAD
    keys = WINDOW + rows
    devices = lax.axis_size(AXES)
    query_gain = query_gain.reshape(1, HEAD)
    key_gain = key_gain.reshape(1, HEAD)
    near_key, far_key = shift(key_raw, 1), shift(key_raw, 2)
    term = shape((rows, width), BF16)
    own = shape((rows, width), F32)
    (
        query_rot, query_scaled, key_rot, key_across, key_scaled,
        cos, sin, own_tables, across, bias, values, grads_out, gains,
    ) = call(
        prepare_kernel,
        "prepare",
        [
            shape((query_heads * rows, HEAD), BF16),
            shape((query_width, rows), F32),
            shape((heads * rows, HEAD), BF16),
            shape((width, rows), BF16),
            shape((heads * rows, HEAD), F32),
            shape((keys, HEAD), F32),
            shape((keys, HEAD), F32),
            shape((2, rows, HEAD), F32),
            shape((2, HEAD, rows), F32),
            shape((keys, rows), F32),
            term,
            shape((rows, query_width), BF16),
            shape((8, HEAD), F32),
        ],
        (doc_lengths, query_raw, key_raw, value_matrix, out_grad, query_gain, key_gain),
        cost(4_000_000, 6_000_000),
        far=7,
        scratch=[
            pltpu.SMEM(doc_lengths.shape, jnp.int32),
            pltpu.VMEM((rows, query_width), BF16),
            pltpu.VMEM((rows, width), BF16),
            pltpu.SemaphoreType.DMA((7,)),
        ],
    )
    near_value, far_value = shift(values, 1), shift(values, 2)
    exps, inverse, halo_across, halo_scaled, far_value_term, near_value_term, own_value = call(
        attend_keys_kernel,
        "attend_keys",
        [
            shape((heads * keys, query_heads // heads * rows), F32),
            shape((heads, query_heads // heads * rows), F32),
            shape((width, WINDOW), BF16),
            shape((heads * WINDOW, HEAD), F32),
            term,
            term,
            own,
        ],
        (near_key, far_key, grads_out, query_rot, key_rot, cos, sin, bias, gains),
        cost(400_000_000, 4_000_000, 800_000),
    )
    near_value_back, far_value_back = shift(near_value_term, -1), shift(far_value_term, -2)
    far_key_term, near_key_term, own_key, query_grad, copies = call(
        attend_values_kernel,
        "attend_values",
        [term, term, own, shape((query_width, rows), BF16), shape((devices, 2, HEAD), F32)],
        (
            far_value, near_value, values, grads_out, exps, inverse, query_rot,
            halo_across, key_across, halo_scaled, key_scaled, query_scaled, cos, sin, across,
        ),
        cost(600_000_000, 4_000_000),
    )
    near_key_back, far_key_back = shift(near_key_term, -1), shift(far_key_term, -2)
    parts = lax.all_to_all(copies, AXES, 0, 0)
    mark = shape((8, HEAD), F32)
    grad_value, first_mark = call(
        finish_values_kernel,
        "finish_values",
        [term, mark],
        (own_value, far_value_back, near_value_back),
        cost(1_000_000, 2_000_000),
    )
    grad_query, key_scaled, key_scale = call(
        finish_queries_kernel,
        "finish_queries",
        [
            shape((rows, query_width), BF16),
            shape((heads * rows, HEAD), F32),
            shape((heads * rows, HEAD), F32),
        ],
        (query_raw, key_raw, query_grad, gains),
        cost(4_000_000, 4_000_000),
        far=2,
        scratch=[
            pltpu.VMEM((rows, query_width), BF16),
            pltpu.VMEM((rows, width), BF16),
            pltpu.SemaphoreType.DMA((2,)),
        ],
    )
    grad_key, second_mark = call(
        finish_keys_kernel,
        "finish_keys",
        [term, mark],
        (own_key, far_key_back, near_key_back, key_scaled, key_scale, own_tables, gains, first_mark),
        cost(4_000_000, 3_000_000),
    )
    grad_query_gain, grad_key_gain = call(
        sum_kernel, "sum_gains", [shape((1, HEAD), F32), shape((1, HEAD), F32)], (parts, second_mark)
    )
    return (
        grad_query, grad_key, grad_value, grad_query_gain.reshape(HEAD), grad_key_gain.reshape(HEAD)
    )


def solution(mesh):
    rows = P(AXES, None)
    return jax.shard_map(
        on_device,
        mesh=mesh,
        in_specs=(P(), rows, rows, rows, rows, P(), P()),
        out_specs=(rows, rows, rows, P(), P()),
        check_vma=False,
    )
```

```python
import math

import jax
import jax.numpy as jnp
import numpy as np
from jax import lax
from jax.experimental import pallas as pl
from jax.experimental.pallas import tpu as pltpu
from jax.sharding import PartitionSpec as P

HEAD = 128
HALF = HEAD // 2
WINDOW = 256
EPS = 1e-06
SCALE = 168.0 ** (-0.5)
ROPE_BASE = 10000.0
MASKED = -1e30
AXES = ("ctx", "grp")
F32 = jnp.float32
BF16 = jnp.bfloat16
VMEM_LIMIT = 32 * 1024 * 1024


def frequencies():
    lane = lax.broadcasted_iota(jnp.int32, (1, HEAD), 1) % HALF
    values = jnp.zeros((1, HEAD), F32)
    for m in range(HALF):
        values = jnp.where(lane == m, np.float32(ROPE_BASE ** (-2.0 * m / HEAD)), values)
    return values


def shift(value, steps, cyclic=True):
    count = lax.axis_size(AXES)
    pairs = [(s, (s + steps) % count) for s in range(count)]
    if not cyclic:
        pairs = [(s, t) for s, t in pairs if t - s == steps]
    return lax.ppermute(value, AXES, pairs)


def own_index():
    return lax.axis_index("ctx") * lax.axis_size("grp") + lax.axis_index("grp")


def roll_half(x):
    return pltpu.roll(x, HALF, 1)


def doc_starts(tokens, lengths_ref):
    def step(doc, carry):
        end, starts = carry
        end = end + lengths_ref[doc]
        return end, jnp.where(tokens >= end, end, starts)

    count = lengths_ref.shape[0]
    return lax.fori_loop(
        0, count, step, (jnp.int32(0), jnp.zeros_like(tokens)), unroll=count if count <= 8 else 1
    )[1]


def cos_sin_lanes(angle, lane):
    turns = jnp.floor(angle * (2.0 / math.pi) + 0.5)
    r = angle - turns * 1.5703125
    r = r - turns * 4.837512969970703125e-4
    r = r - turns * 7.549789948768648e-8
    z = r * r
    sin_r = r + r * z * (-1.6666654611e-1 + z * (8.3321608736e-3 + z * -1.9515295891e-4))
    cos_r = 1.0 - 0.5 * z + z * z * (
        4.166664568298827e-2 + z * (-1.388731625493765e-3 + z * 2.443315711809948e-5)
    )
    quadrant = turns.astype(jnp.int32) - jnp.where(lane >= HALF, 1, 0)
    odd = (quadrant & 1) == 1
    value = jnp.where(odd, sin_r, cos_r)
    negative = ((quadrant + 1) & 2) == 2
    return jnp.where(negative, -value, value)


def ones(rows, columns):
    return jnp.ones((rows, columns), BF16)


def split(x):
    high = x.astype(BF16)
    low = (x - high.astype(F32)).astype(BF16)
    return jnp.concatenate([high, low], 1)


def row_sums(x):
    return jnp.dot(split(x), ones(2 * HEAD, HEAD), preferred_element_type=F32)


def row_scale(x):
    return lax.rsqrt(row_sums(x * x) * (1.0 / HEAD) + EPS)


def turning():
    source = lax.broadcasted_iota(jnp.int32, (HEAD, HEAD), 0)
    target = lax.broadcasted_iota(jnp.int32, (HEAD, HEAD), 1)
    return jnp.where(target == (source + HALF) % HEAD, 1.0, 0.0).astype(BF16)


def turned_rows(raw, matrix):
    return jnp.dot(raw, matrix, preferred_element_type=F32)


def turned_gain(gain):
    return roll_half(jnp.broadcast_to(gain, (8, HEAD)))[:1]


def prepare_kernel(
    lengths_hbm, query_hbm, key_hbm, value_hbm, out_grad_hbm, query_gain_hbm, key_gain_hbm,
    query_rot_ref, query_scaled_ref, key_rot_ref, key_across_ref,
    key_scaled_ref, cos_ref, sin_ref, own_tables_ref, across_ref, bias_ref,
    value_ref, out_grad_ref, gains_ref,
    lengths_ref, query_ref, key_ref, sems,
):
    moves = [
        pltpu.make_async_copy(source, target, sems.at[place])
        for place, (source, target) in enumerate(
            (
                (lengths_hbm, lengths_ref),
                (query_gain_hbm, gains_ref.at[0:1]),
                (key_gain_hbm, gains_ref.at[1:2]),
                (key_hbm, key_ref),
                (query_hbm, query_ref),
                (out_grad_hbm, out_grad_ref),
                (value_hbm, value_ref),
            )
        )
    ]
    for move in moves:
        move.start()
    rows = query_ref.shape[0]
    keys = cos_ref.shape[0]
    base = own_index() * rows - (keys - rows)
    shape = (keys, HEAD)
    lane = lax.broadcasted_iota(jnp.int32, shape, 1)
    tokens = base + lax.broadcasted_iota(jnp.int32, shape, 0)
    frequency = frequencies()
    moves[0].wait()
    positions = tokens - doc_starts(tokens, lengths_ref)
    mixed = cos_sin_lanes(positions.astype(F32) * frequency, lane)
    turned = roll_half(mixed)
    cos = jnp.where(lane < HALF, mixed, turned)
    sin = jnp.where(lane < HALF, -turned, mixed)
    cos_ref[...] = cos
    sin_ref[...] = sin
    queries = base + (keys - rows) + lax.broadcasted_iota(jnp.int32, (1, rows), 1)
    lowest = jnp.maximum(doc_starts(queries, lengths_ref), queries - (WINDOW - 1))
    key_tokens = base + lax.broadcasted_iota(jnp.int32, (keys, rows), 0)
    visible = (key_tokens >= lowest) & (key_tokens <= queries)
    bias_ref[...] = jnp.where(visible, 0.0, MASKED)
    own_cos, own_sin = cos[keys - rows :], sin[keys - rows :]
    moves[1].wait()
    moves[2].wait()
    own_tables_ref[0] = own_cos * SCALE
    own_tables_ref[1] = own_sin * SCALE
    across_ref[0] = own_cos.T
    across_ref[1] = own_sin.T
    matrix = turning()
    for raw_ref, move, row, rot_ref in (
        (key_ref, moves[3], 1, key_rot_ref),
        (query_ref, moves[4], 0, query_rot_ref),
    ):
        gain = gains_ref[row : row + 1]
        cos_gain = own_cos * gain
        sin_gain = own_sin * turned_gain(gain)
        move.wait()
        for head in range(raw_ref.shape[1] // HEAD):
            part = slice(head * rows, (head + 1) * rows)
            across = slice(head * HEAD, (head + 1) * HEAD)
            raw = raw_ref[:, across]
            x = raw.astype(F32)
            scale = row_scale(x)
            scaled = x * scale
            turned = turned_rows(raw, matrix) * scale
            rotated = scaled * cos_gain + turned * sin_gain
            rot_ref[part, :] = rotated.astype(BF16)
            if raw_ref is key_ref:
                key_scaled_ref[part, :] = scaled
                key_across_ref[across, :] = rotated.T.astype(BF16)
            else:
                query_scaled_ref[across, :] = scaled.T
    moves[5].wait()
    moves[6].wait()


def stacked(ref, head, group):
    return jnp.concatenate(
        [ref[:, (head * group + one) * HEAD : (head * group + one + 1) * HEAD] for one in range(group)],
        0,
    )


def attend_keys_kernel(
    near_ref, far_ref, out_grad_ref, query_rot_ref, key_rot_ref, cos_ref, sin_ref, bias_ref,
    gains_ref,
    exps_ref, inverse_ref, halo_across_ref, halo_scaled_ref, far_value_ref, near_value_ref, own_value_ref,
):
    rows = far_ref.shape[0]
    heads = far_ref.shape[1] // HEAD
    group = out_grad_ref.shape[1] // far_ref.shape[1]
    halo = WINDOW
    keys = halo + rows
    key_gain = gains_ref[1:2]
    cos_gain = cos_ref[:halo] * key_gain
    sin_gain = sin_ref[:halo] * turned_gain(key_gain)
    matrix = turning()

    def scores_of(head):
        cols = slice(head * HEAD, (head + 1) * HEAD)
        raw = jnp.concatenate([far_ref[:, cols], near_ref[:, cols]], 0)
        x = raw.astype(F32)
        scale = row_scale(x)
        scaled = x * scale
        turned = turned_rows(raw, matrix) * scale
        part = slice(head * halo, (head + 1) * halo)
        halo_scaled_ref[part, :] = scaled
        rotated = scaled * cos_gain + turned * sin_gain
        halo_across_ref[cols, :] = rotated.T.astype(BF16)
        both = jnp.concatenate(
            [rotated.astype(BF16), key_rot_ref[head * rows : (head + 1) * rows, :]], 0
        )
        queries = query_rot_ref[head * group * rows : (head + 1) * group * rows, :]
        return lax.dot_general(
            both, queries, (((1,), (1,)), ((), ())), preferred_element_type=F32
        )

    later = scores_of(0)
    for head in range(heads):
        scores = later
        if head + 1 < heads:
            later = scores_of(head + 1)
        cols = slice(head * HEAD, (head + 1) * HEAD)
        low = []
        for one in range(group):
            place = (slice(head * keys, (head + 1) * keys), slice(one * rows, (one + 1) * rows))
            part = scores[:, place[1]] * (SCALE * math.log2(math.e)) + bias_ref[...]
            exps = jnp.exp2(part - jnp.max(part, axis=0, keepdims=True))
            exps_ref[place] = exps
            inverse = 1.0 / jnp.sum(exps, axis=0, keepdims=True)
            inverse_ref[head : head + 1, place[1]] = inverse
            low.append((exps_ref[place] * inverse).astype(BF16))
        value_term = jnp.dot(
            jnp.concatenate(low, 1), stacked(out_grad_ref, head, group), preferred_element_type=F32
        )
        far_value_ref[:, cols] = value_term[:rows].astype(BF16)
        near_value_ref[:, cols] = value_term[rows:halo].astype(BF16)
        own_value_ref[:, cols] = value_term[halo:]


def norm_backward(normed_grad, scaled, scale, gain):
    weighted = normed_grad * gain
    mean = row_sums(weighted * scaled) * (1.0 / HEAD)
    return scale * (weighted - scaled * mean)


def attend_values_kernel(
    far_ref, near_ref, value_ref, out_grad_ref, exps_ref, inverse_ref, query_rot_ref,
    halo_across_ref, key_across_ref, halo_scaled_ref, key_scaled_ref,
    query_scaled_ref, cos_ref, sin_ref, across_ref,
    far_key_ref, near_key_ref, own_key_ref, query_grad_ref, copies_ref,
):
    rows = far_ref.shape[0]
    heads = far_ref.shape[1] // HEAD
    group = out_grad_ref.shape[1] // far_ref.shape[1]
    halo = WINDOW
    keys = halo + rows
    cos_across, sin_across = across_ref[0] * SCALE, across_ref[1] * SCALE
    query_acc = jnp.zeros((HEAD, rows), F32)
    key_acc = jnp.zeros((keys, HEAD), F32)
    key_acc_turned = jnp.zeros((keys, HEAD), F32)

    def prob_grad_of(head):
        cols = slice(head * HEAD, (head + 1) * HEAD)
        values = jnp.concatenate([far_ref[:, cols], near_ref[:, cols], value_ref[:, cols]], 0)
        return lax.dot_general(
            values, stacked(out_grad_ref, head, group), (((1,), (1,)), ((), ())),
            preferred_element_type=F32,
        )

    later = prob_grad_of(0)
    for head in range(heads):
        prob_grad = later
        if head + 1 < heads:
            later = prob_grad_of(head + 1)
        cols = slice(head * HEAD, (head + 1) * HEAD)
        halo_part = slice(head * halo, (head + 1) * halo)
        own_part = slice(head * rows, (head + 1) * rows)
        group_part = slice(head * group * rows, (head + 1) * group * rows)
        score_grads = []
        for one in range(group):
            place = (slice(head * keys, (head + 1) * keys), slice(one * rows, (one + 1) * rows))
            part = prob_grad[:, place[1]]
            inverse = inverse_ref[head : head + 1, place[1]]
            delta = jnp.sum(exps_ref[place] * part, axis=0, keepdims=True) * inverse
            score_grads.append((exps_ref[place] * inverse * (part - delta)).astype(BF16))
        score_grad = jnp.concatenate(score_grads, 1)
        key_term = jnp.dot(score_grad, query_rot_ref[group_part, :], preferred_element_type=F32)
        keys_across = jnp.concatenate([halo_across_ref[cols, :], key_across_ref[cols, :]], 1)
        query_term = jnp.dot(keys_across, score_grad, preferred_element_type=F32)
        halo_key = key_term[:halo].astype(BF16)
        far_key_ref[:, cols] = halo_key[:rows]
        near_key_ref[:, cols] = halo_key[rows:]
        own_key_ref[:, cols] = key_term[halo:]
        scaled = jnp.concatenate([halo_scaled_ref[halo_part, :], key_scaled_ref[own_part, :]], 0)
        key_acc = key_acc + key_term * scaled
        key_acc_turned = key_acc_turned + key_term * roll_half(scaled)
        for one in range(group):
            index = head * group + one
            across = slice(index * HEAD, (index + 1) * HEAD)
            grad = query_term[:, one * rows : (one + 1) * rows]
            turned = jnp.concatenate([grad[HALF:], grad[:HALF]], 0)
            normed_grad = grad * cos_across - turned * sin_across
            query_acc = query_acc + normed_grad * query_scaled_ref[across, :]
            query_grad_ref[across, :] = normed_grad.astype(BF16)
    query_sum = jnp.sum(query_acc.T, axis=0, keepdims=True)
    key_sum = jnp.sum(key_acc * cos_ref[...], axis=0, keepdims=True)
    turned_sum = jnp.sum(key_acc_turned * sin_ref[...], axis=0, keepdims=True)
    key_sum = (key_sum + turned_gain(turned_sum)) * SCALE
    both = jnp.concatenate([query_sum, key_sum], 0)
    copies_ref[...] = jnp.broadcast_to(both[None], copies_ref.shape)


def finish_values_kernel(own_ref, far_ref, near_ref, grad_value_ref, mark_ref):
    mark_ref[...] = jnp.zeros_like(mark_ref)
    total = own_ref[...] + near_ref[...].astype(F32) + far_ref[...].astype(F32)
    grad_value_ref[...] = total.astype(BF16)


def finish_queries_kernel(
    query_hbm, key_hbm, query_grad_ref, gains_ref,
    grad_query_ref, key_scaled_ref, key_scale_ref,
    query_ref, key_ref, sems,
):
    rows = query_ref.shape[0]
    loads = [
        pltpu.make_async_copy(query_hbm, query_ref, sems.at[0]),
        pltpu.make_async_copy(key_hbm, key_ref, sems.at[1]),
    ]
    for load in loads:
        load.start()
    gain = gains_ref[0:1]
    loads[0].wait()
    for head in range(query_ref.shape[1] // HEAD):
        cols = slice(head * HEAD, (head + 1) * HEAD)
        x = query_ref[:, cols].astype(F32)
        scale = row_scale(x)
        normed_grad = query_grad_ref[cols, :].astype(F32).T
        grad_query_ref[:, cols] = norm_backward(normed_grad, x * scale, scale, gain).astype(BF16)
    loads[1].wait()
    for head in range(key_ref.shape[1] // HEAD):
        part = slice(head * rows, (head + 1) * rows)
        x = key_ref[:, head * HEAD : (head + 1) * HEAD].astype(F32)
        scale = row_scale(x)
        key_scale_ref[part, :] = scale
        key_scaled_ref[part, :] = x * scale


def finish_keys_kernel(
    own_ref, far_ref, near_ref, key_scaled_ref, key_scale_ref, tables_ref, gains_ref, mark_ref,
    grad_key_ref, next_ref,
):
    next_ref[...] = mark_ref[...]
    rows = own_ref.shape[0]
    cos, sin = tables_ref[0], tables_ref[1]
    gain = gains_ref[1:2]
    for head in range(own_ref.shape[1] // HEAD):
        cols = slice(head * HEAD, (head + 1) * HEAD)
        part = slice(head * rows, (head + 1) * rows)
        total = own_ref[:, cols] + near_ref[:, cols].astype(F32) + far_ref[:, cols].astype(F32)
        normed_grad = total * cos - roll_half(total) * sin
        grad = norm_backward(normed_grad, key_scaled_ref[part, :], key_scale_ref[part, :], gain)
        grad_key_ref[:, cols] = grad.astype(BF16)


def sum_kernel(parts_ref, mark_ref, query_gain_ref, key_gain_ref):
    sums = jnp.sum(parts_ref[...], axis=0)
    query_gain_ref[...] = sums[:1]
    key_gain_ref[...] = sums[1:]


def call(kernel, name, outs, operands, cost=None, far=0, scratch=()):
    spaces = [pltpu.HBM] * far + [pltpu.VMEM] * (len(operands) - far)
    return pl.pallas_call(
        kernel,
        out_shape=outs,
        in_specs=[pl.BlockSpec(memory_space=space) for space in spaces],
        out_specs=[pl.BlockSpec(memory_space=pltpu.VMEM)] * len(outs),
        scratch_shapes=scratch,
        compiler_params=pltpu.CompilerParams(vmem_limit_bytes=VMEM_LIMIT),
        cost_estimate=cost,
        name=name,
    )(*[pltpu.with_memory_space_constraint(x, pltpu.HBM) for x in operands[:far]], *operands[far:])


def cost(flops, size, exps=0):
    return pl.CostEstimate(flops=flops, bytes_accessed=size, transcendentals=exps)


def shape(dims, dtype):
    return jax.ShapeDtypeStruct(dims, dtype)


def on_device(doc_lengths, query_raw, key_raw, value_matrix, out_grad, query_gain, key_gain):
    rows, query_width = query_raw.shape
    width = key_raw.shape[1]
    heads = width // HEAD
    query_heads = query_width // HEAD
    keys = WINDOW + rows
    devices = lax.axis_size(AXES)
    query_gain = query_gain.reshape(1, HEAD)
    key_gain = key_gain.reshape(1, HEAD)
    near_key, far_key = shift(key_raw, 1), shift(key_raw, 2, False)
    term = shape((rows, width), BF16)
    own = shape((rows, width), F32)
    (
        query_rot, query_scaled, key_rot, key_across, key_scaled,
        cos, sin, own_tables, across, bias, values, grads_out, gains,
    ) = call(
        prepare_kernel,
        "prepare",
        [
            shape((query_heads * rows, HEAD), BF16),
            shape((query_width, rows), F32),
            shape((heads * rows, HEAD), BF16),
            shape((width, rows), BF16),
            shape((heads * rows, HEAD), F32),
            shape((keys, HEAD), F32),
            shape((keys, HEAD), F32),
            shape((2, rows, HEAD), F32),
            shape((2, HEAD, rows), F32),
            shape((keys, rows), F32),
            term,
            shape((rows, query_width), BF16),
            shape((8, HEAD), F32),
        ],
        (doc_lengths, query_raw, key_raw, value_matrix, out_grad, query_gain, key_gain),
        cost(4_000_000, 6_000_000),
        far=7,
        scratch=[
            pltpu.SMEM(doc_lengths.shape, jnp.int32),
            pltpu.VMEM((rows, query_width), BF16),
            pltpu.VMEM((rows, width), BF16),
            pltpu.SemaphoreType.DMA((7,)),
        ],
    )
    near_value, far_value = shift(values, 1), shift(values, 2)
    exps, inverse, halo_across, halo_scaled, far_value_term, near_value_term, own_value = call(
        attend_keys_kernel,
        "attend_keys",
        [
            shape((heads * keys, query_heads // heads * rows), F32),
            shape((heads, query_heads // heads * rows), F32),
            shape((width, WINDOW), BF16),
            shape((heads * WINDOW, HEAD), F32),
            term,
            term,
            own,
        ],
        (near_key, far_key, grads_out, query_rot, key_rot, cos, sin, bias, gains),
        cost(400_000_000, 4_000_000, 800_000),
    )
    near_value_back, far_value_back = shift(near_value_term, -1), shift(far_value_term, -2)
    far_key_term, near_key_term, own_key, query_grad, copies = call(
        attend_values_kernel,
        "attend_values",
        [term, term, own, shape((query_width, rows), BF16), shape((devices, 2, HEAD), F32)],
        (
            far_value, near_value, values, grads_out, exps, inverse, query_rot,
            halo_across, key_across, halo_scaled, key_scaled, query_scaled, cos, sin, across,
        ),
        cost(600_000_000, 4_000_000),
    )
    near_key_back, far_key_back = shift(near_key_term, -1), shift(far_key_term, -2)
    parts = lax.all_to_all(copies, AXES, 0, 0)
    mark = shape((8, HEAD), F32)
    grad_value, first_mark = call(
        finish_values_kernel,
        "finish_values",
        [term, mark],
        (own_value, far_value_back, near_value_back),
        cost(1_000_000, 2_000_000),
    )
    grad_query, key_scaled, key_scale = call(
        finish_queries_kernel,
        "finish_queries",
        [
            shape((rows, query_width), BF16),
            shape((heads * rows, HEAD), F32),
            shape((heads * rows, HEAD), F32),
        ],
        (query_raw, key_raw, query_grad, gains),
        cost(4_000_000, 4_000_000),
        far=2,
        scratch=[
            pltpu.VMEM((rows, query_width), BF16),
            pltpu.VMEM((rows, width), BF16),
            pltpu.SemaphoreType.DMA((2,)),
        ],
    )
    grad_key, second_mark = call(
        finish_keys_kernel,
        "finish_keys",
        [term, mark],
        (own_key, far_key_back, near_key_back, key_scaled, key_scale, own_tables, gains, first_mark),
        cost(4_000_000, 3_000_000),
    )
    grad_query_gain, grad_key_gain = call(
        sum_kernel, "sum_gains", [shape((1, HEAD), F32), shape((1, HEAD), F32)], (parts, second_mark)
    )
    return (
        grad_query, grad_key, grad_value, grad_query_gain.reshape(HEAD), grad_key_gain.reshape(HEAD)
    )


def solution(mesh):
    rows = P(AXES, None)
    return jax.shard_map(
        on_device,
        mesh=mesh,
        in_specs=(P(), rows, rows, rows, rows, P(), P()),
        out_specs=(rows, rows, rows, P(), P()),
        check_vma=False,
    )
```

```python
import math

import jax
import jax.numpy as jnp
import numpy as np
from jax import lax
from jax.experimental import pallas as pl
from jax.experimental.pallas import tpu as pltpu
from jax.sharding import PartitionSpec as P

HEAD = 128
HALF = HEAD // 2
WINDOW = 256
EPS = 1e-06
SCALE = 168.0 ** (-0.5)
ROPE_BASE = 10000.0
MASKED = -1e30
AXES = ("ctx", "grp")
F32 = jnp.float32
BF16 = jnp.bfloat16
VMEM_LIMIT = 32 * 1024 * 1024


def frequencies():
    lane = lax.broadcasted_iota(jnp.int32, (1, HEAD), 1) % HALF
    values = jnp.zeros((1, HEAD), F32)
    for m in range(HALF):
        values = jnp.where(lane == m, np.float32(ROPE_BASE ** (-2.0 * m / HEAD)), values)
    return values


def shift(value, steps):
    count = lax.axis_size(AXES)
    return lax.ppermute(value, AXES, [(s, (s + steps) % count) for s in range(count)])


def own_index():
    return lax.axis_index("ctx") * lax.axis_size("grp") + lax.axis_index("grp")


def roll_half(x):
    return pltpu.roll(x, HALF, 1)


def doc_starts(tokens, lengths_ref):
    def step(doc, carry):
        end, starts = carry
        end = end + lengths_ref[doc]
        return end, jnp.where(tokens >= end, end, starts)

    count = lengths_ref.shape[0]
    return lax.fori_loop(
        0, count, step, (jnp.int32(0), jnp.zeros_like(tokens)), unroll=count if count <= 8 else 1
    )[1]


def cos_sin_lanes(angle, lane):
    turns = jnp.floor(angle * (2.0 / math.pi) + 0.5)
    r = angle - turns * 1.5703125
    r = r - turns * 4.837512969970703125e-4
    r = r - turns * 7.549789948768648e-8
    z = r * r
    sin_r = r + r * z * (-1.6666654611e-1 + z * (8.3321608736e-3 + z * -1.9515295891e-4))
    cos_r = 1.0 - 0.5 * z + z * z * (
        4.166664568298827e-2 + z * (-1.388731625493765e-3 + z * 2.443315711809948e-5)
    )
    quadrant = turns.astype(jnp.int32) - jnp.where(lane >= HALF, 1, 0)
    odd = (quadrant & 1) == 1
    value = jnp.where(odd, sin_r, cos_r)
    negative = ((quadrant + 1) & 2) == 2
    return jnp.where(negative, -value, value)


def ones(rows, columns):
    return jnp.ones((rows, columns), BF16)


def split(x):
    high = x.astype(BF16)
    low = (x - high.astype(F32)).astype(BF16)
    return jnp.concatenate([high, low], 1)


def row_sums(x):
    return jnp.dot(split(x), ones(2 * HEAD, HEAD), preferred_element_type=F32)


def row_scale(x):
    return lax.rsqrt(row_sums(x * x) * (1.0 / HEAD) + EPS)


def turning():
    source = lax.broadcasted_iota(jnp.int32, (HEAD, HEAD), 0)
    target = lax.broadcasted_iota(jnp.int32, (HEAD, HEAD), 1)
    return jnp.where(target == (source + HALF) % HEAD, 1.0, 0.0).astype(BF16)


def turned_rows(raw, matrix):
    return jnp.dot(raw, matrix, preferred_element_type=F32)


def turned_gain(gain):
    return roll_half(jnp.broadcast_to(gain, (8, HEAD)))[:1]


def prepare_kernel(
    lengths_hbm, query_hbm, key_hbm, value_hbm, out_grad_hbm, query_gain_hbm, key_gain_hbm,
    query_rot_ref, query_scaled_ref, key_rot_ref, key_across_ref,
    key_scaled_ref, key_turned_ref, cos_ref, sin_ref, own_tables_ref, across_ref, bias_ref,
    value_ref, out_grad_ref, gains_ref,
    lengths_ref, query_ref, key_ref, sems,
):
    moves = [
        pltpu.make_async_copy(source, target, sems.at[place])
        for place, (source, target) in enumerate(
            (
                (lengths_hbm, lengths_ref),
                (query_gain_hbm, gains_ref.at[0:1]),
                (key_gain_hbm, gains_ref.at[1:2]),
                (key_hbm, key_ref),
                (query_hbm, query_ref),
                (out_grad_hbm, out_grad_ref),
                (value_hbm, value_ref),
            )
        )
    ]
    for move in moves:
        move.start()
    rows = query_ref.shape[0]
    keys = cos_ref.shape[0]
    base = own_index() * rows - (keys - rows)
    shape = (keys, HEAD)
    lane = lax.broadcasted_iota(jnp.int32, shape, 1)
    tokens = base + lax.broadcasted_iota(jnp.int32, shape, 0)
    frequency = frequencies()
    moves[0].wait()
    positions = tokens - doc_starts(tokens, lengths_ref)
    mixed = cos_sin_lanes(positions.astype(F32) * frequency, lane)
    turned = roll_half(mixed)
    cos = jnp.where(lane < HALF, mixed, turned)
    sin = jnp.where(lane < HALF, -turned, mixed)
    cos_ref[...] = cos
    sin_ref[...] = sin
    queries = base + (keys - rows) + lax.broadcasted_iota(jnp.int32, (1, rows), 1)
    lowest = jnp.maximum(doc_starts(queries, lengths_ref), queries - (WINDOW - 1))
    key_tokens = base + lax.broadcasted_iota(jnp.int32, (keys, rows), 0)
    visible = (key_tokens >= lowest) & (key_tokens <= queries)
    bias_ref[...] = jnp.where(visible, 0.0, MASKED)
    own_cos, own_sin = cos[keys - rows :], sin[keys - rows :]
    moves[1].wait()
    moves[2].wait()
    own_tables_ref[0] = own_cos * SCALE
    own_tables_ref[1] = own_sin * SCALE
    across_ref[0] = own_cos.T
    across_ref[1] = own_sin.T
    matrix = turning()
    for raw_ref, move, row, rot_ref in (
        (key_ref, moves[3], 1, key_rot_ref),
        (query_ref, moves[4], 0, query_rot_ref),
    ):
        gain = gains_ref[row : row + 1]
        cos_gain = own_cos * gain
        sin_gain = own_sin * turned_gain(gain)
        move.wait()
        for head in range(raw_ref.shape[1] // HEAD):
            part = slice(head * rows, (head + 1) * rows)
            across = slice(head * HEAD, (head + 1) * HEAD)
            raw = raw_ref[:, across]
            x = raw.astype(F32)
            scale = row_scale(x)
            scaled = x * scale
            turned = turned_rows(raw, matrix) * scale
            rotated = scaled * cos_gain + turned * sin_gain
            rot_ref[part, :] = rotated.astype(BF16)
            if raw_ref is key_ref:
                key_scaled_ref[part, :] = scaled
                key_turned_ref[part, :] = turned
                key_across_ref[across, :] = rotated.T.astype(BF16)
            else:
                query_scaled_ref[across, :] = scaled.T
    moves[5].wait()
    moves[6].wait()


def stacked(ref, head, group):
    return jnp.concatenate(
        [ref[:, (head * group + one) * HEAD : (head * group + one + 1) * HEAD] for one in range(group)],
        0,
    )


def attend_keys_kernel(
    near_ref, far_ref, out_grad_ref, query_rot_ref, key_rot_ref, cos_ref, sin_ref, bias_ref,
    gains_ref,
    exps_ref, inverse_ref, halo_across_ref, halo_scaled_ref, halo_turned_ref,
    far_value_ref, near_value_ref, own_value_ref,
):
    rows = far_ref.shape[0]
    heads = far_ref.shape[1] // HEAD
    group = out_grad_ref.shape[1] // far_ref.shape[1]
    halo = WINDOW
    keys = halo + rows
    key_gain = gains_ref[1:2]
    cos_gain = cos_ref[:halo] * key_gain
    sin_gain = sin_ref[:halo] * turned_gain(key_gain)
    matrix = turning()

    def scores_of(head):
        cols = slice(head * HEAD, (head + 1) * HEAD)
        raw = jnp.concatenate([far_ref[:, cols], near_ref[:, cols]], 0)
        x = raw.astype(F32)
        scale = row_scale(x)
        scaled = x * scale
        turned = turned_rows(raw, matrix) * scale
        part = slice(head * halo, (head + 1) * halo)
        halo_scaled_ref[part, :] = scaled
        halo_turned_ref[part, :] = turned
        rotated = scaled * cos_gain + turned * sin_gain
        halo_across_ref[cols, :] = rotated.T.astype(BF16)
        both = jnp.concatenate(
            [rotated.astype(BF16), key_rot_ref[head * rows : (head + 1) * rows, :]], 0
        )
        queries = query_rot_ref[head * group * rows : (head + 1) * group * rows, :]
        return lax.dot_general(
            both, queries, (((1,), (1,)), ((), ())), preferred_element_type=F32
        )

    later = scores_of(0)
    for head in range(heads):
        scores = later
        if head + 1 < heads:
            later = scores_of(head + 1)
        cols = slice(head * HEAD, (head + 1) * HEAD)
        low = []
        for one in range(group):
            place = (slice(head * keys, (head + 1) * keys), slice(one * rows, (one + 1) * rows))
            part = scores[:, place[1]] * (SCALE * math.log2(math.e)) + bias_ref[...]
            exps = jnp.exp2(part - jnp.max(part, axis=0, keepdims=True))
            exps_ref[place] = exps
            inverse = 1.0 / jnp.sum(exps, axis=0, keepdims=True)
            inverse_ref[head : head + 1, place[1]] = inverse
            low.append((exps_ref[place] * inverse).astype(BF16))
        value_term = jnp.dot(
            jnp.concatenate(low, 1), stacked(out_grad_ref, head, group), preferred_element_type=F32
        )
        far_value_ref[:, cols] = value_term[:rows].astype(BF16)
        near_value_ref[:, cols] = value_term[rows:halo].astype(BF16)
        own_value_ref[:, cols] = value_term[halo:]


def norm_backward(normed_grad, scaled, scale, gain):
    weighted = normed_grad * gain
    mean = row_sums(weighted * scaled) * (1.0 / HEAD)
    return scale * (weighted - scaled * mean)


def attend_values_kernel(
    far_ref, near_ref, value_ref, out_grad_ref, exps_ref, inverse_ref, query_rot_ref,
    halo_across_ref, key_across_ref, halo_scaled_ref, halo_turned_ref, key_scaled_ref,
    key_turned_ref, query_scaled_ref, cos_ref, sin_ref, across_ref,
    far_key_ref, near_key_ref, own_key_ref, query_grad_ref, copies_ref,
):
    rows = far_ref.shape[0]
    heads = far_ref.shape[1] // HEAD
    group = out_grad_ref.shape[1] // far_ref.shape[1]
    halo = WINDOW
    keys = halo + rows
    cos_across, sin_across = across_ref[0] * SCALE, across_ref[1] * SCALE
    query_acc = jnp.zeros((HEAD, rows), F32)
    key_acc = jnp.zeros((keys, HEAD), F32)
    key_acc_turned = jnp.zeros((keys, HEAD), F32)

    def prob_grad_of(head):
        cols = slice(head * HEAD, (head + 1) * HEAD)
        values = jnp.concatenate([far_ref[:, cols], near_ref[:, cols], value_ref[:, cols]], 0)
        return lax.dot_general(
            values, stacked(out_grad_ref, head, group), (((1,), (1,)), ((), ())),
            preferred_element_type=F32,
        )

    later = prob_grad_of(0)
    for head in range(heads):
        prob_grad = later
        if head + 1 < heads:
            later = prob_grad_of(head + 1)
        cols = slice(head * HEAD, (head + 1) * HEAD)
        halo_part = slice(head * halo, (head + 1) * halo)
        own_part = slice(head * rows, (head + 1) * rows)
        group_part = slice(head * group * rows, (head + 1) * group * rows)
        score_grads = []
        for one in range(group):
            place = (slice(head * keys, (head + 1) * keys), slice(one * rows, (one + 1) * rows))
            part = prob_grad[:, place[1]]
            inverse = inverse_ref[head : head + 1, place[1]]
            delta = jnp.sum(exps_ref[place] * part, axis=0, keepdims=True) * inverse
            score_grads.append((exps_ref[place] * inverse * (part - delta)).astype(BF16))
        score_grad = jnp.concatenate(score_grads, 1)
        key_term = jnp.dot(score_grad, query_rot_ref[group_part, :], preferred_element_type=F32)
        keys_across = jnp.concatenate([halo_across_ref[cols, :], key_across_ref[cols, :]], 1)
        query_term = jnp.dot(keys_across, score_grad, preferred_element_type=F32)
        halo_key = key_term[:halo].astype(BF16)
        far_key_ref[:, cols] = halo_key[:rows]
        near_key_ref[:, cols] = halo_key[rows:]
        own_key_ref[:, cols] = key_term[halo:]
        scaled = jnp.concatenate([halo_scaled_ref[halo_part, :], key_scaled_ref[own_part, :]], 0)
        key_acc = key_acc + key_term * scaled
        turned = jnp.concatenate([halo_turned_ref[halo_part, :], key_turned_ref[own_part, :]], 0)
        key_acc_turned = key_acc_turned + key_term * turned
        for one in range(group):
            index = head * group + one
            across = slice(index * HEAD, (index + 1) * HEAD)
            grad = query_term[:, one * rows : (one + 1) * rows]
            turned = jnp.concatenate([grad[HALF:], grad[:HALF]], 0)
            normed_grad = grad * cos_across - turned * sin_across
            query_acc = query_acc + normed_grad * query_scaled_ref[across, :]
            query_grad_ref[across, :] = normed_grad.astype(BF16)
    query_sum = jnp.sum(query_acc.T, axis=0, keepdims=True)
    key_sum = jnp.sum(key_acc * cos_ref[...], axis=0, keepdims=True)
    turned_sum = jnp.sum(key_acc_turned * sin_ref[...], axis=0, keepdims=True)
    key_sum = (key_sum + turned_gain(turned_sum)) * SCALE
    both = jnp.concatenate([query_sum, key_sum], 0)
    copies_ref[...] = jnp.broadcast_to(both[None], copies_ref.shape)


def finish_values_kernel(own_ref, far_ref, near_ref, grad_value_ref, mark_ref):
    mark_ref[...] = jnp.zeros_like(mark_ref)
    total = own_ref[...] + near_ref[...].astype(F32) + far_ref[...].astype(F32)
    grad_value_ref[...] = total.astype(BF16)


def finish_queries_kernel(
    query_hbm, key_hbm, query_grad_ref, gains_ref,
    grad_query_ref, key_scaled_ref, key_scale_ref,
    query_ref, key_ref, sems,
):
    rows = query_ref.shape[0]
    loads = [
        pltpu.make_async_copy(query_hbm, query_ref, sems.at[0]),
        pltpu.make_async_copy(key_hbm, key_ref, sems.at[1]),
    ]
    for load in loads:
        load.start()
    gain = gains_ref[0:1]
    loads[0].wait()
    for head in range(query_ref.shape[1] // HEAD):
        cols = slice(head * HEAD, (head + 1) * HEAD)
        x = query_ref[:, cols].astype(F32)
        scale = row_scale(x)
        normed_grad = query_grad_ref[cols, :].astype(F32).T
        grad_query_ref[:, cols] = norm_backward(normed_grad, x * scale, scale, gain).astype(BF16)
    loads[1].wait()
    for head in range(key_ref.shape[1] // HEAD):
        part = slice(head * rows, (head + 1) * rows)
        x = key_ref[:, head * HEAD : (head + 1) * HEAD].astype(F32)
        scale = row_scale(x)
        key_scale_ref[part, :] = scale
        key_scaled_ref[part, :] = x * scale


def finish_keys_kernel(
    own_ref, far_ref, near_ref, key_scaled_ref, key_scale_ref, tables_ref, gains_ref, mark_ref,
    grad_key_ref, next_ref,
):
    next_ref[...] = mark_ref[...]
    rows = own_ref.shape[0]
    cos, sin = tables_ref[0], tables_ref[1]
    gain = gains_ref[1:2]
    for head in range(own_ref.shape[1] // HEAD):
        cols = slice(head * HEAD, (head + 1) * HEAD)
        part = slice(head * rows, (head + 1) * rows)
        total = own_ref[:, cols] + near_ref[:, cols].astype(F32) + far_ref[:, cols].astype(F32)
        normed_grad = total * cos - roll_half(total) * sin
        grad = norm_backward(normed_grad, key_scaled_ref[part, :], key_scale_ref[part, :], gain)
        grad_key_ref[:, cols] = grad.astype(BF16)


def sum_kernel(parts_ref, mark_ref, query_gain_ref, key_gain_ref):
    sums = jnp.sum(parts_ref[...], axis=0)
    query_gain_ref[...] = sums[:1]
    key_gain_ref[...] = sums[1:]


def call(kernel, name, outs, operands, cost=None, far=0, scratch=()):
    spaces = [pltpu.HBM] * far + [pltpu.VMEM] * (len(operands) - far)
    return pl.pallas_call(
        kernel,
        out_shape=outs,
        in_specs=[pl.BlockSpec(memory_space=space) for space in spaces],
        out_specs=[pl.BlockSpec(memory_space=pltpu.VMEM)] * len(outs),
        scratch_shapes=scratch,
        compiler_params=pltpu.CompilerParams(vmem_limit_bytes=VMEM_LIMIT),
        cost_estimate=cost,
        name=name,
    )(*[pltpu.with_memory_space_constraint(x, pltpu.HBM) for x in operands[:far]], *operands[far:])


def cost(flops, size, exps=0):
    return pl.CostEstimate(flops=flops, bytes_accessed=size, transcendentals=exps)


def shape(dims, dtype):
    return jax.ShapeDtypeStruct(dims, dtype)


def on_device(doc_lengths, query_raw, key_raw, value_matrix, out_grad, query_gain, key_gain):
    rows, query_width = query_raw.shape
    width = key_raw.shape[1]
    heads = width // HEAD
    query_heads = query_width // HEAD
    keys = WINDOW + rows
    devices = lax.axis_size(AXES)
    query_gain = query_gain.reshape(1, HEAD)
    key_gain = key_gain.reshape(1, HEAD)
    near_key, far_key = shift(key_raw, 1), shift(key_raw, 2)
    term = shape((rows, width), BF16)
    own = shape((rows, width), F32)
    (
        query_rot, query_scaled, key_rot, key_across, key_scaled, key_turned,
        cos, sin, own_tables, across, bias, values, grads_out, gains,
    ) = call(
        prepare_kernel,
        "prepare",
        [
            shape((query_heads * rows, HEAD), BF16),
            shape((query_width, rows), F32),
            shape((heads * rows, HEAD), BF16),
            shape((width, rows), BF16),
            shape((heads * rows, HEAD), F32),
            shape((heads * rows, HEAD), F32),
            shape((keys, HEAD), F32),
            shape((keys, HEAD), F32),
            shape((2, rows, HEAD), F32),
            shape((2, HEAD, rows), F32),
            shape((keys, rows), F32),
            term,
            shape((rows, query_width), BF16),
            shape((8, HEAD), F32),
        ],
        (doc_lengths, query_raw, key_raw, value_matrix, out_grad, query_gain, key_gain),
        cost(4_000_000, 6_000_000),
        far=7,
        scratch=[
            pltpu.SMEM(doc_lengths.shape, jnp.int32),
            pltpu.VMEM((rows, query_width), BF16),
            pltpu.VMEM((rows, width), BF16),
            pltpu.SemaphoreType.DMA((7,)),
        ],
    )
    near_value, far_value = shift(values, 1), shift(values, 2)
    exps, inverse, halo_across, halo_scaled, halo_turned, far_value_term, near_value_term, own_value = call(
        attend_keys_kernel,
        "attend_keys",
        [
            shape((heads * keys, query_heads // heads * rows), F32),
            shape((heads, query_heads // heads * rows), F32),
            shape((width, WINDOW), BF16),
            shape((heads * WINDOW, HEAD), F32),
            shape((heads * WINDOW, HEAD), F32),
            term,
            term,
            own,
        ],
        (near_key, far_key, grads_out, query_rot, key_rot, cos, sin, bias, gains),
        cost(400_000_000, 4_000_000, 800_000),
    )
    near_value_back, far_value_back = shift(near_value_term, -1), shift(far_value_term, -2)
    far_key_term, near_key_term, own_key, query_grad, copies = call(
        attend_values_kernel,
        "attend_values",
        [term, term, own, shape((query_width, rows), BF16), shape((devices, 2, HEAD), F32)],
        (
            far_value, near_value, values, grads_out, exps, inverse, query_rot,
            halo_across, key_across, halo_scaled, halo_turned, key_scaled, key_turned, query_scaled,
            cos, sin, across,
        ),
        cost(600_000_000, 4_000_000),
    )
    near_key_back, far_key_back = shift(near_key_term, -1), shift(far_key_term, -2)
    parts = lax.all_to_all(copies, AXES, 0, 0)
    mark = shape((8, HEAD), F32)
    grad_value, first_mark = call(
        finish_values_kernel,
        "finish_values",
        [term, mark],
        (own_value, far_value_back, near_value_back),
        cost(1_000_000, 2_000_000),
    )
    grad_query, key_scaled, key_scale = call(
        finish_queries_kernel,
        "finish_queries",
        [
            shape((rows, query_width), BF16),
            shape((heads * rows, HEAD), F32),
            shape((heads * rows, HEAD), F32),
        ],
        (query_raw, key_raw, query_grad, gains),
        cost(4_000_000, 4_000_000),
        far=2,
        scratch=[
            pltpu.VMEM((rows, query_width), BF16),
            pltpu.VMEM((rows, width), BF16),
            pltpu.SemaphoreType.DMA((2,)),
        ],
    )
    grad_key, second_mark = call(
        finish_keys_kernel,
        "finish_keys",
        [term, mark],
        (own_key, far_key_back, near_key_back, key_scaled, key_scale, own_tables, gains, first_mark),
        cost(4_000_000, 3_000_000),
    )
    grad_query_gain, grad_key_gain = call(
        sum_kernel, "sum_gains", [shape((1, HEAD), F32), shape((1, HEAD), F32)], (parts, second_mark)
    )
    return (
        grad_query, grad_key, grad_value, grad_query_gain.reshape(HEAD), grad_key_gain.reshape(HEAD)
    )


def solution(mesh):
    rows = P(AXES, None)
    return jax.shard_map(
        on_device,
        mesh=mesh,
        in_specs=(P(), rows, rows, rows, rows, P(), P()),
        out_specs=(rows, rows, rows, P(), P()),
        check_vma=False,
    )
```

```python
import math

import jax
import jax.numpy as jnp
import numpy as np
from jax import lax
from jax.experimental import pallas as pl
from jax.experimental.pallas import tpu as pltpu
from jax.sharding import PartitionSpec as P

HEAD = 128
HALF = HEAD // 2
WINDOW = 256
EPS = 1e-06
SCALE = 168.0 ** (-0.5)
ROPE_BASE = 10000.0
MASKED = -1e30
AXES = ("ctx", "grp")
F32 = jnp.float32
BF16 = jnp.bfloat16
VMEM_LIMIT = 32 * 1024 * 1024


def frequencies():
    lane = lax.broadcasted_iota(jnp.int32, (1, HEAD), 1) % HALF
    values = jnp.zeros((1, HEAD), F32)
    for m in range(HALF):
        values = jnp.where(lane == m, np.float32(ROPE_BASE ** (-2.0 * m / HEAD)), values)
    return values


def shift(value, steps):
    count = lax.axis_size(AXES)
    return lax.ppermute(value, AXES, [(s, (s + steps) % count) for s in range(count)])


def own_index():
    return lax.axis_index("ctx") * lax.axis_size("grp") + lax.axis_index("grp")


def roll_half(x):
    return pltpu.roll(x, HALF, 1)


def doc_starts(tokens, lengths_ref):
    def step(doc, carry):
        end, starts = carry
        end = end + lengths_ref[doc]
        return end, jnp.where(tokens >= end, end, starts)

    count = lengths_ref.shape[0]
    return lax.fori_loop(
        0, count, step, (jnp.int32(0), jnp.zeros_like(tokens)), unroll=count if count <= 8 else 1
    )[1]


def cos_sin_lanes(angle, lane):
    turns = jnp.floor(angle * (2.0 / math.pi) + 0.5)
    r = angle - turns * 1.5703125
    r = r - turns * 4.837512969970703125e-4
    r = r - turns * 7.549789948768648e-8
    z = r * r
    sin_r = r + r * z * (-1.6666654611e-1 + z * (8.3321608736e-3 + z * -1.9515295891e-4))
    cos_r = 1.0 - 0.5 * z + z * z * (
        4.166664568298827e-2 + z * (-1.388731625493765e-3 + z * 2.443315711809948e-5)
    )
    quadrant = turns.astype(jnp.int32) - jnp.where(lane >= HALF, 1, 0)
    odd = (quadrant & 1) == 1
    value = jnp.where(odd, sin_r, cos_r)
    negative = ((quadrant + 1) & 2) == 2
    return jnp.where(negative, -value, value)


def ones(rows, columns):
    return jnp.ones((rows, columns), BF16)


def split(x):
    high = x.astype(BF16)
    low = (x - high.astype(F32)).astype(BF16)
    return jnp.concatenate([high, low], 1)


def row_sums(x):
    return jnp.dot(split(x), ones(2 * HEAD, HEAD), preferred_element_type=F32)


def row_scale(x):
    return lax.rsqrt(row_sums(x * x) * (1.0 / HEAD) + EPS)


def turning():
    source = lax.broadcasted_iota(jnp.int32, (HEAD, HEAD), 0)
    target = lax.broadcasted_iota(jnp.int32, (HEAD, HEAD), 1)
    return jnp.where(target == (source + HALF) % HEAD, 1.0, 0.0).astype(BF16)


def turned_rows(raw, matrix):
    return jnp.dot(raw, matrix, preferred_element_type=F32)


def turned_gain(gain):
    return roll_half(jnp.broadcast_to(gain, (8, HEAD)))[:1]


def prepare_kernel(
    lengths_hbm, query_hbm, key_hbm, value_hbm, out_grad_hbm, query_gain_hbm, key_gain_hbm,
    query_rot_ref, query_scaled_ref, key_rot_ref, key_across_ref,
    key_scaled_ref, cos_ref, sin_ref, own_tables_ref, across_ref, bias_ref,
    value_ref, out_grad_ref, gains_ref,
    lengths_ref, query_ref, key_ref, sems,
):
    moves = [
        pltpu.make_async_copy(source, target, sems.at[place])
        for place, (source, target) in enumerate(
            (
                (lengths_hbm, lengths_ref),
                (query_gain_hbm, gains_ref.at[0:1]),
                (key_gain_hbm, gains_ref.at[1:2]),
                (key_hbm, key_ref),
                (query_hbm, query_ref),
                (out_grad_hbm, out_grad_ref),
                (value_hbm, value_ref),
            )
        )
    ]
    for move in moves:
        move.start()
    rows = query_ref.shape[0]
    keys = cos_ref.shape[0]
    base = own_index() * rows - (keys - rows)
    shape = (keys, HEAD)
    lane = lax.broadcasted_iota(jnp.int32, shape, 1)
    tokens = base + lax.broadcasted_iota(jnp.int32, shape, 0)
    frequency = frequencies()
    moves[0].wait()
    positions = tokens - doc_starts(tokens, lengths_ref)
    mixed = cos_sin_lanes(positions.astype(F32) * frequency, lane)
    turned = roll_half(mixed)
    cos = jnp.where(lane < HALF, mixed, turned)
    sin = jnp.where(lane < HALF, -turned, mixed)
    cos_ref[...] = cos
    sin_ref[...] = sin
    queries = base + (keys - rows) + lax.broadcasted_iota(jnp.int32, (1, rows), 1)
    lowest = jnp.maximum(doc_starts(queries, lengths_ref), queries - (WINDOW - 1))
    key_tokens = base + lax.broadcasted_iota(jnp.int32, (keys, rows), 0)
    visible = (key_tokens >= lowest) & (key_tokens <= queries)
    bias_ref[...] = jnp.where(visible, 0.0, MASKED)
    own_cos, own_sin = cos[keys - rows :], sin[keys - rows :]
    moves[1].wait()
    moves[2].wait()
    own_tables_ref[0] = own_cos * SCALE
    own_tables_ref[1] = own_sin * SCALE
    across_ref[0] = own_cos.T
    across_ref[1] = own_sin.T
    matrix = turning()
    for raw_ref, move, row, rot_ref in (
        (key_ref, moves[3], 1, key_rot_ref),
        (query_ref, moves[4], 0, query_rot_ref),
    ):
        gain = gains_ref[row : row + 1]
        cos_gain = own_cos * gain
        sin_gain = own_sin * turned_gain(gain)
        move.wait()
        for head in range(raw_ref.shape[1] // HEAD):
            part = slice(head * rows, (head + 1) * rows)
            across = slice(head * HEAD, (head + 1) * HEAD)
            raw = raw_ref[:, across]
            x = raw.astype(F32)
            scale = row_scale(x)
            scaled = x * scale
            turned = turned_rows(raw, matrix) * scale
            rotated = scaled * cos_gain + turned * sin_gain
            rot_ref[part, :] = rotated.astype(BF16)
            if raw_ref is key_ref:
                key_scaled_ref[part, :] = scaled
                key_across_ref[across, :] = rotated.T.astype(BF16)
            else:
                query_scaled_ref[across, :] = scaled.T
    moves[5].wait()
    moves[6].wait()


def stacked(ref, head, group):
    return jnp.concatenate(
        [ref[:, (head * group + one) * HEAD : (head * group + one + 1) * HEAD] for one in range(group)],
        0,
    )


def attend_keys_kernel(
    near_ref, far_ref, out_grad_ref, query_rot_ref, key_rot_ref, cos_ref, sin_ref, bias_ref,
    gains_ref,
    exps_ref, inverse_ref, halo_across_ref, halo_scaled_ref, far_value_ref, near_value_ref, own_value_ref,
):
    rows = far_ref.shape[0]
    heads = far_ref.shape[1] // HEAD
    group = out_grad_ref.shape[1] // far_ref.shape[1]
    halo = WINDOW
    keys = halo + rows
    key_gain = gains_ref[1:2]
    cos_gain = cos_ref[:halo] * key_gain
    sin_gain = sin_ref[:halo] * turned_gain(key_gain)
    matrix = turning()

    def scores_of(head):
        cols = slice(head * HEAD, (head + 1) * HEAD)
        raw = jnp.concatenate([far_ref[:, cols], near_ref[:, cols]], 0)
        x = raw.astype(F32)
        scale = row_scale(x)
        scaled = x * scale
        turned = turned_rows(raw, matrix) * scale
        part = slice(head * halo, (head + 1) * halo)
        halo_scaled_ref[part, :] = scaled
        rotated = scaled * cos_gain + turned * sin_gain
        halo_across_ref[cols, :] = rotated.T.astype(BF16)
        both = jnp.concatenate(
            [rotated.astype(BF16), key_rot_ref[head * rows : (head + 1) * rows, :]], 0
        )
        queries = query_rot_ref[head * group * rows : (head + 1) * group * rows, :]
        return lax.dot_general(
            both, queries, (((1,), (1,)), ((), ())), preferred_element_type=F32
        )

    later = scores_of(0)
    for head in range(heads):
        scores = later
        if head + 1 < heads:
            later = scores_of(head + 1)
        cols = slice(head * HEAD, (head + 1) * HEAD)
        low = []
        for one in range(group):
            place = (slice(head * keys, (head + 1) * keys), slice(one * rows, (one + 1) * rows))
            part = scores[:, place[1]] * (SCALE * math.log2(math.e)) + bias_ref[...]
            exps = jnp.exp2(part - jnp.max(part, axis=0, keepdims=True))
            exps_ref[place] = exps
            inverse = 1.0 / jnp.sum(exps, axis=0, keepdims=True)
            inverse_ref[head : head + 1, place[1]] = inverse
            low.append((exps_ref[place] * inverse).astype(BF16))
        value_term = jnp.dot(
            jnp.concatenate(low, 1), stacked(out_grad_ref, head, group), preferred_element_type=F32
        )
        far_value_ref[:, cols] = value_term[:rows].astype(BF16)
        near_value_ref[:, cols] = value_term[rows:halo].astype(BF16)
        own_value_ref[:, cols] = value_term[halo:]


def norm_backward(normed_grad, scaled, scale, gain):
    weighted = normed_grad * gain
    mean = row_sums(weighted * scaled) * (1.0 / HEAD)
    return scale * (weighted - scaled * mean)


def attend_values_kernel(
    far_ref, near_ref, value_ref, out_grad_ref, exps_ref, inverse_ref, query_rot_ref,
    halo_across_ref, key_across_ref, halo_scaled_ref, key_scaled_ref,
    query_scaled_ref, cos_ref, sin_ref, across_ref,
    far_key_ref, near_key_ref, own_key_ref, query_grad_ref, copies_ref,
):
    rows = far_ref.shape[0]
    heads = far_ref.shape[1] // HEAD
    group = out_grad_ref.shape[1] // far_ref.shape[1]
    halo = WINDOW
    keys = halo + rows
    cos_across, sin_across = across_ref[0] * SCALE, across_ref[1] * SCALE
    query_acc = jnp.zeros((HEAD, rows), F32)
    key_acc = jnp.zeros((keys, HEAD), F32)
    key_acc_turned = jnp.zeros((keys, HEAD), F32)

    def prob_grad_of(head):
        cols = slice(head * HEAD, (head + 1) * HEAD)
        values = jnp.concatenate([far_ref[:, cols], near_ref[:, cols], value_ref[:, cols]], 0)
        return lax.dot_general(
            values, stacked(out_grad_ref, head, group), (((1,), (1,)), ((), ())),
            preferred_element_type=F32,
        )

    later = prob_grad_of(0)
    for head in range(heads):
        prob_grad = later
        if head + 1 < heads:
            later = prob_grad_of(head + 1)
        cols = slice(head * HEAD, (head + 1) * HEAD)
        halo_part = slice(head * halo, (head + 1) * halo)
        own_part = slice(head * rows, (head + 1) * rows)
        group_part = slice(head * group * rows, (head + 1) * group * rows)
        score_grads = []
        for one in range(group):
            place = (slice(head * keys, (head + 1) * keys), slice(one * rows, (one + 1) * rows))
            part = prob_grad[:, place[1]]
            inverse = inverse_ref[head : head + 1, place[1]]
            delta = jnp.sum(exps_ref[place] * part, axis=0, keepdims=True) * inverse
            score_grads.append((exps_ref[place] * inverse * (part - delta)).astype(BF16))
        score_grad = jnp.concatenate(score_grads, 1)
        key_term = jnp.dot(score_grad, query_rot_ref[group_part, :], preferred_element_type=F32)
        keys_across = jnp.concatenate([halo_across_ref[cols, :], key_across_ref[cols, :]], 1)
        query_term = jnp.dot(keys_across, score_grad, preferred_element_type=F32)
        halo_key = key_term[:halo].astype(BF16)
        far_key_ref[:, cols] = halo_key[:rows]
        near_key_ref[:, cols] = halo_key[rows:]
        own_key_ref[:, cols] = key_term[halo:]
        scaled = jnp.concatenate([halo_scaled_ref[halo_part, :], key_scaled_ref[own_part, :]], 0)
        key_acc = key_acc + key_term * scaled
        key_acc_turned = key_acc_turned + key_term * roll_half(scaled)
        for one in range(group):
            index = head * group + one
            across = slice(index * HEAD, (index + 1) * HEAD)
            grad = query_term[:, one * rows : (one + 1) * rows]
            turned = jnp.concatenate([grad[HALF:], grad[:HALF]], 0)
            normed_grad = grad * cos_across - turned * sin_across
            query_acc = query_acc + normed_grad * query_scaled_ref[across, :]
            query_grad_ref[across, :] = normed_grad.astype(BF16)
    query_sum = jnp.sum(query_acc.T, axis=0, keepdims=True)
    key_sum = jnp.sum(key_acc * cos_ref[...], axis=0, keepdims=True)
    turned_sum = jnp.sum(key_acc_turned * sin_ref[...], axis=0, keepdims=True)
    key_sum = (key_sum + turned_gain(turned_sum)) * SCALE
    both = jnp.concatenate([query_sum, key_sum], 0)
    copies_ref[...] = jnp.broadcast_to(both[None], copies_ref.shape)


def finish_values_kernel(own_ref, near_ref, far_ref, grad_value_ref, mark_ref):
    mark_ref[...] = jnp.zeros_like(mark_ref)
    total = own_ref[...] + near_ref[...].astype(F32) + far_ref[...].astype(F32)
    grad_value_ref[...] = total.astype(BF16)


def finish_queries_kernel(
    query_hbm, key_hbm, query_grad_ref, gains_ref,
    grad_query_ref, key_scaled_ref, key_scale_ref,
    query_ref, key_ref, sems,
):
    rows = query_ref.shape[0]
    loads = [
        pltpu.make_async_copy(query_hbm, query_ref, sems.at[0]),
        pltpu.make_async_copy(key_hbm, key_ref, sems.at[1]),
    ]
    for load in loads:
        load.start()
    gain = gains_ref[0:1]
    loads[0].wait()
    for head in range(query_ref.shape[1] // HEAD):
        cols = slice(head * HEAD, (head + 1) * HEAD)
        x = query_ref[:, cols].astype(F32)
        scale = row_scale(x)
        normed_grad = query_grad_ref[cols, :].astype(F32).T
        grad_query_ref[:, cols] = norm_backward(normed_grad, x * scale, scale, gain).astype(BF16)
    loads[1].wait()
    for head in range(key_ref.shape[1] // HEAD):
        part = slice(head * rows, (head + 1) * rows)
        x = key_ref[:, head * HEAD : (head + 1) * HEAD].astype(F32)
        scale = row_scale(x)
        key_scale_ref[part, :] = scale
        key_scaled_ref[part, :] = x * scale


def finish_keys_kernel(
    own_ref, far_ref, near_ref, key_scaled_ref, key_scale_ref, tables_ref, gains_ref, mark_ref,
    grad_key_ref, next_ref,
):
    next_ref[...] = mark_ref[...]
    rows = own_ref.shape[0]
    cos, sin = tables_ref[0], tables_ref[1]
    gain = gains_ref[1:2]
    for head in range(own_ref.shape[1] // HEAD):
        cols = slice(head * HEAD, (head + 1) * HEAD)
        part = slice(head * rows, (head + 1) * rows)
        total = own_ref[:, cols] + near_ref[:, cols].astype(F32) + far_ref[:, cols].astype(F32)
        normed_grad = total * cos - roll_half(total) * sin
        grad = norm_backward(normed_grad, key_scaled_ref[part, :], key_scale_ref[part, :], gain)
        grad_key_ref[:, cols] = grad.astype(BF16)


def sum_kernel(parts_ref, mark_ref, query_gain_ref, key_gain_ref):
    sums = jnp.sum(parts_ref[...], axis=0)
    query_gain_ref[...] = sums[:1]
    key_gain_ref[...] = sums[1:]


def call(kernel, name, outs, operands, cost=None, far=0, scratch=()):
    spaces = [pltpu.HBM] * far + [pltpu.VMEM] * (len(operands) - far)
    return pl.pallas_call(
        kernel,
        out_shape=outs,
        in_specs=[pl.BlockSpec(memory_space=space) for space in spaces],
        out_specs=[pl.BlockSpec(memory_space=pltpu.VMEM)] * len(outs),
        scratch_shapes=scratch,
        compiler_params=pltpu.CompilerParams(vmem_limit_bytes=VMEM_LIMIT),
        cost_estimate=cost,
        name=name,
    )(*[pltpu.with_memory_space_constraint(x, pltpu.HBM) for x in operands[:far]], *operands[far:])


def cost(flops, size, exps=0):
    return pl.CostEstimate(flops=flops, bytes_accessed=size, transcendentals=exps)


def shape(dims, dtype):
    return jax.ShapeDtypeStruct(dims, dtype)


def on_device(doc_lengths, query_raw, key_raw, value_matrix, out_grad, query_gain, key_gain):
    rows, query_width = query_raw.shape
    width = key_raw.shape[1]
    heads = width // HEAD
    query_heads = query_width // HEAD
    keys = WINDOW + rows
    devices = lax.axis_size(AXES)
    query_gain = query_gain.reshape(1, HEAD)
    key_gain = key_gain.reshape(1, HEAD)
    near_key, far_key = shift(key_raw, 1), shift(key_raw, 2)
    term = shape((rows, width), BF16)
    own = shape((rows, width), F32)
    (
        query_rot, query_scaled, key_rot, key_across, key_scaled,
        cos, sin, own_tables, across, bias, values, grads_out, gains,
    ) = call(
        prepare_kernel,
        "prepare",
        [
            shape((query_heads * rows, HEAD), BF16),
            shape((query_width, rows), F32),
            shape((heads * rows, HEAD), BF16),
            shape((width, rows), BF16),
            shape((heads * rows, HEAD), F32),
            shape((keys, HEAD), F32),
            shape((keys, HEAD), F32),
            shape((2, rows, HEAD), F32),
            shape((2, HEAD, rows), F32),
            shape((keys, rows), F32),
            term,
            shape((rows, query_width), BF16),
            shape((8, HEAD), F32),
        ],
        (doc_lengths, query_raw, key_raw, value_matrix, out_grad, query_gain, key_gain),
        cost(4_000_000, 6_000_000),
        far=7,
        scratch=[
            pltpu.SMEM(doc_lengths.shape, jnp.int32),
            pltpu.VMEM((rows, query_width), BF16),
            pltpu.VMEM((rows, width), BF16),
            pltpu.SemaphoreType.DMA((7,)),
        ],
    )
    near_value, far_value = shift(values, 1), shift(values, 2)
    exps, inverse, halo_across, halo_scaled, far_value_term, near_value_term, own_value = call(
        attend_keys_kernel,
        "attend_keys",
        [
            shape((heads * keys, query_heads // heads * rows), F32),
            shape((heads, query_heads // heads * rows), F32),
            shape((width, WINDOW), BF16),
            shape((heads * WINDOW, HEAD), F32),
            term,
            term,
            own,
        ],
        (near_key, far_key, grads_out, query_rot, key_rot, cos, sin, bias, gains),
        cost(400_000_000, 4_000_000, 800_000),
    )
    near_value_back, far_value_back = shift(near_value_term, -1), shift(far_value_term, -2)
    far_key_term, near_key_term, own_key, query_grad, copies = call(
        attend_values_kernel,
        "attend_values",
        [term, term, own, shape((query_width, rows), BF16), shape((devices, 2, HEAD), F32)],
        (
            far_value, near_value, values, grads_out, exps, inverse, query_rot,
            halo_across, key_across, halo_scaled, key_scaled, query_scaled, cos, sin, across,
        ),
        cost(600_000_000, 4_000_000),
    )
    near_key_back, far_key_back = shift(near_key_term, -1), shift(far_key_term, -2)
    parts = lax.all_to_all(copies, AXES, 0, 0)
    mark = shape((8, HEAD), F32)
    grad_value, first_mark = call(
        finish_values_kernel,
        "finish_values",
        [term, mark],
        (own_value, near_value_back, far_value_back),
        cost(1_000_000, 2_000_000),
    )
    grad_query, key_scaled, key_scale = call(
        finish_queries_kernel,
        "finish_queries",
        [
            shape((rows, query_width), BF16),
            shape((heads * rows, HEAD), F32),
            shape((heads * rows, HEAD), F32),
        ],
        (query_raw, key_raw, query_grad, gains),
        cost(4_000_000, 4_000_000),
        far=2,
        scratch=[
            pltpu.VMEM((rows, query_width), BF16),
            pltpu.VMEM((rows, width), BF16),
            pltpu.SemaphoreType.DMA((2,)),
        ],
    )
    grad_key, second_mark = call(
        finish_keys_kernel,
        "finish_keys",
        [term, mark],
        (own_key, far_key_back, near_key_back, key_scaled, key_scale, own_tables, gains, first_mark),
        cost(4_000_000, 3_000_000),
    )
    grad_query_gain, grad_key_gain = call(
        sum_kernel, "sum_gains", [shape((1, HEAD), F32), shape((1, HEAD), F32)], (parts, second_mark)
    )
    return (
        grad_query, grad_key, grad_value, grad_query_gain.reshape(HEAD), grad_key_gain.reshape(HEAD)
    )


def solution(mesh):
    rows = P(AXES, None)
    return jax.shard_map(
        on_device,
        mesh=mesh,
        in_specs=(P(), rows, rows, rows, rows, P(), P()),
        out_specs=(rows, rows, rows, P(), P()),
        check_vma=False,
    )
```

```python
import math

import jax
import jax.numpy as jnp
import numpy as np
from jax import lax
from jax.experimental import pallas as pl
from jax.experimental.pallas import tpu as pltpu
from jax.sharding import PartitionSpec as P

HEAD = 128
HALF = HEAD // 2
WINDOW = 256
EPS = 1e-06
SCALE = 168.0 ** (-0.5)
ROPE_BASE = 10000.0
MASKED = -1e30
AXES = ("ctx", "grp")
F32 = jnp.float32
BF16 = jnp.bfloat16
VMEM_LIMIT = 32 * 1024 * 1024


def frequencies():
    lane = lax.broadcasted_iota(jnp.int32, (1, HEAD), 1) % HALF
    values = jnp.zeros((1, HEAD), F32)
    for m in range(HALF):
        values = jnp.where(lane == m, np.float32(ROPE_BASE ** (-2.0 * m / HEAD)), values)
    return values


def shift(value, steps):
    count = lax.axis_size(AXES)
    return lax.ppermute(value, AXES, [(s, (s + steps) % count) for s in range(count)])


def own_index():
    return lax.axis_index("ctx") * lax.axis_size("grp") + lax.axis_index("grp")


def roll_half(x):
    return pltpu.roll(x, HALF, 1)


def doc_starts(tokens, lengths_ref):
    def step(doc, carry):
        end, starts = carry
        end = end + lengths_ref[doc]
        return end, jnp.where(tokens >= end, end, starts)

    count = lengths_ref.shape[0]
    return lax.fori_loop(
        0, count, step, (jnp.int32(0), jnp.zeros_like(tokens)), unroll=count if count <= 8 else 1
    )[1]


def cos_sin_lanes(angle, lane):
    turns = jnp.floor(angle * (2.0 / math.pi) + 0.5)
    r = angle - turns * 1.5703125
    r = r - turns * 4.837512969970703125e-4
    r = r - turns * 7.549789948768648e-8
    z = r * r
    sin_r = r + r * z * (-1.6666654611e-1 + z * (8.3321608736e-3 + z * -1.9515295891e-4))
    cos_r = 1.0 - 0.5 * z + z * z * (
        4.166664568298827e-2 + z * (-1.388731625493765e-3 + z * 2.443315711809948e-5)
    )
    quadrant = turns.astype(jnp.int32) - jnp.where(lane >= HALF, 1, 0)
    odd = (quadrant & 1) == 1
    value = jnp.where(odd, sin_r, cos_r)
    negative = ((quadrant + 1) & 2) == 2
    return jnp.where(negative, -value, value)


def ones(rows, columns):
    return jnp.ones((rows, columns), BF16)


def split(x):
    high = x.astype(BF16)
    low = (x - high.astype(F32)).astype(BF16)
    return jnp.concatenate([high, low], 1)


def row_sums(x):
    return jnp.dot(split(x), ones(2 * HEAD, HEAD), preferred_element_type=F32)


def row_scale(x):
    return lax.rsqrt(row_sums(x * x) * (1.0 / HEAD) + EPS)


def turning():
    source = lax.broadcasted_iota(jnp.int32, (HEAD, HEAD), 0)
    target = lax.broadcasted_iota(jnp.int32, (HEAD, HEAD), 1)
    return jnp.where(target == (source + HALF) % HEAD, 1.0, 0.0).astype(BF16)


def turned_rows(raw, matrix):
    return jnp.dot(raw, matrix, preferred_element_type=F32)


def turned_gain(gain):
    return roll_half(jnp.broadcast_to(gain, (8, HEAD)))[:1]


def prepare_kernel(
    lengths_hbm, query_hbm, key_hbm, value_hbm, out_grad_hbm, query_gain_hbm, key_gain_hbm,
    query_rot_ref, query_scaled_ref, key_rot_ref, key_across_ref,
    key_scaled_ref, cos_ref, sin_ref, own_tables_ref, across_ref, bias_ref,
    value_ref, out_grad_ref, gains_ref,
    lengths_ref, query_ref, key_ref, sems,
):
    moves = [
        pltpu.make_async_copy(source, target, sems.at[place])
        for place, (source, target) in enumerate(
            (
                (lengths_hbm, lengths_ref),
                (query_gain_hbm, gains_ref.at[0:1]),
                (key_gain_hbm, gains_ref.at[1:2]),
                (key_hbm, key_ref),
                (query_hbm, query_ref),
                (out_grad_hbm, out_grad_ref),
                (value_hbm, value_ref),
            )
        )
    ]
    for move in moves:
        move.start()
    rows = query_ref.shape[0]
    keys = cos_ref.shape[0]
    base = own_index() * rows - (keys - rows)
    shape = (keys, HEAD)
    lane = lax.broadcasted_iota(jnp.int32, shape, 1)
    tokens = base + lax.broadcasted_iota(jnp.int32, shape, 0)
    frequency = frequencies()
    moves[0].wait()
    positions = tokens - doc_starts(tokens, lengths_ref)
    mixed = cos_sin_lanes(positions.astype(F32) * frequency, lane)
    turned = roll_half(mixed)
    cos = jnp.where(lane < HALF, mixed, turned)
    sin = jnp.where(lane < HALF, -turned, mixed)
    cos_ref[...] = cos
    sin_ref[...] = sin
    queries = base + (keys - rows) + lax.broadcasted_iota(jnp.int32, (1, rows), 1)
    lowest = jnp.maximum(doc_starts(queries, lengths_ref), queries - (WINDOW - 1))
    key_tokens = base + lax.broadcasted_iota(jnp.int32, (keys, rows), 0)
    visible = (key_tokens >= lowest) & (key_tokens <= queries)
    bias_ref[...] = jnp.where(visible, 0.0, MASKED)
    own_cos, own_sin = cos[keys - rows :], sin[keys - rows :]
    moves[1].wait()
    moves[2].wait()
    own_tables_ref[0] = own_cos * SCALE
    own_tables_ref[1] = own_sin * SCALE
    across_ref[0] = own_cos.T
    across_ref[1] = own_sin.T
    matrix = turning()
    for raw_ref, move, row, rot_ref in (
        (key_ref, moves[3], 1, key_rot_ref),
        (query_ref, moves[4], 0, query_rot_ref),
    ):
        gain = gains_ref[row : row + 1]
        cos_gain = own_cos * gain
        sin_gain = own_sin * turned_gain(gain)
        move.wait()
        for head in range(raw_ref.shape[1] // HEAD):
            part = slice(head * rows, (head + 1) * rows)
            across = slice(head * HEAD, (head + 1) * HEAD)
            raw = raw_ref[:, across]
            x = raw.astype(F32)
            scale = row_scale(x)
            scaled = x * scale
            turned = turned_rows(raw, matrix) * scale
            rotated = scaled * cos_gain + turned * sin_gain
            rot_ref[part, :] = rotated.astype(BF16)
            if raw_ref is key_ref:
                key_scaled_ref[part, :] = scaled
                key_across_ref[across, :] = rotated.astype(BF16).T
            else:
                query_scaled_ref[across, :] = scaled.T
    moves[5].wait()
    moves[6].wait()


def stacked(ref, head, group):
    return jnp.concatenate(
        [ref[:, (head * group + one) * HEAD : (head * group + one + 1) * HEAD] for one in range(group)],
        0,
    )


def attend_keys_kernel(
    near_ref, far_ref, out_grad_ref, query_rot_ref, key_rot_ref, cos_ref, sin_ref, bias_ref,
    gains_ref,
    exps_ref, inverse_ref, halo_across_ref, halo_scaled_ref, far_value_ref, near_value_ref, own_value_ref,
):
    rows = far_ref.shape[0]
    heads = far_ref.shape[1] // HEAD
    group = out_grad_ref.shape[1] // far_ref.shape[1]
    halo = WINDOW
    keys = halo + rows
    key_gain = gains_ref[1:2]
    cos_gain = cos_ref[:halo] * key_gain
    sin_gain = sin_ref[:halo] * turned_gain(key_gain)
    matrix = turning()

    def scores_of(head):
        cols = slice(head * HEAD, (head + 1) * HEAD)
        raw = jnp.concatenate([far_ref[:, cols], near_ref[:, cols]], 0)
        x = raw.astype(F32)
        scale = row_scale(x)
        scaled = x * scale
        turned = turned_rows(raw, matrix) * scale
        part = slice(head * halo, (head + 1) * halo)
        halo_scaled_ref[part, :] = scaled
        rotated = scaled * cos_gain + turned * sin_gain
        halo_across_ref[cols, :] = rotated.astype(BF16).T
        both = jnp.concatenate(
            [rotated.astype(BF16), key_rot_ref[head * rows : (head + 1) * rows, :]], 0
        )
        queries = query_rot_ref[head * group * rows : (head + 1) * group * rows, :]
        return lax.dot_general(
            both, queries, (((1,), (1,)), ((), ())), preferred_element_type=F32
        )

    later = scores_of(0)
    for head in range(heads):
        scores = later
        if head + 1 < heads:
            later = scores_of(head + 1)
        cols = slice(head * HEAD, (head + 1) * HEAD)
        low = []
        for one in range(group):
            place = (slice(head * keys, (head + 1) * keys), slice(one * rows, (one + 1) * rows))
            part = scores[:, place[1]] * (SCALE * math.log2(math.e)) + bias_ref[...]
            exps = jnp.exp2(part - jnp.max(part, axis=0, keepdims=True))
            exps_ref[place] = exps
            inverse = 1.0 / jnp.sum(exps, axis=0, keepdims=True)
            inverse_ref[head : head + 1, place[1]] = inverse
            low.append((exps_ref[place] * inverse).astype(BF16))
        value_term = jnp.dot(
            jnp.concatenate(low, 1), stacked(out_grad_ref, head, group), preferred_element_type=F32
        )
        far_value_ref[:, cols] = value_term[:rows].astype(BF16)
        near_value_ref[:, cols] = value_term[rows:halo].astype(BF16)
        own_value_ref[:, cols] = value_term[halo:]


def norm_backward(normed_grad, scaled, scale, gain):
    weighted = normed_grad * gain
    mean = row_sums(weighted * scaled) * (1.0 / HEAD)
    return scale * (weighted - scaled * mean)


def attend_values_kernel(
    far_ref, near_ref, value_ref, out_grad_ref, exps_ref, inverse_ref, query_rot_ref,
    halo_across_ref, key_across_ref, halo_scaled_ref, key_scaled_ref,
    query_scaled_ref, cos_ref, sin_ref, across_ref,
    far_key_ref, near_key_ref, own_key_ref, query_grad_ref, copies_ref,
):
    rows = far_ref.shape[0]
    heads = far_ref.shape[1] // HEAD
    group = out_grad_ref.shape[1] // far_ref.shape[1]
    halo = WINDOW
    keys = halo + rows
    cos_across, sin_across = across_ref[0] * SCALE, across_ref[1] * SCALE
    query_acc = jnp.zeros((HEAD, rows), F32)
    key_acc = jnp.zeros((keys, HEAD), F32)
    key_acc_turned = jnp.zeros((keys, HEAD), F32)

    def prob_grad_of(head):
        cols = slice(head * HEAD, (head + 1) * HEAD)
        values = jnp.concatenate([far_ref[:, cols], near_ref[:, cols], value_ref[:, cols]], 0)
        return lax.dot_general(
            values, stacked(out_grad_ref, head, group), (((1,), (1,)), ((), ())),
            preferred_element_type=F32,
        )

    later = prob_grad_of(0)
    for head in range(heads):
        prob_grad = later
        if head + 1 < heads:
            later = prob_grad_of(head + 1)
        cols = slice(head * HEAD, (head + 1) * HEAD)
        halo_part = slice(head * halo, (head + 1) * halo)
        own_part = slice(head * rows, (head + 1) * rows)
        group_part = slice(head * group * rows, (head + 1) * group * rows)
        score_grads = []
        for one in range(group):
            place = (slice(head * keys, (head + 1) * keys), slice(one * rows, (one + 1) * rows))
            part = prob_grad[:, place[1]]
            inverse = inverse_ref[head : head + 1, place[1]]
            delta = jnp.sum(exps_ref[place] * part, axis=0, keepdims=True) * inverse
            score_grads.append((exps_ref[place] * inverse * (part - delta)).astype(BF16))
        score_grad = jnp.concatenate(score_grads, 1)
        key_term = jnp.dot(score_grad, query_rot_ref[group_part, :], preferred_element_type=F32)
        keys_across = jnp.concatenate([halo_across_ref[cols, :], key_across_ref[cols, :]], 1)
        query_term = jnp.dot(keys_across, score_grad, preferred_element_type=F32)
        halo_key = key_term[:halo].astype(BF16)
        far_key_ref[:, cols] = halo_key[:rows]
        near_key_ref[:, cols] = halo_key[rows:]
        own_key_ref[:, cols] = key_term[halo:]
        scaled = jnp.concatenate([halo_scaled_ref[halo_part, :], key_scaled_ref[own_part, :]], 0)
        key_acc = key_acc + key_term * scaled
        key_acc_turned = key_acc_turned + key_term * roll_half(scaled)
        for one in range(group):
            index = head * group + one
            across = slice(index * HEAD, (index + 1) * HEAD)
            grad = query_term[:, one * rows : (one + 1) * rows]
            turned = jnp.concatenate([grad[HALF:], grad[:HALF]], 0)
            normed_grad = grad * cos_across - turned * sin_across
            query_acc = query_acc + normed_grad * query_scaled_ref[across, :]
            query_grad_ref[across, :] = normed_grad.astype(BF16)
    query_sum = jnp.sum(query_acc.T, axis=0, keepdims=True)
    key_sum = jnp.sum(key_acc * cos_ref[...], axis=0, keepdims=True)
    turned_sum = jnp.sum(key_acc_turned * sin_ref[...], axis=0, keepdims=True)
    key_sum = (key_sum + turned_gain(turned_sum)) * SCALE
    both = jnp.concatenate([query_sum, key_sum], 0)
    copies_ref[...] = jnp.broadcast_to(both[None], copies_ref.shape)


def finish_values_kernel(own_ref, far_ref, near_ref, grad_value_ref, mark_ref):
    mark_ref[...] = jnp.zeros_like(mark_ref)
    total = own_ref[...] + near_ref[...].astype(F32) + far_ref[...].astype(F32)
    grad_value_ref[...] = total.astype(BF16)


def finish_queries_kernel(
    query_hbm, key_hbm, query_grad_ref, gains_ref,
    grad_query_ref, key_scaled_ref, key_scale_ref,
    query_ref, key_ref, sems,
):
    rows = query_ref.shape[0]
    loads = [
        pltpu.make_async_copy(query_hbm, query_ref, sems.at[0]),
        pltpu.make_async_copy(key_hbm, key_ref, sems.at[1]),
    ]
    for load in loads:
        load.start()
    gain = gains_ref[0:1]
    loads[0].wait()
    for head in range(query_ref.shape[1] // HEAD):
        cols = slice(head * HEAD, (head + 1) * HEAD)
        x = query_ref[:, cols].astype(F32)
        scale = row_scale(x)
        normed_grad = query_grad_ref[cols, :].astype(F32).T
        grad_query_ref[:, cols] = norm_backward(normed_grad, x * scale, scale, gain).astype(BF16)
    loads[1].wait()
    for head in range(key_ref.shape[1] // HEAD):
        part = slice(head * rows, (head + 1) * rows)
        x = key_ref[:, head * HEAD : (head + 1) * HEAD].astype(F32)
        scale = row_scale(x)
        key_scale_ref[part, :] = scale
        key_scaled_ref[part, :] = x * scale


def finish_keys_kernel(
    own_ref, far_ref, near_ref, key_scaled_ref, key_scale_ref, tables_ref, gains_ref, mark_ref,
    grad_key_ref, next_ref,
):
    next_ref[...] = mark_ref[...]
    rows = own_ref.shape[0]
    cos, sin = tables_ref[0], tables_ref[1]
    gain = gains_ref[1:2]
    for head in range(own_ref.shape[1] // HEAD):
        cols = slice(head * HEAD, (head + 1) * HEAD)
        part = slice(head * rows, (head + 1) * rows)
        total = own_ref[:, cols] + near_ref[:, cols].astype(F32) + far_ref[:, cols].astype(F32)
        normed_grad = total * cos - roll_half(total) * sin
        grad = norm_backward(normed_grad, key_scaled_ref[part, :], key_scale_ref[part, :], gain)
        grad_key_ref[:, cols] = grad.astype(BF16)


def sum_kernel(parts_ref, mark_ref, query_gain_ref, key_gain_ref):
    sums = jnp.sum(parts_ref[...], axis=0)
    query_gain_ref[...] = sums[:1]
    key_gain_ref[...] = sums[1:]


def call(kernel, name, outs, operands, cost=None, far=0, scratch=()):
    spaces = [pltpu.HBM] * far + [pltpu.VMEM] * (len(operands) - far)
    return pl.pallas_call(
        kernel,
        out_shape=outs,
        in_specs=[pl.BlockSpec(memory_space=space) for space in spaces],
        out_specs=[pl.BlockSpec(memory_space=pltpu.VMEM)] * len(outs),
        scratch_shapes=scratch,
        compiler_params=pltpu.CompilerParams(vmem_limit_bytes=VMEM_LIMIT),
        cost_estimate=cost,
        name=name,
    )(*[pltpu.with_memory_space_constraint(x, pltpu.HBM) for x in operands[:far]], *operands[far:])


def cost(flops, size, exps=0):
    return pl.CostEstimate(flops=flops, bytes_accessed=size, transcendentals=exps)


def shape(dims, dtype):
    return jax.ShapeDtypeStruct(dims, dtype)


def on_device(doc_lengths, query_raw, key_raw, value_matrix, out_grad, query_gain, key_gain):
    rows, query_width = query_raw.shape
    width = key_raw.shape[1]
    heads = width // HEAD
    query_heads = query_width // HEAD
    keys = WINDOW + rows
    devices = lax.axis_size(AXES)
    query_gain = query_gain.reshape(1, HEAD)
    key_gain = key_gain.reshape(1, HEAD)
    near_key, far_key = shift(key_raw, 1), shift(key_raw, 2)
    term = shape((rows, width), BF16)
    own = shape((rows, width), F32)
    (
        query_rot, query_scaled, key_rot, key_across, key_scaled,
        cos, sin, own_tables, across, bias, values, grads_out, gains,
    ) = call(
        prepare_kernel,
        "prepare",
        [
            shape((query_heads * rows, HEAD), BF16),
            shape((query_width, rows), F32),
            shape((heads * rows, HEAD), BF16),
            shape((width, rows), BF16),
            shape((heads * rows, HEAD), F32),
            shape((keys, HEAD), F32),
            shape((keys, HEAD), F32),
            shape((2, rows, HEAD), F32),
            shape((2, HEAD, rows), F32),
            shape((keys, rows), F32),
            term,
            shape((rows, query_width), BF16),
            shape((8, HEAD), F32),
        ],
        (doc_lengths, query_raw, key_raw, value_matrix, out_grad, query_gain, key_gain),
        cost(4_000_000, 6_000_000),
        far=7,
        scratch=[
            pltpu.SMEM(doc_lengths.shape, jnp.int32),
            pltpu.VMEM((rows, query_width), BF16),
            pltpu.VMEM((rows, width), BF16),
            pltpu.SemaphoreType.DMA((7,)),
        ],
    )
    near_value, far_value = shift(values, 1), shift(values, 2)
    exps, inverse, halo_across, halo_scaled, far_value_term, near_value_term, own_value = call(
        attend_keys_kernel,
        "attend_keys",
        [
            shape((heads * keys, query_heads // heads * rows), F32),
            shape((heads, query_heads // heads * rows), F32),
            shape((width, WINDOW), BF16),
            shape((heads * WINDOW, HEAD), F32),
            term,
            term,
            own,
        ],
        (near_key, far_key, grads_out, query_rot, key_rot, cos, sin, bias, gains),
        cost(400_000_000, 4_000_000, 800_000),
    )
    near_value_back, far_value_back = shift(near_value_term, -1), shift(far_value_term, -2)
    far_key_term, near_key_term, own_key, query_grad, copies = call(
        attend_values_kernel,
        "attend_values",
        [term, term, own, shape((query_width, rows), BF16), shape((devices, 2, HEAD), F32)],
        (
            far_value, near_value, values, grads_out, exps, inverse, query_rot,
            halo_across, key_across, halo_scaled, key_scaled, query_scaled, cos, sin, across,
        ),
        cost(600_000_000, 4_000_000),
    )
    near_key_back, far_key_back = shift(near_key_term, -1), shift(far_key_term, -2)
    parts = lax.all_to_all(copies, AXES, 0, 0)
    mark = shape((8, HEAD), F32)
    grad_value, first_mark = call(
        finish_values_kernel,
        "finish_values",
        [term, mark],
        (own_value, far_value_back, near_value_back),
        cost(1_000_000, 2_000_000),
    )
    grad_query, key_scaled, key_scale = call(
        finish_queries_kernel,
        "finish_queries",
        [
            shape((rows, query_width), BF16),
            shape((heads * rows, HEAD), F32),
            shape((heads * rows, HEAD), F32),
        ],
        (query_raw, key_raw, query_grad, gains),
        cost(4_000_000, 4_000_000),
        far=2,
        scratch=[
            pltpu.VMEM((rows, query_width), BF16),
            pltpu.VMEM((rows, width), BF16),
            pltpu.SemaphoreType.DMA((2,)),
        ],
    )
    grad_key, second_mark = call(
        finish_keys_kernel,
        "finish_keys",
        [term, mark],
        (own_key, far_key_back, near_key_back, key_scaled, key_scale, own_tables, gains, first_mark),
        cost(4_000_000, 3_000_000),
    )
    grad_query_gain, grad_key_gain = call(
        sum_kernel, "sum_gains", [shape((1, HEAD), F32), shape((1, HEAD), F32)], (parts, second_mark)
    )
    return (
        grad_query, grad_key, grad_value, grad_query_gain.reshape(HEAD), grad_key_gain.reshape(HEAD)
    )


def solution(mesh):
    rows = P(AXES, None)
    return jax.shard_map(
        on_device,
        mesh=mesh,
        in_specs=(P(), rows, rows, rows, rows, P(), P()),
        out_specs=(rows, rows, rows, P(), P()),
        check_vma=False,
    )
```
